32 devices in a mesh: fsdp: 4 (over x, core), ctx: 2 (over y), tp: 4 (over z).
Axes of the slice: x: 2, y: 2, z: 4, core: 2. Of those that a mesh axis runs over, the one named last changes fastest.
Arguments:
- tokens: bfloat16 [4, 2048, 2048], P('fsdp', ('ctx', 'tp')), may hold values from -48 to 48
- segments: int32 [4, 2048], P('fsdp', 'ctx'), may hold values from 0 to 7, as said below
- positions: int32 [4, 2048], P('fsdp', 'ctx'), may hold values from 0 to 2047, as said below
- norm_gain: bfloat16 [2048], P(('fsdp', 'ctx')), may hold values from 0.25 to 1.75
- norm_bias: bfloat16 [2048], P(('fsdp', 'ctx')), may hold values from -3 to 3
- projection_weight: bfloat16 [2048, 3, 2048], P(('fsdp', 'ctx'), None, 'tp'), may hold values from -0.125 to 0.125
- projection_bias: bfloat16 [3, 2048], P(None, 'tp'), may hold values from -3 to 3
- dense_weight: bfloat16 [2048, 2048], P(('fsdp', 'ctx'), 'tp'), may hold values from -0.75 to 0.75
- dense_bias: bfloat16 [2048], P(('fsdp', 'ctx')), may hold values from -3 to 3
- up_weight: bfloat16 [2048, 8192], P(('fsdp', 'ctx'), 'tp'), may hold values from -0.125 to 0.125
- up_bias: bfloat16 [8192], P('tp'), may hold values from -3 to 3
- down_weight: bfloat16 [2048, 8192], P(('fsdp', 'ctx'), 'tp'), may hold values from -0.0625 to 0.0625
- down_bias: bfloat16 [2048], P(('fsdp', 'ctx')), may hold values from -3 to 3
- cotangent: bfloat16 [4, 2048, 2048], P('fsdp', ('ctx', 'tp')), may hold values from -6 to 6
Outputs:
- layer_output: bfloat16 [4, 2048, 2048], P('fsdp', ('ctx', 'tp'))
- input_grad: float32 [4, 2048, 2048], P('fsdp', ('ctx', 'tp'))
- norm_gain_grad: float32 [2048], P(('fsdp', 'ctx'))
- norm_bias_grad: float32 [2048], P(('fsdp', 'ctx'))
- projection_weight_grad: float32 [2048, 3, 2048], P(('fsdp', 'ctx'), None, 'tp')
- projection_bias_grad: float32 [3, 2048], P(None, 'tp')
- dense_weight_grad: float32 [2048, 2048], P(('fsdp', 'ctx'), 'tp')
- dense_bias_grad: float32 [2048], P(('fsdp', 'ctx'))
- up_weight_grad: float32 [2048, 8192], P(('fsdp', 'ctx'), 'tp')
- up_bias_grad: float32 [8192], P('tp')
- down_weight_grad: float32 [2048, 8192], P(('fsdp', 'ctx'), 'tp')
- down_bias_grad: float32 [2048], P(('fsdp', 'ctx'))
The draws below stay inside these ranges and needn't reach their ends.
Inputs may be any that keep to these rules, and one draw needn't show every extreme that they name: `segments`: each sequence holds exactly 8 documents, numbered from 0 in order of place; the tokens at places 2048 // 4 to 1536 of every sequence lie in one document. A token's position counts from its document's first token, except in the first document of a sequence, whose positions run up to 2047 at its last token.
All inputs are finite; a program needn't handle non-finite values.
Results may differ from the reference program's by a relative error of at most 0.011.
Values may be sent and summed in bfloat16 or wider, within the bound.
A program may use at most 192 MiB of HBM per device.

```python
import math
import jax
import jax.numpy as jnp
from jax import lax

D = 2048
H = 32
HD = 64
ROT = 32
FF = 8192
SEQ = 2048
DOCS = 8
SEQS = 4


def packing(key):
    cut_key = jax.random.fold_in(key, 0)
    slot_index = jnp.arange(1, SEQ, dtype=jnp.int32)
    rank_draw = jax.random.randint(cut_key, (SEQS, SEQ - 1), 0, 32768, dtype=jnp.int32)
    barred = ((slot_index > SEQ // 4) & (slot_index <= 3 * SEQ // 4)).astype(jnp.int32)
    scores = rank_draw * (2 * SEQ) + slot_index[None, :] + barred[None, :] * (32768 * 2 * SEQ)
    ignored, picked = lax.top_k(-scores, DOCS - 1)
    cut_points = picked.astype(jnp.int32) + 1
    places = jnp.arange(SEQ, dtype=jnp.int32)
    passed = cut_points[:, None, :] <= places[None, :, None]
    segment = jnp.sum(passed.astype(jnp.int32), axis=2)
    doc_start = jnp.max(jnp.where(passed, cut_points[:, None, :], 0), axis=2)
    first_length = jnp.min(cut_points, axis=1, keepdims=True)
    offset = SEQ - first_length
    position = places[None, :] - doc_start + jnp.where(segment == 0, offset, 0)
    return (segment.astype(jnp.int32), position.astype(jnp.int32))


def draw_segments(key, part):
    return packing(key)[0]


def draw_positions(key, part):
    return packing(key)[1]


def draw_tokens(key, part):
    key = jax.random.fold_in(key, 7)
    base_key, row_key, column_key = jax.random.split(key, 3)
    values = jnp.clip(jax.random.normal(base_key, (SEQS, SEQ, D), jnp.float32), -4.0, 4.0)
    low_end = math.log(0.3)
    high_end = math.log(3.0)
    row_scale = jnp.exp(jax.random.uniform(row_key, (SEQS, SEQ, 1), jnp.float32, low_end, high_end))
    column_scale = jnp.exp(jax.random.uniform(column_key, (1, 1, D), jnp.float32, low_end, high_end))
    return (values * row_scale * column_scale).astype(jnp.bfloat16)


def spiked(values, own_key, source, target, shards_of, factor):
    owner, partner = [(jnp.arange(values.shape[dim]) // (values.shape[dim] // shards_of)).reshape([-1 if axis == dim else 1 for axis in range(values.ndim)]) for dim in (source, target)]
    chosen = jax.random.permutation(own_key, shards_of)[partner]
    strong = (owner == chosen) | (owner == (partner + shards_of // 2) % shards_of)
    return jnp.where(strong, factor * values, values)


def levels(rng, extent, cuts, least, top_value):
    gain = 1.0
    for axis_at, blocks in cuts:
        draws = jax.random.uniform(jax.random.fold_in(jax.random.fold_in(rng, 6), axis_at), (blocks,), jnp.float32, least / len(cuts), top_value / len(cuts))
        gain = gain * jnp.repeat(jnp.exp(draws), extent[axis_at] // blocks).reshape((-1,) + (1,) * (len(extent) - 1 - axis_at))
    return gain


def normal_values(key, dims, scale, most, shards=(), kind=jnp.bfloat16):
    gain = levels(key, dims, shards, -0.22, 0.18) if shards else 1.0
    values = jax.random.normal(key, dims, jnp.float32) * scale * gain
    return jnp.minimum(jnp.maximum(values, -most), most).astype(kind)


def noise_with(rng, dims, scale, reach, pieces, heavy, held_as=jnp.bfloat16):
    result = scale * jax.random.normal(rng, dims, jnp.float32)
    if pieces:
        result = result * levels(rng, dims, pieces, -0.22, 0.18)
    return jnp.clip(spiked(result, jax.random.fold_in(rng, 3), *heavy), -reach, reach).astype(held_as)


def setup_inputs(seed: int = 0) -> dict:
    key_list = jax.random.split(jax.random.key(seed), 15)
    return {
        "tokens": draw_tokens(jax.random.fold_in(key_list[14], 71), 0),
        "segments": draw_segments(jax.random.fold_in(key_list[14], 71), 0),
        "positions": draw_positions(jax.random.fold_in(key_list[14], 71), 0),
        "norm_gain": jnp.clip(1.0 + 0.15 * jax.random.normal(key_list[3], (D,), jnp.float32), 0.25, 1.75).astype(jnp.bfloat16),
        "norm_bias": normal_values(key_list[4], (D,), 0.3, 3.0, ((0, 8),)),
        "projection_weight": normal_values(key_list[5], (D, 3, D), D ** -0.5, 0.125, ((0, 8), (2, 4))),
        "projection_bias": normal_values(key_list[6], (3, D), 0.3, 3.0, ((1, 4),)),
        "dense_weight": normal_values(key_list[7], (D, D), (D // 32) ** -0.5, 0.75, ((0, 8), (1, 4))),
        "dense_bias": normal_values(key_list[8], (D,), 0.3, 3.0, ((0, 8),)),
        "up_weight": normal_values(key_list[9], (D, FF), D ** -0.5, 0.125, ((0, 8), (1, 4))),
        "up_bias": normal_values(key_list[10], (FF,), 0.3, 3.0, ((0, 4),)),
        "down_weight": normal_values(key_list[11], (D, FF), FF ** -0.5, 0.0625, ((0, 8), (1, 4))),
        "down_bias": normal_values(key_list[12], (D,), 0.3, 3.0, ((0, 8),)),
        "cotangent": noise_with(key_list[13], (SEQS, SEQ, D), 1.0, 6.0, ((0, 4), (1, 8)), (0, 2, 4, 2.0)),
    }


@jax.custom_vjp
def low(v):
    return lax.optimization_barrier(v.astype(jnp.bfloat16)).astype(jnp.float32)

@jax.custom_vjp
def low_back(v):
    return v

def low_keep(v):
    return (low(v), None)

def low_pass(kept, grad):
    return (grad,)

def back_keep(v):
    return (v, None)

def back_low(kept, grad):
    return (low(grad),)
low.defvjp(low_keep, low_pass)
low_back.defvjp(back_keep, back_low)
epsilon = 1e-05
big_negative = -1000000000.0
root_two_over_pi = 0.7978845608028654

def product(left, right):
    return jnp.dot(left, right, precision=lax.Precision.HIGHEST, preferred_element_type=jnp.float32)

def layer_norm(values, gain_full, shift_full):
    center = lax.optimization_barrier(jnp.mean(values, axis=-1, keepdims=True))
    centered = values - center
    spread = lax.optimization_barrier(jnp.mean(centered * centered, axis=-1, keepdims=True))
    return centered * lax.rsqrt(spread + epsilon) * gain_full + shift_full

def gelu_new(values):
    return 0.5 * values * (1.0 + jnp.tanh(root_two_over_pi * (values + 0.044715 * values * values * values)))

def angles(position_row):
    exponent = jnp.arange(ROT // 2, dtype=jnp.float32) * 2.0 / ROT
    inverse = 10000.0 ** (-exponent)
    phase_angle = position_row.astype(jnp.float32)[..., None] * inverse
    return (jnp.cos(phase_angle), jnp.sin(phase_angle))

def rotate(values, cosine_table, sine_table):
    half_rot = ROT // 2
    leading = values[..., :half_rot]
    trailing = values[..., half_rot:ROT]
    return jnp.concatenate([leading * cosine_table - trailing * sine_table, trailing * cosine_table + leading * sine_table, values[..., ROT:]], axis=-1)

def layer(params, inputs, segment_row, position_row):
    gain_full, shift_full, proj_matrix, proj_vector, dense_matrix, dense_vector, up_matrix, up_vector, down_matrix, down_vector = params
    score_scale = 1.0 / math.sqrt(HD)
    normed = low(layer_norm(inputs, gain_full, shift_full))
    projected = low_back(product(normed, proj_matrix.reshape(D, 3 * D)) + proj_vector.reshape(3 * D))
    projected = projected.reshape(SEQ, 3, H, HD)
    cosine_table, sine_table = angles(position_row)
    cosine_table = cosine_table[:, None, :]
    sine_table = sine_table[:, None, :]
    query_rows = low(rotate(projected[:, 0], cosine_table, sine_table))
    key_rows = low(rotate(projected[:, 1], cosine_table, sine_table))
    value_rows = low(projected[:, 2])
    places = jnp.arange(SEQ)
    allowed = (segment_row[:, None] == segment_row[None, :]) & (places[None, :] <= places[:, None])

    def one_head(parts):
        query_head, key_head, value_head = parts
        scores = low_back(product(query_head, key_head.T) * score_scale)
        scores = jnp.where(allowed, scores, big_negative)
        highest = lax.optimization_barrier(jnp.max(scores, axis=-1, keepdims=True))
        exps = jnp.exp(scores - highest)
        probs = exps / lax.optimization_barrier(jnp.sum(exps, axis=-1, keepdims=True))
        return product(low(probs), value_head)
    attended = lax.map(jax.checkpoint(one_head), (query_rows.transpose(1, 0, 2), key_rows.transpose(1, 0, 2), value_rows.transpose(1, 0, 2)))
    attended = low(low_back(attended.transpose(1, 0, 2).reshape(SEQ, D)))
    attention_part = product(attended, dense_matrix.T) + dense_vector
    hidden_pre = low_back(product(normed, up_matrix) + up_vector)
    activation = low(gelu_new(hidden_pre))
    forward_part = product(activation, down_matrix.T) + down_vector
    return inputs + attention_part + forward_part

def reference(tokens, segments, positions, norm_gain, norm_bias, projection_weight, projection_bias, dense_weight, dense_bias, up_weight, up_bias, down_weight, down_bias, cotangent):
    params = (norm_gain.astype(jnp.float32), norm_bias.astype(jnp.float32), projection_weight.astype(jnp.float32), projection_bias.astype(jnp.float32), dense_weight.astype(jnp.float32), dense_bias.astype(jnp.float32), up_weight.astype(jnp.float32), up_bias.astype(jnp.float32), down_weight.astype(jnp.float32), down_bias.astype(jnp.float32))

    def forward(weights, inputs):

        def advance(running, element):
            return (running, layer(weights, element[0], element[1], element[2]))
        ignored, outputs = lax.scan(advance, jnp.zeros((), jnp.float32), (inputs, segments, positions))
        return outputs
    outputs, pullback = jax.vjp(forward, params, tokens.astype(jnp.float32))
    grad_params, grad_inputs = pullback(cotangent.astype(jnp.float32))
    return (outputs.astype(jnp.bfloat16), grad_inputs, grad_params[0], grad_params[1], grad_params[2], grad_params[3], grad_params[4], grad_params[5], grad_params[6], grad_params[7], grad_params[8], grad_params[9])
```

```python
import functools
import math

import jax
import jax.numpy as jnp
from jax import lax
from jax.experimental import pallas as pl
from jax.experimental.pallas import tpu as pltpu
from jax.sharding import PartitionSpec as P

HD = 64
ROT = 32
TILE = 256

epsilon = 1e-05
big_negative = -1000000000.0
root_two_over_pi = 0.7978845608028654
contract_rows = (((0,), (0,)), ((), ()))
contract_cols = (((1,), (1,)), ((), ()))
row_by_col = (((0,), (1,)), ((), ()))
MESH = pl.DeviceIdType.MESH
ANY = pl.BlockSpec(memory_space=pl.ANY)
VMEM = pl.BlockSpec(memory_space=pltpu.VMEM)
SMEM = pl.BlockSpec(memory_space=pltpu.SMEM)
DMA = pltpu.SemaphoreType.DMA
f32 = jnp.float32
bf16 = jnp.bfloat16


def layer_norm(values, gain_full, shift_full):
    center = jnp.mean(values, axis=-1, keepdims=True)
    centered = values - center
    spread = jnp.mean(centered * centered, axis=-1, keepdims=True)
    return centered * lax.rsqrt(spread + epsilon) * gain_full + shift_full


def gelu_new(values):
    return (
        0.5
        * values
        * (1.0 + jnp.tanh(root_two_over_pi * (values + 0.044715 * values * values * values)))
    )


class Place:
    def __init__(self, sizes):
        self.chips = sizes["fsdp"] // 2
        self.halves = sizes["ctx"]
        self.depth = sizes["tp"]
        lane = lax.axis_index("fsdp")
        self.chip = lane // 2
        self.core = lane % 2
        self.half = lax.axis_index("ctx")
        self.layer = lax.axis_index("tp")

    def device(self, chip=None, core=None, half=None, layer=None):
        chip = self.chip if chip is None else chip
        core = self.core if core is None else core
        half = self.half if half is None else half
        layer = self.layer if layer is None else layer
        return (chip * 2 + core, half, layer)

    def block(self, chip=None, core=None, half=None):
        chip = self.chip if chip is None else chip
        core = self.core if core is None else core
        half = self.half if half is None else half
        return (chip * 2 + core) * self.halves + half

    def ahead(self, k):
        return (self.chip + k) % self.chips

    def behind(self, k):
        return (self.chip + self.chips - k) % self.chips

    def pair(self):
        return self.device(core=1 - self.core)

    def across(self):
        return self.device(half=1 - self.half)

    def group(self):
        found = []
        for k in range(self.chips):
            for core in range(2):
                for half in range(2):
                    if k or core or half:
                        found.append(
                            (self.ahead(k), (self.core + core) % 2, (self.half + half) % 2)
                        )
        return found


def greet(devices):
    barrier = pltpu.get_barrier_semaphore()
    for device in devices:
        pl.semaphore_signal(barrier, inc=1, device_id=device, device_id_type=MESH)
    pl.semaphore_wait(barrier, len(devices))


def greet_line(place, devices):
    barrier = pltpu.get_barrier_semaphore()
    for device in devices:
        pl.semaphore_signal(barrier, inc=1, device_id=device, device_id_type=MESH)
    up, down = place.layer < place.depth - 1, place.layer > 0

    @pl.when(up)
    def _():
        pl.semaphore_signal(
            barrier, inc=1, device_id=place.device(layer=place.layer + 1), device_id_type=MESH
        )

    @pl.when(down)
    def _():
        pl.semaphore_signal(
            barrier, inc=1, device_id=place.device(layer=place.layer - 1), device_id_type=MESH
        )

    pl.semaphore_wait(barrier, len(devices) + up.astype(jnp.int32) + down.astype(jnp.int32))


def send(source, target, send_sem, recv_sem, device):
    return pltpu.make_async_remote_copy(
        src_ref=source,
        dst_ref=target,
        send_sem=send_sem,
        recv_sem=recv_sem,
        device_id=device,
        device_id_type=MESH,
    )


def plane(place):
    found = [place.device(chip=place.ahead(k)) for k in range(1, place.chips)]
    return found + [place.across(), place.pair()]


def small_gather(sizes, block, pairs):
    count = sizes["fsdp"] * sizes["ctx"]

    def kernel(block_ref, pair_ref, full_ref, other_ref, send_sem, recv_sem, keep_sem, swap_sem):
        place = Place(sizes)
        peers = place.group()
        greet([place.device(chip=a, core=b, half=c) for a, b, c in peers])
        mine = place.block()
        keep = pltpu.make_async_copy(block_ref, full_ref.at[mine], keep_sem)
        keep.start()
        swap = send(pair_ref, other_ref, swap_sem.at[0], swap_sem.at[1], place.across())
        swap.start()
        copies = []
        for at, (chip, core, half) in enumerate(peers):
            copy = send(
                block_ref,
                full_ref.at[mine],
                send_sem.at[at],
                recv_sem.at[at],
                place.device(chip=chip, core=core, half=half),
            )
            copy.start()
            copies.append(copy)
        keep.wait()
        for at, copy in enumerate(copies):
            k, core, half = at_of(at)
            source = place.block(
                place.behind(k), (place.core + core) % 2, (place.half + half) % 2
            )
            copy.wait_send()
            send(
                block_ref, full_ref.at[source], send_sem.at[at], recv_sem.at[at], place.pair()
            ).wait_recv()
        swap.wait()

    def at_of(at):
        return (at + 1) // 4, ((at + 1) // 2) % 2, (at + 1) % 2

    return pl.pallas_call(
        kernel,
        out_shape=(
            jax.ShapeDtypeStruct((count,) + block.shape, block.dtype),
            jax.ShapeDtypeStruct(pairs.shape, pairs.dtype),
        ),
        in_specs=[VMEM, VMEM],
        out_specs=(VMEM, VMEM),
        scratch_shapes=[DMA((count - 1,)), DMA((count - 1,)), DMA, DMA((2,))],
        compiler_params=pltpu.CompilerParams(collective_id=0, has_side_effects=True),
        name="small_gather",
    )(block, pairs)


def gather(sizes, lines, weights, collective_id, name):
    chips, halves, depth = sizes["fsdp"] // 2, sizes["ctx"], sizes["tp"]
    line_count, weight_count = len(lines), len(weights)

    def kernel(*refs):
        refs = list(refs)

        def take(count):
            taken = refs[:count]
            del refs[:count]
            return taken

        line_in, weight_in = take(line_count), take(weight_count)
        line_out, weight_out = take(line_count), take(weight_count)
        keep, line_send, line_recv, near_send, near_recv = take(5)
        turn_send, turn_recv, core_send, core_recv = take(4)
        place = Place(sizes)
        up, down = place.layer < depth - 1, place.layer > 0
        greet_line(place, plane(place))

        def part(ref, block, rows, first=0, count=None):
            count = rows if count is None else count
            start = pl.multiple_of(block * rows + first, 16)
            return ref.at[pl.ds(start, count)]

        pending = []

        def launch(copy, condition=None):
            if condition is None:
                copy.start()
            else:
                pl.when(condition)(copy.start)
            pending.append((copy, condition))

        for a in range(line_count):
            rows = line_in[a].shape[0]
            own = part(line_out[a], place.layer, rows)
            for way, (step, condition) in enumerate(((1, up), (-1, down))):
                launch(
                    send(
                        line_in[a],
                        own,
                        line_send.at[a, way, 0],
                        line_recv.at[a, way, 0],
                        place.device(layer=jnp.clip(place.layer + step, 0, depth - 1)),
                    ),
                    condition,
                )
        for a in range(weight_count):
            rows = weight_in[a].shape[0]
            own = part(weight_out[a], place.block(), rows)
            for k in range(1, chips):
                launch(
                    send(
                        weight_in[a],
                        own,
                        near_send.at[a, k],
                        near_recv.at[a, k],
                        place.device(chip=place.ahead(k)),
                    )
                )
            launch(
                send(weight_in[a], own, near_send.at[a, 0], near_recv.at[a, 0], place.across())
            )
            launch(send(weight_in[a], own, core_send.at[a, 0], core_recv.at[a, 0], place.pair()))
        kept = []
        for a in range(line_count):
            rows = line_in[a].shape[0]
            kept.append(
                pltpu.make_async_copy(
                    line_in[a], part(line_out[a], place.layer, rows), keep.at[a]
                )
            )
        for a in range(weight_count):
            rows = weight_in[a].shape[0]
            kept.append(
                pltpu.make_async_copy(
                    weight_in[a],
                    part(weight_out[a], place.block(), rows),
                    keep.at[line_count + a],
                )
            )
        for copy in kept:
            copy.start()

        def line_step(k):
            for a in range(line_count):
                rows = line_in[a].shape[0]
                for way, step in enumerate((1, -1)):
                    source = place.layer - step * k
                    there = (source >= 0) & (source < depth)
                    source = jnp.clip(source, 0, depth - 1)
                    piece = part(line_out[a], source, rows)
                    target = place.layer + step
                    onward = there & (target >= 0) & (target < depth)
                    device = place.device(layer=jnp.clip(target, 0, depth - 1))
                    arrived = send(
                        piece,
                        piece,
                        line_send.at[a, way, k - 1],
                        line_recv.at[a, way, k - 1],
                        device,
                    )
                    pl.when(there)(arrived.wait_recv)
                    if k < depth - 1:
                        launch(
                            send(
                                piece,
                                piece,
                                line_send.at[a, way, k],
                                line_recv.at[a, way, k],
                                device,
                            ),
                            onward,
                        )

        def near_step():
            for a in range(weight_count):
                rows = weight_in[a].shape[0]
                side = rows // 2
                for k in range(1, chips):
                    block = place.block(chip=place.behind(k))
                    piece = part(weight_out[a], block, rows)
                    send(
                        piece, piece, near_send.at[a, k], near_recv.at[a, k], place.pair()
                    ).wait_recv()
                    top = part(weight_out[a], block, rows, 0, side)
                    launch(
                        send(
                            top, top, turn_send.at[a, 0, k], turn_recv.at[a, 0, k], place.across()
                        )
                    )
                    launch(
                        send(piece, piece, core_send.at[a, k], core_recv.at[a, k], place.pair())
                    )
                block = place.block(half=1 - place.half)
                piece = part(weight_out[a], block, rows)
                send(
                    piece, piece, near_send.at[a, 0], near_recv.at[a, 0], place.pair()
                ).wait_recv()
                low = part(weight_out[a], block, rows, side, side)
                for k in range(1, chips):
                    launch(
                        send(
                            low,
                            low,
                            turn_send.at[a, 1, k],
                            turn_recv.at[a, 1, k],
                            place.device(chip=place.ahead(k)),
                        )
                    )
                launch(
                    send(
                        piece, piece, core_send.at[a, chips], core_recv.at[a, chips], place.pair()
                    )
                )

        def turn_step():
            for a in range(weight_count):
                rows = weight_in[a].shape[0]
                side = rows // 2
                for k in range(1, chips):
                    block = place.block(chip=place.behind(k), half=1 - place.half)
                    for number in range(2):
                        piece = part(weight_out[a], block, rows, number * side, side)
                        send(
                            piece,
                            piece,
                            turn_send.at[a, number, k],
                            turn_recv.at[a, number, k],
                            place.pair(),
                        ).wait_recv()
                    piece = part(weight_out[a], block, rows)
                    launch(
                        send(
                            piece,
                            piece,
                            core_send.at[a, chips + k],
                            core_recv.at[a, chips + k],
                            place.pair(),
                        )
                    )

        def core_step():
            other = 1 - place.core
            for a in range(weight_count):
                rows = weight_in[a].shape[0]
                blocks = [place.block(core=other)]
                blocks += [place.block(place.behind(k), other) for k in range(1, chips)]
                blocks += [place.block(None, other, 1 - place.half)]
                blocks += [
                    place.block(place.behind(k), other, 1 - place.half) for k in range(1, chips)
                ]
                for at, block in enumerate(blocks):
                    piece = part(weight_out[a], block, rows)
                    send(
                        piece, piece, core_send.at[a, at], core_recv.at[a, at], place.pair()
                    ).wait_recv()

        line_step(1)
        near_step()
        for k in range(2, depth):
            line_step(k)
        turn_step()
        core_step()
        for copy in kept:
            copy.wait()
        for copy, condition in pending:
            if condition is None:
                copy.wait_send()
            else:
                pl.when(condition)(copy.wait_send)

    count = sizes["fsdp"] * halves
    shapes = [jax.ShapeDtypeStruct((depth * v.shape[0], v.shape[1]), v.dtype) for v in lines]
    shapes += [jax.ShapeDtypeStruct((count * v.shape[0], v.shape[1]), v.dtype) for v in weights]
    return pl.pallas_call(
        kernel,
        out_shape=tuple(shapes),
        in_specs=[ANY] * (line_count + weight_count),
        out_specs=(ANY,) * (line_count + weight_count),
        scratch_shapes=[
            DMA((line_count + weight_count,)),
            DMA((line_count, 2, depth - 1)),
            DMA((line_count, 2, depth - 1)),
            DMA((weight_count, chips)),
            DMA((weight_count, chips)),
            DMA((weight_count, 2, chips)),
            DMA((weight_count, 2, chips)),
            DMA((weight_count, 2 * chips)),
            DMA((weight_count, 2 * chips)),
        ],
        compiler_params=pltpu.CompilerParams(collective_id=collective_id, has_side_effects=True),
        name=name,
    )(*lines, *weights)


def reduce(sizes, line, weights, small, collective_id, name):
    chips, halves, depth = sizes["fsdp"] // 2, sizes["ctx"], sizes["tp"]
    groups = chips * halves
    weight_count = len(weights)
    line_rows, line_width = line.shape[0] // depth, line.shape[1]
    block_rows = weights[0].shape[0] // (2 * groups)
    widths = [v.shape[1] for v in weights]
    side = block_rows // 2
    has_small = small is not None

    def kernel(*refs):
        refs = list(refs)

        def take(count):
            taken = refs[:count]
            del refs[:count]
            return taken

        (line_ref,) = take(1)
        weight_in = take(weight_count)
        small_ref = take(1)[0] if has_small else None
        (line_out,) = take(1)
        weight_out = take(weight_count)
        small_out = take(1)[0] if has_small else None
        flow, fresh = take(2)
        own, pair, turn_a, turn_b, near = (take(weight_count) for _ in range(5))
        line_send, line_recv, load_sem, core_send, core_recv = take(5)
        turn_send, turn_recv, near_send, near_recv = take(4)
        if has_small:
            small_pair, small_near, small_far, small_send, small_recv = take(5)
        place = Place(sizes)
        greet_line(place, plane(place))
        pending = []

        def launch(copy, condition=None):
            if condition is None:
                copy.start()
            else:
                pl.when(condition)(copy.start)
            pending.append((copy, condition))

        other = 1 - place.core
        for a in range(weight_count):
            for number in range(groups):
                chip, half = number // halves, number % halves
                theirs = place.block(chip, other, half)
                mine = place.block(chip, place.core, half)
                launch(
                    send(
                        weight_in[a].at[
                            pl.ds(pl.multiple_of(theirs * block_rows, 16), block_rows)
                        ],
                        pair[a].at[number],
                        core_send.at[a, number],
                        core_recv.at[a, number],
                        place.pair(),
                    )
                )
                pltpu.make_async_copy(
                    weight_in[a].at[pl.ds(pl.multiple_of(mine * block_rows, 16), block_rows)],
                    own[a].at[number],
                    load_sem.at[a, number],
                ).start()

        def line_ends(way, owner):
            step = 1 if way == 0 else -1
            inner = (place.layer - owner) * step < 0
            first = place.layer == (0 if way == 0 else depth - 1)
            return step, inner, first

        def line_sum(way, hop):
            step = 1 if way == 0 else -1
            owner = depth - 1 - hop if way == 0 else hop
            sends = place.layer < owner if way == 0 else place.layer > owner
            first = place.layer == (0 if way == 0 else depth - 1)
            device = place.device(layer=jnp.clip(place.layer + step, 0, depth - 1))
            rows = line_ref.at[pl.ds(owner * line_rows, line_rows)]

            @pl.when(sends & jnp.logical_not(first))
            def _():
                send(
                    rows, flow.at[way, owner], line_send.at[way, owner], line_recv.at[way, owner], device
                ).wait_recv()

                @pl.loop(0, line_rows, step=16)
                def _(r):
                    at = pl.ds(pl.multiple_of(r, 16), 16)
                    start = pl.ds(pl.multiple_of(owner * line_rows + r, 16), 16)
                    total = line_ref[start, :].astype(f32) + flow[way, owner, at, :].astype(f32)
                    fresh[way, owner, at, :] = total.astype(bf16)

                send(
                    fresh.at[way, owner],
                    flow.at[way, owner],
                    line_send.at[way, owner],
                    line_recv.at[way, owner],
                    device,
                ).start()

            @pl.when(sends & first)
            def _():
                send(
                    rows, flow.at[way, owner], line_send.at[way, owner], line_recv.at[way, owner], device
                ).start()

            pending.append(
                (
                    send(
                        rows,
                        flow.at[way, owner],
                        line_send.at[way, owner],
                        line_recv.at[way, owner],
                        device,
                    ),
                    sends,
                )
            )

        def line_own():
            below, above = place.layer > 0, place.layer < depth - 1
            mine = place.layer
            rows = line_ref.at[pl.ds(pl.multiple_of(mine * line_rows, 16), line_rows)]
            for way, condition in ((0, below), (1, above)):
                pl.when(condition)(
                    send(
                        rows,
                        flow.at[way, mine],
                        line_send.at[way, mine],
                        line_recv.at[way, mine],
                        place.pair(),
                    ).wait_recv
                )

            @pl.loop(0, line_rows, step=16)
            def _(r):
                at = pl.ds(pl.multiple_of(r, 16), 16)
                start = pl.ds(pl.multiple_of(mine * line_rows + r, 16), 16)
                line_out[at, :] = line_ref[start, :].astype(f32)

            for way, condition in ((0, below), (1, above)):

                @pl.when(condition)
                def _(way=way):
                    @pl.loop(0, line_rows, step=16)
                    def _(r):
                        at = pl.ds(pl.multiple_of(r, 16), 16)
                        line_out[at, :] += flow[way, mine, at, :].astype(f32)

        def pair_sum(a, number):
            mine = own[a].at[number]
            theirs = pair[a].at[number]
            pltpu.make_async_copy(mine, mine, load_sem.at[a, number]).wait()
            send(
                theirs, theirs, core_send.at[a, number], core_recv.at[a, number], place.pair()
            ).wait_recv()

            @pl.loop(0, block_rows, step=16)
            def _(r):
                at = pl.ds(pl.multiple_of(r, 16), 16)
                mine[at, :] = (mine[at, :].astype(f32) + theirs[at, :].astype(f32)).astype(bf16)

        def diagonal(a):
            for k in range(1, chips):
                number = place.ahead(k) * halves + 1 - place.half
                pair_sum(a, number)
                launch(
                    send(
                        own[a].at[number, pl.ds(0, side)],
                        turn_a[a].at[k - 1],
                        turn_send.at[a, 0, k],
                        turn_recv.at[a, 0, k],
                        place.across(),
                    )
                )
                launch(
                    send(
                        own[a].at[number, pl.ds(side, side)],
                        turn_b[a].at[k - 1],
                        turn_send.at[a, 1, k],
                        turn_recv.at[a, 1, k],
                        place.device(chip=place.ahead(k)),
                    )
                )

        def direct_pairs(a):
            for k in range(1, chips):
                pair_sum(a, place.ahead(k) * halves + place.half)
            pair_sum(a, place.chip * halves + 1 - place.half)

        def add_turn(a, number, first, refs_at):
            @pl.loop(0, side, step=16)
            def _(r):
                at = pl.ds(pl.multiple_of(first + r, 16), 16)
                total = own[a][number, at, :].astype(f32)
                for ref, k in refs_at:
                    total += ref[k, pl.ds(pl.multiple_of(r, 16), 16), :].astype(f32)
                own[a][number, at, :] = total.astype(bf16)

        def direct(a):
            for k in range(1, chips):
                number = place.ahead(k) * halves + place.half
                piece = turn_a[a].at[k - 1]
                send(
                    piece, piece, turn_send.at[a, 0, k], turn_recv.at[a, 0, k], place.across()
                ).wait_recv()
                add_turn(a, number, 0, [(turn_a[a], k - 1)])
                launch(
                    send(
                        own[a].at[number],
                        near[a].at[k],
                        near_send.at[a, k],
                        near_recv.at[a, k],
                        place.device(chip=place.ahead(k)),
                    )
                )
            for k in range(1, chips):
                piece = turn_b[a].at[k - 1]
                send(
                    piece, piece, turn_send.at[a, 1, k], turn_recv.at[a, 1, k], place.across()
                ).wait_recv()
            number = place.chip * halves + 1 - place.half
            add_turn(a, number, side, [(turn_b[a], k - 1) for k in range(1, chips)])
            launch(
                send(
                    own[a].at[number],
                    near[a].at[0],
                    near_send.at[a, 0],
                    near_recv.at[a, 0],
                    place.across(),
                )
            )

        def finish(a):
            for k in range(chips):
                piece = near[a].at[k]
                send(
                    piece, piece, near_send.at[a, k], near_recv.at[a, k], place.across()
                ).wait_recv()
            number = place.chip * halves + place.half

            @pl.loop(0, block_rows, step=16)
            def _(r):
                at = pl.ds(pl.multiple_of(r, 16), 16)
                total = own[a][number, at, :].astype(f32) + near[a][0, at, :].astype(f32)
                for k in range(1, chips):
                    total += near[a][k, at, :].astype(f32)
                weight_out[a][at, :] = total

        def swap_small(source, target, at, device):
            copy = send(source, target, small_send.at[at], small_recv.at[at], device)
            launch(copy)
            return copy

        for way in range(2):
            line_sum(way, 0)
        if has_small:
            swap_small(small_ref, small_pair, 0, place.pair())
        for a in range(weight_count):
            diagonal(a)
        for way in range(2):
            line_sum(way, 1)
        for a in range(weight_count):
            direct_pairs(a)
        if has_small:
            send(
                small_pair, small_pair, small_send.at[0], small_recv.at[0], place.pair()
            ).wait_recv()
            small_near[0] = small_ref[...] + small_pair[...]
            for k in range(1, chips):
                swap_small(
                    small_near.at[0], small_near.at[k], k, place.device(chip=place.ahead(k))
                )
        for a in range(weight_count):
            direct(a)
        for hop in range(2, depth - 1):
            for way in range(2):
                line_sum(way, hop)
        if has_small:
            total = small_near[0]
            for k in range(1, chips):
                piece = small_near.at[k]
                send(piece, piece, small_send.at[k], small_recv.at[k], place.pair()).wait_recv()
                total += small_near[k]
            small_far[0] = total
            swap_small(small_far.at[0], small_far.at[1], chips, place.across())
        for a in range(weight_count):
            pair_sum(a, place.chip * halves + place.half)
        for a in range(weight_count):
            finish(a)
        if has_small:
            piece = small_far.at[1]
            send(
                piece, piece, small_send.at[chips], small_recv.at[chips], place.pair()
            ).wait_recv()
            small_out[...] = small_far[0] + small_far[1]
        line_own()
        for copy, condition in pending:
            if condition is None:
                copy.wait_send()
            else:
                pl.when(condition)(copy.wait_send)

    shapes = [jax.ShapeDtypeStruct((line_rows, line_width), f32)]
    shapes += [jax.ShapeDtypeStruct((block_rows, w), f32) for w in widths]
    scratch = [
        pltpu.VMEM((2, depth, line_rows, line_width), bf16),
        pltpu.VMEM((2, depth, line_rows, line_width), bf16),
    ]
    for rows in ((groups, block_rows), (groups, block_rows), (chips - 1, side), (chips - 1, side)):
        scratch += [pltpu.VMEM(rows + (w,), bf16) for w in widths]
    scratch += [pltpu.VMEM((chips, block_rows, w), bf16) for w in widths]
    scratch += [
        DMA((2, depth)),
        DMA((2, depth)),
        DMA((weight_count, groups)),
        DMA((weight_count, groups)),
        DMA((weight_count, groups)),
        DMA((weight_count, 2, chips)),
        DMA((weight_count, 2, chips)),
        DMA((weight_count, chips)),
        DMA((weight_count, chips)),
    ]
    arguments = [line, *weights]
    in_specs = [VMEM] + [ANY] * weight_count
    if has_small:
        shapes.append(jax.ShapeDtypeStruct(small.shape, f32))
        scratch += [
            pltpu.VMEM(small.shape, f32),
            pltpu.VMEM((chips,) + small.shape, f32),
            pltpu.VMEM((2,) + small.shape, f32),
            DMA((chips + 1,)),
            DMA((chips + 1,)),
        ]
        arguments.append(small)
        in_specs.append(VMEM)
    return pl.pallas_call(
        kernel,
        out_shape=tuple(shapes),
        in_specs=in_specs,
        out_specs=(VMEM,) * len(shapes),
        scratch_shapes=scratch,
        compiler_params=pltpu.CompilerParams(
            collective_id=collective_id, has_side_effects=True, vmem_limit_bytes=60 << 20
        ),
        name=name,
    )(*arguments)


def small_reduce(sizes, blocks):
    count, depth = sizes["fsdp"] * sizes["ctx"], sizes["tp"]

    def kernel(blocks_ref, out_ref, landed, line, send_sem, recv_sem, line_send, line_recv):
        place = Place(sizes)
        peers = place.group()
        layers = [(place.layer + k) % depth for k in range(1, depth)]
        devices = [place.device(chip=a, core=b, half=c) for a, b, c in peers]
        greet(devices + [place.device(layer=k) for k in layers])
        copies = []
        for at, (chip, core, half) in enumerate(peers):
            copy = send(
                blocks_ref.at[place.block(chip, core, half)],
                landed.at[at],
                send_sem.at[at],
                recv_sem.at[at],
                devices[at],
            )
            copy.start()
            copies.append(copy)
        total = blocks_ref[place.block()]
        for at, copy in enumerate(copies):
            copy.wait()
            total += landed[at]
        line[0] = total
        copies = []
        for k, layer in enumerate(layers):
            copy = send(
                line.at[0],
                line.at[k + 1],
                line_send.at[k],
                line_recv.at[k],
                place.device(layer=layer),
            )
            copy.start()
            copies.append(copy)
        for k, copy in enumerate(copies):
            copy.wait()
            total += line[k + 1]
        out_ref[...] = total

    block = blocks.shape[1:]
    return pl.pallas_call(
        kernel,
        out_shape=jax.ShapeDtypeStruct(block, f32),
        in_specs=[VMEM],
        out_specs=VMEM,
        scratch_shapes=[
            pltpu.VMEM((count - 1,) + block, f32),
            pltpu.VMEM((depth,) + block, f32),
            DMA((count - 1,)),
            DMA((count - 1,)),
            DMA((depth - 1,)),
            DMA((depth - 1,)),
        ],
        compiler_params=pltpu.CompilerParams(collective_id=5, has_side_effects=True),
        name="small_reduce",
    )(blocks)


def attention_kernel(
    low_ref,
    mid_ref,
    first_ref,
    second_ref,
    grad_first_ref,
    grad_second_ref,
    start_ref,
    cosine_ref,
    sine_ref,
    attended_ref,
    back_ref,
    query_t,
    key_t,
    value_t,
    grad_t,
    key_rows,
    value_rows,
    scores,
    probs,
    key_sum,
    value_sum,
):
    length = first_ref.shape[2]
    total_length = 2 * length
    score_scale = 1.0 / math.sqrt(HD)
    for number, ref in enumerate((query_t, key_t, value_t)):
        scale = score_scale if number == 0 else 1.0
        for part, source in enumerate((first_ref, second_ref)):
            piece = source[number]
            ref[:, part * length : (part + 1) * length] = piece * scale if number == 0 else piece
    grad_t[:, :length] = grad_first_ref[...]
    grad_t[:, length:] = grad_second_ref[...]
    key_rows[...] = key_t[...].T
    value_rows[...] = value_t[...].T
    key_sum[...] = jnp.zeros_like(key_sum)
    value_sum[...] = jnp.zeros_like(value_sum)

    def turned_back(values, cosine, sine):
        half_rot = ROT // 2
        leading = values[:half_rot]
        trailing = values[half_rot:ROT]
        return jnp.concatenate(
            [
                leading * cosine + trailing * sine,
                trailing * cosine - leading * sine,
                values[ROT:],
            ],
            axis=0,
        )

    @pl.loop(0, total_length // TILE)
    def _(j):
        here = pl.ds(pl.multiple_of(j * TILE, TILE), TILE)
        query = query_t[:, here]
        grad = grad_t[:, here]
        start = start_ref[:, here]
        low, mid = low_ref[j], mid_ref[j]

        def at(kb):
            return pl.ds(pl.multiple_of(kb * TILE, TILE), TILE)

        def plain(kb, highest):
            found = jnp.dot(key_rows[at(kb), :], query, preferred_element_type=f32)
            scores[at(kb), :] = found
            return jnp.maximum(highest, jnp.max(found, axis=0, keepdims=True))

        def masked(kb, highest):
            found = jnp.dot(key_rows[at(kb), :], query, preferred_element_type=f32)
            places = kb * TILE + lax.broadcasted_iota(jnp.int32, (TILE, TILE), 0)
            own = j * TILE + lax.broadcasted_iota(jnp.int32, (TILE, TILE), 1)
            found = jnp.where((places >= start) & (places <= own), found, big_negative)
            scores[at(kb), :] = found
            return jnp.maximum(highest, jnp.max(found, axis=0, keepdims=True))

        highest = jnp.full((1, TILE), big_negative, f32)
        highest = lax.fori_loop(low, mid, masked, highest)
        highest = lax.fori_loop(mid, j, plain, highest)
        highest = masked(j, highest)

        def weigh(kb, carry):
            total, mixed = carry
            prob = jnp.exp(scores[at(kb), :] - highest)
            total = total + jnp.sum(prob, axis=0, keepdims=True)
            prob = prob.astype(bf16)
            probs[at(kb), :] = prob
            mixed = mixed + jnp.dot(value_t[:, at(kb)], prob, preferred_element_type=f32)
            return total, mixed

        total, mixed = lax.fori_loop(
            low, j + 1, weigh, (jnp.zeros((1, TILE), f32), jnp.zeros((HD, TILE), f32))
        )
        over = 1.0 / total
        mixed = mixed * over
        attended_ref[:, here] = mixed.astype(bf16)
        grad_wide = grad.astype(f32)
        delta = jnp.sum(grad_wide * mixed, axis=0, keepdims=True)
        query_over = (query.astype(f32) * over).T.astype(bf16)
        grad_over = (grad_wide * over).T.astype(bf16)

        def pull(kb, query_back):
            prob = probs[at(kb), :]
            down = jnp.dot(value_rows[at(kb), :], grad, preferred_element_type=f32)
            score_back = (prob.astype(f32) * (down - delta)).astype(bf16)
            value_sum[at(kb), :] += jnp.dot(prob, grad_over, preferred_element_type=f32)
            key_sum[at(kb), :] += jnp.dot(score_back, query_over, preferred_element_type=f32)
            return query_back + jnp.dot(
                key_t[:, at(kb)], score_back, preferred_element_type=f32
            )

        query_back = lax.fori_loop(low, j + 1, pull, jnp.zeros((HD, TILE), f32))
        query_back = query_back * (over * score_scale)
        back_ref[0, :, here] = turned_back(
            query_back, cosine_ref[:, here], sine_ref[:, here]
        ).astype(bf16)

    back_ref[1] = turned_back(key_sum[...].T, cosine_ref[...], sine_ref[...]).astype(bf16)
    back_ref[2] = value_sum[...].T.astype(bf16)


def attention(low, mid, first, second, grad_first, grad_second, start, cosine, sine):
    width, length = first.shape[1], first.shape[2]
    total = 2 * length
    heads = width // HD
    spec = pl.BlockSpec((3, HD, length), lambda h: (0, h, 0))
    grad_spec = pl.BlockSpec((HD, length), lambda h: (h, 0))
    whole = lambda rows: pl.BlockSpec((rows, total), lambda h: (0, 0))
    area = total * total // 2 * heads
    return pl.pallas_call(
        attention_kernel,
        grid=(heads,),
        out_shape=(
            jax.ShapeDtypeStruct((width, total), bf16),
            jax.ShapeDtypeStruct((3, width, total), bf16),
        ),
        in_specs=[
            SMEM,
            SMEM,
            spec,
            spec,
            grad_spec,
            grad_spec,
            whole(1),
            whole(ROT // 2),
            whole(ROT // 2),
        ],
        out_specs=(
            pl.BlockSpec((HD, total), lambda h: (h, 0)),
            pl.BlockSpec((3, HD, total), lambda h: (0, h, 0)),
        ),
        scratch_shapes=[
            pltpu.VMEM((HD, total), bf16),
            pltpu.VMEM((HD, total), bf16),
            pltpu.VMEM((HD, total), bf16),
            pltpu.VMEM((HD, total), bf16),
            pltpu.VMEM((total, HD), bf16),
            pltpu.VMEM((total, HD), bf16),
            pltpu.VMEM((total, TILE), f32),
            pltpu.VMEM((total, TILE), bf16),
            pltpu.VMEM((total, HD), f32),
            pltpu.VMEM((total, HD), f32),
        ],
        compiler_params=pltpu.CompilerParams(vmem_limit_bytes=40 << 20),
        cost_estimate=pl.CostEstimate(
            flops=10 * area * HD, bytes_accessed=8 * width * total, transcendentals=area
        ),
        name="attention",
    )(low, mid, first, second, grad_first, grad_second, start, cosine, sine)


def rotate_rows(values, cosine, sine):
    half_rot = ROT // 2
    leading = values[:, :half_rot]
    trailing = values[:, half_rot:ROT]
    return jnp.concatenate(
        [
            leading * cosine - trailing * sine,
            trailing * cosine + leading * sine,
            values[:, ROT:],
        ],
        axis=1,
    )


def body(
    sizes,
    tokens,
    segments,
    positions,
    norm_gain,
    norm_bias,
    projection_weight,
    projection_bias,
    dense_weight,
    dense_bias,
    up_weight,
    up_bias,
    down_weight,
    down_bias,
    cotangent,
):
    own_len, model_width = tokens.shape[1], tokens.shape[2]
    half_len = segments.shape[1]
    local_width = projection_weight.shape[2]
    hidden_width = up_weight.shape[1]
    shard_rows = norm_gain.shape[0]
    half_width = local_width // 2
    half = lax.axis_index("ctx")
    total_len = 2 * half_len
    swap = [(0, 1), (1, 0)]

    vectors = jnp.stack([norm_gain, norm_bias, dense_bias, down_bias]).astype(f32)
    vectors = jnp.pad(vectors, ((0, 4), (0, 0)))
    numbers = jnp.pad(jnp.concatenate([segments, positions], axis=0), ((0, 6), (0, 0)))
    vectors_full, numbers_other = small_gather(sizes, vectors, numbers)
    gain_full, shift_full, bias_dense, bias_down = (
        vectors_full[:, row].reshape(model_width) for row in range(4)
    )

    def in_order(own, other, axis):
        return jnp.where(
            half == 0,
            jnp.concatenate([own, other], axis=axis),
            jnp.concatenate([other, own], axis=axis),
        )

    sequence = in_order(numbers, numbers_other, 1)
    segment_row, position_row = sequence[0], sequence[1]
    places = jnp.arange(total_len, dtype=jnp.int32)
    edges = jnp.concatenate([jnp.ones((1,), bool), segment_row[1:] != segment_row[:-1]])
    start = lax.cummax(jnp.where(edges, places, 0))
    tile_count = total_len // TILE
    low = start[::TILE] // TILE
    mid = jnp.minimum(
        jnp.maximum((start[TILE - 1 :: TILE] + TILE - 1) // TILE, low),
        jnp.arange(tile_count, dtype=jnp.int32),
    )
    exponent = jnp.arange(ROT // 2, dtype=f32) * 2.0 / ROT
    inverse = 10000.0 ** (-exponent)
    phase_angle = inverse[:, None] * position_row.astype(f32)[None, :]
    cosine_full, sine_full = jnp.cos(phase_angle), jnp.sin(phase_angle)
    own_start = half * half_len
    cosine_own = lax.dynamic_slice_in_dim(cosine_full, own_start, half_len, 1)
    sine_own = lax.dynamic_slice_in_dim(sine_full, own_start, half_len, 1)

    inputs = tokens[0].astype(f32)
    normed_values, norm_pull = jax.vjp(layer_norm, inputs, gain_full, shift_full)
    normed, projection, up_full = gather(
        sizes,
        [normed_values.astype(bf16)],
        [projection_weight.reshape(shard_rows, 3 * local_width), up_weight],
        1,
        "gather_first",
    )
    cotangent_rows, dense_full, down_full = gather(
        sizes, [cotangent[0]], [dense_weight, down_weight], 2, "gather_second"
    )
    projected = lax.dot_general(projection, normed, row_by_col, preferred_element_type=f32)
    projected = projected + projection_bias.astype(f32).reshape(3 * local_width)[:, None]
    projected = projected.reshape(3, local_width, half_len)
    turned = rotate_rows(
        projected[:2].reshape(2 * local_width // HD, HD, half_len), cosine_own, sine_own
    ).reshape(2, local_width, half_len)
    triple = jnp.concatenate([turned, projected[2:]], axis=0).astype(bf16)

    def keep_and_swap(values, axis, width):
        kept = lax.dynamic_slice_in_dim(values, half * width, width, axis)
        sent = lax.dynamic_slice_in_dim(values, (1 - half) * width, width, axis)
        return kept, lax.ppermute(sent, "ctx", swap)

    kept, came = keep_and_swap(triple, 1, half_width)
    first = jnp.where(half == 0, kept, came)
    second = jnp.where(half == 0, came, kept)

    hidden_pre = jnp.dot(normed, up_full, preferred_element_type=f32) + up_bias.astype(f32)
    gelu_values, gelu_pull = jax.vjp(gelu_new, hidden_pre)
    activation = gelu_values.astype(bf16)

    grad_attended = lax.dot_general(
        dense_full, cotangent_rows, row_by_col, preferred_element_type=f32
    ).astype(bf16)
    grad_kept, grad_came = keep_and_swap(grad_attended, 0, half_width)
    grad_first = jnp.where(half == 0, grad_kept, grad_came)
    grad_second = jnp.where(half == 0, grad_came, grad_kept)

    grad_activation = jnp.dot(cotangent_rows, down_full, preferred_element_type=f32)
    grad_hidden = gelu_pull(grad_activation)[0].astype(bf16)

    attended_heads, back_heads = attention(
        low,
        mid,
        first,
        second,
        grad_first,
        grad_second,
        start[None, :],
        cosine_full,
        sine_full,
    )
    att_kept, att_came = keep_and_swap(attended_heads, 1, half_len)
    back_kept, back_came = keep_and_swap(back_heads, 2, half_len)
    attended = in_order(att_kept, att_came, 0)
    grad_projected = in_order(back_kept, back_came, 1).reshape(3 * local_width, half_len)

    block_out = lax.dot_general(
        attended, dense_full, row_by_col, preferred_element_type=f32
    ) + lax.dot_general(activation, down_full, contract_cols, preferred_element_type=f32)
    up_grad = lax.dot_general(normed, grad_hidden, contract_rows, preferred_element_type=f32)
    down_grad = lax.dot_general(
        cotangent_rows, activation, contract_rows, preferred_element_type=f32
    )
    hidden_sum = jnp.sum(grad_hidden.astype(f32), axis=0)
    branch_own, up_part, down_part = reduce(
        sizes,
        block_out.astype(bf16),
        [up_grad.astype(bf16), down_grad.astype(bf16)],
        None,
        3,
        "reduce_first",
    )
    layer_output = (inputs + branch_own + (bias_dense + bias_down)).astype(bf16)

    block_in = lax.dot_general(
        grad_projected, projection, contract_rows_cols, preferred_element_type=f32
    ) + lax.dot_general(grad_hidden, up_full, contract_cols, preferred_element_type=f32)
    projection_grad = lax.dot_general(
        normed, grad_projected, row_by_col, preferred_element_type=f32
    )
    dense_grad = lax.dot_general(
        cotangent_rows, attended, row_by_col, preferred_element_type=f32
    )
    projected_sum = jnp.sum(grad_projected.astype(f32), axis=1)
    small = jnp.concatenate([projected_sum, hidden_sum]).reshape(-1, 128)
    grad_normed_own, projection_part, dense_part, small_total = reduce(
        sizes,
        block_in.astype(bf16),
        [projection_grad.astype(bf16), dense_grad.astype(bf16)],
        small,
        4,
        "reduce_second",
    )
    cotangent_own = cotangent[0].astype(f32)
    grad_inputs, grad_gain, grad_shift = norm_pull(grad_normed_own)
    input_grad = grad_inputs + cotangent_own
    output_sum = jnp.sum(cotangent_own, axis=0)
    sums = jnp.stack([grad_gain, grad_shift, output_sum]).reshape(3, -1, shard_rows)
    sums = jnp.pad(sums.transpose(1, 0, 2), ((0, 0), (0, 5), (0, 0)))
    totals = small_reduce(sizes, sums)
    small_flat = small_total.reshape(-1)
    return (
        layer_output[None],
        input_grad[None],
        totals[0],
        totals[1],
        projection_part.reshape(shard_rows, 3, local_width),
        small_flat[: 3 * local_width].reshape(3, local_width),
        dense_part,
        totals[2],
        up_part,
        small_flat[3 * local_width :],
        down_part,
        totals[2],
    )


contract_rows_cols = (((0,), (1,)), ((), ()))


def solution(mesh):
    placed = (
        P("fsdp", ("ctx", "tp"), None),
        P("fsdp", "ctx"),
        P("fsdp", "ctx"),
        P(("fsdp", "ctx")),
        P(("fsdp", "ctx")),
        P(("fsdp", "ctx"), None, "tp"),
        P(None, "tp"),
        P(("fsdp", "ctx"), "tp"),
        P(("fsdp", "ctx")),
        P(("fsdp", "ctx"), "tp"),
        P("tp"),
        P(("fsdp", "ctx"), "tp"),
        P(("fsdp", "ctx")),
        P("fsdp", ("ctx", "tp"), None),
    )
    return jax.shard_map(
        functools.partial(body, dict(mesh.shape)),
        mesh=mesh,
        in_specs=placed,
        out_specs=(
            P("fsdp", ("ctx", "tp"), None),
            P("fsdp", ("ctx", "tp"), None),
            P(("fsdp", "ctx")),
            P(("fsdp", "ctx")),
            P(("fsdp", "ctx"), None, "tp"),
            P(None, "tp"),
            P(("fsdp", "ctx"), "tp"),
            P(("fsdp", "ctx")),
            P(("fsdp", "ctx"), "tp"),
            P("tp"),
            P(("fsdp", "ctx"), "tp"),
            P(("fsdp", "ctx")),
        ),
        check_vma=False,
    )
```

```python
import functools
import math

import jax
import jax.numpy as jnp
from jax import lax
from jax.experimental import pallas as pl
from jax.experimental.pallas import tpu as pltpu
from jax.sharding import PartitionSpec as P

HD = 64
ROT = 32
TILE = 256

epsilon = 1e-05
big_negative = -1000000000.0
root_two_over_pi = 0.7978845608028654
contract_rows = (((0,), (0,)), ((), ()))
contract_cols = (((1,), (1,)), ((), ()))
row_by_col = (((0,), (1,)), ((), ()))
MESH = pl.DeviceIdType.MESH
ANY = pl.BlockSpec(memory_space=pl.ANY)
VMEM = pl.BlockSpec(memory_space=pltpu.VMEM)
SMEM = pl.BlockSpec(memory_space=pltpu.SMEM)
DMA = pltpu.SemaphoreType.DMA
f32 = jnp.float32
bf16 = jnp.bfloat16


def layer_norm(values, gain_full, shift_full):
    center = jnp.mean(values, axis=-1, keepdims=True)
    centered = values - center
    spread = jnp.mean(centered * centered, axis=-1, keepdims=True)
    return centered * lax.rsqrt(spread + epsilon) * gain_full + shift_full


def gelu_and_slope(values):
    turned = jnp.tanh(root_two_over_pi * (values + 0.044715 * values * values * values))
    slope = 0.5 * (1.0 + turned) + 0.5 * values * (1.0 - turned * turned) * root_two_over_pi * (
        1.0 + 3.0 * 0.044715 * values * values
    )
    return 0.5 * values * (1.0 + turned), slope


class Place:
    def __init__(self, sizes):
        self.chips = sizes["fsdp"] // 2
        self.halves = sizes["ctx"]
        self.depth = sizes["tp"]
        lane = lax.axis_index("fsdp")
        self.chip = lane // 2
        self.core = lane % 2
        self.half = lax.axis_index("ctx")
        self.layer = lax.axis_index("tp")

    def device(self, chip=None, core=None, half=None, layer=None):
        chip = self.chip if chip is None else chip
        core = self.core if core is None else core
        half = self.half if half is None else half
        layer = self.layer if layer is None else layer
        return (chip * 2 + core, half, layer)

    def block(self, chip=None, core=None, half=None):
        chip = self.chip if chip is None else chip
        core = self.core if core is None else core
        half = self.half if half is None else half
        return (chip * 2 + core) * self.halves + half

    def ahead(self, k):
        return (self.chip + k) % self.chips

    def behind(self, k):
        return (self.chip + self.chips - k) % self.chips

    def pair(self):
        return self.device(core=1 - self.core)

    def across(self):
        return self.device(half=1 - self.half)

    def group(self):
        found = []
        for k in range(self.chips):
            for core in range(2):
                for half in range(2):
                    if k or core or half:
                        found.append(
                            (self.ahead(k), (self.core + core) % 2, (self.half + half) % 2)
                        )
        return found


def greet(devices):
    barrier = pltpu.get_barrier_semaphore()
    for device in devices:
        pl.semaphore_signal(barrier, inc=1, device_id=device, device_id_type=MESH)
    pl.semaphore_wait(barrier, len(devices))


def greet_line(place, devices):
    barrier = pltpu.get_barrier_semaphore()
    for device in devices:
        pl.semaphore_signal(barrier, inc=1, device_id=device, device_id_type=MESH)
    up, down = place.layer < place.depth - 1, place.layer > 0

    @pl.when(up)
    def _():
        pl.semaphore_signal(
            barrier, inc=1, device_id=place.device(layer=place.layer + 1), device_id_type=MESH
        )

    @pl.when(down)
    def _():
        pl.semaphore_signal(
            barrier, inc=1, device_id=place.device(layer=place.layer - 1), device_id_type=MESH
        )

    pl.semaphore_wait(barrier, len(devices) + up.astype(jnp.int32) + down.astype(jnp.int32))


def send(source, target, send_sem, recv_sem, device):
    return pltpu.make_async_remote_copy(
        src_ref=source,
        dst_ref=target,
        send_sem=send_sem,
        recv_sem=recv_sem,
        device_id=device,
        device_id_type=MESH,
    )


def plane(place):
    found = [place.device(chip=place.ahead(k)) for k in range(1, place.chips)]
    return found + [place.across(), place.pair()]


def small_gather(sizes, block, pairs):
    count = sizes["fsdp"] * sizes["ctx"]

    def kernel(block_ref, pair_ref, full_ref, other_ref, send_sem, recv_sem, keep_sem, swap_sem):
        place = Place(sizes)
        peers = place.group()
        greet([place.device(chip=a, core=b, half=c) for a, b, c in peers])
        mine = place.block()
        keep = pltpu.make_async_copy(block_ref, full_ref.at[mine], keep_sem)
        keep.start()
        swap = send(pair_ref, other_ref, swap_sem.at[0], swap_sem.at[1], place.across())
        swap.start()
        copies = []
        for at, (chip, core, half) in enumerate(peers):
            copy = send(
                block_ref,
                full_ref.at[mine],
                send_sem.at[at],
                recv_sem.at[at],
                place.device(chip=chip, core=core, half=half),
            )
            copy.start()
            copies.append(copy)
        keep.wait()
        for at, copy in enumerate(copies):
            k, core, half = at_of(at)
            source = place.block(
                place.behind(k), (place.core + core) % 2, (place.half + half) % 2
            )
            copy.wait_send()
            send(
                block_ref, full_ref.at[source], send_sem.at[at], recv_sem.at[at], place.pair()
            ).wait_recv()
        swap.wait()

    def at_of(at):
        return (at + 1) // 4, ((at + 1) // 2) % 2, (at + 1) % 2

    return pl.pallas_call(
        kernel,
        out_shape=(
            jax.ShapeDtypeStruct((count,) + block.shape, block.dtype),
            jax.ShapeDtypeStruct(pairs.shape, pairs.dtype),
        ),
        in_specs=[VMEM, VMEM],
        out_specs=(VMEM, VMEM),
        scratch_shapes=[DMA((count - 1,)), DMA((count - 1,)), DMA, DMA((2,))],
        compiler_params=pltpu.CompilerParams(collective_id=0, has_side_effects=True),
        name="small_gather",
    )(block, pairs)


def gather(sizes, lines, weights, collective_id, name):
    chips, halves, depth = sizes["fsdp"] // 2, sizes["ctx"], sizes["tp"]
    line_count, weight_count = len(lines), len(weights)

    def kernel(*refs):
        refs = list(refs)

        def take(count):
            taken = refs[:count]
            del refs[:count]
            return taken

        line_in, weight_in = take(line_count), take(weight_count)
        line_out, weight_out = take(line_count), take(weight_count)
        keep, near_send, near_recv, turn_send, turn_recv, core_send, core_recv = take(7)
        line_send, line_recv = take(2) if line_count else (None, None)
        place = Place(sizes)
        up, down = place.layer < depth - 1, place.layer > 0
        if line_count:
            greet_line(place, plane(place))
        else:
            greet(plane(place))

        def part(ref, block, rows, first=0, count=None):
            count = rows if count is None else count
            start = pl.multiple_of(block * rows + first, 16)
            return ref.at[pl.ds(start, count)]

        pending = []

        def launch(copy, condition=None):
            if condition is None:
                copy.start()
            else:
                pl.when(condition)(copy.start)
            pending.append((copy, condition))

        for a in range(line_count):
            rows = line_in[a].shape[0]
            own = part(line_out[a], place.layer, rows)
            for way, (step, condition) in enumerate(((1, up), (-1, down))):
                launch(
                    send(
                        line_in[a],
                        own,
                        line_send.at[a, way, 0],
                        line_recv.at[a, way, 0],
                        place.device(layer=jnp.clip(place.layer + step, 0, depth - 1)),
                    ),
                    condition,
                )
        for a in range(weight_count):
            rows = weight_in[a].shape[0]
            own = part(weight_out[a], place.block(), rows)
            for k in range(1, chips):
                launch(
                    send(
                        weight_in[a],
                        own,
                        near_send.at[a, k],
                        near_recv.at[a, k],
                        place.device(chip=place.ahead(k)),
                    )
                )
            launch(
                send(weight_in[a], own, near_send.at[a, 0], near_recv.at[a, 0], place.across())
            )
            launch(send(weight_in[a], own, core_send.at[a, 0], core_recv.at[a, 0], place.pair()))
        kept = []
        for a in range(line_count):
            rows = line_in[a].shape[0]
            kept.append(
                pltpu.make_async_copy(
                    line_in[a], part(line_out[a], place.layer, rows), keep.at[a]
                )
            )
        for a in range(weight_count):
            rows = weight_in[a].shape[0]
            kept.append(
                pltpu.make_async_copy(
                    weight_in[a],
                    part(weight_out[a], place.block(), rows),
                    keep.at[line_count + a],
                )
            )
        for copy in kept:
            copy.start()

        def line_step(k):
            for a in range(line_count):
                rows = line_in[a].shape[0]
                for way, step in enumerate((1, -1)):
                    source = place.layer - step * k
                    there = (source >= 0) & (source < depth)
                    source = jnp.clip(source, 0, depth - 1)
                    piece = part(line_out[a], source, rows)
                    target = place.layer + step
                    onward = there & (target >= 0) & (target < depth)
                    device = place.device(layer=jnp.clip(target, 0, depth - 1))
                    arrived = send(
                        piece,
                        piece,
                        line_send.at[a, way, k - 1],
                        line_recv.at[a, way, k - 1],
                        device,
                    )
                    pl.when(there)(arrived.wait_recv)
                    if k < depth - 1:
                        launch(
                            send(
                                piece,
                                piece,
                                line_send.at[a, way, k],
                                line_recv.at[a, way, k],
                                device,
                            ),
                            onward,
                        )

        def near_step():
            for a in range(weight_count):
                rows = weight_in[a].shape[0]
                side = rows // 2
                for k in range(1, chips):
                    block = place.block(chip=place.behind(k))
                    piece = part(weight_out[a], block, rows)
                    send(
                        piece, piece, near_send.at[a, k], near_recv.at[a, k], place.pair()
                    ).wait_recv()
                    top = part(weight_out[a], block, rows, 0, side)
                    launch(
                        send(
                            top, top, turn_send.at[a, 0, k], turn_recv.at[a, 0, k], place.across()
                        )
                    )
                    launch(
                        send(piece, piece, core_send.at[a, k], core_recv.at[a, k], place.pair())
                    )
                block = place.block(half=1 - place.half)
                piece = part(weight_out[a], block, rows)
                send(
                    piece, piece, near_send.at[a, 0], near_recv.at[a, 0], place.pair()
                ).wait_recv()
                low = part(weight_out[a], block, rows, side, side)
                for k in range(1, chips):
                    launch(
                        send(
                            low,
                            low,
                            turn_send.at[a, 1, k],
                            turn_recv.at[a, 1, k],
                            place.device(chip=place.ahead(k)),
                        )
                    )
                launch(
                    send(
                        piece, piece, core_send.at[a, chips], core_recv.at[a, chips], place.pair()
                    )
                )

        def turn_step():
            for a in range(weight_count):
                rows = weight_in[a].shape[0]
                side = rows // 2
                for k in range(1, chips):
                    block = place.block(chip=place.behind(k), half=1 - place.half)
                    for number in range(2):
                        piece = part(weight_out[a], block, rows, number * side, side)
                        send(
                            piece,
                            piece,
                            turn_send.at[a, number, k],
                            turn_recv.at[a, number, k],
                            place.pair(),
                        ).wait_recv()
                    piece = part(weight_out[a], block, rows)
                    launch(
                        send(
                            piece,
                            piece,
                            core_send.at[a, chips + k],
                            core_recv.at[a, chips + k],
                            place.pair(),
                        )
                    )

        def core_step():
            other = 1 - place.core
            for a in range(weight_count):
                rows = weight_in[a].shape[0]
                blocks = [place.block(core=other)]
                blocks += [place.block(place.behind(k), other) for k in range(1, chips)]
                blocks += [place.block(None, other, 1 - place.half)]
                blocks += [
                    place.block(place.behind(k), other, 1 - place.half) for k in range(1, chips)
                ]
                for at, block in enumerate(blocks):
                    piece = part(weight_out[a], block, rows)
                    send(
                        piece, piece, core_send.at[a, at], core_recv.at[a, at], place.pair()
                    ).wait_recv()

        line_step(1)
        near_step()
        for k in range(2, depth):
            line_step(k)
        turn_step()
        core_step()
        for copy in kept:
            copy.wait()
        for copy, condition in pending:
            if condition is None:
                copy.wait_send()
            else:
                pl.when(condition)(copy.wait_send)

    count = sizes["fsdp"] * halves
    shapes = [jax.ShapeDtypeStruct((depth * v.shape[0], v.shape[1]), v.dtype) for v in lines]
    shapes += [jax.ShapeDtypeStruct((count * v.shape[0], v.shape[1]), v.dtype) for v in weights]
    return pl.pallas_call(
        kernel,
        out_shape=tuple(shapes),
        in_specs=[ANY] * (line_count + weight_count),
        out_specs=(ANY,) * (line_count + weight_count),
        scratch_shapes=[
            DMA((line_count + weight_count,)),
            DMA((weight_count, chips)),
            DMA((weight_count, chips)),
            DMA((weight_count, 2, chips)),
            DMA((weight_count, 2, chips)),
            DMA((weight_count, 2 * chips)),
            DMA((weight_count, 2 * chips)),
        ]
        + ([DMA((line_count, 2, depth - 1))] * 2 if line_count else []),
        compiler_params=pltpu.CompilerParams(collective_id=collective_id, has_side_effects=True),
        cost_estimate=pl.CostEstimate(flops=0, bytes_accessed=380_000_000, transcendentals=0),
        name=name,
    )(*lines, *weights)


def reduce(sizes, paired, rights, small, collective_id, name):
    chips, halves = sizes["fsdp"] // 2, sizes["ctx"]
    groups = chips * halves
    paired_count, made_count = len(paired), len(rights)
    weight_count = paired_count + made_count
    block_rows = paired[0].shape[1]
    widths = [v.shape[2] for v in paired] + [v.shape[0] for _, v in rights]
    side = block_rows // 2

    def kernel(*refs):
        refs = list(refs)

        def take(count):
            taken = refs[:count]
            del refs[:count]
            return taken

        paired_in = take(paired_count)
        factors = take(2 * made_count)
        (small_ref,) = take(1)
        weight_out = take(weight_count)
        (small_out,) = take(1)
        made = take(made_count)
        own, turn_a, turn_b, near = (take(weight_count) for _ in range(4))
        pair = [None] * paired_count + take(made_count)
        load_sem, core_send, core_recv = take(3)
        turn_send, turn_recv, near_send, near_recv = take(4)
        small_pair, small_near, small_far, small_send, small_recv = take(5)
        place = Place(sizes)
        greet(plane(place))
        pending = []

        def launch(copy, condition=None):
            if condition is None:
                copy.start()
            else:
                pl.when(condition)(copy.start)
            pending.append((copy, condition))

        other = 1 - place.core
        for a in range(paired_count):
            for number in range(groups):
                pltpu.make_async_copy(
                    paired_in[a].at[number], own[a].at[number], load_sem.at[a, number]
                ).start()

        def make(a):
            at = a - paired_count
            multiply("tt", factors[2 * at], factors[2 * at + 1], [made[at]])
            for number in range(groups):
                chip, half = number // halves, number % halves
                theirs = place.block(chip, other, half)
                mine = place.block(chip, place.core, half)
                launch(
                    send(
                        made[at].at[pl.ds(pl.multiple_of(theirs * block_rows, 16), block_rows)],
                        pair[a].at[number],
                        core_send.at[a, number],
                        core_recv.at[a, number],
                        place.pair(),
                    )
                )
                pltpu.make_async_copy(
                    made[at].at[pl.ds(pl.multiple_of(mine * block_rows, 16), block_rows)],
                    own[a].at[number],
                    load_sem.at[a, number],
                ).start()

        def pair_sum(a, number):
            mine = own[a].at[number]
            pltpu.make_async_copy(mine, mine, load_sem.at[a, number]).wait()
            if a < paired_count:
                return
            theirs = pair[a].at[number]
            send(
                theirs, theirs, core_send.at[a, number], core_recv.at[a, number], place.pair()
            ).wait_recv()

            @pl.loop(0, block_rows, step=16)
            def _(r):
                at = pl.ds(pl.multiple_of(r, 16), 16)
                mine[at, :] = (mine[at, :].astype(f32) + theirs[at, :].astype(f32)).astype(bf16)

        def diagonal(a):
            for k in range(1, chips):
                number = place.ahead(k) * halves + 1 - place.half
                pair_sum(a, number)
                launch(
                    send(
                        own[a].at[number, pl.ds(0, side)],
                        turn_a[a].at[k - 1],
                        turn_send.at[a, 0, k],
                        turn_recv.at[a, 0, k],
                        place.across(),
                    )
                )
                launch(
                    send(
                        own[a].at[number, pl.ds(side, side)],
                        turn_b[a].at[k - 1],
                        turn_send.at[a, 1, k],
                        turn_recv.at[a, 1, k],
                        place.device(chip=place.ahead(k)),
                    )
                )

        def direct_pairs(a):
            for k in range(1, chips):
                pair_sum(a, place.ahead(k) * halves + place.half)
            pair_sum(a, place.chip * halves + 1 - place.half)

        def add_turn(a, number, first, refs_at):
            @pl.loop(0, side, step=16)
            def _(r):
                at = pl.ds(pl.multiple_of(first + r, 16), 16)
                total = own[a][number, at, :].astype(f32)
                for ref, k in refs_at:
                    total += ref[k, pl.ds(pl.multiple_of(r, 16), 16), :].astype(f32)
                own[a][number, at, :] = total.astype(bf16)

        def direct(a):
            for k in range(1, chips):
                number = place.ahead(k) * halves + place.half
                piece = turn_a[a].at[k - 1]
                send(
                    piece, piece, turn_send.at[a, 0, k], turn_recv.at[a, 0, k], place.across()
                ).wait_recv()
                add_turn(a, number, 0, [(turn_a[a], k - 1)])
                launch(
                    send(
                        own[a].at[number],
                        near[a].at[k],
                        near_send.at[a, k],
                        near_recv.at[a, k],
                        place.device(chip=place.ahead(k)),
                    )
                )
            for k in range(1, chips):
                piece = turn_b[a].at[k - 1]
                send(
                    piece, piece, turn_send.at[a, 1, k], turn_recv.at[a, 1, k], place.across()
                ).wait_recv()
            number = place.chip * halves + 1 - place.half
            add_turn(a, number, side, [(turn_b[a], k - 1) for k in range(1, chips)])
            launch(
                send(
                    own[a].at[number],
                    near[a].at[0],
                    near_send.at[a, 0],
                    near_recv.at[a, 0],
                    place.across(),
                )
            )

        def finish(a):
            for k in range(chips):
                piece = near[a].at[k]
                send(
                    piece, piece, near_send.at[a, k], near_recv.at[a, k], place.across()
                ).wait_recv()
            number = place.chip * halves + place.half

            @pl.loop(0, block_rows, step=16)
            def _(r):
                at = pl.ds(pl.multiple_of(r, 16), 16)
                total = own[a][number, at, :].astype(f32) + near[a][0, at, :].astype(f32)
                for k in range(1, chips):
                    total += near[a][k, at, :].astype(f32)
                weight_out[a][at, :] = total

        def swap_small(source, target, at, device):
            copy = send(source, target, small_send.at[at], small_recv.at[at], device)
            launch(copy)
            return copy

        swap_small(small_ref, small_pair, 0, place.pair())
        for a in range(paired_count):
            diagonal(a)
            direct_pairs(a)
        for a in range(paired_count, weight_count):
            make(a)
        send(small_pair, small_pair, small_send.at[0], small_recv.at[0], place.pair()).wait_recv()
        small_near[0] = small_ref[...] + small_pair[...]
        for k in range(1, chips):
            swap_small(small_near.at[0], small_near.at[k], k, place.device(chip=place.ahead(k)))
        for a in range(paired_count):
            direct(a)
        for a in range(paired_count, weight_count):
            diagonal(a)
            direct_pairs(a)
        total = small_near[0]
        for k in range(1, chips):
            piece = small_near.at[k]
            send(piece, piece, small_send.at[k], small_recv.at[k], place.pair()).wait_recv()
            total += small_near[k]
        small_far[0] = total
        swap_small(small_far.at[0], small_far.at[1], chips, place.across())
        for a in range(weight_count):
            pair_sum(a, place.chip * halves + place.half)
        for a in range(paired_count, weight_count):
            direct(a)
        for a in range(weight_count):
            finish(a)
        piece = small_far.at[1]
        send(piece, piece, small_send.at[chips], small_recv.at[chips], place.pair()).wait_recv()
        small_out[...] = small_far[0] + small_far[1]
        for copy, condition in pending:
            if condition is None:
                copy.wait_send()
            else:
                pl.when(condition)(copy.wait_send)

    shapes = [jax.ShapeDtypeStruct((block_rows, w), f32) for w in widths]
    shapes.append(jax.ShapeDtypeStruct(small.shape, f32))
    made_shapes = [
        jax.ShapeDtypeStruct((2 * groups * block_rows, w), bf16) for w in widths[paired_count:]
    ]
    scratch = [pltpu.VMEM((groups, block_rows, w), bf16) for w in widths]
    scratch += [pltpu.VMEM((chips - 1, side, w), bf16) for w in widths] * 2
    scratch += [pltpu.VMEM((chips, block_rows, w), bf16) for w in widths]
    scratch += [pltpu.VMEM((groups, block_rows, w), bf16) for w in widths[paired_count:]]
    scratch += [
        DMA((weight_count, groups)),
        DMA((weight_count, groups)),
        DMA((weight_count, groups)),
        DMA((weight_count, 2, chips)),
        DMA((weight_count, 2, chips)),
        DMA((weight_count, chips)),
        DMA((weight_count, chips)),
        pltpu.VMEM(small.shape, f32),
        pltpu.VMEM((chips,) + small.shape, f32),
        pltpu.VMEM((2,) + small.shape, f32),
        DMA((chips + 1,)),
        DMA((chips + 1,)),
    ]
    factors = [v for two in rights for v in two]
    return pl.pallas_call(
        kernel,
        out_shape=tuple(shapes + made_shapes),
        in_specs=[ANY] * (paired_count + 2 * made_count) + [VMEM],
        out_specs=(VMEM,) * len(shapes) + (ANY,) * made_count,
        scratch_shapes=scratch,
        compiler_params=pltpu.CompilerParams(
            collective_id=collective_id, has_side_effects=True, vmem_limit_bytes=60 << 20
        ),
        cost_estimate=pl.CostEstimate(flops=0, bytes_accessed=400_000_000, transcendentals=0),
        name=name,
    )(*paired, *factors, small)[: weight_count + 1]


def multiply(kind, left, right, outs, finish=None, extra=(), tile=512):
    dims = (((0 if kind[0] == "t" else 1,), (1 if kind[1] == "t" else 0,)), ((), ()))
    rows = left.shape[1] if kind[0] == "t" else left.shape[0]
    width = right.shape[0] if kind[1] == "t" else right.shape[1]
    depth = right.shape[1] if kind[1] == "t" else right.shape[0]
    tile = min(tile, width)
    right_spec = (
        pl.BlockSpec((tile, depth), lambda n: (n, 0))
        if kind[1] == "t"
        else pl.BlockSpec((depth, tile), lambda n: (0, n))
    )
    out_spec = pl.BlockSpec((rows, tile), lambda n: (0, n))
    extra_specs = [pl.BlockSpec((v.shape[0], tile), lambda n: (0, n)) for v in extra]

    def step(left_ref, right_ref, *rest):
        found = lax.dot_general(left_ref[...], right_ref[...], dims, preferred_element_type=f32)
        results = (found,)
        if finish is not None:
            results = finish(found, *(v[...] for v in rest[: len(extra)]))
        for ref, value in zip(rest[len(extra) :], results):
            ref[...] = value.astype(ref.dtype)

    pltpu.emit_pipeline(
        step,
        grid=(width // tile,),
        in_specs=[pl.BlockSpec(left.shape, lambda n: (0, 0)), right_spec, *extra_specs],
        out_specs=[out_spec] * len(outs),
    )(left, right, *extra, *outs)


def half_rows(ref, half, count):
    return ref.at[pl.ds(pl.multiple_of(half * count, count), count)]


def exchange_forward(sizes, triple, normed, up_full, up_bias, down_full):
    kinds, width, length = triple.shape
    count = width // 2
    rows, hidden = normed.shape[0], up_full.shape[1]

    def kernel(triple_ref, normed_ref, up_ref, bias_ref, down_ref, *rest):
        both, activation, slope, feed, sems = rest
        place = Place(sizes)
        greet([place.across()])

        def heads(half):
            return triple_ref.at[:, pl.ds(pl.multiple_of(half * count, count), count)]

        keep = pltpu.make_async_copy(heads(place.half), both.at[place.half], sems.at[0])
        away = send(
            heads(1 - place.half), both.at[place.half], sems.at[1], sems.at[2], place.across()
        )
        away.start()
        keep.start()

        def gelu(found, bias):
            return gelu_and_slope(found + bias)

        multiply("nn", normed_ref, up_ref, [activation, slope], gelu, [bias_ref])
        multiply("nt", activation, down_ref, [feed])
        keep.wait()
        away.wait_send()
        came = both.at[1 - place.half]
        send(came, came, sems.at[1], sems.at[2], place.across()).wait_recv()

    return pl.pallas_call(
        kernel,
        out_shape=(
            jax.ShapeDtypeStruct((2, kinds, count, length), bf16),
            jax.ShapeDtypeStruct((rows, hidden), bf16),
            jax.ShapeDtypeStruct((rows, hidden), bf16),
            jax.ShapeDtypeStruct((rows, down_full.shape[0]), f32),
        ),
        in_specs=[ANY] * 5,
        out_specs=(ANY,) * 4,
        scratch_shapes=[DMA((3,))],
        compiler_params=pltpu.CompilerParams(
            collective_id=4, has_side_effects=True, vmem_limit_bytes=60 << 20
        ),
        cost_estimate=pl.CostEstimate(flops=0, bytes_accessed=130_000_000, transcendentals=0),
        name="exchange_forward",
    )(triple, normed, up_full, up_bias, down_full)


def exchange_middle(sizes, attended, grad_attended, cotangent, down_full, slope):
    width, total = attended.shape
    length = total // 2
    rows, hidden = slope.shape

    def kernel(attended_ref, grad_ref, cotangent_ref, down_ref, slope_ref, *rest):
        full, both, grad_hidden, sems = rest
        place = Place(sizes)
        greet([place.across()])
        here, there = place.half, 1 - place.half

        def tokens(half):
            return attended_ref.at[:, pl.ds(pl.multiple_of(half * length, length), length)]

        copies = [
            send(
                tokens(there), half_rows(full, here, width), sems.at[0], sems.at[1], place.across()
            ),
            send(
                half_rows(grad_ref, there, width),
                both.at[here],
                sems.at[2],
                sems.at[3],
                place.across(),
            ),
        ]
        kept = [
            pltpu.make_async_copy(tokens(here), half_rows(full, here, width), sems.at[4]),
            pltpu.make_async_copy(half_rows(grad_ref, here, width), both.at[here], sems.at[5]),
        ]
        for copy in copies + kept:
            copy.start()
        multiply(
            "nn",
            cotangent_ref,
            down_ref,
            [grad_hidden],
            lambda found, slope: (found * slope.astype(f32),),
            [slope_ref],
        )
        for copy in kept:
            copy.wait()
        for number, came in enumerate((half_rows(full, there, width), both.at[there])):
            copies[number].wait_send()
            send(
                came, came, sems.at[2 * number], sems.at[2 * number + 1], place.across()
            ).wait_recv()

    return pl.pallas_call(
        kernel,
        out_shape=(
            jax.ShapeDtypeStruct((2 * width, length), bf16),
            jax.ShapeDtypeStruct((2, width, length), bf16),
            jax.ShapeDtypeStruct((rows, hidden), bf16),
        ),
        in_specs=[ANY] * 5,
        out_specs=(ANY,) * 3,
        scratch_shapes=[DMA((6,))],
        compiler_params=pltpu.CompilerParams(
            collective_id=5, has_side_effects=True, vmem_limit_bytes=60 << 20
        ),
        cost_estimate=pl.CostEstimate(flops=0, bytes_accessed=90_000_000, transcendentals=0),
        name="exchange_middle",
    )(attended, grad_attended, cotangent, down_full, slope)


def exchange_back(
    sizes, back, normed, grad_hidden, cotangent, activation, up_full, projection
):
    kinds, width, total = back.shape
    length = total // 2
    chips, halves = sizes["fsdp"] // 2, sizes["ctx"]
    rows, model = normed.shape
    hidden = grad_hidden.shape[1]
    span = model // (2 * chips)

    def kernel(
        back_ref, normed_ref, hidden_ref, cotangent_ref, activation_ref, up_ref, weight_ref, *rest
    ):
        full, up_sum, down_sum, block_in, up_made, down_made, up_came, down_came, feed = rest[:9]
        sems, core_send, core_recv = rest[9:]
        place = Place(sizes)
        greet([place.across(), place.pair()])
        here, there = place.half, 1 - place.half
        other = 1 - place.core

        def tokens(half):
            return back_ref.at[:, :, pl.ds(pl.multiple_of(half * length, length), length)]

        def heads(half):
            return full.at[:, pl.ds(pl.multiple_of(half * width, width), width)]

        away = send(tokens(there), heads(here), sems.at[0], sems.at[1], place.across())
        keep = pltpu.make_async_copy(tokens(here), heads(here), sems.at[2])
        away.start()
        keep.start()

        def to_pair(number, made, came):
            copies = []
            for chip in range(chips):
                copies.append(
                    send(
                        made.at[pl.ds(pl.multiple_of((2 * chip + other) * span, 16), span)],
                        came.at[pl.ds(chip * span, span)],
                        core_send.at[number, chip],
                        core_recv.at[number, chip],
                        place.pair(),
                    )
                )
                copies[-1].start()
            return copies

        def add_pair(copies, made, came, out):
            for copy in copies:
                copy.wait()

            def step(mine, theirs, out_ref):
                out_ref[...] = (mine[...].astype(f32) + theirs[...].astype(f32)).astype(bf16)

            wide = hidden // 2
            pltpu.emit_pipeline(
                step,
                grid=(chips, 2),
                in_specs=[
                    pl.BlockSpec((span, wide), lambda i, j: (2 * i + place.core, j)),
                    pl.BlockSpec((span, wide), lambda i, j: (i, j)),
                ],
                out_specs=[pl.BlockSpec((span, wide), lambda i, j: (i, j))],
            )(made, came, out)

        multiply("tn", normed_ref, hidden_ref, [up_made])
        up_copies = to_pair(0, up_made, up_came)
        multiply("tn", cotangent_ref, activation_ref, [down_made])
        down_copies = to_pair(1, down_made, down_came)
        multiply("nt", hidden_ref, up_ref, [feed])
        add_pair(up_copies, up_made, up_came, up_sum)
        add_pair(down_copies, down_made, down_came, down_sum)
        keep.wait()
        away.wait_send()
        send(heads(there), heads(there), sems.at[0], sems.at[1], place.across()).wait_recv()
        multiply(
            "tt",
            full.reshape(2 * kinds * width, length),
            weight_ref,
            [block_in],
            lambda found, before: (found + before,),
            [feed],
        )

    product = jax.ShapeDtypeStruct((model, hidden), bf16)
    part = jax.ShapeDtypeStruct((model // 2, hidden), bf16)
    results = pl.pallas_call(
        kernel,
        out_shape=(
            jax.ShapeDtypeStruct((kinds, 2 * width, length), bf16),
            part,
            part,
            jax.ShapeDtypeStruct((rows, model), bf16),
            product,
            product,
            part,
            part,
            jax.ShapeDtypeStruct((rows, model), f32),
        ),
        in_specs=[ANY] * 7,
        out_specs=(ANY,) * 9,
        scratch_shapes=[DMA((3,)), DMA((2, chips)), DMA((2, chips))],
        compiler_params=pltpu.CompilerParams(
            collective_id=6, has_side_effects=True, vmem_limit_bytes=60 << 20
        ),
        cost_estimate=pl.CostEstimate(flops=0, bytes_accessed=220_000_000, transcendentals=0),
        name="exchange_back",
    )(back, normed, grad_hidden, cotangent, activation, up_full, projection)
    return results[:4]


def small_reduce(sizes, blocks):
    count, depth = sizes["fsdp"] * sizes["ctx"], sizes["tp"]

    def kernel(blocks_ref, out_ref, landed, line, send_sem, recv_sem, line_send, line_recv):
        place = Place(sizes)
        peers = place.group()
        layers = [(place.layer + k) % depth for k in range(1, depth)]
        devices = [place.device(chip=a, core=b, half=c) for a, b, c in peers]
        greet(devices + [place.device(layer=k) for k in layers])
        copies = []
        for at, (chip, core, half) in enumerate(peers):
            copy = send(
                blocks_ref.at[place.block(chip, core, half)],
                landed.at[at],
                send_sem.at[at],
                recv_sem.at[at],
                devices[at],
            )
            copy.start()
            copies.append(copy)
        total = blocks_ref[place.block()]
        for at, copy in enumerate(copies):
            copy.wait()
            total += landed[at]
        line[0] = total
        copies = []
        for k, layer in enumerate(layers):
            copy = send(
                line.at[0],
                line.at[k + 1],
                line_send.at[k],
                line_recv.at[k],
                place.device(layer=layer),
            )
            copy.start()
            copies.append(copy)
        for k, copy in enumerate(copies):
            copy.wait()
            total += line[k + 1]
        out_ref[...] = total

    block = blocks.shape[1:]
    return pl.pallas_call(
        kernel,
        out_shape=jax.ShapeDtypeStruct(block, f32),
        in_specs=[VMEM],
        out_specs=VMEM,
        scratch_shapes=[
            pltpu.VMEM((count - 1,) + block, f32),
            pltpu.VMEM((depth,) + block, f32),
            DMA((count - 1,)),
            DMA((count - 1,)),
            DMA((depth - 1,)),
            DMA((depth - 1,)),
        ],
        compiler_params=pltpu.CompilerParams(collective_id=3, has_side_effects=True),
        name="small_reduce",
    )(blocks)


def tile_at(number):
    return pl.ds(pl.multiple_of(number * TILE, TILE), TILE)


def allowed(kb, j, start):
    places = kb * TILE + lax.broadcasted_iota(jnp.int32, (TILE, TILE), 0)
    own = j * TILE + lax.broadcasted_iota(jnp.int32, (TILE, TILE), 1)
    return (places >= start) & (places <= own)


def attend_kernel(
    low_ref,
    mid_ref,
    triple_ref,
    start_ref,
    attended_ref,
    log_ref,
    query_t,
    key_t,
    value_t,
    key_rows,
    scores,
):
    length = triple_ref.shape[3]
    heads = triple_ref.shape[2] // HD
    score_scale = 1.0 / math.sqrt(HD)
    for number, ref in enumerate((query_t, key_t, value_t)):
        for part in range(2):
            piece = triple_ref[part, number]
            ref[:, part * length : (part + 1) * length] = (
                piece * score_scale if number == 0 else piece
            )
    rows = [slice(h * HD, (h + 1) * HD) for h in range(heads)]
    for h in range(heads):
        key_rows[h] = key_t[rows[h], :].T

    @pl.loop(0, 2 * length // TILE)
    def _(j):
        here = tile_at(j)
        start = start_ref[:, here]
        low, mid = low_ref[j], mid_ref[j]
        queries = [query_t[row, here] for row in rows]

        def score_with(masked):
            def score(kb, highest):
                ok = allowed(kb, j, start) if masked else None
                raised = []
                for h in range(heads):
                    found = jnp.dot(
                        key_rows[h, tile_at(kb), :], queries[h], preferred_element_type=f32
                    )
                    if masked:
                        found = jnp.where(ok, found, big_negative)
                    scores[h, tile_at(kb), :] = found
                    raised.append(
                        jnp.maximum(highest[h], jnp.max(found, axis=0, keepdims=True))
                    )
                return tuple(raised)

            return score

        highest = tuple(jnp.full((1, TILE), big_negative, f32) for _ in range(heads))
        highest = lax.fori_loop(low, mid, score_with(True), highest)
        highest = lax.fori_loop(mid, j, score_with(False), highest)
        highest = score_with(True)(j, highest)

        def weigh(kb, carry):
            after = []
            for h in range(heads):
                total, mixed = carry[h]
                prob = jnp.exp(scores[h, tile_at(kb), :] - highest[h])
                total = total + jnp.sum(prob, axis=0, keepdims=True)
                mixed = mixed + jnp.dot(
                    value_t[rows[h], tile_at(kb)], prob.astype(bf16), preferred_element_type=f32
                )
                after.append((total, mixed))
            return tuple(after)

        empty = tuple(
            (jnp.zeros((1, TILE), f32), jnp.zeros((HD, TILE), f32)) for _ in range(heads)
        )
        result = lax.fori_loop(low, j + 1, weigh, empty)
        for h in range(heads):
            total, mixed = result[h]
            attended_ref[rows[h], here] = (mixed / total).astype(bf16)
            log_ref[h, :, here] = highest[h] + jnp.log(total)


def turned_back(values, cosine, sine):
    half_rot = ROT // 2
    leading = values[:half_rot]
    trailing = values[half_rot:ROT]
    return jnp.concatenate(
        [
            leading * cosine + trailing * sine,
            trailing * cosine - leading * sine,
            values[ROT:],
        ],
        axis=0,
    )


def attend_back_kernel(
    low_ref,
    mid_ref,
    triple_ref,
    grad_ref,
    attended_ref,
    log_ref,
    start_ref,
    cosine_ref,
    sine_ref,
    back_ref,
    query_t,
    key_t,
    grad_t,
    key_rows,
    value_rows,
    key_sum,
    value_sum,
):
    length = triple_ref.shape[3]
    heads = triple_ref.shape[2] // HD
    score_scale = 1.0 / math.sqrt(HD)
    rows = [slice(h * HD, (h + 1) * HD) for h in range(heads)]
    for part in range(2):
        span = slice(part * length, (part + 1) * length)
        query_t[:, span] = triple_ref[part, 0] * score_scale
        key_t[:, span] = triple_ref[part, 1]
        grad_t[:, span] = grad_ref[part]
        for h in range(heads):
            value_rows[h, span, :] = triple_ref[part, 2, rows[h]].T
    for h in range(heads):
        key_rows[h] = key_t[rows[h], :].T
    key_sum[...] = jnp.zeros_like(key_sum)
    value_sum[...] = jnp.zeros_like(value_sum)

    @pl.loop(0, 2 * length // TILE)
    def _(j):
        here = tile_at(j)
        start = start_ref[:, here]
        low, mid = low_ref[j], mid_ref[j]
        queries = [query_t[row, here] for row in rows]
        grads = [grad_t[row, here] for row in rows]
        query_rows = [value.T for value in queries]
        grad_rows = [value.T for value in grads]
        logs = [log_ref[h, :, here] for h in range(heads)]
        deltas = [
            jnp.sum(
                grads[h].astype(f32) * attended_ref[rows[h], here].astype(f32),
                axis=0,
                keepdims=True,
            )
            for h in range(heads)
        ]

        def pull_with(masked):
            def pull(kb, query_back):
                ok = allowed(kb, j, start) if masked else None
                after = []
                for h in range(heads):
                    score = jnp.dot(
                        key_rows[h, tile_at(kb), :], queries[h], preferred_element_type=f32
                    )
                    if masked:
                        score = jnp.where(ok, score, big_negative)
                    prob = jnp.exp(score - logs[h])
                    down = jnp.dot(
                        value_rows[h, tile_at(kb), :], grads[h], preferred_element_type=f32
                    )
                    score_back = (prob * (down - deltas[h])).astype(bf16)
                    value_sum[h, tile_at(kb), :] += jnp.dot(
                        prob.astype(bf16), grad_rows[h], preferred_element_type=f32
                    )
                    key_sum[h, tile_at(kb), :] += jnp.dot(
                        score_back, query_rows[h], preferred_element_type=f32
                    )
                    after.append(
                        query_back[h]
                        + jnp.dot(
                            key_t[rows[h], tile_at(kb)], score_back, preferred_element_type=f32
                        )
                    )
                return tuple(after)

            return pull

        query_back = tuple(jnp.zeros((HD, TILE), f32) for _ in range(heads))
        query_back = lax.fori_loop(low, mid, pull_with(True), query_back)
        query_back = lax.fori_loop(mid, j, pull_with(False), query_back)
        query_back = pull_with(True)(j, query_back)
        for h in range(heads):
            back_ref[0, rows[h], here] = turned_back(
                query_back[h] * score_scale, cosine_ref[:, here], sine_ref[:, here]
            ).astype(bf16)

    for h in range(heads):
        back_ref[1, rows[h], :] = turned_back(
            key_sum[h].T, cosine_ref[...], sine_ref[...]
        ).astype(bf16)
        back_ref[2, rows[h], :] = value_sum[h].T.astype(bf16)


def attend(low, mid, triple, start):
    width, length = triple.shape[2], triple.shape[3]
    total, heads = 2 * length, width // HD
    area = total * total // 3 * heads
    return pl.pallas_call(
        attend_kernel,
        out_shape=(
            jax.ShapeDtypeStruct((width, total), bf16),
            jax.ShapeDtypeStruct((heads, 1, total), f32),
        ),
        in_specs=[SMEM, SMEM, VMEM, VMEM],
        out_specs=(VMEM, VMEM),
        scratch_shapes=[pltpu.VMEM((width, total), bf16)] * 3
        + [pltpu.VMEM((heads, total, HD), bf16), pltpu.VMEM((heads, total, TILE), f32)],
        compiler_params=pltpu.CompilerParams(vmem_limit_bytes=48 << 20),
        cost_estimate=pl.CostEstimate(
            flops=50 * area * HD, bytes_accessed=8 * width * total, transcendentals=area
        ),
        name="attend",
    )(low, mid, triple, start)


def attend_back(low, mid, triple, grad, attended, log_sum, start, cosine, sine):
    width, length = triple.shape[2], triple.shape[3]
    total, heads = 2 * length, width // HD
    area = total * total // 3 * heads
    return pl.pallas_call(
        attend_back_kernel,
        out_shape=jax.ShapeDtypeStruct((3, width, total), bf16),
        in_specs=[SMEM, SMEM] + [VMEM] * 7,
        out_specs=VMEM,
        scratch_shapes=[pltpu.VMEM((width, total), bf16)] * 3
        + [pltpu.VMEM((heads, total, HD), bf16)] * 2
        + [pltpu.VMEM((heads, total, HD), f32)] * 2,
        compiler_params=pltpu.CompilerParams(vmem_limit_bytes=48 << 20),
        cost_estimate=pl.CostEstimate(
            flops=100 * area * HD, bytes_accessed=12 * width * total, transcendentals=area
        ),
        name="attend_back",
    )(low, mid, triple, grad, attended, log_sum, start, cosine, sine)


def rotate_rows(values, cosine, sine):
    half_rot = ROT // 2
    leading = values[:, :half_rot]
    trailing = values[:, half_rot:ROT]
    return jnp.concatenate(
        [
            leading * cosine - trailing * sine,
            trailing * cosine + leading * sine,
            values[:, ROT:],
        ],
        axis=1,
    )


def ordered(*values):
    return lax.optimization_barrier(values)


def body(
    sizes,
    tokens,
    segments,
    positions,
    norm_gain,
    norm_bias,
    projection_weight,
    projection_bias,
    dense_weight,
    dense_bias,
    up_weight,
    up_bias,
    down_weight,
    down_bias,
    cotangent,
):
    own_len, model_width = tokens.shape[1], tokens.shape[2]
    half_len = segments.shape[1]
    local_width = projection_weight.shape[2]
    hidden_width = up_weight.shape[1]
    shard_rows = norm_gain.shape[0]
    half = lax.axis_index("ctx")
    total_len = 2 * half_len

    vectors = jnp.stack([norm_gain, norm_bias, dense_bias, down_bias]).astype(f32)
    vectors = jnp.pad(vectors, ((0, 4), (0, 0)))
    numbers = jnp.pad(jnp.concatenate([segments, positions], axis=0), ((0, 6), (0, 0)))
    vectors_full, numbers_other = small_gather(sizes, vectors, numbers)
    gain_full, shift_full, bias_dense, bias_down = (
        vectors_full[:, row].reshape(model_width) for row in range(4)
    )

    def in_order(own, other, axis):
        return jnp.where(
            half == 0,
            jnp.concatenate([own, other], axis=axis),
            jnp.concatenate([other, own], axis=axis),
        )

    sequence = in_order(numbers, numbers_other, 1)
    segment_row, position_row = sequence[0], sequence[1]
    places = jnp.arange(total_len, dtype=jnp.int32)
    edges = jnp.concatenate([jnp.ones((1,), bool), segment_row[1:] != segment_row[:-1]])
    start = lax.cummax(jnp.where(edges, places, 0))
    tile_count = total_len // TILE
    low = start[::TILE] // TILE
    mid = jnp.minimum(
        jnp.maximum((start[TILE - 1 :: TILE] + TILE - 1) // TILE, low),
        jnp.arange(tile_count, dtype=jnp.int32),
    )
    exponent = jnp.arange(ROT // 2, dtype=f32) * 2.0 / ROT
    inverse = 10000.0 ** (-exponent)
    phase_angle = inverse[:, None] * position_row.astype(f32)[None, :]
    cosine_full, sine_full = jnp.cos(phase_angle), jnp.sin(phase_angle)
    own_start = half * half_len
    cosine_own = lax.dynamic_slice_in_dim(cosine_full, own_start, half_len, 1)
    sine_own = lax.dynamic_slice_in_dim(sine_full, own_start, half_len, 1)

    inputs = tokens[0].astype(f32)
    normed_values, norm_pull = jax.vjp(layer_norm, inputs, gain_full, shift_full)
    normed = lax.all_gather(normed_values.astype(bf16), "tp", axis=0, tiled=True)
    projection, up_full, dense_full, down_full = gather(
        sizes,
        [],
        [
            projection_weight.reshape(shard_rows, 3 * local_width),
            up_weight,
            dense_weight,
            down_weight,
        ],
        1,
        "gather_weights",
    )
    cotangent_rows = lax.all_gather(cotangent[0], "tp", axis=0, tiled=True)
    projected = lax.dot_general(projection, normed, row_by_col, preferred_element_type=f32)
    projected = projected + projection_bias.astype(f32).reshape(3 * local_width)[:, None]
    projected = projected.reshape(3, local_width, half_len)
    turned = rotate_rows(
        projected[:2].reshape(2 * local_width // HD, HD, half_len), cosine_own, sine_own
    ).reshape(2, local_width, half_len)
    triple = jnp.concatenate([turned, projected[2:]], axis=0).astype(bf16)
    both, activation, slope, feed_out = exchange_forward(
        sizes, triple, normed, up_full, up_bias.astype(f32)[None, :], down_full
    )
    attended_heads, log_sum = attend(low, mid, both, start[None, :])
    cotangent_rows, log_sum = ordered(cotangent_rows, log_sum)
    grad_attended = lax.dot_general(
        dense_full, cotangent_rows, row_by_col, preferred_element_type=f32
    ).astype(bf16)
    attended, grad_both, grad_hidden = exchange_middle(
        sizes, attended_heads, grad_attended, cotangent_rows, down_full, slope
    )
    block_out = (
        lax.dot_general(attended, dense_full, row_by_col, preferred_element_type=f32) + feed_out
    ).astype(bf16)
    branch_own = lax.psum_scatter(block_out, "tp", scatter_dimension=0, tiled=True)
    grad_both, block_out = ordered(grad_both, block_out)
    back_heads = attend_back(
        low,
        mid,
        both,
        grad_both,
        attended_heads,
        log_sum,
        start[None, :],
        cosine_full,
        sine_full,
    )
    grad_projected, up_sum, down_sum, block_in = exchange_back(
        sizes, back_heads, normed, grad_hidden, cotangent_rows, activation, up_full, projection
    )
    grad_projected = grad_projected.reshape(3 * local_width, half_len)
    block_in, branch_own = ordered(block_in, branch_own)
    grad_normed_own = lax.psum_scatter(block_in, "tp", scatter_dimension=0, tiled=True).astype(f32)
    hidden_sum = jnp.sum(grad_hidden.astype(f32), axis=0)
    projected_sum = jnp.sum(grad_projected.astype(f32), axis=1)
    small = jnp.concatenate([projected_sum, hidden_sum]).reshape(-1, 128)
    groups = sizes["fsdp"] // 2 * sizes["ctx"]
    up_part, down_part, projection_part, dense_part, small_total = reduce(
        sizes,
        [v.reshape(groups, shard_rows, hidden_width) for v in (up_sum, down_sum)],
        [(normed, grad_projected), (cotangent_rows, attended)],
        small,
        2,
        "reduce_weights",
    )
    layer_output = (inputs + branch_own.astype(f32) + (bias_dense + bias_down)).astype(bf16)
    cotangent_own = cotangent[0].astype(f32)
    grad_inputs, grad_gain, grad_shift = norm_pull(grad_normed_own)
    input_grad = grad_inputs + cotangent_own
    output_sum = jnp.sum(cotangent_own, axis=0)
    sums = jnp.stack([grad_gain, grad_shift, output_sum]).reshape(3, -1, shard_rows)
    sums = jnp.pad(sums.transpose(1, 0, 2), ((0, 0), (0, 5), (0, 0)))
    totals = small_reduce(sizes, sums)
    small_flat = small_total.reshape(-1)
    return (
        layer_output[None],
        input_grad[None],
        totals[0],
        totals[1],
        projection_part.reshape(shard_rows, 3, local_width),
        small_flat[: 3 * local_width].reshape(3, local_width),
        dense_part,
        totals[2],
        up_part,
        small_flat[3 * local_width :],
        down_part,
        totals[2],
    )


def solution(mesh):
    placed = (
        P("fsdp", ("ctx", "tp"), None),
        P("fsdp", "ctx"),
        P("fsdp", "ctx"),
        P(("fsdp", "ctx")),
        P(("fsdp", "ctx")),
        P(("fsdp", "ctx"), None, "tp"),
        P(None, "tp"),
        P(("fsdp", "ctx"), "tp"),
        P(("fsdp", "ctx")),
        P(("fsdp", "ctx"), "tp"),
        P("tp"),
        P(("fsdp", "ctx"), "tp"),
        P(("fsdp", "ctx")),
        P("fsdp", ("ctx", "tp"), None),
    )
    return jax.shard_map(
        functools.partial(body, dict(mesh.shape)),
        mesh=mesh,
        in_specs=placed,
        out_specs=(
            P("fsdp", ("ctx", "tp"), None),
            P("fsdp", ("ctx", "tp"), None),
            P(("fsdp", "ctx")),
            P(("fsdp", "ctx")),
            P(("fsdp", "ctx"), None, "tp"),
            P(None, "tp"),
            P(("fsdp", "ctx"), "tp"),
            P(("fsdp", "ctx")),
            P(("fsdp", "ctx"), "tp"),
            P("tp"),
            P(("fsdp", "ctx"), "tp"),
            P(("fsdp", "ctx")),
        ),
        check_vma=False,
    )
```

```python
import functools
import math

import jax
import jax.numpy as jnp
from jax import lax
from jax.experimental import pallas as pl
from jax.experimental.pallas import tpu as pltpu
from jax.sharding import PartitionSpec as P

HD = 64
ROT = 32
TILE = 256

epsilon = 1e-05
big_negative = -1000000000.0
root_two_over_pi = 0.7978845608028654
contract_rows = (((0,), (0,)), ((), ()))
contract_cols = (((1,), (1,)), ((), ()))
row_by_col = (((0,), (1,)), ((), ()))
MESH = pl.DeviceIdType.MESH
ANY = pl.BlockSpec(memory_space=pl.ANY)
VMEM = pl.BlockSpec(memory_space=pltpu.VMEM)
SMEM = pl.BlockSpec(memory_space=pltpu.SMEM)
DMA = pltpu.SemaphoreType.DMA
f32 = jnp.float32
bf16 = jnp.bfloat16


def layer_norm(values, gain_full, shift_full):
    center = jnp.mean(values, axis=-1, keepdims=True)
    centered = values - center
    spread = jnp.mean(centered * centered, axis=-1, keepdims=True)
    return centered * lax.rsqrt(spread + epsilon) * gain_full + shift_full


def gelu_and_slope(values):
    turned = jnp.tanh(root_two_over_pi * (values + 0.044715 * values * values * values))
    slope = 0.5 * (1.0 + turned) + 0.5 * values * (1.0 - turned * turned) * root_two_over_pi * (
        1.0 + 3.0 * 0.044715 * values * values
    )
    return 0.5 * values * (1.0 + turned), slope


class Place:
    def __init__(self, sizes):
        self.chips = sizes["fsdp"] // 2
        self.halves = sizes["ctx"]
        self.depth = sizes["tp"]
        lane = lax.axis_index("fsdp")
        self.chip = lane // 2
        self.core = lane % 2
        self.half = lax.axis_index("ctx")
        self.layer = lax.axis_index("tp")

    def device(self, chip=None, core=None, half=None, layer=None):
        chip = self.chip if chip is None else chip
        core = self.core if core is None else core
        half = self.half if half is None else half
        layer = self.layer if layer is None else layer
        return (chip * 2 + core, half, layer)

    def block(self, chip=None, core=None, half=None):
        chip = self.chip if chip is None else chip
        core = self.core if core is None else core
        half = self.half if half is None else half
        return (chip * 2 + core) * self.halves + half

    def ahead(self, k):
        return (self.chip + k) % self.chips

    def behind(self, k):
        return (self.chip + self.chips - k) % self.chips

    def pair(self):
        return self.device(core=1 - self.core)

    def across(self):
        return self.device(half=1 - self.half)

    def group(self):
        found = []
        for k in range(self.chips):
            for core in range(2):
                for half in range(2):
                    if k or core or half:
                        found.append(
                            (self.ahead(k), (self.core + core) % 2, (self.half + half) % 2)
                        )
        return found


def greet(devices):
    barrier = pltpu.get_barrier_semaphore()
    for device in devices:
        pl.semaphore_signal(barrier, inc=1, device_id=device, device_id_type=MESH)
    pl.semaphore_wait(barrier, len(devices))


def send(source, target, send_sem, recv_sem, device):
    return pltpu.make_async_remote_copy(
        src_ref=source,
        dst_ref=target,
        send_sem=send_sem,
        recv_sem=recv_sem,
        device_id=device,
        device_id_type=MESH,
    )


def plane(place):
    found = [place.device(chip=place.ahead(k)) for k in range(1, place.chips)]
    return found + [place.across(), place.pair()]


def small_gather(sizes, block, pairs):
    count = sizes["fsdp"] * sizes["ctx"]

    def kernel(block_ref, pair_ref, full_ref, other_ref, send_sem, recv_sem, keep_sem, swap_sem):
        place = Place(sizes)
        peers = place.group()
        greet([place.device(chip=a, core=b, half=c) for a, b, c in peers])
        mine = place.block()
        keep = pltpu.make_async_copy(block_ref, full_ref.at[mine], keep_sem)
        keep.start()
        swap = send(pair_ref, other_ref, swap_sem.at[0], swap_sem.at[1], place.across())
        swap.start()
        copies = []
        for at, (chip, core, half) in enumerate(peers):
            copy = send(
                block_ref,
                full_ref.at[mine],
                send_sem.at[at],
                recv_sem.at[at],
                place.device(chip=chip, core=core, half=half),
            )
            copy.start()
            copies.append(copy)
        keep.wait()
        for at, copy in enumerate(copies):
            k, core, half = at_of(at)
            source = place.block(
                place.behind(k), (place.core + core) % 2, (place.half + half) % 2
            )
            copy.wait_send()
            send(
                block_ref, full_ref.at[source], send_sem.at[at], recv_sem.at[at], place.pair()
            ).wait_recv()
        swap.wait()

    def at_of(at):
        return (at + 1) // 4, ((at + 1) // 2) % 2, (at + 1) % 2

    return pl.pallas_call(
        kernel,
        out_shape=(
            jax.ShapeDtypeStruct((count,) + block.shape, block.dtype),
            jax.ShapeDtypeStruct(pairs.shape, pairs.dtype),
        ),
        in_specs=[VMEM, VMEM],
        out_specs=(VMEM, VMEM),
        scratch_shapes=[DMA((count - 1,)), DMA((count - 1,)), DMA, DMA((2,))],
        compiler_params=pltpu.CompilerParams(collective_id=0, has_side_effects=True),
        name="small_gather",
    )(block, pairs)


def gather(sizes, weights, collective_id, name):
    chips, halves = sizes["fsdp"] // 2, sizes["ctx"]
    weight_count = len(weights)

    def kernel(*refs):
        weight_in, weight_out = refs[:weight_count], refs[weight_count : 2 * weight_count]
        keep, near_send, near_recv, turn_send, turn_recv, core_send, core_recv = refs[
            2 * weight_count :
        ]
        place = Place(sizes)
        greet(plane(place))

        def part(a, block, first=0, count=None):
            rows = weight_in[a].shape[-2]
            count = rows if count is None else count
            span = pl.ds(pl.multiple_of(block * rows + first, 16), count)
            if len(weight_out[a].shape) == 3:
                return weight_out[a].at[:, span]
            return weight_out[a].at[span]

        pending = []

        def launch(copy):
            copy.start()
            pending.append(copy)

        for a in range(weight_count):
            own = part(a, place.block())
            for k in range(1, chips):
                launch(
                    send(
                        weight_in[a],
                        own,
                        near_send.at[a, k],
                        near_recv.at[a, k],
                        place.device(chip=place.ahead(k)),
                    )
                )
            launch(
                send(weight_in[a], own, near_send.at[a, 0], near_recv.at[a, 0], place.across())
            )
            launch(send(weight_in[a], own, core_send.at[a, 0], core_recv.at[a, 0], place.pair()))
        kept = []
        for a in range(weight_count):
            kept.append(pltpu.make_async_copy(weight_in[a], part(a, place.block()), keep.at[a]))
            kept[-1].start()

        for a in range(weight_count):
            side = weight_in[a].shape[-2] // 2
            for k in range(1, chips):
                block = place.block(chip=place.behind(k))
                piece = part(a, block)
                send(
                    piece, piece, near_send.at[a, k], near_recv.at[a, k], place.pair()
                ).wait_recv()
                top = part(a, block, 0, side)
                launch(
                    send(top, top, turn_send.at[a, 0, k], turn_recv.at[a, 0, k], place.across())
                )
                launch(send(piece, piece, core_send.at[a, k], core_recv.at[a, k], place.pair()))
            block = place.block(half=1 - place.half)
            piece = part(a, block)
            send(piece, piece, near_send.at[a, 0], near_recv.at[a, 0], place.pair()).wait_recv()
            low = part(a, block, side, side)
            for k in range(1, chips):
                launch(
                    send(
                        low,
                        low,
                        turn_send.at[a, 1, k],
                        turn_recv.at[a, 1, k],
                        place.device(chip=place.ahead(k)),
                    )
                )
            launch(
                send(piece, piece, core_send.at[a, chips], core_recv.at[a, chips], place.pair())
            )

        for a in range(weight_count):
            side = weight_in[a].shape[-2] // 2
            for k in range(1, chips):
                block = place.block(chip=place.behind(k), half=1 - place.half)
                for number in range(2):
                    piece = part(a, block, number * side, side)
                    send(
                        piece,
                        piece,
                        turn_send.at[a, number, k],
                        turn_recv.at[a, number, k],
                        place.pair(),
                    ).wait_recv()
                piece = part(a, block)
                launch(
                    send(
                        piece,
                        piece,
                        core_send.at[a, chips + k],
                        core_recv.at[a, chips + k],
                        place.pair(),
                    )
                )

        other = 1 - place.core
        for a in range(weight_count):
            blocks = [place.block(core=other)]
            blocks += [place.block(place.behind(k), other) for k in range(1, chips)]
            blocks += [place.block(None, other, 1 - place.half)]
            blocks += [
                place.block(place.behind(k), other, 1 - place.half) for k in range(1, chips)
            ]
            for at, block in enumerate(blocks):
                piece = part(a, block)
                send(
                    piece, piece, core_send.at[a, at], core_recv.at[a, at], place.pair()
                ).wait_recv()
        for copy in kept:
            copy.wait()
        for copy in pending:
            copy.wait_send()

    count = sizes["fsdp"] * halves
    return pl.pallas_call(
        kernel,
        out_shape=tuple(
            jax.ShapeDtypeStruct(v.shape[:-2] + (count * v.shape[-2], v.shape[-1]), v.dtype)
            for v in weights
        ),
        in_specs=[VMEM] * weight_count,
        out_specs=(ANY,) * weight_count,
        scratch_shapes=[
            DMA((weight_count,)),
            DMA((weight_count, chips)),
            DMA((weight_count, chips)),
            DMA((weight_count, 2, chips)),
            DMA((weight_count, 2, chips)),
            DMA((weight_count, 2 * chips)),
            DMA((weight_count, 2 * chips)),
        ],
        compiler_params=pltpu.CompilerParams(collective_id=collective_id, has_side_effects=True),
        cost_estimate=pl.CostEstimate(flops=0, bytes_accessed=380_000_000, transcendentals=0),
        name=name,
    )(*weights)


def reduce(sizes, paired, turned, rights, splits, small, collective_id, name):
    chips, halves = sizes["fsdp"] // 2, sizes["ctx"]
    groups = chips * halves
    paired_count, made_count = len(paired), len(rights)
    weight_count = paired_count + made_count
    block_rows = paired[0].shape[1]
    widths = [v.shape[2] for v in paired] + [v.shape[0] for _, v in rights]
    side = block_rows // 2

    def kernel(*refs):
        refs = list(refs)

        def take(count):
            taken = refs[:count]
            del refs[:count]
            return taken

        paired_in = take(paired_count)
        turned_in = take(2 * paired_count)
        factors = take(2 * made_count)
        (small_ref,) = take(1)
        weight_out = take(weight_count)
        (small_out,) = take(1)
        made = take(made_count)
        own, turn_a, turn_b, near = (take(weight_count) for _ in range(4))
        pair = [None] * paired_count + take(made_count)
        load_sem, core_send, core_recv = take(3)
        turn_send, turn_recv, near_send, near_recv = take(4)
        small_pair, small_near, small_far, small_send, small_recv = take(5)
        place = Place(sizes)
        greet(plane(place))
        pending = []

        def launch(copy, condition=None):
            if condition is None:
                copy.start()
            else:
                pl.when(condition)(copy.start)
            pending.append((copy, condition))

        other = 1 - place.core
        for a in range(paired_count):
            needed = [place.ahead(k) * halves + place.half for k in range(1, chips)]
            needed += [place.chip * halves + half for half in range(halves)]
            for number in needed:
                pltpu.make_async_copy(
                    paired_in[a].at[number], own[a].at[number], load_sem.at[a, number]
                ).start()
            for way, target in enumerate((turn_a[a], turn_b[a])):
                for k in range(1, chips):
                    pltpu.make_async_copy(
                        turned_in[2 * a + way].at[k - 1],
                        target.at[k - 1],
                        turn_recv.at[a, way, k],
                    ).start()

        def make(a):
            at = a - paired_count
            multiply("tt", factors[2 * at], factors[2 * at + 1], [made[at]])
            for number in range(groups):
                chip, half = number // halves, number % halves
                theirs = place.block(chip, other, half)
                mine = place.block(chip, place.core, half)
                launch(
                    send(
                        made[at].at[pl.ds(pl.multiple_of(theirs * block_rows, 16), block_rows)],
                        pair[a].at[number],
                        core_send.at[a, number],
                        core_recv.at[a, number],
                        place.pair(),
                    )
                )
                pltpu.make_async_copy(
                    made[at].at[pl.ds(pl.multiple_of(mine * block_rows, 16), block_rows)],
                    own[a].at[number],
                    load_sem.at[a, number],
                ).start()

        def pair_sum(a, number):
            mine = own[a].at[number]
            pltpu.make_async_copy(mine, mine, load_sem.at[a, number]).wait()
            if a < paired_count:
                return
            theirs = pair[a].at[number]
            send(
                theirs, theirs, core_send.at[a, number], core_recv.at[a, number], place.pair()
            ).wait_recv()

            @pl.loop(0, block_rows, step=16)
            def _(r):
                at = pl.ds(pl.multiple_of(r, 16), 16)
                mine[at, :] = (mine[at, :].astype(f32) + theirs[at, :].astype(f32)).astype(bf16)

        def diagonal(a):
            for k in range(1, chips):
                number = place.ahead(k) * halves + 1 - place.half
                pair_sum(a, number)
                launch(
                    send(
                        own[a].at[number, pl.ds(0, side)],
                        turn_a[a].at[k - 1],
                        turn_send.at[a, 0, k],
                        turn_recv.at[a, 0, k],
                        place.across(),
                    )
                )
                launch(
                    send(
                        own[a].at[number, pl.ds(side, side)],
                        turn_b[a].at[k - 1],
                        turn_send.at[a, 1, k],
                        turn_recv.at[a, 1, k],
                        place.device(chip=place.ahead(k)),
                    )
                )

        def direct_pairs(a):
            for k in range(1, chips):
                pair_sum(a, place.ahead(k) * halves + place.half)
            pair_sum(a, place.chip * halves + 1 - place.half)

        def add_turn(a, number, first, refs_at):
            @pl.loop(0, side, step=16)
            def _(r):
                at = pl.ds(pl.multiple_of(first + r, 16), 16)
                total = own[a][number, at, :].astype(f32)
                for ref, k in refs_at:
                    total += ref[k, pl.ds(pl.multiple_of(r, 16), 16), :].astype(f32)
                own[a][number, at, :] = total.astype(bf16)

        def turn_wait(a, way, k):
            piece = (turn_a, turn_b)[way][a].at[k - 1]
            if a < paired_count:
                pltpu.make_async_copy(piece, piece, turn_recv.at[a, way, k]).wait()
            else:
                send(
                    piece, piece, turn_send.at[a, way, k], turn_recv.at[a, way, k], place.across()
                ).wait_recv()

        def direct(a):
            for k in range(1, chips):
                number = place.ahead(k) * halves + place.half
                turn_wait(a, 0, k)
                add_turn(a, number, 0, [(turn_a[a], k - 1)])
                launch(
                    send(
                        own[a].at[number],
                        near[a].at[k],
                        near_send.at[a, k],
                        near_recv.at[a, k],
                        place.device(chip=place.ahead(k)),
                    )
                )
            for k in range(1, chips):
                turn_wait(a, 1, k)
            number = place.chip * halves + 1 - place.half
            add_turn(a, number, side, [(turn_b[a], k - 1) for k in range(1, chips)])
            launch(
                send(
                    own[a].at[number],
                    near[a].at[0],
                    near_send.at[a, 0],
                    near_recv.at[a, 0],
                    place.across(),
                )
            )

        def finish(a):
            for k in range(chips):
                piece = near[a].at[k]
                send(
                    piece, piece, near_send.at[a, k], near_recv.at[a, k], place.across()
                ).wait_recv()
            number = place.chip * halves + place.half

            @pl.loop(0, block_rows, step=16)
            def _(r):
                at = pl.ds(pl.multiple_of(r, 16), 16)
                total = own[a][number, at, :].astype(f32) + near[a][0, at, :].astype(f32)
                for k in range(1, chips):
                    total += near[a][k, at, :].astype(f32)
                if splits[a] == 1:
                    weight_out[a][at, :] = total
                else:
                    wide = widths[a] // splits[a]
                    for kind in range(splits[a]):
                        weight_out[a][kind, at, :] = total[:, kind * wide : (kind + 1) * wide]

        def swap_small(source, target, at, device):
            copy = send(source, target, small_send.at[at], small_recv.at[at], device)
            launch(copy)
            return copy

        swap_small(small_ref, small_pair, 0, place.pair())
        for a in range(paired_count):
            direct_pairs(a)
            direct(a)
        for a in range(paired_count, weight_count):
            make(a)
        send(small_pair, small_pair, small_send.at[0], small_recv.at[0], place.pair()).wait_recv()
        small_near[0] = small_ref[...] + small_pair[...]
        for k in range(1, chips):
            swap_small(small_near.at[0], small_near.at[k], k, place.device(chip=place.ahead(k)))
        for a in range(paired_count, weight_count):
            diagonal(a)
            direct_pairs(a)
        total = small_near[0]
        for k in range(1, chips):
            piece = small_near.at[k]
            send(piece, piece, small_send.at[k], small_recv.at[k], place.pair()).wait_recv()
            total += small_near[k]
        small_far[0] = total
        swap_small(small_far.at[0], small_far.at[1], chips, place.across())
        for a in range(weight_count):
            pair_sum(a, place.chip * halves + place.half)
        for a in range(paired_count, weight_count):
            direct(a)
        for a in range(weight_count):
            finish(a)
        piece = small_far.at[1]
        send(piece, piece, small_send.at[chips], small_recv.at[chips], place.pair()).wait_recv()
        small_out[...] = small_far[0] + small_far[1]
        for copy, condition in pending:
            if condition is None:
                copy.wait_send()
            else:
                pl.when(condition)(copy.wait_send)

    shapes = [
        jax.ShapeDtypeStruct((block_rows, w) if n == 1 else (n, block_rows, w // n), f32)
        for w, n in zip(widths, splits)
    ]
    shapes.append(jax.ShapeDtypeStruct(small.shape, f32))
    made_shapes = [
        jax.ShapeDtypeStruct((2 * groups * block_rows, w), bf16) for w in widths[paired_count:]
    ]
    scratch = [pltpu.VMEM((groups, block_rows, w), bf16) for w in widths]
    scratch += [pltpu.VMEM((chips - 1, side, w), bf16) for w in widths] * 2
    scratch += [pltpu.VMEM((chips, block_rows, w), bf16) for w in widths]
    scratch += [pltpu.VMEM((groups, block_rows, w), bf16) for w in widths[paired_count:]]
    scratch += [
        DMA((weight_count, groups)),
        DMA((weight_count, groups)),
        DMA((weight_count, groups)),
        DMA((weight_count, 2, chips)),
        DMA((weight_count, 2, chips)),
        DMA((weight_count, chips)),
        DMA((weight_count, chips)),
        pltpu.VMEM(small.shape, f32),
        pltpu.VMEM((chips,) + small.shape, f32),
        pltpu.VMEM((2,) + small.shape, f32),
        DMA((chips + 1,)),
        DMA((chips + 1,)),
    ]
    factors = [v for two in rights for v in two]
    return pl.pallas_call(
        kernel,
        out_shape=tuple(shapes + made_shapes),
        in_specs=[ANY] * (3 * paired_count + 2 * made_count) + [VMEM],
        out_specs=(VMEM,) * len(shapes) + (ANY,) * made_count,
        scratch_shapes=scratch,
        compiler_params=pltpu.CompilerParams(
            collective_id=collective_id, has_side_effects=True, vmem_limit_bytes=60 << 20
        ),
        cost_estimate=pl.CostEstimate(flops=0, bytes_accessed=400_000_000, transcendentals=0),
        name=name,
    )(*paired, *turned, *factors, small)[: weight_count + 1]


def multiply(kind, left, right, outs, finish=None, extra=(), tile=512):
    dims = (((0 if kind[0] == "t" else 1,), (1 if kind[1] == "t" else 0,)), ((), ()))
    rows = left.shape[1] if kind[0] == "t" else left.shape[0]
    width = right.shape[0] if kind[1] == "t" else right.shape[1]
    depth = right.shape[1] if kind[1] == "t" else right.shape[0]
    tile = min(tile, width)
    right_spec = (
        pl.BlockSpec((tile, depth), lambda n: (n, 0))
        if kind[1] == "t"
        else pl.BlockSpec((depth, tile), lambda n: (0, n))
    )
    out_spec = pl.BlockSpec((rows, tile), lambda n: (0, n))
    extra_specs = [pl.BlockSpec((v.shape[0], tile), lambda n: (0, n)) for v in extra]

    def step(left_ref, right_ref, *rest):
        found = lax.dot_general(left_ref[...], right_ref[...], dims, preferred_element_type=f32)
        results = (found,)
        if finish is not None:
            results = finish(found, *(v[...] for v in rest[: len(extra)]))
        for ref, value in zip(rest[len(extra) :], results):
            ref[...] = value.astype(ref.dtype)

    pltpu.emit_pipeline(
        step,
        grid=(width // tile,),
        in_specs=[pl.BlockSpec(left.shape, lambda n: (0, 0)), right_spec, *extra_specs],
        out_specs=[out_spec] * len(outs),
    )(left, right, *extra, *outs)


def half_rows(ref, half, count):
    return ref.at[pl.ds(pl.multiple_of(half * count, count), count)]


def exchange_forward(sizes, triple, normed, up_full, up_bias, down_full):
    kinds, width, length = triple.shape
    count = width // 2
    rows, hidden = normed.shape[0], up_full.shape[1]

    def kernel(triple_ref, normed_ref, up_ref, bias_ref, down_ref, *rest):
        both, activation, slope, feed, stage, sems = rest
        place = Place(sizes)
        greet([place.across()])

        def heads(half):
            return triple_ref.at[:, pl.ds(pl.multiple_of(half * count, count), count)]

        load = pltpu.make_async_copy(heads(place.half), stage, sems.at[0])
        keep = pltpu.make_async_copy(stage, both.at[place.half], sems.at[3])
        away = send(
            heads(1 - place.half), both.at[place.half], sems.at[1], sems.at[2], place.across()
        )
        away.start()
        load.start()
        load.wait()
        keep.start()

        def gelu(found, bias):
            return gelu_and_slope(found + bias)

        multiply("nn", normed_ref, up_ref, [activation, slope], gelu, [bias_ref])
        multiply("nt", activation, down_ref, [feed])
        keep.wait()
        away.wait_send()
        came = both.at[1 - place.half]
        send(came, came, sems.at[1], sems.at[2], place.across()).wait_recv()

    return pl.pallas_call(
        kernel,
        out_shape=(
            jax.ShapeDtypeStruct((2, kinds, count, length), bf16),
            jax.ShapeDtypeStruct((rows, hidden), bf16),
            jax.ShapeDtypeStruct((rows, hidden), bf16),
            jax.ShapeDtypeStruct((rows, down_full.shape[0]), f32),
        ),
        in_specs=[ANY] * 5,
        out_specs=(ANY,) * 4,
        scratch_shapes=[pltpu.VMEM((kinds, count, length), bf16), DMA((4,))],
        compiler_params=pltpu.CompilerParams(
            collective_id=4, has_side_effects=True, vmem_limit_bytes=60 << 20
        ),
        cost_estimate=pl.CostEstimate(flops=0, bytes_accessed=130_000_000, transcendentals=0),
        name="exchange_forward",
    )(triple, normed, up_full, up_bias, down_full)


def exchange_middle(sizes, attended, grad_attended, cotangent, down_full, slope):
    width, total = attended.shape
    length = total // 2
    rows, hidden = slope.shape

    def kernel(attended_ref, grad_ref, cotangent_ref, down_ref, slope_ref, *rest):
        full, both, grad_hidden, token_stage, head_stage, sems = rest
        place = Place(sizes)
        greet([place.across()])
        here, there = place.half, 1 - place.half

        def tokens(half):
            return attended_ref.at[:, pl.ds(pl.multiple_of(half * length, length), length)]

        copies = [
            send(
                tokens(there), half_rows(full, here, width), sems.at[0], sems.at[1], place.across()
            ),
            send(
                half_rows(grad_ref, there, width),
                both.at[here],
                sems.at[2],
                sems.at[3],
                place.across(),
            ),
        ]
        loads = [
            pltpu.make_async_copy(tokens(here), token_stage, sems.at[4]),
            pltpu.make_async_copy(half_rows(grad_ref, here, width), head_stage, sems.at[5]),
        ]
        kept = [
            pltpu.make_async_copy(token_stage, half_rows(full, here, width), sems.at[6]),
            pltpu.make_async_copy(head_stage, both.at[here], sems.at[7]),
        ]
        for copy in copies + loads:
            copy.start()
        for load, copy in zip(loads, kept):
            load.wait()
            copy.start()
        multiply(
            "nn",
            cotangent_ref,
            down_ref,
            [grad_hidden],
            lambda found, slope: (found * slope.astype(f32),),
            [slope_ref],
        )
        for copy in kept:
            copy.wait()
        for number, came in enumerate((half_rows(full, there, width), both.at[there])):
            copies[number].wait_send()
            send(
                came, came, sems.at[2 * number], sems.at[2 * number + 1], place.across()
            ).wait_recv()

    return pl.pallas_call(
        kernel,
        out_shape=(
            jax.ShapeDtypeStruct((2 * width, length), bf16),
            jax.ShapeDtypeStruct((2, width, length), bf16),
            jax.ShapeDtypeStruct((rows, hidden), bf16),
        ),
        in_specs=[ANY] * 5,
        out_specs=(ANY,) * 3,
        scratch_shapes=[pltpu.VMEM((width, length), bf16)] * 2 + [DMA((8,))],
        compiler_params=pltpu.CompilerParams(
            collective_id=5, has_side_effects=True, vmem_limit_bytes=60 << 20
        ),
        cost_estimate=pl.CostEstimate(flops=0, bytes_accessed=90_000_000, transcendentals=0),
        name="exchange_middle",
    )(attended, grad_attended, cotangent, down_full, slope)


def exchange_back(
    sizes, back, normed, grad_hidden, cotangent, activation, up_full, projection
):
    kinds, width, total = back.shape
    length = total // 2
    chips, halves = sizes["fsdp"] // 2, sizes["ctx"]
    rows, model = normed.shape
    hidden = grad_hidden.shape[1]
    span = model // (2 * chips)
    shard = span // halves
    side = shard // 2

    def kernel(
        back_ref, normed_ref, hidden_ref, cotangent_ref, activation_ref, up_ref, weight_ref, *rest
    ):
        full, sums, turns, block_in = rest[0], rest[1:3], rest[3:7], rest[7]
        made_in, came_in, feed = rest[8:10], rest[10:12], rest[12]
        stage, sems, core_send, core_recv, turn_send, turn_recv = rest[13:]
        place = Place(sizes)
        greet(plane(place))
        here, there = place.half, 1 - place.half
        other = 1 - place.core

        def tokens(half):
            return back_ref.at[:, :, pl.ds(pl.multiple_of(half * length, length), length)]

        def heads(half):
            return full.at[:, pl.ds(pl.multiple_of(half * width, width), width)]

        away = send(tokens(there), heads(here), sems.at[0], sems.at[1], place.across())
        load = pltpu.make_async_copy(tokens(here), stage, sems.at[2])
        keep = pltpu.make_async_copy(stage, heads(here), sems.at[3])
        away.start()
        load.start()
        load.wait()
        keep.start()

        def to_pair(number):
            made, came = made_in[number], came_in[number]
            copies = []
            for chip in range(chips):
                copies.append(
                    send(
                        made.at[pl.ds(pl.multiple_of((2 * chip + other) * span, 16), span)],
                        came.at[pl.ds(chip * span, span)],
                        core_send.at[number, chip],
                        core_recv.at[number, chip],
                        place.pair(),
                    )
                )
                copies[-1].start()
            return copies

        def add_pair(number, copies):
            made, came, out = made_in[number], came_in[number], sums[number]
            for copy in copies:
                copy.wait()

            def step(mine, theirs, out_ref):
                out_ref[...] = (mine[...].astype(f32) + theirs[...].astype(f32)).astype(bf16)

            wide = hidden // 2
            pltpu.emit_pipeline(
                step,
                grid=(chips, 2),
                in_specs=[
                    pl.BlockSpec((span, wide), lambda i, j: (2 * i + place.core, j)),
                    pl.BlockSpec((span, wide), lambda i, j: (i, j)),
                ],
                out_specs=[pl.BlockSpec((span, wide), lambda i, j: (i, j))],
            )(made, came, out)

        def turn(number):
            out = sums[number]
            copies = []
            for k in range(1, chips):
                block = (place.ahead(k) * halves + there) * shard
                for way, device in enumerate(
                    (place.across(), place.device(chip=place.ahead(k)))
                ):
                    copies.append(
                        send(
                            out.at[pl.ds(pl.multiple_of(block + way * side, 16), side)],
                            turns[2 * number + way].at[k - 1],
                            turn_send.at[number, way, k],
                            turn_recv.at[number, way, k],
                            device,
                        )
                    )
                    copies[-1].start()
            return copies

        multiply("tn", normed_ref, hidden_ref, [made_in[0]])
        up_copies = to_pair(0)
        multiply("tn", cotangent_ref, activation_ref, [made_in[1]])
        down_copies = to_pair(1)
        add_pair(0, up_copies)
        turned = turn(0)
        multiply("nt", hidden_ref, up_ref, [feed])
        add_pair(1, down_copies)
        turned += turn(1)
        keep.wait()
        away.wait_send()
        send(heads(there), heads(there), sems.at[0], sems.at[1], place.across()).wait_recv()
        flat = full.reshape(2 * kinds * width, length)

        def step(left_ref, right_ref, before_ref, out_ref):
            found = before_ref[...]
            for kind in range(kinds):
                rows_of = pl.ds(kind * 2 * width, 2 * width)
                found += lax.dot_general(
                    left_ref[rows_of, :],
                    right_ref[kind],
                    row_by_col,
                    preferred_element_type=f32,
                )
            out_ref[...] = found.astype(bf16)

        tile = min(512, model)
        pltpu.emit_pipeline(
            step,
            grid=(model // tile,),
            in_specs=[
                pl.BlockSpec(flat.shape, lambda n: (0, 0)),
                pl.BlockSpec((kinds, tile, 2 * width), lambda n: (0, n, 0)),
                pl.BlockSpec((rows, tile), lambda n: (0, n)),
            ],
            out_specs=[pl.BlockSpec((rows, tile), lambda n: (0, n))],
        )(flat, weight_ref, feed, block_in)
        for copy in turned:
            copy.wait()

    product = jax.ShapeDtypeStruct((model, hidden), bf16)
    part = jax.ShapeDtypeStruct((model // 2, hidden), bf16)
    results = pl.pallas_call(
        kernel,
        out_shape=(
            jax.ShapeDtypeStruct((kinds, 2 * width, length), bf16),
            part,
            part,
            *[jax.ShapeDtypeStruct((chips - 1, side, hidden), bf16)] * 4,
            jax.ShapeDtypeStruct((rows, model), bf16),
            product,
            product,
            part,
            part,
            jax.ShapeDtypeStruct((rows, model), f32),
        ),
        in_specs=[ANY] * 7,
        out_specs=(ANY,) * 13,
        scratch_shapes=[
            pltpu.VMEM((kinds, width, length), bf16),
            DMA((4,)),
            DMA((2, chips)),
            DMA((2, chips)),
            DMA((2, 2, chips)),
            DMA((2, 2, chips)),
        ],
        compiler_params=pltpu.CompilerParams(
            collective_id=6, has_side_effects=True, vmem_limit_bytes=60 << 20
        ),
        cost_estimate=pl.CostEstimate(flops=0, bytes_accessed=220_000_000, transcendentals=0),
        name="exchange_back",
    )(back, normed, grad_hidden, cotangent, activation, up_full, projection)
    return results[:8]


def small_reduce(sizes, blocks):
    count, depth = sizes["fsdp"] * sizes["ctx"], sizes["tp"]

    def kernel(blocks_ref, out_ref, landed, line, send_sem, recv_sem, line_send, line_recv):
        place = Place(sizes)
        peers = place.group()
        layers = [(place.layer + k) % depth for k in range(1, depth)]
        devices = [place.device(chip=a, core=b, half=c) for a, b, c in peers]
        greet(devices + [place.device(layer=k) for k in layers])
        copies = []
        for at, (chip, core, half) in enumerate(peers):
            copy = send(
                blocks_ref.at[place.block(chip, core, half)],
                landed.at[at],
                send_sem.at[at],
                recv_sem.at[at],
                devices[at],
            )
            copy.start()
            copies.append(copy)
        total = blocks_ref[place.block()]
        for at, copy in enumerate(copies):
            copy.wait()
            total += landed[at]
        line[0] = total
        copies = []
        for k, layer in enumerate(layers):
            copy = send(
                line.at[0],
                line.at[k + 1],
                line_send.at[k],
                line_recv.at[k],
                place.device(layer=layer),
            )
            copy.start()
            copies.append(copy)
        for k, copy in enumerate(copies):
            copy.wait()
            total += line[k + 1]
        out_ref[...] = total

    block = blocks.shape[1:]
    return pl.pallas_call(
        kernel,
        out_shape=jax.ShapeDtypeStruct(block, f32),
        in_specs=[VMEM],
        out_specs=VMEM,
        scratch_shapes=[
            pltpu.VMEM((count - 1,) + block, f32),
            pltpu.VMEM((depth,) + block, f32),
            DMA((count - 1,)),
            DMA((count - 1,)),
            DMA((depth - 1,)),
            DMA((depth - 1,)),
        ],
        compiler_params=pltpu.CompilerParams(collective_id=3, has_side_effects=True),
        name="small_reduce",
    )(blocks)


def tile_at(number):
    return pl.ds(pl.multiple_of(number * TILE, TILE), TILE)


def allowed(kb, j, start):
    places = kb * TILE + lax.broadcasted_iota(jnp.int32, (TILE, TILE), 0)
    own = j * TILE + lax.broadcasted_iota(jnp.int32, (TILE, TILE), 1)
    return (places >= start) & (places <= own)


def attend_kernel(
    low_ref,
    mid_ref,
    triple_ref,
    start_ref,
    attended_ref,
    log_ref,
    query_t,
    key_t,
    value_t,
    key_rows,
    scores,
):
    length = triple_ref.shape[3]
    heads = triple_ref.shape[2] // HD
    score_scale = 1.0 / math.sqrt(HD)
    for number, ref in enumerate((query_t, key_t, value_t)):
        for part in range(2):
            piece = triple_ref[part, number]
            ref[:, part * length : (part + 1) * length] = (
                piece * score_scale if number == 0 else piece
            )
    rows = [slice(h * HD, (h + 1) * HD) for h in range(heads)]
    for h in range(heads):
        key_rows[h] = key_t[rows[h], :].T

    @pl.loop(0, 2 * length // TILE)
    def _(j):
        here = tile_at(j)
        start = start_ref[:, here]
        low, mid = low_ref[j], mid_ref[j]
        queries = [query_t[row, here] for row in rows]

        def score_with(masked):
            def score(kb, highest):
                ok = allowed(kb, j, start) if masked else None
                raised = []
                for h in range(heads):
                    found = jnp.dot(
                        key_rows[h, tile_at(kb), :], queries[h], preferred_element_type=f32
                    )
                    if masked:
                        found = jnp.where(ok, found, big_negative)
                    scores[h, tile_at(kb), :] = found
                    raised.append(
                        jnp.maximum(highest[h], jnp.max(found, axis=0, keepdims=True))
                    )
                return tuple(raised)

            return score

        highest = tuple(jnp.full((1, TILE), big_negative, f32) for _ in range(heads))
        highest = lax.fori_loop(low, mid, score_with(True), highest)
        highest = lax.fori_loop(mid, j, score_with(False), highest)
        highest = score_with(True)(j, highest)

        def weigh(kb, carry):
            after = []
            for h in range(heads):
                total, mixed = carry[h]
                prob = jnp.exp(scores[h, tile_at(kb), :] - highest[h])
                total = total + jnp.sum(prob, axis=0, keepdims=True)
                mixed = mixed + jnp.dot(
                    value_t[rows[h], tile_at(kb)], prob.astype(bf16), preferred_element_type=f32
                )
                after.append((total, mixed))
            return tuple(after)

        empty = tuple(
            (jnp.zeros((1, TILE), f32), jnp.zeros((HD, TILE), f32)) for _ in range(heads)
        )
        result = lax.fori_loop(low, j + 1, weigh, empty)
        for h in range(heads):
            total, mixed = result[h]
            attended_ref[rows[h], here] = (mixed / total).astype(bf16)
            log_ref[h, :, here] = highest[h] + jnp.log(total)


def turned_back(values, cosine, sine):
    half_rot = ROT // 2
    leading = values[:half_rot]
    trailing = values[half_rot:ROT]
    return jnp.concatenate(
        [
            leading * cosine + trailing * sine,
            trailing * cosine - leading * sine,
            values[ROT:],
        ],
        axis=0,
    )


def attend_back_kernel(
    low_ref,
    mid_ref,
    triple_ref,
    grad_ref,
    attended_ref,
    log_ref,
    start_ref,
    cosine_ref,
    sine_ref,
    back_ref,
    query_t,
    key_t,
    grad_t,
    key_rows,
    value_rows,
    key_sum,
    value_sum,
):
    length = triple_ref.shape[3]
    heads = triple_ref.shape[2] // HD
    score_scale = 1.0 / math.sqrt(HD)
    rows = [slice(h * HD, (h + 1) * HD) for h in range(heads)]
    for part in range(2):
        span = slice(part * length, (part + 1) * length)
        query_t[:, span] = triple_ref[part, 0] * score_scale
        key_t[:, span] = triple_ref[part, 1]
        grad_t[:, span] = grad_ref[part]
        for h in range(heads):
            value_rows[h, span, :] = triple_ref[part, 2, rows[h]].T
    for h in range(heads):
        key_rows[h] = key_t[rows[h], :].T
    key_sum[...] = jnp.zeros_like(key_sum)
    value_sum[...] = jnp.zeros_like(value_sum)

    @pl.loop(0, 2 * length // TILE)
    def _(j):
        here = tile_at(j)
        start = start_ref[:, here]
        low, mid = low_ref[j], mid_ref[j]
        queries = [query_t[row, here] for row in rows]
        grads = [grad_t[row, here] for row in rows]
        query_rows = [value.T for value in queries]
        grad_rows = [value.T for value in grads]
        logs = [log_ref[h, :, here] for h in range(heads)]
        deltas = [
            jnp.sum(
                grads[h].astype(f32) * attended_ref[rows[h], here].astype(f32),
                axis=0,
                keepdims=True,
            )
            for h in range(heads)
        ]

        def pull_with(masked):
            def pull(kb, query_back):
                ok = allowed(kb, j, start) if masked else None
                after = []
                for h in range(heads):
                    score = jnp.dot(
                        key_rows[h, tile_at(kb), :], queries[h], preferred_element_type=f32
                    )
                    if masked:
                        score = jnp.where(ok, score, big_negative)
                    prob = jnp.exp(score - logs[h])
                    down = jnp.dot(
                        value_rows[h, tile_at(kb), :], grads[h], preferred_element_type=f32
                    )
                    score_back = (prob * (down - deltas[h])).astype(bf16)
                    value_sum[h, tile_at(kb), :] += jnp.dot(
                        prob.astype(bf16), grad_rows[h], preferred_element_type=f32
                    )
                    key_sum[h, tile_at(kb), :] += jnp.dot(
                        score_back, query_rows[h], preferred_element_type=f32
                    )
                    after.append(
                        query_back[h]
                        + jnp.dot(
                            key_t[rows[h], tile_at(kb)], score_back, preferred_element_type=f32
                        )
                    )
                return tuple(after)

            return pull

        query_back = tuple(jnp.zeros((HD, TILE), f32) for _ in range(heads))
        query_back = lax.fori_loop(low, mid, pull_with(True), query_back)
        query_back = lax.fori_loop(mid, j, pull_with(False), query_back)
        query_back = pull_with(True)(j, query_back)
        for h in range(heads):
            back_ref[0, rows[h], here] = turned_back(
                query_back[h] * score_scale, cosine_ref[:, here], sine_ref[:, here]
            ).astype(bf16)

    for h in range(heads):
        back_ref[1, rows[h], :] = turned_back(
            key_sum[h].T, cosine_ref[...], sine_ref[...]
        ).astype(bf16)
        back_ref[2, rows[h], :] = value_sum[h].T.astype(bf16)


def attend(low, mid, triple, start):
    width, length = triple.shape[2], triple.shape[3]
    total, heads = 2 * length, width // HD
    area = total * total // 3 * heads
    return pl.pallas_call(
        attend_kernel,
        out_shape=(
            jax.ShapeDtypeStruct((width, total), bf16),
            jax.ShapeDtypeStruct((heads, 1, total), f32),
        ),
        in_specs=[SMEM, SMEM, VMEM, VMEM],
        out_specs=(VMEM, VMEM),
        scratch_shapes=[pltpu.VMEM((width, total), bf16)] * 3
        + [pltpu.VMEM((heads, total, HD), bf16), pltpu.VMEM((heads, total, TILE), f32)],
        compiler_params=pltpu.CompilerParams(vmem_limit_bytes=48 << 20),
        cost_estimate=pl.CostEstimate(
            flops=50 * area * HD, bytes_accessed=8 * width * total, transcendentals=area
        ),
        name="attend",
    )(low, mid, triple, start)


def attend_back(low, mid, triple, grad, attended, log_sum, start, cosine, sine):
    width, length = triple.shape[2], triple.shape[3]
    total, heads = 2 * length, width // HD
    area = total * total // 3 * heads
    return pl.pallas_call(
        attend_back_kernel,
        out_shape=jax.ShapeDtypeStruct((3, width, total), bf16),
        in_specs=[SMEM, SMEM] + [VMEM] * 7,
        out_specs=VMEM,
        scratch_shapes=[pltpu.VMEM((width, total), bf16)] * 3
        + [pltpu.VMEM((heads, total, HD), bf16)] * 2
        + [pltpu.VMEM((heads, total, HD), f32)] * 2,
        compiler_params=pltpu.CompilerParams(vmem_limit_bytes=48 << 20),
        cost_estimate=pl.CostEstimate(
            flops=100 * area * HD, bytes_accessed=12 * width * total, transcendentals=area
        ),
        name="attend_back",
    )(low, mid, triple, grad, attended, log_sum, start, cosine, sine)


def rotate_rows(values, cosine, sine):
    half_rot = ROT // 2
    leading = values[:, :half_rot]
    trailing = values[:, half_rot:ROT]
    return jnp.concatenate(
        [
            leading * cosine - trailing * sine,
            trailing * cosine + leading * sine,
            values[:, ROT:],
        ],
        axis=1,
    )


def ordered(*values):
    return lax.optimization_barrier(values)


def body(
    sizes,
    tokens,
    segments,
    positions,
    norm_gain,
    norm_bias,
    projection_weight,
    projection_bias,
    dense_weight,
    dense_bias,
    up_weight,
    up_bias,
    down_weight,
    down_bias,
    cotangent,
):
    own_len, model_width = tokens.shape[1], tokens.shape[2]
    half_len = segments.shape[1]
    local_width = projection_weight.shape[2]
    hidden_width = up_weight.shape[1]
    shard_rows = norm_gain.shape[0]
    half = lax.axis_index("ctx")
    total_len = 2 * half_len

    vectors = jnp.stack([norm_gain, norm_bias, dense_bias, down_bias]).astype(f32)
    vectors = jnp.pad(vectors, ((0, 4), (0, 0)))
    numbers = jnp.pad(jnp.concatenate([segments, positions], axis=0), ((0, 6), (0, 0)))
    vectors_full, numbers_other = small_gather(sizes, vectors, numbers)
    gain_full, shift_full, bias_dense, bias_down = (
        vectors_full[:, row].reshape(model_width) for row in range(4)
    )

    def in_order(own, other, axis):
        return jnp.where(
            half == 0,
            jnp.concatenate([own, other], axis=axis),
            jnp.concatenate([other, own], axis=axis),
        )

    sequence = in_order(numbers, numbers_other, 1)
    segment_row, position_row = sequence[0], sequence[1]
    places = jnp.arange(total_len, dtype=jnp.int32)
    edges = jnp.concatenate([jnp.ones((1,), bool), segment_row[1:] != segment_row[:-1]])
    start = lax.cummax(jnp.where(edges, places, 0))
    tile_count = total_len // TILE
    low = start[::TILE] // TILE
    mid = jnp.minimum(
        jnp.maximum((start[TILE - 1 :: TILE] + TILE - 1) // TILE, low),
        jnp.arange(tile_count, dtype=jnp.int32),
    )
    exponent = jnp.arange(ROT // 2, dtype=f32) * 2.0 / ROT
    inverse = 10000.0 ** (-exponent)
    phase_angle = inverse[:, None] * position_row.astype(f32)[None, :]
    cosine_full, sine_full = jnp.cos(phase_angle), jnp.sin(phase_angle)
    own_start = half * half_len
    cosine_own = lax.dynamic_slice_in_dim(cosine_full, own_start, half_len, 1)
    sine_own = lax.dynamic_slice_in_dim(sine_full, own_start, half_len, 1)

    inputs = tokens[0].astype(f32)
    normed_values, norm_pull = jax.vjp(layer_norm, inputs, gain_full, shift_full)
    normed = lax.all_gather(normed_values.astype(bf16), "tp", axis=0, tiled=True)
    projection, up_full, dense_full, down_full = gather(
        sizes,
        [projection_weight.transpose(1, 0, 2), up_weight, dense_weight, down_weight],
        1,
        "gather_weights",
    )
    cotangent_rows = lax.all_gather(cotangent[0], "tp", axis=0, tiled=True)
    projected = lax.dot_general(
        projection, normed, (((1,), (1,)), ((), ())), preferred_element_type=f32
    )
    projected = projected + projection_bias.astype(f32)[:, :, None]
    turned = rotate_rows(
        projected[:2].reshape(2 * local_width // HD, HD, half_len), cosine_own, sine_own
    ).reshape(2, local_width, half_len)
    triple = jnp.concatenate([turned, projected[2:]], axis=0).astype(bf16)
    both, activation, slope, feed_out = exchange_forward(
        sizes, triple, normed, up_full, up_bias.astype(f32)[None, :], down_full
    )
    attended_heads, log_sum = attend(low, mid, both, start[None, :])
    cotangent_rows, log_sum = ordered(cotangent_rows, log_sum)
    grad_attended = lax.dot_general(
        dense_full, cotangent_rows, row_by_col, preferred_element_type=f32
    ).astype(bf16)
    attended, grad_both, grad_hidden = exchange_middle(
        sizes, attended_heads, grad_attended, cotangent_rows, down_full, slope
    )
    block_out = (
        lax.dot_general(attended, dense_full, row_by_col, preferred_element_type=f32) + feed_out
    ).astype(bf16)
    branch_own = lax.psum_scatter(block_out, "tp", scatter_dimension=0, tiled=True)
    grad_both, block_out = ordered(grad_both, block_out)
    back_heads = attend_back(
        low,
        mid,
        both,
        grad_both,
        attended_heads,
        log_sum,
        start[None, :],
        cosine_full,
        sine_full,
    )
    grad_projected, up_sum, down_sum, *turned, block_in = exchange_back(
        sizes, back_heads, normed, grad_hidden, cotangent_rows, activation, up_full, projection
    )
    grad_projected = grad_projected.reshape(3 * local_width, half_len)
    block_in, branch_own = ordered(block_in, branch_own)
    grad_normed_own = lax.psum_scatter(block_in, "tp", scatter_dimension=0, tiled=True).astype(f32)
    hidden_sum = jnp.sum(grad_hidden.astype(f32), axis=0)
    projected_sum = jnp.sum(grad_projected.astype(f32), axis=1)
    small = jnp.concatenate([projected_sum, hidden_sum]).reshape(-1, 128)
    groups = sizes["fsdp"] // 2 * sizes["ctx"]
    up_part, down_part, projection_part, dense_part, small_total = reduce(
        sizes,
        [v.reshape(groups, shard_rows, hidden_width) for v in (up_sum, down_sum)],
        turned,
        [(normed, grad_projected), (cotangent_rows, attended)],
        [1, 1, 3, 1],
        small,
        2,
        "reduce_weights",
    )
    layer_output = (inputs + branch_own.astype(f32) + (bias_dense + bias_down)).astype(bf16)
    cotangent_own = cotangent[0].astype(f32)
    grad_inputs, grad_gain, grad_shift = norm_pull(grad_normed_own)
    input_grad = grad_inputs + cotangent_own
    output_sum = jnp.sum(cotangent_own, axis=0)
    sums = jnp.stack([grad_gain, grad_shift, output_sum]).reshape(3, -1, shard_rows)
    sums = jnp.pad(sums.transpose(1, 0, 2), ((0, 0), (0, 5), (0, 0)))
    totals = small_reduce(sizes, sums)
    small_flat = small_total.reshape(-1)
    return (
        layer_output[None],
        input_grad[None],
        totals[0],
        totals[1],
        projection_part.transpose(1, 0, 2),
        small_flat[: 3 * local_width].reshape(3, local_width),
        dense_part,
        totals[2],
        up_part,
        small_flat[3 * local_width :],
        down_part,
        totals[2],
    )


def solution(mesh):
    placed = (
        P("fsdp", ("ctx", "tp"), None),
        P("fsdp", "ctx"),
        P("fsdp", "ctx"),
        P(("fsdp", "ctx")),
        P(("fsdp", "ctx")),
        P(("fsdp", "ctx"), None, "tp"),
        P(None, "tp"),
        P(("fsdp", "ctx"), "tp"),
        P(("fsdp", "ctx")),
        P(("fsdp", "ctx"), "tp"),
        P("tp"),
        P(("fsdp", "ctx"), "tp"),
        P(("fsdp", "ctx")),
        P("fsdp", ("ctx", "tp"), None),
    )
    return jax.shard_map(
        functools.partial(body, dict(mesh.shape)),
        mesh=mesh,
        in_specs=placed,
        out_specs=(
            P("fsdp", ("ctx", "tp"), None),
            P("fsdp", ("ctx", "tp"), None),
            P(("fsdp", "ctx")),
            P(("fsdp", "ctx")),
            P(("fsdp", "ctx"), None, "tp"),
            P(None, "tp"),
            P(("fsdp", "ctx"), "tp"),
            P(("fsdp", "ctx")),
            P(("fsdp", "ctx"), "tp"),
            P("tp"),
            P(("fsdp", "ctx"), "tp"),
            P(("fsdp", "ctx")),
        ),
        check_vma=False,
    )
```

```python
import functools
import math

import jax
import jax.numpy as jnp
from jax import lax
from jax.experimental import pallas as pl
from jax.experimental.pallas import tpu as pltpu
from jax.sharding import PartitionSpec as P

HD = 64
ROT = 32
TILE = 256

epsilon = 1e-05
big_negative = -1000000000.0
root_two_over_pi = 0.7978845608028654
contract_rows = (((0,), (0,)), ((), ()))
contract_cols = (((1,), (1,)), ((), ()))
row_by_col = (((0,), (1,)), ((), ()))
MESH = pl.DeviceIdType.MESH
ANY = pl.BlockSpec(memory_space=pl.ANY)
VMEM = pl.BlockSpec(memory_space=pltpu.VMEM)
SMEM = pl.BlockSpec(memory_space=pltpu.SMEM)
DMA = pltpu.SemaphoreType.DMA
f32 = jnp.float32
bf16 = jnp.bfloat16


def layer_norm(values, gain_full, shift_full):
    center = jnp.mean(values, axis=-1, keepdims=True)
    centered = values - center
    spread = jnp.mean(centered * centered, axis=-1, keepdims=True)
    return centered * lax.rsqrt(spread + epsilon) * gain_full + shift_full


def gelu_and_slope(values):
    turned = jnp.tanh(root_two_over_pi * (values + 0.044715 * values * values * values))
    slope = 0.5 * (1.0 + turned) + 0.5 * values * (1.0 - turned * turned) * root_two_over_pi * (
        1.0 + 3.0 * 0.044715 * values * values
    )
    return 0.5 * values * (1.0 + turned), slope


class Place:
    def __init__(self, sizes):
        self.chips = sizes["fsdp"] // 2
        self.halves = sizes["ctx"]
        self.depth = sizes["tp"]
        lane = lax.axis_index("fsdp")
        self.chip = lane // 2
        self.core = lane % 2
        self.half = lax.axis_index("ctx")
        self.layer = lax.axis_index("tp")

    def device(self, chip=None, core=None, half=None, layer=None):
        chip = self.chip if chip is None else chip
        core = self.core if core is None else core
        half = self.half if half is None else half
        layer = self.layer if layer is None else layer
        return (chip * 2 + core, half, layer)

    def block(self, chip=None, core=None, half=None):
        chip = self.chip if chip is None else chip
        core = self.core if core is None else core
        half = self.half if half is None else half
        return (chip * 2 + core) * self.halves + half

    def ahead(self, k):
        return (self.chip + k) % self.chips

    def behind(self, k):
        return (self.chip + self.chips - k) % self.chips

    def pair(self):
        return self.device(core=1 - self.core)

    def across(self):
        return self.device(half=1 - self.half)

    def group(self):
        found = []
        for k in range(self.chips):
            for core in range(2):
                for half in range(2):
                    if k or core or half:
                        found.append(
                            (self.ahead(k), (self.core + core) % 2, (self.half + half) % 2)
                        )
        return found


def greet(devices):
    barrier = pltpu.get_barrier_semaphore()
    for device in devices:
        pl.semaphore_signal(barrier, inc=1, device_id=device, device_id_type=MESH)
    pl.semaphore_wait(barrier, len(devices))


def send(source, target, send_sem, recv_sem, device):
    return pltpu.make_async_remote_copy(
        src_ref=source,
        dst_ref=target,
        send_sem=send_sem,
        recv_sem=recv_sem,
        device_id=device,
        device_id_type=MESH,
    )


def plane(place):
    found = [place.device(chip=place.ahead(k)) for k in range(1, place.chips)]
    return found + [place.across(), place.pair()]


def reduce(sizes, paired, turned, rights, splits, small, collective_id, name):
    chips, halves = sizes["fsdp"] // 2, sizes["ctx"]
    groups = chips * halves
    paired_count, made_count = len(paired), len(rights)
    weight_count = paired_count + made_count
    block_rows = paired[0].shape[1]
    widths = [v.shape[2] for v in paired] + [v.shape[0] for _, v in rights]
    side = block_rows // 2

    def kernel(*refs):
        refs = list(refs)

        def take(count):
            taken = refs[:count]
            del refs[:count]
            return taken

        paired_in = take(paired_count)
        turned_in = take(2 * paired_count)
        lefts = [take(len(left)) for left, _ in rights]
        factors = take(made_count)
        (small_ref,) = take(1)
        weight_out = take(weight_count)
        (small_out,) = take(1)
        made = take(made_count)
        own, turn_a, turn_b, near = (take(weight_count) for _ in range(4))
        pair = [None] * paired_count + take(made_count)
        load_sem, core_send, core_recv = take(3)
        turn_send, turn_recv, near_send, near_recv = take(4)
        small_pair, small_near, small_far, small_send, small_recv = take(5)
        place = Place(sizes)
        greet(plane(place))
        pending = []

        def launch(copy, condition=None):
            if condition is None:
                copy.start()
            else:
                pl.when(condition)(copy.start)
            pending.append((copy, condition))

        other = 1 - place.core
        for a in range(paired_count):
            needed = [place.ahead(k) * halves + place.half for k in range(1, chips)]
            needed += [place.chip * halves + half for half in range(halves)]
            for number in needed:
                pltpu.make_async_copy(
                    paired_in[a].at[number], own[a].at[number], load_sem.at[a, number]
                ).start()
            for way, target in enumerate((turn_a[a], turn_b[a])):
                for k in range(1, chips):
                    pltpu.make_async_copy(
                        turned_in[2 * a + way].at[k - 1],
                        target.at[k - 1],
                        turn_recv.at[a, way, k],
                    ).start()

        def make(a):
            at = a - paired_count
            rows = made[at].shape[0] // len(lefts[at])
            for number, left in enumerate(lefts[at]):
                span = pl.ds(number * rows, rows)
                multiply("tt", [(left, factors[at])], [made[at].at[span]])
            for number in range(groups):
                chip, half = number // halves, number % halves
                theirs = place.block(chip, other, half)
                mine = place.block(chip, place.core, half)
                launch(
                    send(
                        made[at].at[pl.ds(pl.multiple_of(theirs * block_rows, 16), block_rows)],
                        pair[a].at[number],
                        core_send.at[a, number],
                        core_recv.at[a, number],
                        place.pair(),
                    )
                )
                pltpu.make_async_copy(
                    made[at].at[pl.ds(pl.multiple_of(mine * block_rows, 16), block_rows)],
                    own[a].at[number],
                    load_sem.at[a, number],
                ).start()

        def pair_sum(a, number):
            mine = own[a].at[number]
            pltpu.make_async_copy(mine, mine, load_sem.at[a, number]).wait()
            if a < paired_count:
                return
            theirs = pair[a].at[number]
            send(
                theirs, theirs, core_send.at[a, number], core_recv.at[a, number], place.pair()
            ).wait_recv()

            @pl.loop(0, block_rows, step=16)
            def _(r):
                at = pl.ds(pl.multiple_of(r, 16), 16)
                mine[at, :] = (mine[at, :].astype(f32) + theirs[at, :].astype(f32)).astype(bf16)

        def diagonal(a):
            for k in range(1, chips):
                number = place.ahead(k) * halves + 1 - place.half
                pair_sum(a, number)
                launch(
                    send(
                        own[a].at[number, pl.ds(0, side)],
                        turn_a[a].at[k - 1],
                        turn_send.at[a, 0, k],
                        turn_recv.at[a, 0, k],
                        place.across(),
                    )
                )
                launch(
                    send(
                        own[a].at[number, pl.ds(side, side)],
                        turn_b[a].at[k - 1],
                        turn_send.at[a, 1, k],
                        turn_recv.at[a, 1, k],
                        place.device(chip=place.ahead(k)),
                    )
                )

        def direct_pairs(a):
            for k in range(1, chips):
                pair_sum(a, place.ahead(k) * halves + place.half)
            pair_sum(a, place.chip * halves + 1 - place.half)

        def add_turn(a, number, first, refs_at):
            @pl.loop(0, side, step=16)
            def _(r):
                at = pl.ds(pl.multiple_of(first + r, 16), 16)
                total = own[a][number, at, :].astype(f32)
                for ref, k in refs_at:
                    total += ref[k, pl.ds(pl.multiple_of(r, 16), 16), :].astype(f32)
                own[a][number, at, :] = total.astype(bf16)

        def turn_wait(a, way, k):
            piece = (turn_a, turn_b)[way][a].at[k - 1]
            if a < paired_count:
                pltpu.make_async_copy(piece, piece, turn_recv.at[a, way, k]).wait()
            else:
                send(
                    piece, piece, turn_send.at[a, way, k], turn_recv.at[a, way, k], place.across()
                ).wait_recv()

        def direct(a):
            for k in range(1, chips):
                number = place.ahead(k) * halves + place.half
                turn_wait(a, 0, k)
                add_turn(a, number, 0, [(turn_a[a], k - 1)])
                launch(
                    send(
                        own[a].at[number],
                        near[a].at[k],
                        near_send.at[a, k],
                        near_recv.at[a, k],
                        place.device(chip=place.ahead(k)),
                    )
                )
            for k in range(1, chips):
                turn_wait(a, 1, k)
            number = place.chip * halves + 1 - place.half
            add_turn(a, number, side, [(turn_b[a], k - 1) for k in range(1, chips)])
            launch(
                send(
                    own[a].at[number],
                    near[a].at[0],
                    near_send.at[a, 0],
                    near_recv.at[a, 0],
                    place.across(),
                )
            )

        def finish(a):
            for k in range(chips):
                piece = near[a].at[k]
                send(
                    piece, piece, near_send.at[a, k], near_recv.at[a, k], place.across()
                ).wait_recv()
            number = place.chip * halves + place.half

            @pl.loop(0, block_rows, step=16)
            def _(r):
                at = pl.ds(pl.multiple_of(r, 16), 16)
                total = own[a][number, at, :].astype(f32) + near[a][0, at, :].astype(f32)
                for k in range(1, chips):
                    total += near[a][k, at, :].astype(f32)
                if splits[a] == 1:
                    weight_out[a][at, :] = total
                else:
                    wide = widths[a] // splits[a]
                    for kind in range(splits[a]):
                        weight_out[a][kind, at, :] = total[:, kind * wide : (kind + 1) * wide]

        def swap_small(source, target, at, device):
            copy = send(source, target, small_send.at[at], small_recv.at[at], device)
            launch(copy)
            return copy

        swap_small(small_ref, small_pair, 0, place.pair())
        for a in range(paired_count):
            direct_pairs(a)
            direct(a)
        for a in range(paired_count, weight_count):
            make(a)
        send(small_pair, small_pair, small_send.at[0], small_recv.at[0], place.pair()).wait_recv()
        small_near[0] = small_ref[...] + small_pair[...]
        for k in range(1, chips):
            swap_small(small_near.at[0], small_near.at[k], k, place.device(chip=place.ahead(k)))
        for a in range(paired_count, weight_count):
            diagonal(a)
            direct_pairs(a)
        total = small_near[0]
        for k in range(1, chips):
            piece = small_near.at[k]
            send(piece, piece, small_send.at[k], small_recv.at[k], place.pair()).wait_recv()
            total += small_near[k]
        small_far[0] = total
        swap_small(small_far.at[0], small_far.at[1], chips, place.across())
        for a in range(weight_count):
            pair_sum(a, place.chip * halves + place.half)
        for a in range(paired_count, weight_count):
            direct(a)
        for a in range(weight_count):
            finish(a)
        piece = small_far.at[1]
        send(piece, piece, small_send.at[chips], small_recv.at[chips], place.pair()).wait_recv()
        small_out[...] = small_far[0] + small_far[1]
        for copy, condition in pending:
            if condition is None:
                copy.wait_send()
            else:
                pl.when(condition)(copy.wait_send)

    shapes = [
        jax.ShapeDtypeStruct((block_rows, w) if n == 1 else (n, block_rows, w // n), f32)
        for w, n in zip(widths, splits)
    ]
    shapes.append(jax.ShapeDtypeStruct(small.shape, f32))
    made_shapes = [
        jax.ShapeDtypeStruct((2 * groups * block_rows, w), bf16) for w in widths[paired_count:]
    ]
    scratch = [pltpu.VMEM((groups, block_rows, w), bf16) for w in widths]
    scratch += [pltpu.VMEM((chips - 1, side, w), bf16) for w in widths] * 2
    scratch += [pltpu.VMEM((chips, block_rows, w), bf16) for w in widths]
    scratch += [pltpu.VMEM((groups, block_rows, w), bf16) for w in widths[paired_count:]]
    scratch += [
        DMA((weight_count, groups)),
        DMA((weight_count, groups)),
        DMA((weight_count, groups)),
        DMA((weight_count, 2, chips)),
        DMA((weight_count, 2, chips)),
        DMA((weight_count, chips)),
        DMA((weight_count, chips)),
        pltpu.VMEM(small.shape, f32),
        pltpu.VMEM((chips,) + small.shape, f32),
        pltpu.VMEM((2,) + small.shape, f32),
        DMA((chips + 1,)),
        DMA((chips + 1,)),
    ]
    lefts = [v for left, _ in rights for v in left]
    factors = [v for _, v in rights]
    return pl.pallas_call(
        kernel,
        out_shape=tuple(shapes + made_shapes),
        in_specs=[ANY] * (3 * paired_count + len(lefts) + made_count) + [VMEM],
        out_specs=(VMEM,) * len(shapes) + (ANY,) * made_count,
        scratch_shapes=scratch,
        compiler_params=pltpu.CompilerParams(
            collective_id=collective_id, has_side_effects=True, vmem_limit_bytes=60 << 20
        ),
        cost_estimate=pl.CostEstimate(flops=0, bytes_accessed=400_000_000, transcendentals=0),
        name=name,
    )(*paired, *turned, *lefts, *factors, small)[: weight_count + 1]


def multiply(kind, parts, outs, finish=None, extra=(), tile=512):
    dims = (((0 if kind[0] == "t" else 1,), (1 if kind[1] == "t" else 0,)), ((), ()))
    left, right = parts[0]
    rows = left.shape[1] if kind[0] == "t" else left.shape[0]
    width = right.shape[0] if kind[1] == "t" else right.shape[1]
    tile = min(tile, width)
    specs = []
    for left, right in parts:
        specs.append(pl.BlockSpec(left.shape, lambda n: (0, 0)))
        if kind[1] == "t":
            specs.append(pl.BlockSpec((tile, right.shape[1]), lambda n: (n, 0)))
        else:
            specs.append(pl.BlockSpec((right.shape[0], tile), lambda n: (0, n)))
    specs += [pl.BlockSpec((v.shape[0], tile), lambda n: (0, n)) for v in extra]

    def step(*refs):
        found = None
        for number in range(len(parts)):
            product = lax.dot_general(
                refs[2 * number][...],
                refs[2 * number + 1][...],
                dims,
                preferred_element_type=f32,
            )
            found = product if found is None else found + product
        rest = refs[2 * len(parts) :]
        results = (found,)
        if finish is not None:
            results = finish(found, *(v[...] for v in rest[: len(extra)]))
        for ref, value in zip(rest[len(extra) :], results):
            ref[...] = value.astype(ref.dtype)

    factors = [v for pair in parts for v in pair]
    pltpu.emit_pipeline(
        step,
        grid=(width // tile,),
        in_specs=specs,
        out_specs=[pl.BlockSpec((rows, tile), lambda n: (0, n))] * len(outs),
    )(*factors, *extra, *outs)


def half_rows(ref, half, count):
    return ref.at[pl.ds(pl.multiple_of(half * count, count), count)]


def front(
    sizes, tokens, cotangent, vectors, numbers, weights, projection_bias, up_bias, cosine, sine
):
    chips, halves, depth = sizes["fsdp"] // 2, sizes["ctx"], sizes["tp"]
    groups = sizes["fsdp"] * halves
    own_len, model = tokens.shape
    length = own_len * depth
    projection, up, dense, down = weights
    weight_count = len(weights)
    kinds, local = projection.shape[0], projection.shape[2]
    count = local // 2
    hidden = up.shape[1]
    shard = vectors.shape[1]
    half_rot = ROT // 2
    early_width = model // 2

    def kernel(*refs):
        refs = list(refs)

        def take(number):
            taken = refs[:number]
            del refs[:number]
            return taken

        tokens_ref, cotangent_ref, vector_ref, number_ref = take(4)
        weight_in = take(weight_count)
        bias_ref, up_bias_ref, cosine_ref, sine_ref = take(4)
        vectors_out, numbers_out, normed, cotangent_rows = take(4)
        weight_out = take(weight_count)
        both, activation, slope, triple = take(4)
        landed, normed_own, stage = take(3)
        vector_send, vector_recv, single, line_send, line_recv = take(5)
        keep, near_send, near_recv, turn_send, turn_recv, core_send, core_recv = take(7)
        place = Place(sizes)
        peers = place.group()
        up_there, down_there = place.layer < depth - 1, place.layer > 0
        above = place.device(layer=jnp.minimum(place.layer + 1, depth - 1))
        below = place.device(layer=jnp.maximum(place.layer - 1, 0))
        barrier = pltpu.get_barrier_semaphore()
        for chip, core, half in peers:
            pl.semaphore_signal(
                barrier,
                inc=1,
                device_id=place.device(chip=chip, core=core, half=half),
                device_id_type=MESH,
            )
        for there, device in ((up_there, above), (down_there, below)):

            @pl.when(there)
            def _(device=device):
                pl.semaphore_signal(barrier, inc=1, device_id=device, device_id_type=MESH)

        pl.semaphore_wait(
            barrier,
            len(peers) + up_there.astype(jnp.int32) + down_there.astype(jnp.int32),
        )
        pending = []

        def launch(copy, condition=None):
            if condition is None:
                copy.start()
            else:
                pl.when(condition)(copy.start)
            pending.append((copy, condition))

        def part(a, block, first=0, rows=None):
            rows = weight_in[a].shape[-2] if rows is None else rows
            start = pl.multiple_of(block * weight_in[a].shape[-2] + first, 16)
            span = pl.ds(start, rows)
            return weight_out[a].at[:, span] if a == 0 else weight_out[a].at[span]

        def arrive(piece, recv_sem):
            send(piece, piece, recv_sem, recv_sem, place.pair()).wait_recv()

        mine = place.block()
        vector_keep = pltpu.make_async_copy(vector_ref, landed.at[mine], single.at[0])
        vector_keep.start()
        for at, (chip, core, half) in enumerate(peers):
            launch(
                send(
                    vector_ref,
                    landed.at[mine],
                    vector_send.at[at],
                    vector_recv.at[at],
                    place.device(chip=chip, core=core, half=half),
                )
            )
        launch(send(number_ref, numbers_out, single.at[1], single.at[2], place.across()))

        def near_start(a):
            own = part(a, place.block())
            for k in range(1, chips):
                launch(
                    send(
                        weight_in[a],
                        own,
                        near_send.at[a, k],
                        near_recv.at[a, k],
                        place.device(chip=place.ahead(k)),
                    )
                )
            launch(
                send(weight_in[a], own, near_send.at[a, 0], near_recv.at[a, 0], place.across())
            )
            launch(send(weight_in[a], own, core_send.at[a, 0], core_recv.at[a, 0], place.pair()))
            pltpu.make_async_copy(weight_in[a], own, keep.at[a]).start()

        def near_step(a):
            side = weight_in[a].shape[-2] // 4
            rest = weight_in[a].shape[-2] - side
            for k in range(1, chips):
                block = place.block(chip=place.behind(k))
                piece = part(a, block)
                arrive(piece, near_recv.at[a, k])
                top = part(a, block, 0, side)
                launch(
                    send(top, top, turn_send.at[a, 0, k], turn_recv.at[a, 0, k], place.across())
                )
                launch(send(piece, piece, core_send.at[a, k], core_recv.at[a, k], place.pair()))
            block = place.block(half=1 - place.half)
            piece = part(a, block)
            arrive(piece, near_recv.at[a, 0])
            low = part(a, block, side, rest)
            for k in range(1, chips):
                launch(
                    send(
                        low,
                        low,
                        turn_send.at[a, 1, k],
                        turn_recv.at[a, 1, k],
                        place.device(chip=place.ahead(k)),
                    )
                )
            launch(
                send(piece, piece, core_send.at[a, chips], core_recv.at[a, chips], place.pair())
            )

        def turn_step(a):
            side = weight_in[a].shape[-2] // 4
            rest = weight_in[a].shape[-2] - side
            for k in range(1, chips):
                block = place.block(chip=place.behind(k), half=1 - place.half)
                arrive(part(a, block, 0, side), turn_recv.at[a, 0, k])
                arrive(part(a, block, side, rest), turn_recv.at[a, 1, k])
                piece = part(a, block)
                launch(
                    send(
                        piece,
                        piece,
                        core_send.at[a, chips + k],
                        core_recv.at[a, chips + k],
                        place.pair(),
                    )
                )

        def core_step(a):
            other = 1 - place.core
            blocks = [place.block(core=other)]
            blocks += [place.block(place.behind(k), other) for k in range(1, chips)]
            blocks += [place.block(None, other, 1 - place.half)]
            blocks += [
                place.block(place.behind(k), other, 1 - place.half) for k in range(1, chips)
            ]
            for at, block in enumerate(blocks):
                arrive(part(a, block), core_recv.at[a, at])
            pltpu.make_async_copy(weight_in[a], part(a, place.block()), keep.at[a]).wait()

        near_start(0)

        vector_keep.wait()
        for at in range(len(peers)):
            place_in = at + 1
            source = place.block(
                place.behind(place_in // 4),
                (place.core + place_in // 2 % 2) % 2,
                (place.half + place_in % 2) % 2,
            )
            arrive(landed.at[source], vector_recv.at[at])
        for number in range(groups):
            vectors_out[:, number * shard : (number + 1) * shard] = landed[number]

        @pl.loop(0, own_len, step=32)
        def _(r):
            at = pl.ds(pl.multiple_of(r, 32), 32)
            values = tokens_ref[at, :].astype(f32)
            normed_own[at, :] = layer_norm(
                values, vectors_out[0:1, :], vectors_out[1:2, :]
            ).astype(bf16)

        early = cotangent_ref.at[:, pl.ds(0, early_width)]
        line_own, line_full = (normed_own, early), (normed, cotangent_rows)

        def line(number, source):
            return line_full[number].at[pl.ds(pl.multiple_of(source * own_len, 16), own_len)]

        def line_keep(number):
            return pltpu.make_async_copy(
                line_own[number], line(number, place.layer), single.at[(3, 8)[number]]
            )

        def line_start(number):
            for way, (there, device) in enumerate(((up_there, above), (down_there, below))):
                launch(
                    send(
                        line_own[number],
                        line(number, place.layer),
                        line_send.at[number, way, 0],
                        line_recv.at[number, way, 0],
                        device,
                    ),
                    there,
                )
            line_keep(number).start()

        def line_step(number, k):
            for way, (onward, device) in enumerate(((up_there, above), (down_there, below))):
                source = place.layer - k if way == 0 else place.layer + k
                there = (source >= 0) & (source < depth)
                piece = line(number, jnp.clip(source, 0, depth - 1))
                arrived = send(
                    piece,
                    piece,
                    line_send.at[number, way, k - 1],
                    line_recv.at[number, way, k - 1],
                    device,
                )
                pl.when(there)(arrived.wait_recv)
                if k < depth - 1:
                    launch(
                        send(
                            piece,
                            piece,
                            line_send.at[number, way, k],
                            line_recv.at[number, way, k],
                            device,
                        ),
                        there & onward,
                    )

        line_start(0)
        near_start(1)
        near_step(0)
        line_step(0, 1)
        near_start(3)
        near_start(2)
        turn_step(0)
        near_step(1)
        for k in range(2, depth):
            line_step(0, k)
        line_start(1)
        line_keep(0).wait()
        core_step(0)
        near_step(3)

        def project(weight, rows, cosine_here, sine_here, out):
            for kind in range(kinds):
                found = lax.dot_general(
                    weight[kind], rows[...], row_by_col, preferred_element_type=f32
                )
                found = found + bias_ref[kind * local : (kind + 1) * local, :]
                if kind == 2:
                    out[kind] = found.astype(bf16)
                    continue
                for head in range(local // HD):
                    first = head * HD
                    leading = found[first : first + half_rot]
                    trailing = found[first + half_rot : first + ROT]
                    turned = (
                        leading * cosine_here[...] - trailing * sine_here[...],
                        trailing * cosine_here[...] + leading * sine_here[...],
                        found[first + ROT : first + HD],
                    )
                    out[kind, first : first + HD] = jnp.concatenate(turned, axis=0).astype(bf16)

        tile = min(512, length)
        pltpu.emit_pipeline(
            project,
            grid=(length // tile,),
            in_specs=[
                pl.BlockSpec(weight_out[0].shape, lambda n: (0, 0, 0)),
                pl.BlockSpec((tile, model), lambda n: (n, 0)),
                pl.BlockSpec((half_rot, tile), lambda n: (0, n)),
                pl.BlockSpec((half_rot, tile), lambda n: (0, n)),
            ],
            out_specs=[pl.BlockSpec((kinds, local, tile), lambda n: (0, 0, n))],
        )(weight_out[0], normed, cosine_ref, sine_ref, triple)

        def heads(half):
            return triple.at[:, pl.ds(pl.multiple_of(half * count, count), count)]

        here, there = place.half, 1 - place.half
        launch(send(heads(there), both.at[here], single.at[4], single.at[5], place.across()))
        load = pltpu.make_async_copy(heads(here), stage, single.at[6])
        load.start()
        load.wait()
        stage_keep = pltpu.make_async_copy(stage, both.at[here], single.at[7])
        stage_keep.start()
        near_step(2)
        line_step(1, 1)
        turn_step(1)
        core_step(1)
        wide = hidden // 2
        for number in range(2):
            span = pl.ds(number * wide, wide)
            multiply(
                "nn",
                [(normed, weight_out[1].at[:, span])],
                [activation.at[:, span], slope.at[:, span]],
                lambda found, bias: gelu_and_slope(found + bias),
                [up_bias_ref.at[:, span]],
            )
            if number == 0 and depth > 2:
                line_step(1, 2)
        turn_step(3)
        core_step(3)
        turn_step(2)
        core_step(2)
        for k in range(3, depth):
            line_step(1, k)
        line_keep(1).wait()
        stage_keep.wait()
        arrive(both.at[there], single.at[5])
        arrive(numbers_out, single.at[2])
        for copy, condition in pending:
            if condition is None:
                copy.wait_send()
            else:
                pl.when(condition)(copy.wait_send)

    out_shape = [
        jax.ShapeDtypeStruct((vectors.shape[0], groups * shard), f32),
        jax.ShapeDtypeStruct(numbers.shape, numbers.dtype),
        jax.ShapeDtypeStruct((length, model), bf16),
        jax.ShapeDtypeStruct((length, early_width), bf16),
    ]
    out_shape += [
        jax.ShapeDtypeStruct(v.shape[:-2] + (groups * v.shape[-2], v.shape[-1]), v.dtype)
        for v in weights
    ]
    out_shape += [
        jax.ShapeDtypeStruct((2, kinds, count, length), bf16),
        jax.ShapeDtypeStruct((length, hidden), bf16),
        jax.ShapeDtypeStruct((length, hidden), bf16),
        jax.ShapeDtypeStruct((kinds, local, length), bf16),
    ]
    results = pl.pallas_call(
        kernel,
        out_shape=tuple(out_shape),
        in_specs=[VMEM] * (4 + weight_count) + [VMEM, ANY, ANY, ANY],
        out_specs=(VMEM, VMEM) + (ANY,) * (len(out_shape) - 2),
        scratch_shapes=[
            pltpu.VMEM((groups,) + vectors.shape, f32),
            pltpu.VMEM((own_len, model), bf16),
            pltpu.VMEM((kinds, count, length), bf16),
            DMA((groups - 1,)),
            DMA((groups - 1,)),
            DMA((9,)),
            DMA((2, 2, depth - 1)),
            DMA((2, 2, depth - 1)),
            DMA((weight_count,)),
            DMA((weight_count, chips)),
            DMA((weight_count, chips)),
            DMA((weight_count, 2, chips)),
            DMA((weight_count, 2, chips)),
            DMA((weight_count, 2 * chips)),
            DMA((weight_count, 2 * chips)),
        ],
        compiler_params=pltpu.CompilerParams(
            collective_id=0, has_side_effects=True, vmem_limit_bytes=60 << 20
        ),
        cost_estimate=pl.CostEstimate(flops=0, bytes_accessed=480_000_000, transcendentals=0),
        name="front",
    )(tokens, cotangent, vectors, numbers, *weights, projection_bias, up_bias, cosine, sine)
    return results[:-1]


def exchange_attended(sizes, attended, activation, down_full, dense_full):
    width, total = attended.shape
    length = total // 2
    rows, model = activation.shape[0], down_full.shape[0]

    def kernel(attended_ref, activation_ref, down_ref, dense_ref, *rest):
        full, block_out, feed, stage, sems = rest
        place = Place(sizes)
        greet([place.across()])
        here, there = place.half, 1 - place.half

        def tokens(half):
            return attended_ref.at[:, pl.ds(pl.multiple_of(half * length, length), length)]

        away = send(
            tokens(there), half_rows(full, here, width), sems.at[0], sems.at[1], place.across()
        )
        load = pltpu.make_async_copy(tokens(here), stage, sems.at[2])
        keep = pltpu.make_async_copy(stage, half_rows(full, here, width), sems.at[3])
        away.start()
        load.start()
        load.wait()
        keep.start()
        multiply("nt", [(activation_ref, down_ref)], [feed])
        keep.wait()
        away.wait_send()
        came = half_rows(full, there, width)
        send(came, came, sems.at[0], sems.at[1], place.across()).wait_recv()
        multiply(
            "tt",
            [(full, dense_ref)],
            [block_out],
            lambda found, before: (found + before,),
            [feed],
        )

    return pl.pallas_call(
        kernel,
        out_shape=(
            jax.ShapeDtypeStruct((2 * width, length), bf16),
            jax.ShapeDtypeStruct((rows, model), bf16),
            jax.ShapeDtypeStruct((rows, model), f32),
        ),
        in_specs=[ANY] * 4,
        out_specs=(ANY,) * 3,
        scratch_shapes=[pltpu.VMEM((width, length), bf16), DMA((4,))],
        compiler_params=pltpu.CompilerParams(
            collective_id=4, has_side_effects=True, vmem_limit_bytes=60 << 20
        ),
        cost_estimate=pl.CostEstimate(flops=0, bytes_accessed=90_000_000, transcendentals=0),
        name="exchange_attended",
    )(attended, activation, down_full, dense_full)[:2]


def exchange_gradient(sizes, cotangents, dense_full, down_full, slope):
    rows, hidden = slope.shape
    local = dense_full.shape[1]
    width = local // 2
    count = len(cotangents)

    def kernel(*refs):
        cotangent_refs, (dense_ref, down_ref, slope_ref) = refs[:count], refs[count : count + 3]
        both, grad_hidden, made, stage, sems = refs[count + 3 :]
        place = Place(sizes)
        greet([place.across()])
        here, there = place.half, 1 - place.half

        def parts(weight_ref):
            found, first = [], 0
            for ref in cotangent_refs:
                found.append((ref, weight_ref.at[pl.ds(first, ref.shape[1])]))
                first += ref.shape[1]
            return found

        multiply("tt", [(b, a) for a, b in parts(dense_ref)], [made])
        away = send(
            half_rows(made, there, width), both.at[here], sems.at[0], sems.at[1], place.across()
        )
        load = pltpu.make_async_copy(half_rows(made, here, width), stage, sems.at[2])
        keep = pltpu.make_async_copy(stage, both.at[here], sems.at[3])
        away.start()
        load.start()
        load.wait()
        keep.start()
        multiply(
            "nn",
            parts(down_ref),
            [grad_hidden],
            lambda found, slope: (found * slope.astype(f32),),
            [slope_ref],
        )
        keep.wait()
        away.wait_send()
        came = both.at[there]
        send(came, came, sems.at[0], sems.at[1], place.across()).wait_recv()

    return pl.pallas_call(
        kernel,
        out_shape=(
            jax.ShapeDtypeStruct((2, width, rows), bf16),
            jax.ShapeDtypeStruct((rows, hidden), bf16),
            jax.ShapeDtypeStruct((local, rows), bf16),
        ),
        in_specs=[ANY] * (count + 3),
        out_specs=(ANY,) * 3,
        scratch_shapes=[pltpu.VMEM((width, rows), bf16), DMA((4,))],
        compiler_params=pltpu.CompilerParams(
            collective_id=5, has_side_effects=True, vmem_limit_bytes=60 << 20
        ),
        cost_estimate=pl.CostEstimate(flops=0, bytes_accessed=85_000_000, transcendentals=0),
        name="exchange_gradient",
    )(*cotangents, dense_full, down_full, slope)[:2]


def exchange_back(
    sizes, back, normed, grad_hidden, cotangents, activation, up_full, projection
):
    kinds, width, total = back.shape
    length = total // 2
    chips, halves = sizes["fsdp"] // 2, sizes["ctx"]
    rows, model = normed.shape
    hidden = grad_hidden.shape[1]
    span = model // (2 * chips)
    shard = span // halves
    side = shard // 2

    count = len(cotangents)

    def kernel(back_ref, normed_ref, hidden_ref, *rest):
        cotangent_refs, rest = rest[:count], rest[count:]
        (activation_ref, up_ref, weight_ref), rest = rest[:3], rest[3:]
        full, sums, turns, block_in = rest[0], rest[1:3], rest[3:7], rest[7]
        made_in, came_in, feed = rest[8:10], rest[10:12], rest[12]
        stage, sems, core_send, core_recv, turn_send, turn_recv = rest[13:]
        place = Place(sizes)
        greet(plane(place))
        here, there = place.half, 1 - place.half
        other = 1 - place.core

        def tokens(half):
            return back_ref.at[:, :, pl.ds(pl.multiple_of(half * length, length), length)]

        def heads(half):
            return full.at[:, pl.ds(pl.multiple_of(half * width, width), width)]

        away = send(tokens(there), heads(here), sems.at[0], sems.at[1], place.across())
        load = pltpu.make_async_copy(tokens(here), stage, sems.at[2])
        keep = pltpu.make_async_copy(stage, heads(here), sems.at[3])
        away.start()
        load.start()
        load.wait()
        keep.start()

        def to_pair(number):
            made, came = made_in[number], came_in[number]
            copies = []
            for chip in range(chips):
                copies.append(
                    send(
                        made.at[pl.ds(pl.multiple_of((2 * chip + other) * span, 16), span)],
                        came.at[pl.ds(chip * span, span)],
                        core_send.at[number, chip],
                        core_recv.at[number, chip],
                        place.pair(),
                    )
                )
                copies[-1].start()
            return copies

        def add_pair(number, copies):
            made, came, out = made_in[number], came_in[number], sums[number]
            for copy in copies:
                copy.wait()

            def step(mine, theirs, out_ref):
                out_ref[...] = (mine[...].astype(f32) + theirs[...].astype(f32)).astype(bf16)

            wide = hidden // 2
            pltpu.emit_pipeline(
                step,
                grid=(chips, 2),
                in_specs=[
                    pl.BlockSpec((span, wide), lambda i, j: (2 * i + place.core, j)),
                    pl.BlockSpec((span, wide), lambda i, j: (i, j)),
                ],
                out_specs=[pl.BlockSpec((span, wide), lambda i, j: (i, j))],
            )(made, came, out)

        def turn(number):
            out = sums[number]
            copies = []
            for k in range(1, chips):
                block = (place.ahead(k) * halves + there) * shard
                for way, device in enumerate(
                    (place.across(), place.device(chip=place.ahead(k)))
                ):
                    copies.append(
                        send(
                            out.at[pl.ds(pl.multiple_of(block + way * side, 16), side)],
                            turns[2 * number + way].at[k - 1],
                            turn_send.at[number, way, k],
                            turn_recv.at[number, way, k],
                            device,
                        )
                    )
                    copies[-1].start()
            return copies

        multiply("tn", [(normed_ref, hidden_ref)], [made_in[0]])
        up_copies = to_pair(0)
        first = 0
        for ref in cotangent_refs:
            span_of = pl.ds(first, ref.shape[1])
            multiply("tn", [(ref, activation_ref)], [made_in[1].at[span_of]])
            first += ref.shape[1]
        down_copies = to_pair(1)
        add_pair(0, up_copies)
        turned = turn(0)
        multiply("nt", [(hidden_ref, up_ref)], [feed])
        add_pair(1, down_copies)
        turned += turn(1)
        keep.wait()
        away.wait_send()
        send(heads(there), heads(there), sems.at[0], sems.at[1], place.across()).wait_recv()
        flat = full.reshape(2 * kinds * width, length)

        def step(left_ref, right_ref, before_ref, out_ref):
            found = before_ref[...]
            for kind in range(kinds):
                rows_of = pl.ds(kind * 2 * width, 2 * width)
                found += lax.dot_general(
                    left_ref[rows_of, :],
                    right_ref[kind],
                    row_by_col,
                    preferred_element_type=f32,
                )
            out_ref[...] = found.astype(bf16)

        tile = min(512, model)
        pltpu.emit_pipeline(
            step,
            grid=(model // tile,),
            in_specs=[
                pl.BlockSpec(flat.shape, lambda n: (0, 0)),
                pl.BlockSpec((kinds, tile, 2 * width), lambda n: (0, n, 0)),
                pl.BlockSpec((rows, tile), lambda n: (0, n)),
            ],
            out_specs=[pl.BlockSpec((rows, tile), lambda n: (0, n))],
        )(flat, weight_ref, feed, block_in)
        for copy in turned:
            copy.wait()

    product = jax.ShapeDtypeStruct((model, hidden), bf16)
    part = jax.ShapeDtypeStruct((model // 2, hidden), bf16)
    results = pl.pallas_call(
        kernel,
        out_shape=(
            jax.ShapeDtypeStruct((kinds, 2 * width, length), bf16),
            part,
            part,
            *[jax.ShapeDtypeStruct((chips - 1, side, hidden), bf16)] * 4,
            jax.ShapeDtypeStruct((rows, model), bf16),
            product,
            product,
            part,
            part,
            jax.ShapeDtypeStruct((rows, model), f32),
        ),
        in_specs=[ANY] * (6 + count),
        out_specs=(ANY,) * 13,
        scratch_shapes=[
            pltpu.VMEM((kinds, width, length), bf16),
            DMA((4,)),
            DMA((2, chips)),
            DMA((2, chips)),
            DMA((2, 2, chips)),
            DMA((2, 2, chips)),
        ],
        compiler_params=pltpu.CompilerParams(
            collective_id=6, has_side_effects=True, vmem_limit_bytes=60 << 20
        ),
        cost_estimate=pl.CostEstimate(flops=0, bytes_accessed=220_000_000, transcendentals=0),
        name="exchange_back",
    )(back, normed, grad_hidden, *cotangents, activation, up_full, projection)
    return results[:8]


def small_reduce(sizes, blocks):
    count, depth = sizes["fsdp"] * sizes["ctx"], sizes["tp"]

    def kernel(blocks_ref, out_ref, landed, line, send_sem, recv_sem, line_send, line_recv):
        place = Place(sizes)
        peers = place.group()
        layers = [(place.layer + k) % depth for k in range(1, depth)]
        devices = [place.device(chip=a, core=b, half=c) for a, b, c in peers]
        greet(devices + [place.device(layer=k) for k in layers])
        copies = []
        for at, (chip, core, half) in enumerate(peers):
            copy = send(
                blocks_ref.at[place.block(chip, core, half)],
                landed.at[at],
                send_sem.at[at],
                recv_sem.at[at],
                devices[at],
            )
            copy.start()
            copies.append(copy)
        total = blocks_ref[place.block()]
        for at, copy in enumerate(copies):
            copy.wait()
            total += landed[at]
        line[0] = total
        copies = []
        for k, layer in enumerate(layers):
            copy = send(
                line.at[0],
                line.at[k + 1],
                line_send.at[k],
                line_recv.at[k],
                place.device(layer=layer),
            )
            copy.start()
            copies.append(copy)
        for k, copy in enumerate(copies):
            copy.wait()
            total += line[k + 1]
        out_ref[...] = total

    block = blocks.shape[1:]
    return pl.pallas_call(
        kernel,
        out_shape=jax.ShapeDtypeStruct(block, f32),
        in_specs=[VMEM],
        out_specs=VMEM,
        scratch_shapes=[
            pltpu.VMEM((count - 1,) + block, f32),
            pltpu.VMEM((depth,) + block, f32),
            DMA((count - 1,)),
            DMA((count - 1,)),
            DMA((depth - 1,)),
            DMA((depth - 1,)),
        ],
        compiler_params=pltpu.CompilerParams(collective_id=3, has_side_effects=True),
        name="small_reduce",
    )(blocks)


def tile_at(number):
    return pl.ds(pl.multiple_of(number * TILE, TILE), TILE)


def allowed(kb, j, start):
    places = kb * TILE + lax.broadcasted_iota(jnp.int32, (TILE, TILE), 0)
    own = j * TILE + lax.broadcasted_iota(jnp.int32, (TILE, TILE), 1)
    return (places >= start) & (places <= own)


def attend_kernel(
    low_ref,
    mid_ref,
    triple_ref,
    start_ref,
    attended_ref,
    log_ref,
    query_t,
    key_t,
    value_t,
    key_rows,
    scores,
):
    length = triple_ref.shape[3]
    heads = triple_ref.shape[2] // HD
    score_scale = 1.0 / math.sqrt(HD)
    for number, ref in enumerate((query_t, key_t, value_t)):
        for part in range(2):
            piece = triple_ref[part, number]
            ref[:, part * length : (part + 1) * length] = (
                piece * score_scale if number == 0 else piece
            )
    rows = [slice(h * HD, (h + 1) * HD) for h in range(heads)]
    for h in range(heads):
        key_rows[h] = key_t[rows[h], :].T

    @pl.loop(0, 2 * length // TILE)
    def _(j):
        here = tile_at(j)
        start = start_ref[:, here]
        low, mid = low_ref[j], mid_ref[j]
        queries = [query_t[row, here] for row in rows]

        def score_with(masked):
            def score(kb, highest):
                ok = allowed(kb, j, start) if masked else None
                raised = []
                for h in range(heads):
                    found = jnp.dot(
                        key_rows[h, tile_at(kb), :], queries[h], preferred_element_type=f32
                    )
                    if masked:
                        found = jnp.where(ok, found, big_negative)
                    scores[h, tile_at(kb), :] = found
                    raised.append(
                        jnp.maximum(highest[h], jnp.max(found, axis=0, keepdims=True))
                    )
                return tuple(raised)

            return score

        highest = tuple(jnp.full((1, TILE), big_negative, f32) for _ in range(heads))
        highest = lax.fori_loop(low, mid, score_with(True), highest)
        highest = lax.fori_loop(mid, j, score_with(False), highest)
        highest = score_with(True)(j, highest)

        def weigh(kb, carry):
            after = []
            for h in range(heads):
                total, mixed = carry[h]
                prob = jnp.exp(scores[h, tile_at(kb), :] - highest[h])
                total = total + jnp.sum(prob, axis=0, keepdims=True)
                mixed = mixed + jnp.dot(
                    value_t[rows[h], tile_at(kb)], prob.astype(bf16), preferred_element_type=f32
                )
                after.append((total, mixed))
            return tuple(after)

        empty = tuple(
            (jnp.zeros((1, TILE), f32), jnp.zeros((HD, TILE), f32)) for _ in range(heads)
        )
        result = lax.fori_loop(low, j + 1, weigh, empty)
        for h in range(heads):
            total, mixed = result[h]
            attended_ref[rows[h], here] = (mixed / total).astype(bf16)
            log_ref[h, :, here] = highest[h] + jnp.log(total)


def turned_back(values, cosine, sine):
    half_rot = ROT // 2
    leading = values[:half_rot]
    trailing = values[half_rot:ROT]
    return jnp.concatenate(
        [
            leading * cosine + trailing * sine,
            trailing * cosine - leading * sine,
            values[ROT:],
        ],
        axis=0,
    )


def attend_back_kernel(
    low_ref,
    mid_ref,
    triple_ref,
    grad_ref,
    attended_ref,
    log_ref,
    start_ref,
    cosine_ref,
    sine_ref,
    back_ref,
    query_t,
    key_t,
    grad_t,
    key_rows,
    value_rows,
    key_sum,
    value_sum,
):
    length = triple_ref.shape[3]
    heads = triple_ref.shape[2] // HD
    score_scale = 1.0 / math.sqrt(HD)
    rows = [slice(h * HD, (h + 1) * HD) for h in range(heads)]
    for part in range(2):
        span = slice(part * length, (part + 1) * length)
        query_t[:, span] = triple_ref[part, 0] * score_scale
        key_t[:, span] = triple_ref[part, 1]
        grad_t[:, span] = grad_ref[part]
        for h in range(heads):
            value_rows[h, span, :] = triple_ref[part, 2, rows[h]].T
    for h in range(heads):
        key_rows[h] = key_t[rows[h], :].T
    key_sum[...] = jnp.zeros_like(key_sum)
    value_sum[...] = jnp.zeros_like(value_sum)

    @pl.loop(0, 2 * length // TILE)
    def _(j):
        here = tile_at(j)
        start = start_ref[:, here]
        low, mid = low_ref[j], mid_ref[j]
        queries = [query_t[row, here] for row in rows]
        grads = [grad_t[row, here] for row in rows]
        query_rows = [value.T for value in queries]
        grad_rows = [value.T for value in grads]
        logs = [log_ref[h, :, here] for h in range(heads)]
        deltas = [
            jnp.sum(
                grads[h].astype(f32) * attended_ref[rows[h], here].astype(f32),
                axis=0,
                keepdims=True,
            )
            for h in range(heads)
        ]

        def pull_with(masked):
            def pull(kb, query_back):
                ok = allowed(kb, j, start) if masked else None
                after = []
                for h in range(heads):
                    score = jnp.dot(
                        key_rows[h, tile_at(kb), :], queries[h], preferred_element_type=f32
                    )
                    if masked:
                        score = jnp.where(ok, score, big_negative)
                    prob = jnp.exp(score - logs[h])
                    down = jnp.dot(
                        value_rows[h, tile_at(kb), :], grads[h], preferred_element_type=f32
                    )
                    score_back = (prob * (down - deltas[h])).astype(bf16)
                    value_sum[h, tile_at(kb), :] += jnp.dot(
                        prob.astype(bf16), grad_rows[h], preferred_element_type=f32
                    )
                    key_sum[h, tile_at(kb), :] += jnp.dot(
                        score_back, query_rows[h], preferred_element_type=f32
                    )
                    after.append(
                        query_back[h]
                        + jnp.dot(
                            key_t[rows[h], tile_at(kb)], score_back, preferred_element_type=f32
                        )
                    )
                return tuple(after)

            return pull

        query_back = tuple(jnp.zeros((HD, TILE), f32) for _ in range(heads))
        query_back = lax.fori_loop(low, mid, pull_with(True), query_back)
        query_back = lax.fori_loop(mid, j, pull_with(False), query_back)
        query_back = pull_with(True)(j, query_back)
        for h in range(heads):
            back_ref[0, rows[h], here] = turned_back(
                query_back[h] * score_scale, cosine_ref[:, here], sine_ref[:, here]
            ).astype(bf16)

    for h in range(heads):
        back_ref[1, rows[h], :] = turned_back(
            key_sum[h].T, cosine_ref[...], sine_ref[...]
        ).astype(bf16)
        back_ref[2, rows[h], :] = value_sum[h].T.astype(bf16)


def attend(low, mid, triple, start):
    width, length = triple.shape[2], triple.shape[3]
    total, heads = 2 * length, width // HD
    area = total * total // 3 * heads
    return pl.pallas_call(
        attend_kernel,
        out_shape=(
            jax.ShapeDtypeStruct((width, total), bf16),
            jax.ShapeDtypeStruct((heads, 1, total), f32),
        ),
        in_specs=[SMEM, SMEM, VMEM, VMEM],
        out_specs=(VMEM, VMEM),
        scratch_shapes=[pltpu.VMEM((width, total), bf16)] * 3
        + [pltpu.VMEM((heads, total, HD), bf16), pltpu.VMEM((heads, total, TILE), f32)],
        compiler_params=pltpu.CompilerParams(vmem_limit_bytes=48 << 20),
        cost_estimate=pl.CostEstimate(
            flops=50 * area * HD, bytes_accessed=8 * width * total, transcendentals=area
        ),
        name="attend",
    )(low, mid, triple, start)


def attend_back(low, mid, triple, grad, attended, log_sum, start, cosine, sine):
    width, length = triple.shape[2], triple.shape[3]
    total, heads = 2 * length, width // HD
    area = total * total // 3 * heads
    return pl.pallas_call(
        attend_back_kernel,
        out_shape=jax.ShapeDtypeStruct((3, width, total), bf16),
        in_specs=[SMEM, SMEM] + [VMEM] * 7,
        out_specs=VMEM,
        scratch_shapes=[pltpu.VMEM((width, total), bf16)] * 3
        + [pltpu.VMEM((heads, total, HD), bf16)] * 2
        + [pltpu.VMEM((heads, total, HD), f32)] * 2,
        compiler_params=pltpu.CompilerParams(vmem_limit_bytes=48 << 20),
        cost_estimate=pl.CostEstimate(
            flops=100 * area * HD, bytes_accessed=12 * width * total, transcendentals=area
        ),
        name="attend_back",
    )(low, mid, triple, grad, attended, log_sum, start, cosine, sine)


def rotate_rows(values, cosine, sine):
    half_rot = ROT // 2
    leading = values[:, :half_rot]
    trailing = values[:, half_rot:ROT]
    return jnp.concatenate(
        [
            leading * cosine - trailing * sine,
            trailing * cosine + leading * sine,
            values[:, ROT:],
        ],
        axis=1,
    )


def ordered(*values):
    return lax.optimization_barrier(values)


def body(
    sizes,
    tokens,
    segments,
    positions,
    norm_gain,
    norm_bias,
    projection_weight,
    projection_bias,
    dense_weight,
    dense_bias,
    up_weight,
    up_bias,
    down_weight,
    down_bias,
    cotangent,
):
    own_len, model_width = tokens.shape[1], tokens.shape[2]
    half_len = segments.shape[1]
    local_width = projection_weight.shape[2]
    hidden_width = up_weight.shape[1]
    shard_rows = norm_gain.shape[0]
    half = lax.axis_index("ctx")
    total_len = 2 * half_len

    vectors = jnp.concatenate([norm_gain, norm_bias, dense_bias, down_bias]).astype(f32)
    vectors = jnp.pad(vectors.reshape(4, shard_rows), ((0, 4), (0, 0)))
    numbers = jnp.pad(jnp.concatenate([segments, positions], axis=0), ((0, 6), (0, 0)))
    exponent = jnp.arange(ROT // 2, dtype=f32) * 2.0 / ROT
    inverse = 10000.0 ** (-exponent)

    def angles(places_of):
        phase_angle = inverse[:, None] * places_of.astype(f32)[None, :]
        return jnp.cos(phase_angle), jnp.sin(phase_angle)

    cosine_own, sine_own = angles(positions[0])
    (
        vectors_full,
        numbers_other,
        normed,
        cotangent_early,
        projection,
        up_full,
        dense_full,
        down_full,
        both,
        activation,
        slope,
    ) = front(
        sizes,
        tokens[0],
        cotangent[0],
        vectors,
        numbers,
        [projection_weight.transpose(1, 0, 2), up_weight, dense_weight, down_weight],
        projection_bias.astype(f32).reshape(3 * local_width, 1),
        up_bias.astype(f32)[None, :],
        cosine_own,
        sine_own,
    )
    gain_full, shift_full, bias_dense, bias_down = (vectors_full[row] for row in range(4))

    cotangent_late, normed = ordered(cotangent[0, :, cotangent_early.shape[1] :], normed)
    cotangent_late = lax.all_gather(cotangent_late, "tp", axis=0, tiled=True)
    cotangents = [cotangent_early, cotangent_late]

    def in_order(own, other, axis):
        return jnp.where(
            half == 0,
            jnp.concatenate([own, other], axis=axis),
            jnp.concatenate([other, own], axis=axis),
        )

    sequence = in_order(numbers, numbers_other, 1)
    segment_row, position_row = sequence[0], sequence[1]
    places = jnp.arange(total_len, dtype=jnp.int32)
    edges = jnp.concatenate([jnp.ones((1,), bool), segment_row[1:] != segment_row[:-1]])
    start = lax.cummax(jnp.where(edges, places, 0))
    tile_count = total_len // TILE
    low = start[::TILE] // TILE
    mid = jnp.minimum(
        jnp.maximum((start[TILE - 1 :: TILE] + TILE - 1) // TILE, low),
        jnp.arange(tile_count, dtype=jnp.int32),
    )
    cosine_full, sine_full = angles(position_row)
    attended_heads, log_sum = attend(low, mid, both, start[None, :])
    attended, block_out = exchange_attended(
        sizes, attended_heads, activation, down_full, dense_full
    )
    branch_own = lax.psum_scatter(block_out, "tp", scatter_dimension=0, tiled=True)
    cotangent_late, block_out = ordered(cotangent_late, block_out)
    cotangents = [cotangent_early, cotangent_late]
    grad_both, grad_hidden = exchange_gradient(sizes, cotangents, dense_full, down_full, slope)
    back_heads = attend_back(
        low,
        mid,
        both,
        grad_both,
        attended_heads,
        log_sum,
        start[None, :],
        cosine_full,
        sine_full,
    )
    grad_projected, up_sum, down_sum, *turned, block_in = exchange_back(
        sizes, back_heads, normed, grad_hidden, cotangents, activation, up_full, projection
    )
    grad_projected = grad_projected.reshape(3 * local_width, half_len)
    block_in, branch_own = ordered(block_in, branch_own)
    grad_normed_own = lax.psum_scatter(block_in, "tp", scatter_dimension=0, tiled=True).astype(f32)
    hidden_sum = jnp.sum(grad_hidden.astype(f32), axis=0)
    projected_sum = jnp.sum(grad_projected.astype(f32), axis=1)
    small = jnp.concatenate([projected_sum, hidden_sum]).reshape(-1, 128)
    groups = sizes["fsdp"] // 2 * sizes["ctx"]
    up_part, down_part, projection_part, dense_part, small_total = reduce(
        sizes,
        [v.reshape(groups, shard_rows, hidden_width) for v in (up_sum, down_sum)],
        turned,
        [([normed], grad_projected), (cotangents, attended)],
        [1, 1, 3, 1],
        small,
        2,
        "reduce_weights",
    )
    tokens_late, grad_normed_own = ordered(tokens[0], grad_normed_own)
    inputs = tokens_late.astype(f32)
    _, norm_pull = jax.vjp(layer_norm, inputs, gain_full, shift_full)
    layer_output = (inputs + branch_own.astype(f32) + (bias_dense + bias_down)).astype(bf16)
    cotangent_own = cotangent[0].astype(f32)
    grad_inputs, grad_gain, grad_shift = norm_pull(grad_normed_own)
    input_grad = grad_inputs + cotangent_own
    output_sum = jnp.sum(cotangent_own, axis=0)
    sums = jnp.stack([grad_gain, grad_shift, output_sum]).reshape(3, -1, shard_rows)
    sums = jnp.pad(sums.transpose(1, 0, 2), ((0, 0), (0, 5), (0, 0)))
    totals = small_reduce(sizes, sums)
    small_flat = small_total.reshape(-1)
    return (
        layer_output[None],
        input_grad[None],
        totals[0],
        totals[1],
        projection_part.transpose(1, 0, 2),
        small_flat[: 3 * local_width].reshape(3, local_width),
        dense_part,
        totals[2],
        up_part,
        small_flat[3 * local_width :],
        down_part,
        totals[2],
    )


def solution(mesh):
    placed = (
        P("fsdp", ("ctx", "tp"), None),
        P("fsdp", "ctx"),
        P("fsdp", "ctx"),
        P(("fsdp", "ctx")),
        P(("fsdp", "ctx")),
        P(("fsdp", "ctx"), None, "tp"),
        P(None, "tp"),
        P(("fsdp", "ctx"), "tp"),
        P(("fsdp", "ctx")),
        P(("fsdp", "ctx"), "tp"),
        P("tp"),
        P(("fsdp", "ctx"), "tp"),
        P(("fsdp", "ctx")),
        P("fsdp", ("ctx", "tp"), None),
    )
    return jax.shard_map(
        functools.partial(body, dict(mesh.shape)),
        mesh=mesh,
        in_specs=placed,
        out_specs=(
            P("fsdp", ("ctx", "tp"), None),
            P("fsdp", ("ctx", "tp"), None),
            P(("fsdp", "ctx")),
            P(("fsdp", "ctx")),
            P(("fsdp", "ctx"), None, "tp"),
            P(None, "tp"),
            P(("fsdp", "ctx"), "tp"),
            P(("fsdp", "ctx")),
            P(("fsdp", "ctx"), "tp"),
            P("tp"),
            P(("fsdp", "ctx"), "tp"),
            P(("fsdp", "ctx")),
        ),
        check_vma=False,
    )
```

```python
import functools
import math

import jax
import jax.numpy as jnp
from jax import lax
from jax.experimental import pallas as pl
from jax.experimental.pallas import tpu as pltpu
from jax.sharding import PartitionSpec as P

HD = 64
ROT = 32
TILE = 256

epsilon = 1e-05
big_negative = -1000000000.0
root_two_over_pi = 0.7978845608028654
contract_rows = (((0,), (0,)), ((), ()))
contract_cols = (((1,), (1,)), ((), ()))
row_by_col = (((0,), (1,)), ((), ()))
MESH = pl.DeviceIdType.MESH
ANY = pl.BlockSpec(memory_space=pl.ANY)
VMEM = pl.BlockSpec(memory_space=pltpu.VMEM)
SMEM = pl.BlockSpec(memory_space=pltpu.SMEM)
DMA = pltpu.SemaphoreType.DMA
f32 = jnp.float32
bf16 = jnp.bfloat16


def layer_norm(values, gain_full, shift_full):
    center = jnp.mean(values, axis=-1, keepdims=True)
    centered = values - center
    spread = jnp.mean(centered * centered, axis=-1, keepdims=True)
    return centered * lax.rsqrt(spread + epsilon) * gain_full + shift_full


def gelu_and_slope(values):
    turned = jnp.tanh(root_two_over_pi * (values + 0.044715 * values * values * values))
    slope = 0.5 * (1.0 + turned) + 0.5 * values * (1.0 - turned * turned) * root_two_over_pi * (
        1.0 + 3.0 * 0.044715 * values * values
    )
    return 0.5 * values * (1.0 + turned), slope


class Place:
    def __init__(self, sizes):
        self.chips = sizes["fsdp"] // 2
        self.halves = sizes["ctx"]
        self.depth = sizes["tp"]
        lane = lax.axis_index("fsdp")
        self.chip = lane // 2
        self.core = lane % 2
        self.half = lax.axis_index("ctx")
        self.layer = lax.axis_index("tp")

    def device(self, chip=None, core=None, half=None, layer=None):
        chip = self.chip if chip is None else chip
        core = self.core if core is None else core
        half = self.half if half is None else half
        layer = self.layer if layer is None else layer
        return (chip * 2 + core, half, layer)

    def block(self, chip=None, core=None, half=None):
        chip = self.chip if chip is None else chip
        core = self.core if core is None else core
        half = self.half if half is None else half
        return (chip * 2 + core) * self.halves + half

    def ahead(self, k):
        return (self.chip + k) % self.chips

    def behind(self, k):
        return (self.chip + self.chips - k) % self.chips

    def neighbours(self):
        last = self.depth - 1
        return (
            (self.layer < last, self.device(layer=jnp.minimum(self.layer + 1, last))),
            (self.layer > 0, self.device(layer=jnp.maximum(self.layer - 1, 0))),
        )

    def pair(self):
        return self.device(core=1 - self.core)

    def across(self):
        return self.device(half=1 - self.half)

    def group(self):
        found = []
        for k in range(self.chips):
            for core in range(2):
                for half in range(2):
                    if k or core or half:
                        found.append(
                            (self.ahead(k), (self.core + core) % 2, (self.half + half) % 2)
                        )
        return found


def greet(devices):
    barrier = pltpu.get_barrier_semaphore()
    for device in devices:
        pl.semaphore_signal(barrier, inc=1, device_id=device, device_id_type=MESH)
    pl.semaphore_wait(barrier, len(devices))


def greet_line(place, devices):
    barrier = pltpu.get_barrier_semaphore()
    for device in devices:
        pl.semaphore_signal(barrier, inc=1, device_id=device, device_id_type=MESH)
    count = len(devices)
    for there, device in place.neighbours():

        @pl.when(there)
        def _(device=device):
            pl.semaphore_signal(barrier, inc=1, device_id=device, device_id_type=MESH)

        count = count + there.astype(jnp.int32)
    pl.semaphore_wait(barrier, count)


def send(source, target, send_sem, recv_sem, device):
    return pltpu.make_async_remote_copy(
        src_ref=source,
        dst_ref=target,
        send_sem=send_sem,
        recv_sem=recv_sem,
        device_id=device,
        device_id_type=MESH,
    )


class Line:
    def __init__(self, place, own, full, send_sem, recv_sem, keep_sem):
        self.place, self.own, self.full = place, own, full
        self.send_sem, self.recv_sem = send_sem, recv_sem
        self.rows = own.shape[0]
        self.pending = []
        self.keep = pltpu.make_async_copy(own, self.block(place.layer), keep_sem)

    def block(self, source):
        return self.full.at[pl.ds(pl.multiple_of(source * self.rows, 16), self.rows)]

    def copy(self, piece, target, way, hop, device):
        return send(piece, target, self.send_sem.at[way, hop], self.recv_sem.at[way, hop], device)

    def launch(self, copy, condition):
        pl.when(condition)(copy.start)
        self.pending.append((copy, condition))

    def start(self):
        for way, (there, device) in enumerate(self.place.neighbours()):
            target = self.block(self.place.layer)
            self.launch(self.copy(self.own, target, way, 0, device), there)
        self.keep.start()

    def step(self, k):
        last = self.place.depth - 1
        for way, (onward, device) in enumerate(self.place.neighbours()):
            source = self.place.layer - k if way == 0 else self.place.layer + k
            there = (source >= 0) & (source <= last)
            piece = self.block(jnp.clip(source, 0, last))
            pl.when(there)(self.copy(piece, piece, way, k - 1, device).wait_recv)
            if k < last:
                self.launch(self.copy(piece, piece, way, k, device), there & onward)

    def end(self):
        for copy, condition in self.pending:
            pl.when(condition)(copy.wait_send)


def plane(place):
    found = [place.device(chip=place.ahead(k)) for k in range(1, place.chips)]
    return found + [place.across(), place.pair()]


def reduce(sizes, paired, turned, rights, small, collective_id, name):
    chips, halves = sizes["fsdp"] // 2, sizes["ctx"]
    groups = chips * halves
    paired_count, made_count = len(paired), len(rights)
    weight_count = paired_count + made_count
    whole_count = weight_count - 1
    block_rows = paired[0][0].shape[0] // (2 * groups)
    widths = [v.shape[1] for v, _ in paired] + [v.shape[0] for _, v in rights]
    sides = [turned[2 * a].shape[1] for a in range(paired_count)] + [block_rows // 2] * made_count

    def kernel(*refs):
        refs = list(refs)

        def take(count):
            taken = refs[:count]
            del refs[:count]
            return taken

        paired_in = [take(2) for _ in range(paired_count)]
        turned_in = take(2 * paired_count)
        lefts = [take(len(left)) for left, _ in rights]
        factors = take(made_count)
        (small_ref,) = take(1)
        weight_out = take(whole_count)
        (small_out,) = take(1)
        held_out, made = take(weight_count - whole_count), take(made_count)
        own, turn_a, turn_b = (take(weight_count) for _ in range(3))
        near = take(whole_count)
        pair = take(weight_count)
        load_sem, core_send, core_recv = take(3)
        turn_send, turn_recv, near_send, near_recv = take(4)
        small_pair, small_near, small_far, small_send, small_recv = take(5)
        place = Place(sizes)
        greet(plane(place))
        pending = []

        def launch(copy, condition=None):
            if condition is None:
                copy.start()
            else:
                pl.when(condition)(copy.start)
            pending.append((copy, condition))

        other = 1 - place.core
        needed = [place.ahead(k) * halves + place.half for k in range(1, chips)]
        needed += [place.chip * halves + 1 - place.half, place.chip * halves + place.half]
        for a in range(paired_count):
            for at, number in enumerate(needed):
                chip = place.ahead(at + 1) if at < chips - 1 else place.chip
                half = 1 - place.half if at == chips - 1 else place.half
                mine = place.block(chip, place.core, half)
                pltpu.make_async_copy(
                    paired_in[a][0].at[pl.ds(pl.multiple_of(mine * block_rows, 16), block_rows)],
                    own[a].at[number],
                    load_sem.at[a, number],
                ).start()
                pltpu.make_async_copy(
                    paired_in[a][1].at[pl.ds(pl.multiple_of(number * block_rows, 16), block_rows)],
                    pair[a].at[at],
                    core_recv.at[a, number],
                ).start()
            for way, target in enumerate((turn_a[a], turn_b[a])):
                for k in range(1, chips):
                    pltpu.make_async_copy(
                        turned_in[2 * a + way].at[k - 1],
                        target.at[k - 1],
                        turn_recv.at[a, way, k],
                    ).start()

        def make(a):
            at = a - paired_count
            first = 0
            for left in lefts[at]:
                span = pl.ds(first, left.shape[1])
                multiply("tt", [(left, factors[at])], [made[at].at[span]])
                first += left.shape[1]
            for number in range(groups):
                chip, half = number // halves, number % halves
                theirs = place.block(chip, other, half)
                mine = place.block(chip, place.core, half)
                launch(
                    send(
                        made[at].at[pl.ds(pl.multiple_of(theirs * block_rows, 16), block_rows)],
                        pair[a].at[number],
                        core_send.at[a, number],
                        core_recv.at[a, number],
                        place.pair(),
                    )
                )
                pltpu.make_async_copy(
                    made[at].at[pl.ds(pl.multiple_of(mine * block_rows, 16), block_rows)],
                    own[a].at[number],
                    load_sem.at[a, number],
                ).start()

        def pair_sum(a, number, at_needed=None):
            mine = own[a].at[number]
            pltpu.make_async_copy(mine, mine, load_sem.at[a, number]).wait()
            if a < paired_count:
                theirs = pair[a].at[at_needed]
                pltpu.make_async_copy(theirs, theirs, core_recv.at[a, number]).wait()
            else:
                theirs = pair[a].at[number]
                send(
                    theirs, theirs, core_send.at[a, number], core_recv.at[a, number], place.pair()
                ).wait_recv()

            @pl.loop(0, block_rows, step=16)
            def _(r):
                at = pl.ds(pl.multiple_of(r, 16), 16)
                mine[at, :] = (mine[at, :].astype(f32) + theirs[at, :].astype(f32)).astype(bf16)

        def diagonal(a):
            for k in range(1, chips):
                number = place.ahead(k) * halves + 1 - place.half
                pair_sum(a, number)
                launch(
                    send(
                        own[a].at[number, pl.ds(0, sides[a])],
                        turn_a[a].at[k - 1],
                        turn_send.at[a, 0, k],
                        turn_recv.at[a, 0, k],
                        place.across(),
                    )
                )
                launch(
                    send(
                        own[a].at[number, pl.ds(sides[a], block_rows - sides[a])],
                        turn_b[a].at[k - 1],
                        turn_send.at[a, 1, k],
                        turn_recv.at[a, 1, k],
                        place.device(chip=place.ahead(k)),
                    )
                )

        def direct_pairs(a):
            for k in range(1, chips):
                pair_sum(a, place.ahead(k) * halves + place.half, k - 1)
            pair_sum(a, place.chip * halves + 1 - place.half, chips - 1)

        def add_turn(a, number, first, count, refs_at):
            @pl.loop(0, count, step=16)
            def _(r):
                at = pl.ds(pl.multiple_of(first + r, 16), 16)
                total = own[a][number, at, :].astype(f32)
                for ref, k in refs_at:
                    total += ref[k, pl.ds(pl.multiple_of(r, 16), 16), :].astype(f32)
                own[a][number, at, :] = total.astype(bf16)

        def turn_wait(a, way, k):
            piece = (turn_a, turn_b)[way][a].at[k - 1]
            if a < paired_count:
                pltpu.make_async_copy(piece, piece, turn_recv.at[a, way, k]).wait()
            else:
                send(
                    piece, piece, turn_send.at[a, way, k], turn_recv.at[a, way, k], place.across()
                ).wait_recv()

        def hand(a, at, number):
            pltpu.make_async_copy(
                own[a].at[number], held_out[a - whole_count].at[at], near_send.at[a, at]
            ).start()

        def direct(a):
            for k in range(1, chips):
                number = place.ahead(k) * halves + place.half
                turn_wait(a, 0, k)
                add_turn(a, number, 0, sides[a], [(turn_a[a], k - 1)])
                if a >= whole_count:
                    hand(a, k, number)
                    continue
                launch(
                    send(
                        own[a].at[number],
                        near[a].at[k],
                        near_send.at[a, k],
                        near_recv.at[a, k],
                        place.device(chip=place.ahead(k)),
                    )
                )
            for k in range(1, chips):
                turn_wait(a, 1, k)
            number = place.chip * halves + 1 - place.half
            add_turn(
                a,
                number,
                sides[a],
                block_rows - sides[a],
                [(turn_b[a], k - 1) for k in range(1, chips)],
            )
            if a >= whole_count:
                hand(a, 0, number)
                return
            launch(
                send(
                    own[a].at[number],
                    near[a].at[0],
                    near_send.at[a, 0],
                    near_recv.at[a, 0],
                    place.across(),
                )
            )

        def finish(a):
            for k in range(chips):
                piece = near[a].at[k]
                send(
                    piece, piece, near_send.at[a, k], near_recv.at[a, k], place.across()
                ).wait_recv()
                pltpu.make_async_copy(piece, weight_out[a].at[k], load_sem.at[a, k]).start()
            number = place.chip * halves + place.half
            pltpu.make_async_copy(
                own[a].at[number], weight_out[a].at[chips], load_sem.at[a, chips]
            ).start()

        def finish_end(a):
            for k in range(chips + 1):
                piece = weight_out[a].at[k]
                pltpu.make_async_copy(piece, piece, load_sem.at[a, k]).wait()

        def swap_small(source, target, at, device):
            copy = send(source, target, small_send.at[at], small_recv.at[at], device)
            launch(copy)
            return copy

        swap_small(small_ref, small_pair, 0, place.pair())
        for a in range(paired_count):
            direct_pairs(a)
            direct(a)
        for a in range(paired_count, weight_count):
            make(a)
        send(small_pair, small_pair, small_send.at[0], small_recv.at[0], place.pair()).wait_recv()
        small_near[0] = small_ref[...] + small_pair[...]
        for k in range(1, chips):
            swap_small(small_near.at[0], small_near.at[k], k, place.device(chip=place.ahead(k)))
        for a in range(paired_count, weight_count):
            diagonal(a)
            direct_pairs(a)
        total = small_near[0]
        for k in range(1, chips):
            piece = small_near.at[k]
            send(piece, piece, small_send.at[k], small_recv.at[k], place.pair()).wait_recv()
            total += small_near[k]
        small_far[0] = total
        swap_small(small_far.at[0], small_far.at[1], chips, place.across())
        for a in range(weight_count):
            pair_sum(a, place.chip * halves + place.half, chips)
        for a in range(paired_count, weight_count):
            direct(a)
            if a >= whole_count:
                hand(a, chips, place.chip * halves + place.half)
        for a in range(whole_count):
            finish(a)
        for a in range(whole_count):
            finish_end(a)
        for a in range(whole_count, weight_count):
            for at in range(chips + 1):
                piece = held_out[a - whole_count].at[at]
                pltpu.make_async_copy(piece, piece, near_send.at[a, at]).wait()
        piece = small_far.at[1]
        send(piece, piece, small_send.at[chips], small_recv.at[chips], place.pair()).wait_recv()
        small_out[...] = small_far[0] + small_far[1]
        for copy, condition in pending:
            if condition is None:
                copy.wait_send()
            else:
                pl.when(condition)(copy.wait_send)

    shapes = [
        jax.ShapeDtypeStruct((chips + 1, block_rows, w), bf16) for w in widths[:whole_count]
    ]
    shapes.append(jax.ShapeDtypeStruct(small.shape, f32))
    held_shapes = [
        jax.ShapeDtypeStruct((chips + 1, block_rows, w), bf16) for w in widths[whole_count:]
    ]
    made_shapes = [
        jax.ShapeDtypeStruct((2 * groups * block_rows, w), bf16) for w in widths[paired_count:]
    ]
    scratch = [pltpu.VMEM((groups, block_rows, w), bf16) for w in widths]
    scratch += [pltpu.VMEM((chips - 1, n, w), bf16) for w, n in zip(widths, sides)]
    scratch += [pltpu.VMEM((chips - 1, block_rows - n, w), bf16) for w, n in zip(widths, sides)]
    scratch += [pltpu.VMEM((chips, block_rows, w), bf16) for w in widths[:whole_count]]
    scratch += [pltpu.VMEM((chips + 1, block_rows, w), bf16) for w in widths[:paired_count]]
    scratch += [pltpu.VMEM((groups, block_rows, w), bf16) for w in widths[paired_count:]]
    scratch += [
        DMA((weight_count, groups + 1)),
        DMA((weight_count, groups)),
        DMA((weight_count, groups)),
        DMA((weight_count, 2, chips)),
        DMA((weight_count, 2, chips)),
        DMA((weight_count, chips + 1)),
        DMA((weight_count, chips + 1)),
        pltpu.VMEM(small.shape, f32),
        pltpu.VMEM((chips,) + small.shape, f32),
        pltpu.VMEM((2,) + small.shape, f32),
        DMA((chips + 1,)),
        DMA((chips + 1,)),
    ]
    lefts = [v for left, _ in rights for v in left]
    factors = [v for _, v in rights]
    return pl.pallas_call(
        kernel,
        out_shape=tuple(shapes + held_shapes + made_shapes),
        in_specs=[ANY] * (4 * paired_count + len(lefts) + made_count) + [VMEM],
        out_specs=(ANY,) * whole_count + (VMEM,) + (ANY,) * (weight_count - whole_count + made_count),
        scratch_shapes=scratch,
        compiler_params=pltpu.CompilerParams(
            collective_id=collective_id, has_side_effects=True, vmem_limit_bytes=60 << 20
        ),
        cost_estimate=pl.CostEstimate(flops=0, bytes_accessed=400_000_000, transcendentals=0),
        name=name,
    )(*[v for two in paired for v in two], *turned, *lefts, *factors, small)[: weight_count + 1]


def multiply(kind, parts, outs, finish=None, extra=(), tile=512):
    dims = (((0 if kind[0] == "t" else 1,), (1 if kind[1] == "t" else 0,)), ((), ()))
    left, right = parts[0]
    rows = left.shape[1] if kind[0] == "t" else left.shape[0]
    width = right.shape[0] if kind[1] == "t" else right.shape[1]
    tile = min(tile, width)
    specs = []
    for left, right in parts:
        specs.append(pl.BlockSpec(left.shape, lambda n: (0, 0)))
        if kind[1] == "t":
            specs.append(pl.BlockSpec((tile, right.shape[1]), lambda n: (n, 0)))
        else:
            specs.append(pl.BlockSpec((right.shape[0], tile), lambda n: (0, n)))
    specs += [pl.BlockSpec((v.shape[0], tile), lambda n: (0, n)) for v in extra]

    def step(*refs):
        found = None
        for number in range(len(parts)):
            product = lax.dot_general(
                refs[2 * number][...],
                refs[2 * number + 1][...],
                dims,
                preferred_element_type=f32,
            )
            found = product if found is None else found + product
        rest = refs[2 * len(parts) :]
        results = (found,)
        if finish is not None:
            results = finish(found, *(v[...] for v in rest[: len(extra)]))
        for ref, value in zip(rest[len(extra) :], results):
            ref[...] = value.astype(ref.dtype)

    factors = [v for pair in parts for v in pair]
    pltpu.emit_pipeline(
        step,
        grid=(width // tile,),
        in_specs=specs,
        out_specs=[pl.BlockSpec((v.shape[0], tile), lambda n: (0, n)) for v in outs],
    )(*factors, *extra, *outs)


def half_rows(ref, half, count):
    return ref.at[pl.ds(pl.multiple_of(half * count, count), count)]


def front(sizes, tokens, cotangent, vectors, numbers, weights, projection_bias, up_bias):
    chips, halves, depth = sizes["fsdp"] // 2, sizes["ctx"], sizes["tp"]
    groups = sizes["fsdp"] * halves
    own_len, model = tokens.shape
    length = own_len * depth
    projection, up, dense, down = weights
    weight_count = len(weights)
    kinds, local = projection.shape[0], projection.shape[2]
    count = local // 2
    hidden = up.shape[1]
    shard = vectors[0].shape[0]
    half_rot = ROT // 2
    early_width = model // 4 * 3

    def kernel(*refs):
        refs = list(refs)

        def take(number):
            taken = refs[:number]
            del refs[:number]
            return taken

        tokens_ref, cotangent_ref = take(2)
        vector_in, number_in = take(len(vectors)), take(len(numbers))
        weight_in = take(weight_count)
        bias_in, up_bias_in = take(2)
        vectors_out, *numbers_out = take(1 + len(numbers))
        normed, cotangent_rows, cotangent_late = take(3)
        weight_out = take(weight_count)
        both, activation, slope, triple = take(4)
        landed, normed_own, stage, vector_ref, bias_ref, up_bias_ref, cosine_ref, sine_ref = take(8)
        vector_send, vector_recv, number_sems, single, line_send, line_recv = take(6)
        keep, near_send, near_recv, turn_send, turn_recv, core_send, core_recv = take(7)
        place = Place(sizes)
        peers = place.group()
        greet_line(place, [place.device(chip=a, core=b, half=c) for a, b, c in peers])
        pending = []

        def launch(copy):
            copy.start()
            pending.append(copy)

        def part(a, block, first=0, rows=None):
            rows = weight_in[a].shape[-2] if rows is None else rows
            start = pl.multiple_of(block * weight_in[a].shape[-2] + first, 16)
            span = pl.ds(start, rows)
            return weight_out[a].at[:, span] if a == 0 else weight_out[a].at[span]

        def arrive(piece, recv_sem):
            send(piece, piece, recv_sem, recv_sem, place.pair()).wait_recv()

        mine = place.block()
        vector_ref[...] = jnp.zeros_like(vector_ref)
        for row, ref in enumerate(vector_in):
            vector_ref[row : row + 1, :] = ref[...].astype(f32).reshape(1, shard)
        vector_keep = pltpu.make_async_copy(vector_ref, landed.at[mine], single.at[0])
        vector_keep.start()
        for at, (chip, core, half) in enumerate(peers):
            launch(
                send(
                    vector_ref,
                    landed.at[mine],
                    vector_send.at[at],
                    vector_recv.at[at],
                    place.device(chip=chip, core=core, half=half),
                )
            )
        for number in range(len(numbers)):
            launch(
                send(
                    number_in[number],
                    numbers_out[number],
                    number_sems.at[0, number],
                    number_sems.at[1, number],
                    place.across(),
                )
            )

        def near_start(a):
            own = part(a, place.block())
            for k in range(1, chips):
                launch(
                    send(
                        weight_in[a],
                        own,
                        near_send.at[a, k],
                        near_recv.at[a, k],
                        place.device(chip=place.ahead(k)),
                    )
                )
            launch(
                send(weight_in[a], own, near_send.at[a, 0], near_recv.at[a, 0], place.across())
            )
            launch(send(weight_in[a], own, core_send.at[a, 0], core_recv.at[a, 0], place.pair()))
            pltpu.make_async_copy(weight_in[a], own, keep.at[a]).start()

        def near_step(a):
            side = weight_in[a].shape[-2] // 4
            rest = weight_in[a].shape[-2] - side
            for k in range(1, chips):
                block = place.block(chip=place.behind(k))
                piece = part(a, block)
                arrive(piece, near_recv.at[a, k])
                top = part(a, block, 0, side)
                launch(
                    send(top, top, turn_send.at[a, 0, k], turn_recv.at[a, 0, k], place.across())
                )
                launch(send(piece, piece, core_send.at[a, k], core_recv.at[a, k], place.pair()))
            block = place.block(half=1 - place.half)
            piece = part(a, block)
            arrive(piece, near_recv.at[a, 0])
            low = part(a, block, side, rest)
            for k in range(1, chips):
                launch(
                    send(
                        low,
                        low,
                        turn_send.at[a, 1, k],
                        turn_recv.at[a, 1, k],
                        place.device(chip=place.ahead(k)),
                    )
                )
            launch(
                send(piece, piece, core_send.at[a, chips], core_recv.at[a, chips], place.pair())
            )

        def turn_step(a):
            side = weight_in[a].shape[-2] // 4
            rest = weight_in[a].shape[-2] - side
            for k in range(1, chips):
                block = place.block(chip=place.behind(k), half=1 - place.half)
                arrive(part(a, block, 0, side), turn_recv.at[a, 0, k])
                arrive(part(a, block, side, rest), turn_recv.at[a, 1, k])
                piece = part(a, block)
                launch(
                    send(
                        piece,
                        piece,
                        core_send.at[a, chips + k],
                        core_recv.at[a, chips + k],
                        place.pair(),
                    )
                )

        def core_step(a):
            other = 1 - place.core
            blocks = [place.block(core=other)]
            blocks += [place.block(place.behind(k), other) for k in range(1, chips)]
            blocks += [place.block(None, other, 1 - place.half)]
            blocks += [
                place.block(place.behind(k), other, 1 - place.half) for k in range(1, chips)
            ]
            for at, block in enumerate(blocks):
                arrive(part(a, block), core_recv.at[a, at])
            pltpu.make_async_copy(weight_in[a], part(a, place.block()), keep.at[a]).wait()

        near_start(0)

        vector_keep.wait()
        for at in range(len(peers)):
            place_in = at + 1
            source = place.block(
                place.behind(place_in // 4),
                (place.core + place_in // 2 % 2) % 2,
                (place.half + place_in % 2) % 2,
            )
            arrive(landed.at[source], vector_recv.at[at])
        for number in range(groups):
            vectors_out[:, number * shard : (number + 1) * shard] = landed[number]

        @pl.loop(0, own_len, step=32)
        def _(r):
            at = pl.ds(pl.multiple_of(r, 32), 32)
            values = tokens_ref[at, :].astype(f32)
            normed_own[at, :] = layer_norm(
                values, vectors_out[0:1, :], vectors_out[1:2, :]
            ).astype(bf16)

        early = cotangent_ref.at[:, pl.ds(0, early_width)]
        lines = (
            Line(place, normed_own, normed, line_send.at[0], line_recv.at[0], single.at[3]),
            Line(place, early, cotangent_rows, line_send.at[1], line_recv.at[1], single.at[8]),
        )

        lines[0].start()
        near_start(1)
        late_keep = pltpu.make_async_copy(
            cotangent_ref.at[:, pl.ds(early_width, model - early_width)],
            cotangent_late,
            single.at[1],
        )
        late_keep.start()
        bias_ref[...] = bias_in[...].astype(f32).T
        up_bias_ref[...] = up_bias_in[...].astype(f32).reshape(1, hidden)
        turns = lax.broadcasted_iota(jnp.int32, (half_rot, 1), 0)
        inverse = jnp.zeros((half_rot, 1), f32)
        for row in range(half_rot):
            inverse = jnp.where(turns == row, 10000.0 ** (-2.0 * row / ROT), inverse)
        phase = inverse * number_in[1][...].astype(f32)
        cosine_ref[...] = jnp.cos(phase)
        sine_ref[...] = jnp.sin(phase)
        near_step(0)
        lines[0].step(1)
        near_start(3)
        near_start(2)
        turn_step(0)
        near_step(1)
        for k in range(2, depth):
            lines[0].step(k)
        lines[1].start()
        lines[0].keep.wait()
        core_step(0)
        near_step(3)

        def project(weight, rows, cosine_here, sine_here, out):
            for kind in range(kinds):
                found = lax.dot_general(
                    weight[kind], rows[...], row_by_col, preferred_element_type=f32
                )
                found = found + bias_ref[:, kind : kind + 1]
                if kind == 2:
                    out[kind] = found.astype(bf16)
                    continue
                for head in range(local // HD):
                    first = head * HD
                    leading = found[first : first + half_rot]
                    trailing = found[first + half_rot : first + ROT]
                    turned = (
                        leading * cosine_here[...] - trailing * sine_here[...],
                        trailing * cosine_here[...] + leading * sine_here[...],
                        found[first + ROT : first + HD],
                    )
                    out[kind, first : first + HD] = jnp.concatenate(turned, axis=0).astype(bf16)

        tile = min(512, length)
        pltpu.emit_pipeline(
            project,
            grid=(length // tile,),
            in_specs=[
                pl.BlockSpec(weight_out[0].shape, lambda n: (0, 0, 0)),
                pl.BlockSpec((tile, model), lambda n: (n, 0)),
                pl.BlockSpec((half_rot, tile), lambda n: (0, n)),
                pl.BlockSpec((half_rot, tile), lambda n: (0, n)),
            ],
            out_specs=[pl.BlockSpec((kinds, local, tile), lambda n: (0, 0, n))],
        )(weight_out[0], normed, cosine_ref, sine_ref, triple)

        def heads(half):
            return triple.at[:, pl.ds(pl.multiple_of(half * count, count), count)]

        here, there = place.half, 1 - place.half
        launch(send(heads(there), both.at[here], single.at[4], single.at[5], place.across()))
        load = pltpu.make_async_copy(heads(here), stage, single.at[6])
        load.start()
        load.wait()
        stage_keep = pltpu.make_async_copy(stage, both.at[here], single.at[7])
        stage_keep.start()
        near_step(2)
        lines[1].step(1)
        turn_step(1)
        core_step(1)
        wide = hidden // 2
        for number in range(2):
            span = pl.ds(number * wide, wide)
            multiply(
                "nn",
                [(normed, weight_out[1].at[:, span])],
                [activation.at[:, span], slope.at[:, span]],
                lambda found, bias: gelu_and_slope(found + bias),
                [up_bias_ref.at[:, span]],
            )
            if number == 0 and depth > 2:
                lines[1].step(2)
        turn_step(3)
        core_step(3)
        turn_step(2)
        core_step(2)
        for k in range(3, depth):
            lines[1].step(k)
        lines[1].keep.wait()
        stage_keep.wait()
        arrive(both.at[there], single.at[5])
        for number in range(len(numbers)):
            arrive(numbers_out[number], number_sems.at[1, number])
        late_keep.wait()
        for copy in pending:
            copy.wait_send()
        for run in lines:
            run.end()

    out_shape = [
        jax.ShapeDtypeStruct((8, groups * shard), f32),
        *[jax.ShapeDtypeStruct(v.shape, v.dtype) for v in numbers],
        jax.ShapeDtypeStruct((length, model), bf16),
        jax.ShapeDtypeStruct((length, early_width), bf16),
        jax.ShapeDtypeStruct((own_len, model - early_width), bf16),
    ]
    out_shape += [
        jax.ShapeDtypeStruct(v.shape[:-2] + (groups * v.shape[-2], v.shape[-1]), v.dtype)
        for v in weights
    ]
    out_shape += [
        jax.ShapeDtypeStruct((2, kinds, count, length), bf16),
        jax.ShapeDtypeStruct((length, hidden), bf16),
        jax.ShapeDtypeStruct((length, hidden), bf16),
        jax.ShapeDtypeStruct((kinds, local, length), bf16),
    ]
    results = pl.pallas_call(
        kernel,
        out_shape=tuple(out_shape),
        in_specs=[VMEM] * (4 + len(vectors) + len(numbers) + weight_count),
        out_specs=(VMEM,) * (1 + len(numbers)) + (ANY,) * (len(out_shape) - 1 - len(numbers)),
        scratch_shapes=[
            pltpu.VMEM((groups, 8, shard), f32),
            pltpu.VMEM((own_len, model), bf16),
            pltpu.VMEM((kinds, count, length), bf16),
            pltpu.VMEM((8, shard), f32),
            pltpu.VMEM((local, kinds), f32),
            pltpu.VMEM((1, hidden), f32),
            pltpu.VMEM((half_rot, length), f32),
            pltpu.VMEM((half_rot, length), f32),
            DMA((groups - 1,)),
            DMA((groups - 1,)),
            DMA((2, len(numbers))),
            DMA((9,)),
            DMA((2, 2, depth - 1)),
            DMA((2, 2, depth - 1)),
            DMA((weight_count,)),
            DMA((weight_count, chips)),
            DMA((weight_count, chips)),
            DMA((weight_count, 2, chips)),
            DMA((weight_count, 2, chips)),
            DMA((weight_count, 2 * chips)),
            DMA((weight_count, 2 * chips)),
        ],
        compiler_params=pltpu.CompilerParams(
            collective_id=0, has_side_effects=True, vmem_limit_bytes=60 << 20
        ),
        cost_estimate=pl.CostEstimate(flops=0, bytes_accessed=480_000_000, transcendentals=0),
        name="front",
    )(tokens, cotangent, *vectors, *numbers, *weights, projection_bias, up_bias)
    return results[:-1]


class Held:
    def __init__(self, sources, buffers, sems):
        self.copies = {}
        self.buffers = buffers
        for number, (source, buffer) in enumerate(zip(sources, buffers)):
            copy = pltpu.make_async_copy(source, buffer, sems.at[number])
            copy.start()
            self.copies[number] = copy

    def __getitem__(self, number):
        if number in self.copies:
            self.copies.pop(number).wait()
        return self.buffers[number]


def buffers_for(*arrays):
    return [pltpu.VMEM(v.shape, v.dtype) for v in arrays]


def exchange_middle(
    sizes, attended, activation, down_full, dense_full, cotangent_early, cotangent_late, slope
):
    width, total = attended.shape
    length = total // 2
    rows, model = activation.shape[0], down_full.shape[0]
    hidden = slope.shape[1]
    depth = sizes["tp"]
    late_width = cotangent_late.shape[1]
    holds = [activation, down_full, dense_full, cotangent_early, slope]

    def kernel(attended_ref, cotangent_ref, *refs):
        held_refs, refs = refs[: len(holds)], refs[len(holds) :]
        full_out, block_out, late_out, both, grad_hidden, hidden_sum = refs[:6]
        full, feed, late, made, *buffers, sems, held_sems, line_send, line_recv = refs[6:]
        place = Place(sizes)
        here, there = place.half, 1 - place.half

        def tokens(half):
            return attended_ref.at[:, pl.ds(pl.multiple_of(half * length, length), length)]

        mine = half_rows(full, here, width)
        load = pltpu.make_async_copy(tokens(here), mine, sems.at[0])
        load.start()
        held = Held(held_refs, buffers, held_sems)
        greet_line(place, [place.across()])
        line = Line(place, cotangent_ref, late, line_send, line_recv, sems.at[1])
        line.start()
        away = send(tokens(there), mine, sems.at[2], sems.at[3], place.across())
        away.start()
        half = model // 2
        for number in range(2):
            part = pl.ds(number * half, half)
            multiply("nt", [(held[0], held[1].at[part])], [feed.at[:, part]])
            if depth > number + 1:
                line.step(number + 1)
        load.wait()
        away.wait_send()
        came = half_rows(full, there, width)
        send(came, came, sems.at[2], sems.at[3], place.across()).wait_recv()
        full_keep = pltpu.make_async_copy(full, full_out, sems.at[4])
        full_keep.start()
        multiply(
            "tt",
            [(full, held[2])],
            [block_out],
            lambda found, before: (found + before,),
            [feed],
        )
        for k in range(3, depth):
            line.step(k)
        line.keep.wait()
        late_keep = pltpu.make_async_copy(late, late_out, sems.at[5])
        late_keep.start()

        def parts(weight):
            first = model - late_width
            return [
                (held[3], weight.at[pl.ds(0, first)]),
                (late, weight.at[pl.ds(first, late_width)]),
            ]

        multiply("tt", [(b, a) for a, b in parts(held[2])], [made])
        away = send(
            half_rows(made, there, width), both.at[here], sems.at[6], sems.at[7], place.across()
        )
        keep = pltpu.make_async_copy(half_rows(made, here, width), both.at[here], sems.at[8])
        away.start()
        keep.start()

        def scaled(found, slope):
            found = found * slope.astype(f32)
            return found, jnp.sum(found, axis=0, keepdims=True)

        multiply("nn", parts(held[1]), [grad_hidden, hidden_sum], scaled, [held[4]])
        for copy in (keep, full_keep, late_keep):
            copy.wait()
        away.wait_send()
        came = both.at[there]
        send(came, came, sems.at[6], sems.at[7], place.across()).wait_recv()
        line.end()

    return pl.pallas_call(
        kernel,
        out_shape=(
            jax.ShapeDtypeStruct((2 * width, length), bf16),
            jax.ShapeDtypeStruct((rows, model), bf16),
            jax.ShapeDtypeStruct((rows, late_width), bf16),
            jax.ShapeDtypeStruct((2, width, length), bf16),
            jax.ShapeDtypeStruct((rows, hidden), bf16),
            jax.ShapeDtypeStruct((1, hidden), f32),
        ),
        in_specs=[ANY] * (2 + len(holds)),
        out_specs=(ANY,) * 5 + (VMEM,),
        scratch_shapes=[
            pltpu.VMEM((2 * width, length), bf16),
            pltpu.VMEM((rows, model), f32),
            pltpu.VMEM((rows, late_width), bf16),
            pltpu.VMEM((2 * width, length), bf16),
            *buffers_for(*holds),
            DMA((9,)),
            DMA((len(holds),)),
            DMA((2, depth - 1)),
            DMA((2, depth - 1)),
        ],
        compiler_params=pltpu.CompilerParams(
            collective_id=4, has_side_effects=True, vmem_limit_bytes=60 << 20
        ),
        cost_estimate=pl.CostEstimate(flops=0, bytes_accessed=140_000_000, transcendentals=0),
        name="exchange_middle",
    )(attended, cotangent_late, *holds)


def exchange_back(sizes, back, normed, grad_hidden, cotangents, activation, up_full, projection):
    kinds, width, total = back.shape
    length = total // 2
    chips, halves = sizes["fsdp"] // 2, sizes["ctx"]
    rows, model = normed.shape
    hidden = grad_hidden.shape[1]
    span = model // (2 * chips)
    shard = span // halves
    sides = (shard // 4, shard // 2)
    count = len(cotangents)

    def kernel(back_ref, *rest):
        held_refs, rest = rest[: 4 + count], rest[4 + count :]
        weight_ref, full_out, made, came, turns, block_in, feed = (
            rest[0],
            rest[1],
            rest[2:4],
            rest[4:6],
            rest[6:10],
            rest[10],
            rest[11],
        )
        full, diagonal, stage = rest[12:15]
        buffers = rest[15 : 19 + count]
        held_sems, sems, stage_sems, core_send, core_recv, turn_send, turn_recv = rest[19 + count :]
        held = Held(held_refs, buffers, held_sems)
        place = Place(sizes)
        here, there = place.half, 1 - place.half
        other = 1 - place.core

        def tokens(half):
            return back_ref.at[:, :, pl.ds(pl.multiple_of(half * length, length), length)]

        def heads(half):
            return full.at[:, pl.ds(pl.multiple_of(half * width, width), width)]

        load = pltpu.make_async_copy(tokens(here), heads(here), sems.at[2])
        load.start()
        greet(plane(place))
        away = send(tokens(there), heads(here), sems.at[0], sems.at[1], place.across())
        away.start()

        def to_pair(number):
            copies = []
            for chip in range(chips):
                copies.append(
                    send(
                        made[number].at[pl.ds(pl.multiple_of((2 * chip + other) * span, 16), span)],
                        came[number].at[pl.ds(chip * span, span)],
                        core_send.at[number, chip],
                        core_recv.at[number, chip],
                        place.pair(),
                    )
                )
                copies[-1].start()
            return copies

        def turn(number, copies):
            for copy in copies:
                copy.wait()
            sent = []
            for k in range(1, chips):
                chip = place.ahead(k)
                mine = (place.block(chip, place.core, there)) * shard
                theirs = (chip * halves + there) * shard
                loads = (
                    pltpu.make_async_copy(
                        made[number].at[pl.ds(pl.multiple_of(mine, 16), shard)],
                        stage.at[0],
                        stage_sems.at[0],
                    ),
                    pltpu.make_async_copy(
                        came[number].at[pl.ds(pl.multiple_of(theirs, 16), shard)],
                        stage.at[1],
                        stage_sems.at[1],
                    ),
                )
                for copy in loads:
                    copy.start()
                for copy in loads:
                    copy.wait()

                @pl.loop(0, shard, step=16)
                def _(r):
                    at = pl.ds(pl.multiple_of(r, 16), 16)
                    diagonal[number, k - 1, at, :] = (
                        stage[0, at, :].astype(f32) + stage[1, at, :].astype(f32)
                    ).astype(bf16)

                for way, device in enumerate((place.across(), place.device(chip=chip))):
                    side = sides[number]
                    part = pl.ds(0, side) if way == 0 else pl.ds(side, shard - side)
                    sent.append(
                        send(
                            diagonal.at[number, k - 1, part],
                            turns[2 * number + way].at[k - 1],
                            turn_send.at[number, way, k],
                            turn_recv.at[number, way, k],
                            device,
                        )
                    )
                    sent[-1].start()
            return sent

        multiply("tn", [(held[0], held[1])], [made[0]])
        up_copies = to_pair(0)
        first = 0
        for number in range(count):
            ref = held[2 + number]
            part = pl.ds(first, ref.shape[1])
            multiply("tn", [(ref, held[2 + count])], [made[1].at[part]])
            first += ref.shape[1]
            if number == 0:
                turned = turn(0, up_copies)
        down_copies = to_pair(1)
        half = model // 2
        for number in range(2):
            part = pl.ds(number * half, half)
            multiply("nt", [(held[1], held[3 + count].at[part])], [feed.at[:, part]])
            if number == 0:
                turned += turn(1, down_copies)
        load.wait()
        away.wait_send()
        send(heads(there), heads(there), sems.at[0], sems.at[1], place.across()).wait_recv()
        keep = pltpu.make_async_copy(full, full_out, sems.at[3])
        keep.start()

        def step(right_ref, before_ref, out_ref):
            found = before_ref[...]
            for kind in range(kinds):
                found += lax.dot_general(
                    full[kind], right_ref[kind], row_by_col, preferred_element_type=f32
                )
            out_ref[...] = found.astype(bf16)

        tile = min(512, model)
        pltpu.emit_pipeline(
            step,
            grid=(model // tile,),
            in_specs=[
                pl.BlockSpec((kinds, tile, 2 * width), lambda n: (0, n, 0)),
                pl.BlockSpec((rows, tile), lambda n: (0, n)),
            ],
            out_specs=[pl.BlockSpec((rows, tile), lambda n: (0, n))],
        )(weight_ref, feed, block_in)
        keep.wait()
        for copy in turned:
            copy.wait()

    product = jax.ShapeDtypeStruct((model, hidden), bf16)
    part = jax.ShapeDtypeStruct((model // 2, hidden), bf16)
    holds = [normed, grad_hidden, *cotangents, activation, up_full]
    results = pl.pallas_call(
        kernel,
        out_shape=(
            jax.ShapeDtypeStruct((kinds, 2 * width, length), bf16),
            product,
            product,
            part,
            part,
            *[
                jax.ShapeDtypeStruct((chips - 1, n, hidden), bf16)
                for side in sides
                for n in (side, shard - side)
            ],
            jax.ShapeDtypeStruct((rows, model), bf16),
            jax.ShapeDtypeStruct((rows, model), f32),
        ),
        in_specs=[ANY] * (len(holds) + 2),
        out_specs=(ANY,) * 11,
        scratch_shapes=[
            pltpu.VMEM((kinds, 2 * width, length), bf16),
            pltpu.VMEM((2, chips - 1, shard, hidden), bf16),
            pltpu.VMEM((2, shard, hidden), bf16),
            *buffers_for(*holds),
            DMA((len(holds),)),
            DMA((4,)),
            DMA((2,)),
            DMA((2, chips)),
            DMA((2, chips)),
            DMA((2, 2, chips)),
            DMA((2, 2, chips)),
        ],
        compiler_params=pltpu.CompilerParams(
            collective_id=5, has_side_effects=True, vmem_limit_bytes=60 << 20
        ),
        cost_estimate=pl.CostEstimate(flops=0, bytes_accessed=180_000_000, transcendentals=0),
        name="exchange_back",
    )(back, *holds, projection)
    full, up_made, down_made, up_came, down_came, *turned = results[:9]
    return full, [(up_made, up_came), (down_made, down_came)], turned, results[9]


def finish_all(sizes, grad, tokens, cotangent, vectors, partials, splits):
    chips, halves, depth = sizes["fsdp"] // 2, sizes["ctx"], sizes["tp"]
    groups = sizes["fsdp"] * halves
    own_len, model = tokens.shape
    shard = model // groups
    count = len(partials)
    step_rows = 64

    def kernel(grad_ref, tokens_ref, cotangent_ref, vector_ref, *refs):
        partial_in, refs = refs[:count], refs[count:]
        input_ref, small_ref = refs[:2]
        weight_out, refs = refs[2 : 2 + count], refs[2 + count :]
        near, refs = refs[:count], refs[count:]
        sums, blocks, landed, line, near_send, near_recv, load_sem, *sems = refs
        block_send, block_recv, line_send, line_recv = sems
        place = Place(sizes)
        peers = place.group()
        layers = [(place.layer + k) % depth for k in range(1, depth)]
        devices = [place.device(chip=a, core=b, half=c) for a, b, c in peers]
        greet(devices + [place.device(layer=k) for k in layers])
        pending = []
        for a in range(count):
            targets = [place.across()] + [
                place.device(chip=place.ahead(k)) for k in range(1, chips)
            ]
            for at, device in enumerate(targets):
                pending.append(
                    send(
                        partial_in[a].at[at],
                        near[a].at[at],
                        near_send.at[a, at],
                        near_recv.at[a, at],
                        device,
                    )
                )
                pending[-1].start()
            pltpu.make_async_copy(
                partial_in[a].at[chips], near[a].at[chips], load_sem.at[a]
            ).start()

        gain = vector_ref[0:1, :]
        sums[...] = jnp.zeros_like(sums)

        @pl.loop(0, own_len, step=step_rows)
        def _(r):
            at = pl.ds(pl.multiple_of(r, step_rows), step_rows)
            values = tokens_ref[at, :].astype(f32)
            centered = values - jnp.mean(values, axis=-1, keepdims=True)
            spread = jnp.mean(centered * centered, axis=-1, keepdims=True)
            scale = lax.rsqrt(spread + epsilon)
            normal = centered * scale
            found = grad_ref[at, :].astype(f32)
            away = cotangent_ref[at, :].astype(f32)
            inner = found * gain
            mean = jnp.mean(inner, axis=-1, keepdims=True)
            along = jnp.mean(inner * normal, axis=-1, keepdims=True)
            input_ref[at, :] = (scale * (inner - mean - normal * along)).astype(bf16)
            sums[0:1, :] += jnp.sum(found * normal, axis=0, keepdims=True)
            sums[1:2, :] += jnp.sum(found, axis=0, keepdims=True)
            sums[2:3, :] += jnp.sum(away, axis=0, keepdims=True)

        for number in range(groups):
            blocks[number] = sums[:, number * shard : (number + 1) * shard]
        copies = []
        for at, (chip, core, half) in enumerate(peers):
            copies.append(
                send(
                    blocks.at[place.block(chip, core, half)],
                    landed.at[at],
                    block_send.at[at],
                    block_recv.at[at],
                    devices[at],
                )
            )
            copies[-1].start()
        total = blocks[place.block()]
        for at, copy in enumerate(copies):
            copy.wait()
            total += landed[at]
        line[0] = total
        copies = []
        for k, layer in enumerate(layers):
            copies.append(
                send(
                    line.at[0],
                    line.at[k + 1],
                    line_send.at[k],
                    line_recv.at[k],
                    place.device(layer=layer),
                )
            )
            copies[-1].start()
        for k, copy in enumerate(copies):
            copy.wait()
            total += line[k + 1]
        small_ref[...] = total

        for copy in pending:
            copy.wait()
        for a in range(count):
            own = near[a].at[chips]
            pltpu.make_async_copy(own, own, load_sem.at[a]).wait()
            rows, width = partials[a].shape[1:]

            @pl.loop(0, rows, step=16)
            def _(r, a=a, width=width):
                at = pl.ds(pl.multiple_of(r, 16), 16)
                found = near[a][0, at, :].astype(f32)
                for number in range(1, chips + 1):
                    found += near[a][number, at, :].astype(f32)
                if splits[a] == 1:
                    weight_out[a][at, :] = found
                else:
                    wide = width // splits[a]
                    for kind in range(splits[a]):
                        weight_out[a][kind, at, :] = found[:, kind * wide : (kind + 1) * wide]

    out_shape = [
        jax.ShapeDtypeStruct((own_len, model), bf16),
        jax.ShapeDtypeStruct((8, shard), f32),
    ]
    for v, n in zip(partials, splits):
        rows, width = v.shape[1:]
        out_shape.append(
            jax.ShapeDtypeStruct((rows, width) if n == 1 else (n, rows, width // n), f32)
        )
    return pl.pallas_call(
        kernel,
        out_shape=tuple(out_shape),
        in_specs=[VMEM] * 4 + [ANY] * count,
        out_specs=(VMEM,) * len(out_shape),
        scratch_shapes=[
            *buffers_for(*partials),
            pltpu.VMEM((8, model), f32),
            pltpu.VMEM((groups, 8, shard), f32),
            pltpu.VMEM((groups - 1, 8, shard), f32),
            pltpu.VMEM((depth, 8, shard), f32),
            DMA((count, chips)),
            DMA((count, chips)),
            DMA((count,)),
            DMA((groups - 1,)),
            DMA((groups - 1,)),
            DMA((depth - 1,)),
            DMA((depth - 1,)),
        ],
        compiler_params=pltpu.CompilerParams(
            collective_id=3, has_side_effects=True, vmem_limit_bytes=60 << 20
        ),
        cost_estimate=pl.CostEstimate(flops=0, bytes_accessed=90_000_000, transcendentals=0),
        name="finish_all",
    )(grad, tokens, cotangent, vectors, *partials)


def tile_at(number):
    return pl.ds(pl.multiple_of(number * TILE, TILE), TILE)


def allowed(kb, j, start):
    places = kb * TILE + lax.broadcasted_iota(jnp.int32, (TILE, TILE), 0)
    own = j * TILE + lax.broadcasted_iota(jnp.int32, (TILE, TILE), 1)
    return (places >= start) & (places <= own)


def attend_kernel(
    low_ref,
    mid_ref,
    triple_ref,
    start_ref,
    attended_ref,
    log_ref,
    query_t,
    key_t,
    value_t,
    key_rows,
    scores,
):
    length = triple_ref.shape[3]
    heads = triple_ref.shape[2] // HD
    score_scale = 1.0 / math.sqrt(HD)
    for number, ref in enumerate((query_t, key_t, value_t)):
        for part in range(2):
            piece = triple_ref[part, number]
            ref[:, part * length : (part + 1) * length] = (
                piece * score_scale if number == 0 else piece
            )
    rows = [slice(h * HD, (h + 1) * HD) for h in range(heads)]
    for h in range(heads):
        key_rows[h] = key_t[rows[h], :].T

    @pl.loop(0, 2 * length // TILE)
    def _(j):
        here = tile_at(j)
        start = start_ref[:, here]
        low, mid = low_ref[j], mid_ref[j]
        queries = [query_t[row, here] for row in rows]

        def score_with(masked):
            def score(kb, highest):
                ok = allowed(kb, j, start) if masked else None
                raised = []
                for h in range(heads):
                    found = jnp.dot(
                        key_rows[h, tile_at(kb), :], queries[h], preferred_element_type=f32
                    )
                    if masked:
                        found = jnp.where(ok, found, big_negative)
                    scores[h, tile_at(kb), :] = found
                    raised.append(
                        jnp.maximum(highest[h], jnp.max(found, axis=0, keepdims=True))
                    )
                return tuple(raised)

            return score

        highest = tuple(jnp.full((1, TILE), big_negative, f32) for _ in range(heads))
        highest = lax.fori_loop(low, mid, score_with(True), highest)
        highest = lax.fori_loop(mid, j, score_with(False), highest)
        highest = score_with(True)(j, highest)

        def weigh(kb, carry):
            after = []
            for h in range(heads):
                total, mixed = carry[h]
                prob = jnp.exp(scores[h, tile_at(kb), :] - highest[h])
                total = total + jnp.sum(prob, axis=0, keepdims=True)
                mixed = mixed + jnp.dot(
                    value_t[rows[h], tile_at(kb)], prob.astype(bf16), preferred_element_type=f32
                )
                after.append((total, mixed))
            return tuple(after)

        empty = tuple(
            (jnp.zeros((1, TILE), f32), jnp.zeros((HD, TILE), f32)) for _ in range(heads)
        )
        result = lax.fori_loop(low, j + 1, weigh, empty)
        for h in range(heads):
            total, mixed = result[h]
            attended_ref[rows[h], here] = (mixed / total).astype(bf16)
            log_ref[h, :, here] = highest[h] + jnp.log(total)


def turned_back(values, cosine, sine):
    half_rot = ROT // 2
    leading = values[:half_rot]
    trailing = values[half_rot:ROT]
    return jnp.concatenate(
        [
            leading * cosine + trailing * sine,
            trailing * cosine - leading * sine,
            values[ROT:],
        ],
        axis=0,
    )


def attend_back_kernel(
    low_ref,
    mid_ref,
    triple_ref,
    grad_ref,
    attended_ref,
    log_ref,
    start_ref,
    cosine_ref,
    sine_ref,
    back_ref,
    query_t,
    key_t,
    grad_t,
    key_rows,
    value_rows,
    key_sum,
    value_sum,
):
    length = triple_ref.shape[3]
    heads = triple_ref.shape[2] // HD
    score_scale = 1.0 / math.sqrt(HD)
    rows = [slice(h * HD, (h + 1) * HD) for h in range(heads)]
    for part in range(2):
        span = slice(part * length, (part + 1) * length)
        query_t[:, span] = triple_ref[part, 0] * score_scale
        key_t[:, span] = triple_ref[part, 1]
        grad_t[:, span] = grad_ref[part]
        for h in range(heads):
            value_rows[h, span, :] = triple_ref[part, 2, rows[h]].T
    for h in range(heads):
        key_rows[h] = key_t[rows[h], :].T
    key_sum[...] = jnp.zeros_like(key_sum)
    value_sum[...] = jnp.zeros_like(value_sum)

    @pl.loop(0, 2 * length // TILE)
    def _(j):
        here = tile_at(j)
        start = start_ref[:, here]
        low, mid = low_ref[j], mid_ref[j]
        queries = [query_t[row, here] for row in rows]
        grads = [grad_t[row, here] for row in rows]
        query_rows = [value.T for value in queries]
        grad_rows = [value.T for value in grads]
        logs = [log_ref[h, :, here] for h in range(heads)]
        deltas = [
            jnp.sum(
                grads[h].astype(f32) * attended_ref[rows[h], here].astype(f32),
                axis=0,
                keepdims=True,
            )
            for h in range(heads)
        ]

        def pull_with(masked):
            def pull(kb, query_back):
                ok = allowed(kb, j, start) if masked else None
                after = []
                for h in range(heads):
                    score = jnp.dot(
                        key_rows[h, tile_at(kb), :], queries[h], preferred_element_type=f32
                    )
                    if masked:
                        score = jnp.where(ok, score, big_negative)
                    prob = jnp.exp(score - logs[h])
                    down = jnp.dot(
                        value_rows[h, tile_at(kb), :], grads[h], preferred_element_type=f32
                    )
                    score_back = (prob * (down - deltas[h])).astype(bf16)
                    value_sum[h, tile_at(kb), :] += jnp.dot(
                        prob.astype(bf16), grad_rows[h], preferred_element_type=f32
                    )
                    key_sum[h, tile_at(kb), :] += jnp.dot(
                        score_back, query_rows[h], preferred_element_type=f32
                    )
                    after.append(
                        query_back[h]
                        + jnp.dot(
                            key_t[rows[h], tile_at(kb)], score_back, preferred_element_type=f32
                        )
                    )
                return tuple(after)

            return pull

        query_back = tuple(jnp.zeros((HD, TILE), f32) for _ in range(heads))
        query_back = lax.fori_loop(low, mid, pull_with(True), query_back)
        query_back = lax.fori_loop(mid, j, pull_with(False), query_back)
        query_back = pull_with(True)(j, query_back)
        for h in range(heads):
            back_ref[0, rows[h], here] = turned_back(
                query_back[h] * score_scale, cosine_ref[:, here], sine_ref[:, here]
            ).astype(bf16)

    for h in range(heads):
        back_ref[1, rows[h], :] = turned_back(
            key_sum[h].T, cosine_ref[...], sine_ref[...]
        ).astype(bf16)
        back_ref[2, rows[h], :] = value_sum[h].T.astype(bf16)


def attend(low, mid, triple, start):
    width, length = triple.shape[2], triple.shape[3]
    total, heads = 2 * length, width // HD
    area = total * total // 3 * heads
    return pl.pallas_call(
        attend_kernel,
        out_shape=(
            jax.ShapeDtypeStruct((width, total), bf16),
            jax.ShapeDtypeStruct((heads, 1, total), f32),
        ),
        in_specs=[SMEM, SMEM, VMEM, VMEM],
        out_specs=(VMEM, VMEM),
        scratch_shapes=[pltpu.VMEM((width, total), bf16)] * 3
        + [pltpu.VMEM((heads, total, HD), bf16), pltpu.VMEM((heads, total, TILE), f32)],
        compiler_params=pltpu.CompilerParams(vmem_limit_bytes=48 << 20),
        cost_estimate=pl.CostEstimate(
            flops=50 * area * HD, bytes_accessed=8 * width * total, transcendentals=area
        ),
        name="attend",
    )(low, mid, triple, start)


def attend_back(low, mid, triple, grad, attended, log_sum, start, cosine, sine):
    width, length = triple.shape[2], triple.shape[3]
    total, heads = 2 * length, width // HD
    area = total * total // 3 * heads
    return pl.pallas_call(
        attend_back_kernel,
        out_shape=jax.ShapeDtypeStruct((3, width, total), bf16),
        in_specs=[SMEM, SMEM] + [VMEM] * 7,
        out_specs=VMEM,
        scratch_shapes=[pltpu.VMEM((width, total), bf16)] * 3
        + [pltpu.VMEM((heads, total, HD), bf16)] * 2
        + [pltpu.VMEM((heads, total, HD), f32)] * 2,
        compiler_params=pltpu.CompilerParams(vmem_limit_bytes=48 << 20),
        cost_estimate=pl.CostEstimate(
            flops=100 * area * HD, bytes_accessed=12 * width * total, transcendentals=area
        ),
        name="attend_back",
    )(low, mid, triple, grad, attended, log_sum, start, cosine, sine)


def rotate_rows(values, cosine, sine):
    half_rot = ROT // 2
    leading = values[:, :half_rot]
    trailing = values[:, half_rot:ROT]
    return jnp.concatenate(
        [
            leading * cosine - trailing * sine,
            trailing * cosine + leading * sine,
            values[:, ROT:],
        ],
        axis=1,
    )


def ordered(*values):
    return lax.optimization_barrier(values)


def body(
    sizes,
    tokens,
    segments,
    positions,
    norm_gain,
    norm_bias,
    projection_weight,
    projection_bias,
    dense_weight,
    dense_bias,
    up_weight,
    up_bias,
    down_weight,
    down_bias,
    cotangent,
):
    own_len, model_width = tokens.shape[1], tokens.shape[2]
    half_len = segments.shape[1]
    local_width = projection_weight.shape[2]
    hidden_width = up_weight.shape[1]
    shard_rows = norm_gain.shape[0]
    half = lax.axis_index("ctx")
    total_len = 2 * half_len

    numbers = [segments, positions]
    (
        vectors_full,
        segments_other,
        positions_other,
        normed,
        cotangent_early,
        cotangent_late,
        projection,
        up_full,
        dense_full,
        down_full,
        both,
        activation,
        slope,
    ) = front(
        sizes,
        tokens[0],
        cotangent[0],
        [norm_gain, norm_bias, dense_bias, down_bias],
        numbers,
        [projection_weight.transpose(1, 0, 2), up_weight, dense_weight, down_weight],
        projection_bias,
        up_bias,
    )

    def in_order(own, other, axis):
        return jnp.where(
            half == 0,
            jnp.concatenate([own, other], axis=axis),
            jnp.concatenate([other, own], axis=axis),
        )

    segment_row = in_order(segments[0], segments_other[0], 0)
    position_row = in_order(positions[0], positions_other[0], 0)
    places = jnp.arange(total_len, dtype=jnp.int32)
    edges = jnp.concatenate([jnp.ones((1,), bool), segment_row[1:] != segment_row[:-1]])
    start = lax.cummax(jnp.where(edges, places, 0))
    tile_count = total_len // TILE
    low = start[::TILE] // TILE
    mid = jnp.minimum(
        jnp.maximum((start[TILE - 1 :: TILE] + TILE - 1) // TILE, low),
        jnp.arange(tile_count, dtype=jnp.int32),
    )
    exponent = jnp.arange(ROT // 2, dtype=f32) * 2.0 / ROT
    phase_angle = (10000.0 ** (-exponent))[:, None] * position_row.astype(f32)[None, :]
    cosine_full, sine_full = jnp.cos(phase_angle), jnp.sin(phase_angle)
    attended_heads, log_sum = attend(low, mid, both, start[None, :])
    attended, block_out, cotangent_late, grad_both, grad_hidden, hidden_sum = exchange_middle(
        sizes,
        attended_heads,
        activation,
        down_full,
        dense_full,
        cotangent_early,
        cotangent_late,
        slope,
    )
    cotangents = [cotangent_early, cotangent_late]
    branch_own = lax.psum_scatter(block_out, "tp", scatter_dimension=0, tiled=True)
    back_heads = attend_back(
        low,
        mid,
        both,
        grad_both,
        attended_heads,
        log_sum,
        start[None, :],
        cosine_full,
        sine_full,
    )
    grad_projected, paired, turned, block_in = exchange_back(
        sizes, back_heads, normed, grad_hidden, cotangents, activation, up_full, projection
    )
    grad_projected = grad_projected.reshape(3 * local_width, half_len)
    block_in, branch_own = ordered(block_in, branch_own)
    grad_normed_own = lax.psum_scatter(block_in, "tp", scatter_dimension=0, tiled=True)
    projected_sum = jnp.sum(grad_projected.astype(f32), axis=1)
    small = jnp.concatenate([projected_sum, hidden_sum[0]]).reshape(-1, 128)
    *pieces, small_total, partial = reduce(
        sizes,
        paired,
        turned,
        [(cotangents, attended), ([normed], grad_projected)],
        small,
        2,
        "reduce_weights",
    )
    up_part, down_part, dense_part = (jnp.sum(v.astype(f32), axis=0) for v in pieces)
    up_part, down_part, dense_part, grad_normed_own = ordered(
        up_part, down_part, dense_part, grad_normed_own
    )
    input_part, totals, projection_part = finish_all(
        sizes,
        grad_normed_own,
        tokens[0],
        cotangent[0],
        vectors_full,
        [partial],
        [3],
    )
    bias_dense, bias_down = vectors_full[2], vectors_full[3]
    layer_output = (
        tokens[0].astype(f32) + branch_own.astype(f32) + (bias_dense + bias_down)
    ).astype(bf16)
    input_grad = cotangent[0].astype(f32) + input_part.astype(f32)
    small_flat = small_total.reshape(-1)
    return (
        layer_output[None],
        input_grad[None],
        totals[0],
        totals[1],
        projection_part.transpose(1, 0, 2),
        small_flat[: 3 * local_width].reshape(3, local_width),
        dense_part,
        totals[2],
        up_part,
        small_flat[3 * local_width :],
        down_part,
        totals[2],
    )


def solution(mesh):
    placed = (
        P("fsdp", ("ctx", "tp"), None),
        P("fsdp", "ctx"),
        P("fsdp", "ctx"),
        P(("fsdp", "ctx")),
        P(("fsdp", "ctx")),
        P(("fsdp", "ctx"), None, "tp"),
        P(None, "tp"),
        P(("fsdp", "ctx"), "tp"),
        P(("fsdp", "ctx")),
        P(("fsdp", "ctx"), "tp"),
        P("tp"),
        P(("fsdp", "ctx"), "tp"),
        P(("fsdp", "ctx")),
        P("fsdp", ("ctx", "tp"), None),
    )
    return jax.shard_map(
        functools.partial(body, dict(mesh.shape)),
        mesh=mesh,
        in_specs=placed,
        out_specs=(
            P("fsdp", ("ctx", "tp"), None),
            P("fsdp", ("ctx", "tp"), None),
            P(("fsdp", "ctx")),
            P(("fsdp", "ctx")),
            P(("fsdp", "ctx"), None, "tp"),
            P(None, "tp"),
            P(("fsdp", "ctx"), "tp"),
            P(("fsdp", "ctx")),
            P(("fsdp", "ctx"), "tp"),
            P("tp"),
            P(("fsdp", "ctx"), "tp"),
            P(("fsdp", "ctx")),
        ),
        check_vma=False,
    )
```

```python
import functools
import math

import jax
import jax.numpy as jnp
from jax import lax
from jax.experimental import pallas as pl
from jax.experimental.pallas import tpu as pltpu
from jax.sharding import PartitionSpec as P

HD = 64
ROT = 32
TILE = 256

epsilon = 1e-05
big_negative = -1000000000.0
root_two_over_pi = 0.7978845608028654
contract_rows = (((0,), (0,)), ((), ()))
contract_cols = (((1,), (1,)), ((), ()))
row_by_col = (((0,), (1,)), ((), ()))
MESH = pl.DeviceIdType.MESH
ANY = pl.BlockSpec(memory_space=pl.ANY)
VMEM = pl.BlockSpec(memory_space=pltpu.VMEM)
SMEM = pl.BlockSpec(memory_space=pltpu.SMEM)
DMA = pltpu.SemaphoreType.DMA
f32 = jnp.float32
bf16 = jnp.bfloat16


def layer_norm(values, gain_full, shift_full):
    center = jnp.mean(values, axis=-1, keepdims=True)
    centered = values - center
    spread = jnp.mean(centered * centered, axis=-1, keepdims=True)
    return centered * lax.rsqrt(spread + epsilon) * gain_full + shift_full


def gelu_and_slope(values):
    turned = jnp.tanh(root_two_over_pi * (values + 0.044715 * values * values * values))
    slope = 0.5 * (1.0 + turned) + 0.5 * values * (1.0 - turned * turned) * root_two_over_pi * (
        1.0 + 3.0 * 0.044715 * values * values
    )
    return 0.5 * values * (1.0 + turned), slope


class Place:
    def __init__(self, sizes):
        self.chips = sizes["fsdp"] // 2
        self.halves = sizes["ctx"]
        self.depth = sizes["tp"]
        lane = lax.axis_index("fsdp")
        self.chip = lane // 2
        self.core = lane % 2
        self.half = lax.axis_index("ctx")
        self.layer = lax.axis_index("tp")

    def device(self, chip=None, core=None, half=None, layer=None):
        chip = self.chip if chip is None else chip
        core = self.core if core is None else core
        half = self.half if half is None else half
        layer = self.layer if layer is None else layer
        return (chip * 2 + core, half, layer)

    def block(self, chip=None, core=None, half=None):
        chip = self.chip if chip is None else chip
        core = self.core if core is None else core
        half = self.half if half is None else half
        return (chip * 2 + core) * self.halves + half

    def ahead(self, k):
        return (self.chip + k) % self.chips

    def behind(self, k):
        return (self.chip + self.chips - k) % self.chips

    def neighbours(self):
        last = self.depth - 1
        return (
            (self.layer < last, self.device(layer=jnp.minimum(self.layer + 1, last))),
            (self.layer > 0, self.device(layer=jnp.maximum(self.layer - 1, 0))),
        )

    def pair(self):
        return self.device(core=1 - self.core)

    def across(self):
        return self.device(half=1 - self.half)

    def group(self):
        found = []
        for k in range(self.chips):
            for core in range(2):
                for half in range(2):
                    if k or core or half:
                        found.append(
                            (self.ahead(k), (self.core + core) % 2, (self.half + half) % 2)
                        )
        return found


def greet(devices):
    barrier = pltpu.get_barrier_semaphore()
    for device in devices:
        pl.semaphore_signal(barrier, inc=1, device_id=device, device_id_type=MESH)
    pl.semaphore_wait(barrier, len(devices))


def greet_line(place, devices):
    barrier = pltpu.get_barrier_semaphore()
    for device in devices:
        pl.semaphore_signal(barrier, inc=1, device_id=device, device_id_type=MESH)
    count = len(devices)
    for there, device in place.neighbours():

        @pl.when(there)
        def _(device=device):
            pl.semaphore_signal(barrier, inc=1, device_id=device, device_id_type=MESH)

        count = count + there.astype(jnp.int32)
    pl.semaphore_wait(barrier, count)


def send(source, target, send_sem, recv_sem, device):
    return pltpu.make_async_remote_copy(
        src_ref=source,
        dst_ref=target,
        send_sem=send_sem,
        recv_sem=recv_sem,
        device_id=device,
        device_id_type=MESH,
    )


class Line:
    def __init__(self, place, own, full, send_sem, recv_sem, keep_sem):
        self.place, self.own, self.full = place, own, full
        self.send_sem, self.recv_sem = send_sem, recv_sem
        self.rows = own.shape[0]
        self.pending = []
        self.keep = pltpu.make_async_copy(own, self.block(place.layer), keep_sem)

    def block(self, source):
        return self.full.at[pl.ds(pl.multiple_of(source * self.rows, 16), self.rows)]

    def copy(self, piece, target, way, hop, device):
        return send(piece, target, self.send_sem.at[way, hop], self.recv_sem.at[way, hop], device)

    def launch(self, copy, condition):
        pl.when(condition)(copy.start)
        self.pending.append((copy, condition))

    def start(self):
        for way, (there, device) in enumerate(self.place.neighbours()):
            target = self.block(self.place.layer)
            self.launch(self.copy(self.own, target, way, 0, device), there)
        self.keep.start()

    def step(self, k):
        last = self.place.depth - 1
        for way, (onward, device) in enumerate(self.place.neighbours()):
            source = self.place.layer - k if way == 0 else self.place.layer + k
            there = (source >= 0) & (source <= last)
            piece = self.block(jnp.clip(source, 0, last))
            pl.when(there)(self.copy(piece, piece, way, k - 1, device).wait_recv)
            if k < last:
                self.launch(self.copy(piece, piece, way, k, device), there & onward)

    def end(self):
        for copy, condition in self.pending:
            pl.when(condition)(copy.wait_send)


def plane(place):
    found = [place.device(chip=place.ahead(k)) for k in range(1, place.chips)]
    return found + [place.across(), place.pair()]


def reduce(sizes, paired, turned, rights, small, collective_id, name):
    chips, halves = sizes["fsdp"] // 2, sizes["ctx"]
    groups = chips * halves
    paired_count, made_count = len(paired), len(rights)
    weight_count = paired_count + made_count
    whole_count = weight_count - 1
    block_rows = paired[0][0].shape[0] // (2 * groups)
    widths = [v.shape[1] for v, _ in paired] + [v.shape[0] for _, v in rights]
    sides = [turned[2 * a].shape[1] for a in range(paired_count)] + [block_rows // 2] * made_count

    def kernel(*refs):
        refs = list(refs)

        def take(count):
            taken = refs[:count]
            del refs[:count]
            return taken

        paired_in = [take(2) for _ in range(paired_count)]
        turned_in = take(2 * paired_count)
        lefts = [take(len(left)) for left, _ in rights]
        factors = take(made_count)
        small_in = take(len(small))
        weight_out = take(whole_count)
        (small_out,) = take(1)
        held_out, made = take(weight_count - whole_count), take(made_count)
        own, turn_a, turn_b = (take(weight_count) for _ in range(3))
        near = take(whole_count)
        pair = take(weight_count)
        load_sem, core_send, core_recv = take(3)
        turn_send, turn_recv, near_send, near_recv = take(4)
        small_ref, small_pair, small_near, small_far, small_send, small_recv = take(6)
        place = Place(sizes)
        greet(plane(place))
        pending = []

        def launch(copy, condition=None):
            if condition is None:
                copy.start()
            else:
                pl.when(condition)(copy.start)
            pending.append((copy, condition))

        other = 1 - place.core
        needed = [place.ahead(k) * halves + place.half for k in range(1, chips)]
        needed += [place.chip * halves + 1 - place.half, place.chip * halves + place.half]
        for a in range(paired_count):
            for at, number in enumerate(needed):
                chip = place.ahead(at + 1) if at < chips - 1 else place.chip
                half = 1 - place.half if at == chips - 1 else place.half
                mine = place.block(chip, place.core, half)
                pltpu.make_async_copy(
                    paired_in[a][0].at[pl.ds(pl.multiple_of(mine * block_rows, 16), block_rows)],
                    own[a].at[number],
                    load_sem.at[a, number],
                ).start()
                pltpu.make_async_copy(
                    paired_in[a][1].at[pl.ds(pl.multiple_of(number * block_rows, 16), block_rows)],
                    pair[a].at[at],
                    core_recv.at[a, number],
                ).start()
            for way, target in enumerate((turn_a[a], turn_b[a])):
                for k in range(1, chips):
                    pltpu.make_async_copy(
                        turned_in[2 * a + way].at[k - 1],
                        target.at[k - 1],
                        turn_recv.at[a, way, k],
                    ).start()

        def make(a):
            at = a - paired_count
            first = 0
            for left in lefts[at]:
                span = pl.ds(first, left.shape[1])
                multiply("tt", [(left, factors[at])], [made[at].at[span]])
                first += left.shape[1]
            for number in range(groups):
                chip, half = number // halves, number % halves
                theirs = place.block(chip, other, half)
                mine = place.block(chip, place.core, half)
                launch(
                    send(
                        made[at].at[pl.ds(pl.multiple_of(theirs * block_rows, 16), block_rows)],
                        pair[a].at[number],
                        core_send.at[a, number],
                        core_recv.at[a, number],
                        place.pair(),
                    )
                )
                pltpu.make_async_copy(
                    made[at].at[pl.ds(pl.multiple_of(mine * block_rows, 16), block_rows)],
                    own[a].at[number],
                    load_sem.at[a, number],
                ).start()

        def pair_sum(a, number, at_needed=None):
            mine = own[a].at[number]
            pltpu.make_async_copy(mine, mine, load_sem.at[a, number]).wait()
            if a < paired_count:
                theirs = pair[a].at[at_needed]
                pltpu.make_async_copy(theirs, theirs, core_recv.at[a, number]).wait()
            else:
                theirs = pair[a].at[number]
                send(
                    theirs, theirs, core_send.at[a, number], core_recv.at[a, number], place.pair()
                ).wait_recv()

            @pl.loop(0, block_rows, step=16)
            def _(r):
                at = pl.ds(pl.multiple_of(r, 16), 16)
                mine[at, :] = (mine[at, :].astype(f32) + theirs[at, :].astype(f32)).astype(bf16)

        def diagonal(a):
            for k in range(1, chips):
                number = place.ahead(k) * halves + 1 - place.half
                pair_sum(a, number)
                launch(
                    send(
                        own[a].at[number, pl.ds(0, sides[a])],
                        turn_a[a].at[k - 1],
                        turn_send.at[a, 0, k],
                        turn_recv.at[a, 0, k],
                        place.across(),
                    )
                )
                launch(
                    send(
                        own[a].at[number, pl.ds(sides[a], block_rows - sides[a])],
                        turn_b[a].at[k - 1],
                        turn_send.at[a, 1, k],
                        turn_recv.at[a, 1, k],
                        place.device(chip=place.ahead(k)),
                    )
                )

        def direct_pairs(a):
            for k in range(1, chips):
                pair_sum(a, place.ahead(k) * halves + place.half, k - 1)
            pair_sum(a, place.chip * halves + 1 - place.half, chips - 1)

        def add_turn(a, number, first, count, refs_at):
            @pl.loop(0, count, step=16)
            def _(r):
                at = pl.ds(pl.multiple_of(first + r, 16), 16)
                total = own[a][number, at, :].astype(f32)
                for ref, k in refs_at:
                    total += ref[k, pl.ds(pl.multiple_of(r, 16), 16), :].astype(f32)
                own[a][number, at, :] = total.astype(bf16)

        def turn_wait(a, way, k):
            piece = (turn_a, turn_b)[way][a].at[k - 1]
            if a < paired_count:
                pltpu.make_async_copy(piece, piece, turn_recv.at[a, way, k]).wait()
            else:
                send(
                    piece, piece, turn_send.at[a, way, k], turn_recv.at[a, way, k], place.across()
                ).wait_recv()

        def hand(a, at, number):
            pltpu.make_async_copy(
                own[a].at[number], held_out[a - whole_count].at[at], near_send.at[a, at]
            ).start()

        def direct(a):
            for k in range(1, chips):
                number = place.ahead(k) * halves + place.half
                turn_wait(a, 0, k)
                add_turn(a, number, 0, sides[a], [(turn_a[a], k - 1)])
                if a >= whole_count:
                    hand(a, k, number)
                    continue
                launch(
                    send(
                        own[a].at[number],
                        near[a].at[k],
                        near_send.at[a, k],
                        near_recv.at[a, k],
                        place.device(chip=place.ahead(k)),
                    )
                )
            for k in range(1, chips):
                turn_wait(a, 1, k)
            number = place.chip * halves + 1 - place.half
            add_turn(
                a,
                number,
                sides[a],
                block_rows - sides[a],
                [(turn_b[a], k - 1) for k in range(1, chips)],
            )
            if a >= whole_count:
                hand(a, 0, number)
                return
            launch(
                send(
                    own[a].at[number],
                    near[a].at[0],
                    near_send.at[a, 0],
                    near_recv.at[a, 0],
                    place.across(),
                )
            )

        def finish(a):
            for k in range(chips):
                piece = near[a].at[k]
                send(
                    piece, piece, near_send.at[a, k], near_recv.at[a, k], place.across()
                ).wait_recv()
            number = place.chip * halves + place.half

            @pl.loop(0, block_rows, step=16)
            def _(r):
                at = pl.ds(pl.multiple_of(r, 16), 16)
                total = own[a][number, at, :].astype(f32)
                for k in range(chips):
                    total += near[a][k, at, :].astype(f32)
                weight_out[a][at, :] = total

        def swap_small(source, target, at, device):
            copy = send(source, target, small_send.at[at], small_recv.at[at], device)
            launch(copy)
            return copy

        small_ref[...] = jnp.zeros_like(small_ref)
        first = 0
        for ref in small_in:
            small_ref[first : first + ref.shape[0], : ref.shape[1]] = ref[...]
            first += ref.shape[0]
        swap_small(small_ref, small_pair, 0, place.pair())
        for a in range(paired_count):
            direct_pairs(a)
            direct(a)
        for a in range(paired_count, weight_count):
            make(a)
        send(small_pair, small_pair, small_send.at[0], small_recv.at[0], place.pair()).wait_recv()
        small_near[0] = small_ref[...] + small_pair[...]
        for k in range(1, chips):
            swap_small(small_near.at[0], small_near.at[k], k, place.device(chip=place.ahead(k)))
        for a in range(paired_count, weight_count):
            diagonal(a)
            direct_pairs(a)
        total = small_near[0]
        for k in range(1, chips):
            piece = small_near.at[k]
            send(piece, piece, small_send.at[k], small_recv.at[k], place.pair()).wait_recv()
            total += small_near[k]
        small_far[0] = total
        swap_small(small_far.at[0], small_far.at[1], chips, place.across())
        for a in range(weight_count):
            pair_sum(a, place.chip * halves + place.half, chips)
        for a in range(paired_count, weight_count):
            direct(a)
            if a >= whole_count:
                hand(a, chips, place.chip * halves + place.half)
        for a in range(whole_count):
            finish(a)
        for a in range(whole_count, weight_count):
            for at in range(chips + 1):
                piece = held_out[a - whole_count].at[at]
                pltpu.make_async_copy(piece, piece, near_send.at[a, at]).wait()
        piece = small_far.at[1]
        send(piece, piece, small_send.at[chips], small_recv.at[chips], place.pair()).wait_recv()
        small_out[...] = small_far[0] + small_far[1]
        for copy, condition in pending:
            if condition is None:
                copy.wait_send()
            else:
                pl.when(condition)(copy.wait_send)

    shapes = [jax.ShapeDtypeStruct((block_rows, w), f32) for w in widths[:whole_count]]
    small_shape = (8, max(v.shape[1] for v in small))
    shapes.append(jax.ShapeDtypeStruct(small_shape, f32))
    held_shapes = [
        jax.ShapeDtypeStruct((chips + 1, block_rows, w), bf16) for w in widths[whole_count:]
    ]
    made_shapes = [
        jax.ShapeDtypeStruct((2 * groups * block_rows, w), bf16) for w in widths[paired_count:]
    ]
    scratch = [pltpu.VMEM((groups, block_rows, w), bf16) for w in widths]
    scratch += [pltpu.VMEM((chips - 1, n, w), bf16) for w, n in zip(widths, sides)]
    scratch += [pltpu.VMEM((chips - 1, block_rows - n, w), bf16) for w, n in zip(widths, sides)]
    scratch += [pltpu.VMEM((chips, block_rows, w), bf16) for w in widths[:whole_count]]
    scratch += [pltpu.VMEM((chips + 1, block_rows, w), bf16) for w in widths[:paired_count]]
    scratch += [pltpu.VMEM((groups, block_rows, w), bf16) for w in widths[paired_count:]]
    scratch += [
        DMA((weight_count, groups)),
        DMA((weight_count, groups)),
        DMA((weight_count, groups)),
        DMA((weight_count, 2, chips)),
        DMA((weight_count, 2, chips)),
        DMA((weight_count, chips + 1)),
        DMA((weight_count, chips + 1)),
        pltpu.VMEM(small_shape, f32),
        pltpu.VMEM(small_shape, f32),
        pltpu.VMEM((chips,) + small_shape, f32),
        pltpu.VMEM((2,) + small_shape, f32),
        DMA((chips + 1,)),
        DMA((chips + 1,)),
    ]
    lefts = [v for left, _ in rights for v in left]
    factors = [v for _, v in rights]
    return pl.pallas_call(
        kernel,
        out_shape=tuple(shapes + held_shapes + made_shapes),
        in_specs=[ANY] * (4 * paired_count + len(lefts) + made_count) + [VMEM] * len(small),
        out_specs=(VMEM,) * (whole_count + 1)
        + (ANY,) * (weight_count - whole_count + made_count),
        scratch_shapes=scratch,
        compiler_params=pltpu.CompilerParams(
            collective_id=collective_id, has_side_effects=True, vmem_limit_bytes=60 << 20
        ),
        cost_estimate=pl.CostEstimate(flops=0, bytes_accessed=400_000_000, transcendentals=0),
        name=name,
    )(*[v for two in paired for v in two], *turned, *lefts, *factors, *small)[: weight_count + 1]


def multiply(kind, parts, outs, finish=None, extra=(), tile=512):
    dims = (((0 if kind[0] == "t" else 1,), (1 if kind[1] == "t" else 0,)), ((), ()))
    left, right = parts[0]
    rows = left.shape[1] if kind[0] == "t" else left.shape[0]
    width = right.shape[0] if kind[1] == "t" else right.shape[1]
    tile = min(tile, width)
    specs = []
    for left, right in parts:
        specs.append(pl.BlockSpec(left.shape, lambda n: (0, 0)))
        if kind[1] == "t":
            specs.append(pl.BlockSpec((tile, right.shape[1]), lambda n: (n, 0)))
        else:
            specs.append(pl.BlockSpec((right.shape[0], tile), lambda n: (0, n)))
    specs += [pl.BlockSpec((v.shape[0], tile), lambda n: (0, n)) for v in extra]

    def step(*refs):
        found = None
        for number in range(len(parts)):
            product = lax.dot_general(
                refs[2 * number][...],
                refs[2 * number + 1][...],
                dims,
                preferred_element_type=f32,
            )
            found = product if found is None else found + product
        rest = refs[2 * len(parts) :]
        results = (found,)
        if finish is not None:
            results = finish(found, *(v[...] for v in rest[: len(extra)]))
        for ref, value in zip(rest[len(extra) :], results):
            ref[...] = value.astype(ref.dtype)

    factors = [v for pair in parts for v in pair]
    pltpu.emit_pipeline(
        step,
        grid=(width // tile,),
        in_specs=specs,
        out_specs=[pl.BlockSpec((v.shape[0], tile), lambda n: (0, n)) for v in outs],
    )(*factors, *extra, *outs)


def half_rows(ref, half, count):
    return ref.at[pl.ds(pl.multiple_of(half * count, count), count)]


def front(sizes, tokens, cotangent, vectors, numbers, weights, projection_bias, up_bias):
    chips, halves, depth = sizes["fsdp"] // 2, sizes["ctx"], sizes["tp"]
    groups = sizes["fsdp"] * halves
    own_len, model = tokens.shape
    length = own_len * depth
    projection, up, dense, down = weights
    weight_count = len(weights)
    kinds, local = projection.shape[0], projection.shape[2]
    count = local // 2
    hidden = up.shape[1]
    shard = vectors[0].shape[0]
    half_rot = ROT // 2
    early_width = model // 4 * 3
    first_width = model // 8

    def kernel(*refs):
        refs = list(refs)

        def take(number):
            taken = refs[:number]
            del refs[:number]
            return taken

        tokens_ref, cotangent_ref = take(2)
        vector_in, number_in = take(len(vectors)), take(len(numbers))
        weight_in = take(weight_count)
        bias_in, up_bias_in = take(2)
        vectors_out, *numbers_out = take(1 + len(numbers))
        normed, cotangent_rows, cotangent_late = take(3)
        weight_out = take(weight_count)
        both, activation, slope, triple = take(4)
        landed, normed_own, stage, vector_ref, bias_ref, up_bias_ref, cosine_ref, sine_ref = take(8)
        vector_send, vector_recv, number_sems, single, line_send, line_recv = take(6)
        keep, near_send, near_recv, turn_send, turn_recv, core_send, core_recv = take(7)
        place = Place(sizes)
        peers = place.group()
        greet_line(place, [place.device(chip=a, core=b, half=c) for a, b, c in peers])
        pending = []

        def launch(copy):
            copy.start()
            pending.append(copy)

        def part(a, block, first=0, rows=None):
            rows = weight_in[a].shape[-2] if rows is None else rows
            start = pl.multiple_of(block * weight_in[a].shape[-2] + first, 16)
            span = pl.ds(start, rows)
            return weight_out[a].at[:, span] if a == 0 else weight_out[a].at[span]

        def arrive(piece, recv_sem):
            send(piece, piece, recv_sem, recv_sem, place.pair()).wait_recv()

        mine = place.block()
        vector_ref[...] = jnp.zeros_like(vector_ref)
        for row, ref in enumerate(vector_in):
            vector_ref[row : row + 1, :] = ref[...].astype(f32).reshape(1, shard)
        vector_keep = pltpu.make_async_copy(vector_ref, landed.at[mine], single.at[0])
        vector_keep.start()
        for at, (chip, core, half) in enumerate(peers):
            launch(
                send(
                    vector_ref,
                    landed.at[mine],
                    vector_send.at[at],
                    vector_recv.at[at],
                    place.device(chip=chip, core=core, half=half),
                )
            )
        for number in range(len(numbers)):
            launch(
                send(
                    number_in[number],
                    numbers_out[number],
                    number_sems.at[0, number],
                    number_sems.at[1, number],
                    place.across(),
                )
            )

        def near_start(a):
            own = part(a, place.block())
            for k in range(1, chips):
                launch(
                    send(
                        weight_in[a],
                        own,
                        near_send.at[a, k],
                        near_recv.at[a, k],
                        place.device(chip=place.ahead(k)),
                    )
                )
            launch(
                send(weight_in[a], own, near_send.at[a, 0], near_recv.at[a, 0], place.across())
            )
            launch(send(weight_in[a], own, core_send.at[a, 0], core_recv.at[a, 0], place.pair()))
            pltpu.make_async_copy(weight_in[a], own, keep.at[a]).start()

        def near_step(a):
            side = weight_in[a].shape[-2] // 4
            rest = weight_in[a].shape[-2] - side
            for k in range(1, chips):
                block = place.block(chip=place.behind(k))
                piece = part(a, block)
                arrive(piece, near_recv.at[a, k])
                top = part(a, block, 0, side)
                launch(
                    send(top, top, turn_send.at[a, 0, k], turn_recv.at[a, 0, k], place.across())
                )
                launch(send(piece, piece, core_send.at[a, k], core_recv.at[a, k], place.pair()))
            block = place.block(half=1 - place.half)
            piece = part(a, block)
            arrive(piece, near_recv.at[a, 0])
            low = part(a, block, side, rest)
            for k in range(1, chips):
                launch(
                    send(
                        low,
                        low,
                        turn_send.at[a, 1, k],
                        turn_recv.at[a, 1, k],
                        place.device(chip=place.ahead(k)),
                    )
                )
            launch(
                send(piece, piece, core_send.at[a, chips], core_recv.at[a, chips], place.pair())
            )

        def turn_step(a):
            side = weight_in[a].shape[-2] // 4
            rest = weight_in[a].shape[-2] - side
            for k in range(1, chips):
                block = place.block(chip=place.behind(k), half=1 - place.half)
                arrive(part(a, block, 0, side), turn_recv.at[a, 0, k])
                arrive(part(a, block, side, rest), turn_recv.at[a, 1, k])
                piece = part(a, block)
                launch(
                    send(
                        piece,
                        piece,
                        core_send.at[a, chips + k],
                        core_recv.at[a, chips + k],
                        place.pair(),
                    )
                )

        def core_step(a):
            other = 1 - place.core
            blocks = [place.block(core=other)]
            blocks += [place.block(place.behind(k), other) for k in range(1, chips)]
            blocks += [place.block(None, other, 1 - place.half)]
            blocks += [
                place.block(place.behind(k), other, 1 - place.half) for k in range(1, chips)
            ]
            for at, block in enumerate(blocks):
                arrive(part(a, block), core_recv.at[a, at])
            pltpu.make_async_copy(weight_in[a], part(a, place.block()), keep.at[a]).wait()

        near_start(0)
        rest_width = early_width - first_width
        early = cotangent_ref.at[:, pl.ds(first_width, rest_width)]
        early_rows = cotangent_rows.at[:, pl.ds(first_width, rest_width)]
        first = cotangent_ref.at[:, pl.ds(0, first_width)]
        first_rows = cotangent_rows.at[:, pl.ds(0, first_width)]
        lines = (
            Line(place, normed_own, normed, line_send.at[0], line_recv.at[0], single.at[3]),
            Line(place, early, early_rows, line_send.at[1], line_recv.at[1], single.at[8]),
            Line(place, first, first_rows, line_send.at[2], line_recv.at[2], single.at[2]),
        )
        lines[2].start()

        vector_keep.wait()
        for at in range(len(peers)):
            place_in = at + 1
            source = place.block(
                place.behind(place_in // 4),
                (place.core + place_in // 2 % 2) % 2,
                (place.half + place_in % 2) % 2,
            )
            arrive(landed.at[source], vector_recv.at[at])
        for number in range(groups):
            vectors_out[:, number * shard : (number + 1) * shard] = landed[number]

        @pl.loop(0, own_len, step=32)
        def _(r):
            at = pl.ds(pl.multiple_of(r, 32), 32)
            values = tokens_ref[at, :].astype(f32)
            normed_own[at, :] = layer_norm(
                values, vectors_out[0:1, :], vectors_out[1:2, :]
            ).astype(bf16)

        lines[2].step(1)
        lines[0].start()
        near_start(1)
        late_keep = pltpu.make_async_copy(
            cotangent_ref.at[:, pl.ds(early_width, model - early_width)],
            cotangent_late,
            single.at[1],
        )
        late_keep.start()
        bias_ref[...] = bias_in[...].astype(f32).T
        up_bias_ref[...] = up_bias_in[...].astype(f32).reshape(1, hidden)
        turns = lax.broadcasted_iota(jnp.int32, (half_rot, 1), 0)
        inverse = jnp.zeros((half_rot, 1), f32)
        for row in range(half_rot):
            inverse = jnp.where(turns == row, 10000.0 ** (-2.0 * row / ROT), inverse)
        phase = inverse * number_in[1][...].astype(f32)
        cosine_ref[...] = jnp.cos(phase)
        sine_ref[...] = jnp.sin(phase)
        if depth > 2:
            lines[2].step(2)
        near_step(0)
        lines[0].step(1)
        for k in range(3, depth):
            lines[2].step(k)
        near_start(3)
        near_start(2)
        turn_step(0)
        near_step(1)
        for k in range(2, depth):
            lines[0].step(k)
        lines[1].start()
        lines[0].keep.wait()
        core_step(0)
        near_step(3)

        def project(weight, rows, cosine_here, sine_here, out):
            for kind in range(kinds):
                found = lax.dot_general(
                    weight[kind], rows[...], row_by_col, preferred_element_type=f32
                )
                found = found + bias_ref[:, kind : kind + 1]
                if kind == 2:
                    out[kind] = found.astype(bf16)
                    continue
                for head in range(local // HD):
                    first = head * HD
                    leading = found[first : first + half_rot]
                    trailing = found[first + half_rot : first + ROT]
                    turned = (
                        leading * cosine_here[...] - trailing * sine_here[...],
                        trailing * cosine_here[...] + leading * sine_here[...],
                        found[first + ROT : first + HD],
                    )
                    out[kind, first : first + HD] = jnp.concatenate(turned, axis=0).astype(bf16)

        tile = min(512, length)
        pltpu.emit_pipeline(
            project,
            grid=(length // tile,),
            in_specs=[
                pl.BlockSpec(weight_out[0].shape, lambda n: (0, 0, 0)),
                pl.BlockSpec((tile, model), lambda n: (n, 0)),
                pl.BlockSpec((half_rot, tile), lambda n: (0, n)),
                pl.BlockSpec((half_rot, tile), lambda n: (0, n)),
            ],
            out_specs=[pl.BlockSpec((kinds, local, tile), lambda n: (0, 0, n))],
        )(weight_out[0], normed, cosine_ref, sine_ref, triple)

        def heads(half):
            return triple.at[:, pl.ds(pl.multiple_of(half * count, count), count)]

        here, there = place.half, 1 - place.half
        launch(send(heads(there), both.at[here], single.at[4], single.at[5], place.across()))
        load = pltpu.make_async_copy(heads(here), stage, single.at[6])
        load.start()
        load.wait()
        stage_keep = pltpu.make_async_copy(stage, both.at[here], single.at[7])
        stage_keep.start()
        near_step(2)
        lines[1].step(1)
        turn_step(1)
        core_step(1)
        wide = hidden // 2
        for number in range(2):
            span = pl.ds(number * wide, wide)
            multiply(
                "nn",
                [(normed, weight_out[1].at[:, span])],
                [activation.at[:, span], slope.at[:, span]],
                lambda found, bias: gelu_and_slope(found + bias),
                [up_bias_ref.at[:, span]],
            )
            if number == 0 and depth > 2:
                lines[1].step(2)
        turn_step(3)
        core_step(3)
        turn_step(2)
        core_step(2)
        for k in range(3, depth):
            lines[1].step(k)
        lines[1].keep.wait()
        lines[2].keep.wait()
        stage_keep.wait()
        arrive(both.at[there], single.at[5])
        for number in range(len(numbers)):
            arrive(numbers_out[number], number_sems.at[1, number])
        late_keep.wait()
        for copy in pending:
            copy.wait_send()
        for run in lines:
            run.end()

    out_shape = [
        jax.ShapeDtypeStruct((8, groups * shard), f32),
        *[jax.ShapeDtypeStruct(v.shape, v.dtype) for v in numbers],
        jax.ShapeDtypeStruct((length, model), bf16),
        jax.ShapeDtypeStruct((length, early_width), bf16),
        jax.ShapeDtypeStruct((own_len, model - early_width), bf16),
    ]
    out_shape += [
        jax.ShapeDtypeStruct(v.shape[:-2] + (groups * v.shape[-2], v.shape[-1]), v.dtype)
        for v in weights
    ]
    out_shape += [
        jax.ShapeDtypeStruct((2, kinds, count, length), bf16),
        jax.ShapeDtypeStruct((length, hidden), bf16),
        jax.ShapeDtypeStruct((length, hidden), bf16),
        jax.ShapeDtypeStruct((kinds, local, length), bf16),
    ]
    results = pl.pallas_call(
        kernel,
        out_shape=tuple(out_shape),
        in_specs=[VMEM] * (4 + len(vectors) + len(numbers) + weight_count),
        out_specs=(VMEM,) * (1 + len(numbers)) + (ANY,) * (len(out_shape) - 1 - len(numbers)),
        scratch_shapes=[
            pltpu.VMEM((groups, 8, shard), f32),
            pltpu.VMEM((own_len, model), bf16),
            pltpu.VMEM((kinds, count, length), bf16),
            pltpu.VMEM((8, shard), f32),
            pltpu.VMEM((local, kinds), f32),
            pltpu.VMEM((1, hidden), f32),
            pltpu.VMEM((half_rot, length), f32),
            pltpu.VMEM((half_rot, length), f32),
            DMA((groups - 1,)),
            DMA((groups - 1,)),
            DMA((2, len(numbers))),
            DMA((9,)),
            DMA((3, 2, depth - 1)),
            DMA((3, 2, depth - 1)),
            DMA((weight_count,)),
            DMA((weight_count, chips)),
            DMA((weight_count, chips)),
            DMA((weight_count, 2, chips)),
            DMA((weight_count, 2, chips)),
            DMA((weight_count, 2 * chips)),
            DMA((weight_count, 2 * chips)),
        ],
        compiler_params=pltpu.CompilerParams(
            collective_id=0, has_side_effects=True, vmem_limit_bytes=60 << 20
        ),
        cost_estimate=pl.CostEstimate(flops=0, bytes_accessed=480_000_000, transcendentals=0),
        name="front",
    )(tokens, cotangent, *vectors, *numbers, *weights, projection_bias, up_bias)
    return results[:-1]


class Held:
    def __init__(self, sources, buffers, sems):
        self.copies = {}
        self.buffers = buffers
        for number, (source, buffer) in enumerate(zip(sources, buffers)):
            copy = pltpu.make_async_copy(source, buffer, sems.at[number])
            copy.start()
            self.copies[number] = copy

    def __getitem__(self, number):
        if number in self.copies:
            self.copies.pop(number).wait()
        return self.buffers[number]


def buffers_for(*arrays):
    return [pltpu.VMEM(v.shape, v.dtype) for v in arrays]


def exchange_middle(
    sizes, attended, activation, down_full, dense_full, cotangent_early, late_blocks, slope
):
    width, total = attended.shape
    length = total // 2
    rows, model = activation.shape[0], down_full.shape[0]
    hidden = slope.shape[1]
    depth = sizes["tp"]
    late_rows, late_width = late_blocks[0].shape
    holds = [activation, down_full, dense_full, cotangent_early, slope]

    def kernel(attended_ref, *refs):
        late_refs, refs = refs[:depth], refs[depth:]
        held_refs, refs = refs[: len(holds)], refs[len(holds) :]
        full_out, block_out, late_out, both, grad_hidden, hidden_sum = refs[:6]
        full, feed, late, made, *buffers, sems, held_sems, late_sems = refs[6:]
        place = Place(sizes)
        here, there = place.half, 1 - place.half

        def tokens(half):
            return attended_ref.at[:, pl.ds(pl.multiple_of(half * length, length), length)]

        mine = half_rows(full, here, width)
        load = pltpu.make_async_copy(tokens(here), mine, sems.at[0])
        load.start()
        held = Held(held_refs, buffers, held_sems)
        late_loads = []
        for k in range(depth):
            source = (place.layer + depth - k) % depth
            span = pl.ds(pl.multiple_of(source * late_rows, 16), late_rows)
            late_loads.append(pltpu.make_async_copy(late_refs[k], late.at[span], late_sems.at[k]))
            late_loads[-1].start()
        greet([place.across()])
        away = send(tokens(there), mine, sems.at[2], sems.at[3], place.across())
        away.start()
        multiply("nt", [(held[0], held[1])], [feed])
        load.wait()
        away.wait_send()
        came = half_rows(full, there, width)
        send(came, came, sems.at[2], sems.at[3], place.across()).wait_recv()
        full_keep = pltpu.make_async_copy(full, full_out, sems.at[4])
        full_keep.start()
        multiply(
            "tt",
            [(full, held[2])],
            [block_out],
            lambda found, before: (found + before,),
            [feed],
        )
        for copy in late_loads:
            copy.wait()
        late_keep = pltpu.make_async_copy(late, late_out, sems.at[5])
        late_keep.start()

        def parts(weight):
            first = model - late_width
            return [
                (held[3], weight.at[pl.ds(0, first)]),
                (late, weight.at[pl.ds(first, late_width)]),
            ]

        multiply("tt", [(b, a) for a, b in parts(held[2])], [made])
        away = send(
            half_rows(made, there, width), both.at[here], sems.at[6], sems.at[7], place.across()
        )
        keep = pltpu.make_async_copy(half_rows(made, here, width), both.at[here], sems.at[8])
        away.start()
        keep.start()

        def scaled(found, slope):
            found = found * slope.astype(f32)
            return found, jnp.sum(found, axis=0, keepdims=True)

        multiply("nn", parts(held[1]), [grad_hidden, hidden_sum], scaled, [held[4]])
        for copy in (keep, full_keep, late_keep):
            copy.wait()
        away.wait_send()
        came = both.at[there]
        send(came, came, sems.at[6], sems.at[7], place.across()).wait_recv()

    return pl.pallas_call(
        kernel,
        out_shape=(
            jax.ShapeDtypeStruct((2 * width, length), bf16),
            jax.ShapeDtypeStruct((rows, model), bf16),
            jax.ShapeDtypeStruct((rows, late_width), bf16),
            jax.ShapeDtypeStruct((2, width, length), bf16),
            jax.ShapeDtypeStruct((rows, hidden), bf16),
            jax.ShapeDtypeStruct((1, hidden), f32),
        ),
        in_specs=[ANY] * (1 + depth + len(holds)),
        out_specs=(ANY,) * 5 + (VMEM,),
        scratch_shapes=[
            pltpu.VMEM((2 * width, length), bf16),
            pltpu.VMEM((rows, model), f32),
            pltpu.VMEM((rows, late_width), bf16),
            pltpu.VMEM((2 * width, length), bf16),
            *buffers_for(*holds),
            DMA((9,)),
            DMA((len(holds),)),
            DMA((depth,)),
        ],
        compiler_params=pltpu.CompilerParams(
            collective_id=4, has_side_effects=True, vmem_limit_bytes=60 << 20
        ),
        cost_estimate=pl.CostEstimate(flops=0, bytes_accessed=140_000_000, transcendentals=0),
        name="exchange_middle",
    )(attended, *late_blocks, *holds)


def exchange_back(sizes, back, normed, grad_hidden, cotangents, activation, up_full, projection):
    kinds, width, total = back.shape
    length = total // 2
    chips, halves = sizes["fsdp"] // 2, sizes["ctx"]
    rows, model = normed.shape
    hidden = grad_hidden.shape[1]
    span = model // (2 * chips)
    shard = span // halves
    sides = (shard // 4, shard // 2)
    count = len(cotangents)

    def kernel(back_ref, *rest):
        held_refs, rest = rest[: 4 + count], rest[4 + count :]
        weight_ref, full_out, made, came, turns, block_in, feed = (
            rest[0],
            rest[1],
            rest[2:4],
            rest[4:6],
            rest[6:10],
            rest[10],
            rest[11],
        )
        sums, full, diagonal, stage = rest[12:16]
        normed_held, hidden_held, cotangent_held, activation_held, up_held = rest[16:21]
        held_sems, sems, stage_sems, core_send, core_recv, turn_send, turn_recv = rest[21:]
        buffers, first = [normed_held, hidden_held], 0
        for ref in held_refs[2 : 2 + count]:
            buffers.append(cotangent_held.at[:, pl.ds(first, ref.shape[1])])
            first += ref.shape[1]
        held = Held(held_refs, buffers + [activation_held, up_held], held_sems)
        place = Place(sizes)
        here, there = place.half, 1 - place.half
        other = 1 - place.core

        def tokens(half):
            return back_ref.at[:, :, pl.ds(pl.multiple_of(half * length, length), length)]

        def heads(half):
            return full.at[:, pl.ds(pl.multiple_of(half * width, width), width)]

        load = pltpu.make_async_copy(tokens(here), heads(here), sems.at[2])
        load.start()
        greet(plane(place))
        away = send(tokens(there), heads(here), sems.at[0], sems.at[1], place.across())
        away.start()

        def to_pair(number):
            copies = []
            for chip in range(chips):
                copies.append(
                    send(
                        made[number].at[pl.ds(pl.multiple_of((2 * chip + other) * span, 16), span)],
                        came[number].at[pl.ds(chip * span, span)],
                        core_send.at[number, chip],
                        core_recv.at[number, chip],
                        place.pair(),
                    )
                )
                copies[-1].start()
            return copies

        def stage_loads(number, k):
            chip = place.ahead(k)
            mine = place.block(chip, place.core, there) * shard
            theirs = (chip * halves + there) * shard
            return [
                pltpu.make_async_copy(
                    ref.at[pl.ds(pl.multiple_of(block, 16), shard)],
                    stage.at[at, k - 1],
                    stage_sems.at[at, k],
                )
                for at, (ref, block) in enumerate(((made[number], mine), (came[number], theirs)))
            ]

        def turn_load(number, copies):
            for copy in copies:
                copy.wait()
            for k in range(1, chips):
                for copy in stage_loads(number, k):
                    copy.start()

        def turn(number):
            sent = []
            step = min(64, shard)
            for k in range(1, chips):
                for copy in stage_loads(number, k):
                    copy.wait()

                @pl.loop(0, shard, step=step)
                def _(r):
                    at = pl.ds(pl.multiple_of(r, step), step)
                    diagonal[number, k - 1, at, :] = (
                        stage[0, k - 1, at, :].astype(f32) + stage[1, k - 1, at, :].astype(f32)
                    ).astype(bf16)

                for way, device in enumerate(
                    (place.across(), place.device(chip=place.ahead(k)))
                ):
                    side = sides[number]
                    part = pl.ds(0, side) if way == 0 else pl.ds(side, shard - side)
                    sent.append(
                        send(
                            diagonal.at[number, k - 1, part],
                            turns[2 * number + way].at[k - 1],
                            turn_send.at[number, way, k],
                            turn_recv.at[number, way, k],
                            device,
                        )
                    )
                    sent[-1].start()
            return sent

        multiply("tn", [(held[0], held[1])], [made[0]])
        up_copies = to_pair(0)
        for number in range(count):
            held[2 + number]
        half = hidden // 2
        for number in range(2):
            part = pl.ds(number * half, half)
            multiply(
                "tn",
                [(cotangent_held, held[2 + count].at[:, part])],
                [made[1].at[:, part]],
            )
            if number == 0:
                turn_load(0, up_copies)
                turned = turn(0)
        down_copies = to_pair(1)
        half = model // 2
        for number in range(2):
            part = pl.ds(number * half, half)
            multiply("nt", [(held[1], held[3 + count].at[part])], [feed.at[:, part]])
            if number == 0:
                turn_load(1, down_copies)
                turned += turn(1)
        load.wait()
        away.wait_send()
        send(heads(there), heads(there), sems.at[0], sems.at[1], place.across()).wait_recv()
        keep = pltpu.make_async_copy(full, full_out, sems.at[3])
        keep.start()
        ones = jnp.ones((8, length), bf16)
        for kind in range(kinds):
            total_of = lax.dot_general(ones, full[kind], contract_cols, preferred_element_type=f32)
            sums[kind : kind + 1, :] = total_of[0:1, :]

        def step(right_ref, before_ref, out_ref):
            found = before_ref[...]
            for kind in range(kinds):
                found += lax.dot_general(
                    full[kind], right_ref[kind], row_by_col, preferred_element_type=f32
                )
            out_ref[...] = found.astype(bf16)

        tile = min(512, model)
        pltpu.emit_pipeline(
            step,
            grid=(model // tile,),
            in_specs=[
                pl.BlockSpec((kinds, tile, 2 * width), lambda n: (0, n, 0)),
                pl.BlockSpec((rows, tile), lambda n: (0, n)),
            ],
            out_specs=[pl.BlockSpec((rows, tile), lambda n: (0, n))],
        )(weight_ref, feed, block_in)
        keep.wait()
        for copy in turned:
            copy.wait()

    product = jax.ShapeDtypeStruct((model, hidden), bf16)
    part = jax.ShapeDtypeStruct((model // 2, hidden), bf16)
    holds = [normed, grad_hidden, *cotangents, activation, up_full]
    results = pl.pallas_call(
        kernel,
        out_shape=(
            jax.ShapeDtypeStruct((kinds, 2 * width, length), bf16),
            product,
            product,
            part,
            part,
            *[
                jax.ShapeDtypeStruct((chips - 1, n, hidden), bf16)
                for side in sides
                for n in (side, shard - side)
            ],
            jax.ShapeDtypeStruct((rows, model), bf16),
            jax.ShapeDtypeStruct((rows, model), f32),
            jax.ShapeDtypeStruct((kinds, 2 * width), f32),
        ),
        in_specs=[ANY] * (len(holds) + 2),
        out_specs=(ANY,) * 11 + (VMEM,),
        scratch_shapes=[
            pltpu.VMEM((kinds, 2 * width, length), bf16),
            pltpu.VMEM((2, chips - 1, shard, hidden), bf16),
            pltpu.VMEM((2, chips - 1, shard, hidden), bf16),
            *buffers_for(normed, grad_hidden, normed, activation, up_full),
            DMA((len(holds),)),
            DMA((4,)),
            DMA((2, chips)),
            DMA((2, chips)),
            DMA((2, chips)),
            DMA((2, 2, chips)),
            DMA((2, 2, chips)),
        ],
        compiler_params=pltpu.CompilerParams(
            collective_id=5, has_side_effects=True, vmem_limit_bytes=60 << 20
        ),
        cost_estimate=pl.CostEstimate(flops=0, bytes_accessed=180_000_000, transcendentals=0),
        name="exchange_back",
    )(back, *holds, projection)
    full, up_made, down_made, up_came, down_came, *turned = results[:9]
    paired = [(up_made, up_came), (down_made, down_came)]
    return full, paired, turned, results[9], results[11]


def finish_all(sizes, grad, tokens, cotangent, vectors, partials, splits):
    chips, halves, depth = sizes["fsdp"] // 2, sizes["ctx"], sizes["tp"]
    groups = sizes["fsdp"] * halves
    own_len, model = tokens.shape
    shard = model // groups
    count = len(partials)
    step_rows = 64

    def kernel(grad_ref, tokens_ref, cotangent_ref, vector_ref, *refs):
        partial_in, refs = refs[:count], refs[count:]
        input_ref, small_ref = refs[:2]
        weight_out, refs = refs[2 : 2 + count], refs[2 + count :]
        near, refs = refs[:count], refs[count:]
        sums, blocks, landed, line, near_send, near_recv, load_sem, *sems = refs
        block_send, block_recv, line_send, line_recv = sems
        place = Place(sizes)
        peers = place.group()
        layers = [(place.layer + k) % depth for k in range(1, depth)]
        devices = [place.device(chip=a, core=b, half=c) for a, b, c in peers]
        greet(devices + [place.device(layer=k) for k in layers])
        pending = []
        for a in range(count):
            targets = [place.across()] + [
                place.device(chip=place.ahead(k)) for k in range(1, chips)
            ]
            for at, device in enumerate(targets):
                pending.append(
                    send(
                        partial_in[a].at[at],
                        near[a].at[at],
                        near_send.at[a, at],
                        near_recv.at[a, at],
                        device,
                    )
                )
                pending[-1].start()
            pltpu.make_async_copy(
                partial_in[a].at[chips], near[a].at[chips], load_sem.at[a]
            ).start()

        gain = vector_ref[0:1, :]
        sums[...] = jnp.zeros_like(sums)

        @pl.loop(0, own_len, step=step_rows)
        def _(r):
            at = pl.ds(pl.multiple_of(r, step_rows), step_rows)
            values = tokens_ref[at, :].astype(f32)
            centered = values - jnp.mean(values, axis=-1, keepdims=True)
            spread = jnp.mean(centered * centered, axis=-1, keepdims=True)
            scale = lax.rsqrt(spread + epsilon)
            normal = centered * scale
            found = grad_ref[at, :].astype(f32)
            away = cotangent_ref[at, :].astype(f32)
            inner = found * gain
            mean = jnp.mean(inner, axis=-1, keepdims=True)
            along = jnp.mean(inner * normal, axis=-1, keepdims=True)
            input_ref[at, :] = (scale * (inner - mean - normal * along)).astype(bf16)
            sums[0:1, :] += jnp.sum(found * normal, axis=0, keepdims=True)
            sums[1:2, :] += jnp.sum(found, axis=0, keepdims=True)
            sums[2:3, :] += jnp.sum(away, axis=0, keepdims=True)

        for number in range(groups):
            blocks[number] = sums[:, number * shard : (number + 1) * shard]
        copies = []
        for at, (chip, core, half) in enumerate(peers):
            copies.append(
                send(
                    blocks.at[place.block(chip, core, half)],
                    landed.at[at],
                    block_send.at[at],
                    block_recv.at[at],
                    devices[at],
                )
            )
            copies[-1].start()
        total = blocks[place.block()]
        for at, copy in enumerate(copies):
            copy.wait()
            total += landed[at]
        line[0] = total
        copies = []
        for k, layer in enumerate(layers):
            copies.append(
                send(
                    line.at[0],
                    line.at[k + 1],
                    line_send.at[k],
                    line_recv.at[k],
                    place.device(layer=layer),
                )
            )
            copies[-1].start()
        for k, copy in enumerate(copies):
            copy.wait()
            total += line[k + 1]
        small_ref[...] = total

        for copy in pending:
            copy.wait()
        for a in range(count):
            own = near[a].at[chips]
            pltpu.make_async_copy(own, own, load_sem.at[a]).wait()
            rows, width = partials[a].shape[1:]

            @pl.loop(0, rows, step=16)
            def _(r, a=a, width=width):
                at = pl.ds(pl.multiple_of(r, 16), 16)
                found = near[a][0, at, :].astype(f32)
                for number in range(1, chips + 1):
                    found += near[a][number, at, :].astype(f32)
                if splits[a] == 1:
                    weight_out[a][at, :] = found
                else:
                    wide = width // splits[a]
                    for kind in range(splits[a]):
                        weight_out[a][kind, at, :] = found[:, kind * wide : (kind + 1) * wide]

    out_shape = [
        jax.ShapeDtypeStruct((own_len, model), bf16),
        jax.ShapeDtypeStruct((8, shard), f32),
    ]
    for v, n in zip(partials, splits):
        rows, width = v.shape[1:]
        out_shape.append(
            jax.ShapeDtypeStruct((rows, width) if n == 1 else (n, rows, width // n), f32)
        )
    return pl.pallas_call(
        kernel,
        out_shape=tuple(out_shape),
        in_specs=[VMEM] * 4 + [ANY] * count,
        out_specs=(VMEM,) * len(out_shape),
        scratch_shapes=[
            *buffers_for(*partials),
            pltpu.VMEM((8, model), f32),
            pltpu.VMEM((groups, 8, shard), f32),
            pltpu.VMEM((groups - 1, 8, shard), f32),
            pltpu.VMEM((depth, 8, shard), f32),
            DMA((count, chips)),
            DMA((count, chips)),
            DMA((count,)),
            DMA((groups - 1,)),
            DMA((groups - 1,)),
            DMA((depth - 1,)),
            DMA((depth - 1,)),
        ],
        compiler_params=pltpu.CompilerParams(
            collective_id=3, has_side_effects=True, vmem_limit_bytes=60 << 20
        ),
        cost_estimate=pl.CostEstimate(flops=0, bytes_accessed=90_000_000, transcendentals=0),
        name="finish_all",
    )(grad, tokens, cotangent, vectors, *partials)


def tile_at(number):
    return pl.ds(pl.multiple_of(number * TILE, TILE), TILE)


def allowed(kb, j, start):
    places = kb * TILE + lax.broadcasted_iota(jnp.int32, (TILE, TILE), 0)
    own = j * TILE + lax.broadcasted_iota(jnp.int32, (TILE, TILE), 1)
    return (places >= start) & (places <= own)


def attend_kernel(
    low_ref,
    mid_ref,
    triple_ref,
    start_ref,
    attended_ref,
    log_ref,
    query_t,
    key_t,
    value_t,
    key_rows,
    scores,
):
    length = triple_ref.shape[3]
    heads = triple_ref.shape[2] // HD
    score_scale = 1.0 / math.sqrt(HD)
    for number, ref in enumerate((query_t, key_t, value_t)):
        for part in range(2):
            piece = triple_ref[part, number]
            ref[:, part * length : (part + 1) * length] = (
                piece * score_scale if number == 0 else piece
            )
    rows = [slice(h * HD, (h + 1) * HD) for h in range(heads)]
    for h in range(heads):
        key_rows[h] = key_t[rows[h], :].T

    @pl.loop(0, 2 * length // TILE)
    def _(j):
        here = tile_at(j)
        start = start_ref[:, here]
        low, mid = low_ref[j], mid_ref[j]
        queries = [query_t[row, here] for row in rows]

        def score_with(masked):
            def score(kb, highest):
                ok = allowed(kb, j, start) if masked else None
                raised = []
                for h in range(heads):
                    found = jnp.dot(
                        key_rows[h, tile_at(kb), :], queries[h], preferred_element_type=f32
                    )
                    if masked:
                        found = jnp.where(ok, found, big_negative)
                    scores[h, tile_at(kb), :] = found
                    raised.append(
                        jnp.maximum(highest[h], jnp.max(found, axis=0, keepdims=True))
                    )
                return tuple(raised)

            return score

        highest = tuple(jnp.full((1, TILE), big_negative, f32) for _ in range(heads))
        highest = lax.fori_loop(low, mid, score_with(True), highest)
        highest = lax.fori_loop(mid, j, score_with(False), highest)
        highest = score_with(True)(j, highest)

        def weigh(kb, carry):
            after = []
            for h in range(heads):
                total, mixed = carry[h]
                prob = jnp.exp(scores[h, tile_at(kb), :] - highest[h])
                total = total + jnp.sum(prob, axis=0, keepdims=True)
                mixed = mixed + jnp.dot(
                    value_t[rows[h], tile_at(kb)], prob.astype(bf16), preferred_element_type=f32
                )
                after.append((total, mixed))
            return tuple(after)

        empty = tuple(
            (jnp.zeros((1, TILE), f32), jnp.zeros((HD, TILE), f32)) for _ in range(heads)
        )
        result = lax.fori_loop(low, j + 1, weigh, empty)
        for h in range(heads):
            total, mixed = result[h]
            attended_ref[rows[h], here] = (mixed / total).astype(bf16)
            log_ref[h, :, here] = highest[h] + jnp.log(total)


def turned_back(values, cosine, sine):
    half_rot = ROT // 2
    leading = values[:half_rot]
    trailing = values[half_rot:ROT]
    return jnp.concatenate(
        [
            leading * cosine + trailing * sine,
            trailing * cosine - leading * sine,
            values[ROT:],
        ],
        axis=0,
    )


def attend_back_kernel(
    low_ref,
    mid_ref,
    triple_ref,
    grad_ref,
    attended_ref,
    log_ref,
    start_ref,
    cosine_ref,
    sine_ref,
    back_ref,
    query_t,
    key_t,
    grad_t,
    key_rows,
    value_rows,
    key_sum,
    value_sum,
):
    length = triple_ref.shape[3]
    heads = triple_ref.shape[2] // HD
    score_scale = 1.0 / math.sqrt(HD)
    rows = [slice(h * HD, (h + 1) * HD) for h in range(heads)]
    for part in range(2):
        span = slice(part * length, (part + 1) * length)
        query_t[:, span] = triple_ref[part, 0] * score_scale
        key_t[:, span] = triple_ref[part, 1]
        grad_t[:, span] = grad_ref[part]
        for h in range(heads):
            value_rows[h, span, :] = triple_ref[part, 2, rows[h]].T
    for h in range(heads):
        key_rows[h] = key_t[rows[h], :].T
    key_sum[...] = jnp.zeros_like(key_sum)
    value_sum[...] = jnp.zeros_like(value_sum)

    @pl.loop(0, 2 * length // TILE)
    def _(j):
        here = tile_at(j)
        start = start_ref[:, here]
        low, mid = low_ref[j], mid_ref[j]
        queries = [query_t[row, here] for row in rows]
        grads = [grad_t[row, here] for row in rows]
        query_rows = [value.T for value in queries]
        grad_rows = [value.T for value in grads]
        logs = [log_ref[h, :, here] for h in range(heads)]
        deltas = [
            jnp.sum(
                grads[h].astype(f32) * attended_ref[rows[h], here].astype(f32),
                axis=0,
                keepdims=True,
            )
            for h in range(heads)
        ]

        def pull_with(masked):
            def pull(kb, query_back):
                ok = allowed(kb, j, start) if masked else None
                after = []
                for h in range(heads):
                    score = jnp.dot(
                        key_rows[h, tile_at(kb), :], queries[h], preferred_element_type=f32
                    )
                    if masked:
                        score = jnp.where(ok, score, big_negative)
                    prob = jnp.exp(score - logs[h])
                    down = jnp.dot(
                        value_rows[h, tile_at(kb), :], grads[h], preferred_element_type=f32
                    )
                    score_back = (prob * (down - deltas[h])).astype(bf16)
                    value_sum[h, tile_at(kb), :] += jnp.dot(
                        prob.astype(bf16), grad_rows[h], preferred_element_type=f32
                    )
                    key_sum[h, tile_at(kb), :] += jnp.dot(
                        score_back, query_rows[h], preferred_element_type=f32
                    )
                    after.append(
                        query_back[h]
                        + jnp.dot(
                            key_t[rows[h], tile_at(kb)], score_back, preferred_element_type=f32
                        )
                    )
                return tuple(after)

            return pull

        query_back = tuple(jnp.zeros((HD, TILE), f32) for _ in range(heads))
        query_back = lax.fori_loop(low, mid, pull_with(True), query_back)
        query_back = lax.fori_loop(mid, j, pull_with(False), query_back)
        query_back = pull_with(True)(j, query_back)
        for h in range(heads):
            back_ref[0, rows[h], here] = turned_back(
                query_back[h] * score_scale, cosine_ref[:, here], sine_ref[:, here]
            ).astype(bf16)

    for h in range(heads):
        back_ref[1, rows[h], :] = turned_back(
            key_sum[h].T, cosine_ref[...], sine_ref[...]
        ).astype(bf16)
        back_ref[2, rows[h], :] = value_sum[h].T.astype(bf16)


def attend(low, mid, triple, start):
    width, length = triple.shape[2], triple.shape[3]
    total, heads = 2 * length, width // HD
    area = total * total // 3 * heads
    return pl.pallas_call(
        attend_kernel,
        out_shape=(
            jax.ShapeDtypeStruct((width, total), bf16),
            jax.ShapeDtypeStruct((heads, 1, total), f32),
        ),
        in_specs=[SMEM, SMEM, VMEM, VMEM],
        out_specs=(VMEM, VMEM),
        scratch_shapes=[pltpu.VMEM((width, total), bf16)] * 3
        + [pltpu.VMEM((heads, total, HD), bf16), pltpu.VMEM((heads, total, TILE), f32)],
        compiler_params=pltpu.CompilerParams(vmem_limit_bytes=48 << 20),
        cost_estimate=pl.CostEstimate(
            flops=50 * area * HD, bytes_accessed=8 * width * total, transcendentals=area
        ),
        name="attend",
    )(low, mid, triple, start)


def attend_back(low, mid, triple, grad, attended, log_sum, start, cosine, sine):
    width, length = triple.shape[2], triple.shape[3]
    total, heads = 2 * length, width // HD
    area = total * total // 3 * heads
    return pl.pallas_call(
        attend_back_kernel,
        out_shape=jax.ShapeDtypeStruct((3, width, total), bf16),
        in_specs=[SMEM, SMEM] + [VMEM] * 7,
        out_specs=VMEM,
        scratch_shapes=[pltpu.VMEM((width, total), bf16)] * 3
        + [pltpu.VMEM((heads, total, HD), bf16)] * 2
        + [pltpu.VMEM((heads, total, HD), f32)] * 2,
        compiler_params=pltpu.CompilerParams(vmem_limit_bytes=48 << 20),
        cost_estimate=pl.CostEstimate(
            flops=100 * area * HD, bytes_accessed=12 * width * total, transcendentals=area
        ),
        name="attend_back",
    )(low, mid, triple, grad, attended, log_sum, start, cosine, sine)


def rotate_rows(values, cosine, sine):
    half_rot = ROT // 2
    leading = values[:, :half_rot]
    trailing = values[:, half_rot:ROT]
    return jnp.concatenate(
        [
            leading * cosine - trailing * sine,
            trailing * cosine + leading * sine,
            values[:, ROT:],
        ],
        axis=1,
    )


def ordered(*values):
    return lax.optimization_barrier(values)


def body(
    sizes,
    tokens,
    segments,
    positions,
    norm_gain,
    norm_bias,
    projection_weight,
    projection_bias,
    dense_weight,
    dense_bias,
    up_weight,
    up_bias,
    down_weight,
    down_bias,
    cotangent,
):
    own_len, model_width = tokens.shape[1], tokens.shape[2]
    half_len = segments.shape[1]
    local_width = projection_weight.shape[2]
    hidden_width = up_weight.shape[1]
    shard_rows = norm_gain.shape[0]
    half = lax.axis_index("ctx")
    total_len = 2 * half_len

    numbers = [segments, positions]
    (
        vectors_full,
        segments_other,
        positions_other,
        normed,
        cotangent_early,
        cotangent_late,
        projection,
        up_full,
        dense_full,
        down_full,
        both,
        activation,
        slope,
    ) = front(
        sizes,
        tokens[0],
        cotangent[0],
        [norm_gain, norm_bias, dense_bias, down_bias],
        numbers,
        [projection_weight.transpose(1, 0, 2), up_weight, dense_weight, down_weight],
        projection_bias,
        up_bias,
    )

    def in_order(own, other, axis):
        return jnp.where(
            half == 0,
            jnp.concatenate([own, other], axis=axis),
            jnp.concatenate([other, own], axis=axis),
        )

    segment_row = in_order(segments[0], segments_other[0], 0)
    position_row = in_order(positions[0], positions_other[0], 0)
    places = jnp.arange(total_len, dtype=jnp.int32)
    edges = jnp.concatenate([jnp.ones((1,), bool), segment_row[1:] != segment_row[:-1]])
    start = lax.cummax(jnp.where(edges, places, 0))
    tile_count = total_len // TILE
    low = start[::TILE] // TILE
    mid = jnp.minimum(
        jnp.maximum((start[TILE - 1 :: TILE] + TILE - 1) // TILE, low),
        jnp.arange(tile_count, dtype=jnp.int32),
    )
    exponent = jnp.arange(ROT // 2, dtype=f32) * 2.0 / ROT
    phase_angle = (10000.0 ** (-exponent))[:, None] * position_row.astype(f32)[None, :]
    cosine_full, sine_full = jnp.cos(phase_angle), jnp.sin(phase_angle)
    depth = sizes["tp"]
    late_blocks = [cotangent_late] + [
        lax.ppermute(cotangent_late, "tp", [(z, (z + k) % depth) for z in range(depth)])
        for k in range(1, depth)
    ]
    attended_heads, log_sum = attend(low, mid, both, start[None, :])
    attended, block_out, cotangent_late, grad_both, grad_hidden, hidden_sum = exchange_middle(
        sizes,
        attended_heads,
        activation,
        down_full,
        dense_full,
        cotangent_early,
        late_blocks,
        slope,
    )
    cotangents = [cotangent_early, cotangent_late]
    branch_own = lax.psum_scatter(block_out, "tp", scatter_dimension=0, tiled=True)
    back_heads = attend_back(
        low,
        mid,
        both,
        grad_both,
        attended_heads,
        log_sum,
        start[None, :],
        cosine_full,
        sine_full,
    )
    grad_projected, paired, turned, block_in, projected_sum = exchange_back(
        sizes, back_heads, normed, grad_hidden, cotangents, activation, up_full, projection
    )
    grad_projected = grad_projected.reshape(3 * local_width, half_len)
    block_in, branch_own = ordered(block_in, branch_own)
    grad_normed_own = lax.psum_scatter(block_in, "tp", scatter_dimension=0, tiled=True)
    up_part, down_part, dense_part, small_total, partial = reduce(
        sizes,
        paired,
        turned,
        [(cotangents, attended), ([normed], grad_projected)],
        [hidden_sum, projected_sum],
        2,
        "reduce_weights",
    )
    input_part, totals, projection_part = finish_all(
        sizes,
        grad_normed_own,
        tokens[0],
        cotangent[0],
        vectors_full,
        [partial],
        [3],
    )
    bias_dense, bias_down = vectors_full[2], vectors_full[3]
    layer_output = (
        tokens[0].astype(f32) + branch_own.astype(f32) + (bias_dense + bias_down)
    ).astype(bf16)
    input_grad = cotangent[0].astype(f32) + input_part.astype(f32)
    return (
        layer_output[None],
        input_grad[None],
        totals[0],
        totals[1],
        projection_part.transpose(1, 0, 2),
        small_total[1:4, :local_width],
        dense_part,
        totals[2],
        up_part,
        small_total[0],
        down_part,
        totals[2],
    )


def solution(mesh):
    placed = (
        P("fsdp", ("ctx", "tp"), None),
        P("fsdp", "ctx"),
        P("fsdp", "ctx"),
        P(("fsdp", "ctx")),
        P(("fsdp", "ctx")),
        P(("fsdp", "ctx"), None, "tp"),
        P(None, "tp"),
        P(("fsdp", "ctx"), "tp"),
        P(("fsdp", "ctx")),
        P(("fsdp", "ctx"), "tp"),
        P("tp"),
        P(("fsdp", "ctx"), "tp"),
        P(("fsdp", "ctx")),
        P("fsdp", ("ctx", "tp"), None),
    )
    return jax.shard_map(
        functools.partial(body, dict(mesh.shape)),
        mesh=mesh,
        in_specs=placed,
        out_specs=(
            P("fsdp", ("ctx", "tp"), None),
            P("fsdp", ("ctx", "tp"), None),
            P(("fsdp", "ctx")),
            P(("fsdp", "ctx")),
            P(("fsdp", "ctx"), None, "tp"),
            P(None, "tp"),
            P(("fsdp", "ctx"), "tp"),
            P(("fsdp", "ctx")),
            P(("fsdp", "ctx"), "tp"),
            P("tp"),
            P(("fsdp", "ctx"), "tp"),
            P(("fsdp", "ctx")),
        ),
        check_vma=False,
    )
```

```python
import functools
import math

import jax
import jax.numpy as jnp
from jax import lax
from jax.experimental import pallas as pl
from jax.experimental.pallas import tpu as pltpu
from jax.sharding import PartitionSpec as P

HD = 64
ROT = 32
TILE = 256

epsilon = 1e-05
big_negative = -1000000000.0
root_two_over_pi = 0.7978845608028654
contract_rows = (((0,), (0,)), ((), ()))
contract_cols = (((1,), (1,)), ((), ()))
row_by_col = (((0,), (1,)), ((), ()))
MESH = pl.DeviceIdType.MESH
ANY = pl.BlockSpec(memory_space=pl.ANY)
VMEM = pl.BlockSpec(memory_space=pltpu.VMEM)
SMEM = pl.BlockSpec(memory_space=pltpu.SMEM)
DMA = pltpu.SemaphoreType.DMA
f32 = jnp.float32
bf16 = jnp.bfloat16


def layer_norm(values, gain_full, shift_full):
    center = jnp.mean(values, axis=-1, keepdims=True)
    centered = values - center
    spread = jnp.mean(centered * centered, axis=-1, keepdims=True)
    return centered * lax.rsqrt(spread + epsilon) * gain_full + shift_full


def gelu_and_slope(values):
    turned = jnp.tanh(root_two_over_pi * (values + 0.044715 * values * values * values))
    slope = 0.5 * (1.0 + turned) + 0.5 * values * (1.0 - turned * turned) * root_two_over_pi * (
        1.0 + 3.0 * 0.044715 * values * values
    )
    return 0.5 * values * (1.0 + turned), slope


class Place:
    def __init__(self, sizes):
        self.chips = sizes["fsdp"] // 2
        self.halves = sizes["ctx"]
        self.depth = sizes["tp"]
        lane = lax.axis_index("fsdp")
        self.chip = lane // 2
        self.core = lane % 2
        self.half = lax.axis_index("ctx")
        self.layer = lax.axis_index("tp")

    def device(self, chip=None, core=None, half=None, layer=None):
        chip = self.chip if chip is None else chip
        core = self.core if core is None else core
        half = self.half if half is None else half
        layer = self.layer if layer is None else layer
        return (chip * 2 + core, half, layer)

    def block(self, chip=None, core=None, half=None):
        chip = self.chip if chip is None else chip
        core = self.core if core is None else core
        half = self.half if half is None else half
        return (chip * 2 + core) * self.halves + half

    def ahead(self, k):
        return (self.chip + k) % self.chips

    def behind(self, k):
        return (self.chip + self.chips - k) % self.chips

    def neighbours(self):
        last = self.depth - 1
        return (
            (self.layer < last, self.device(layer=jnp.minimum(self.layer + 1, last))),
            (self.layer > 0, self.device(layer=jnp.maximum(self.layer - 1, 0))),
        )

    def pair(self):
        return self.device(core=1 - self.core)

    def across(self):
        return self.device(half=1 - self.half)

    def group(self):
        found = []
        for k in range(self.chips):
            for core in range(2):
                for half in range(2):
                    if k or core or half:
                        found.append(
                            (self.ahead(k), (self.core + core) % 2, (self.half + half) % 2)
                        )
        return found


def greet(devices):
    barrier = pltpu.get_barrier_semaphore()
    for device in devices:
        pl.semaphore_signal(barrier, inc=1, device_id=device, device_id_type=MESH)
    pl.semaphore_wait(barrier, len(devices))


def greet_line(place, devices):
    barrier = pltpu.get_barrier_semaphore()
    for device in devices:
        pl.semaphore_signal(barrier, inc=1, device_id=device, device_id_type=MESH)
    count = len(devices)
    for there, device in place.neighbours():

        @pl.when(there)
        def _(device=device):
            pl.semaphore_signal(barrier, inc=1, device_id=device, device_id_type=MESH)

        count = count + there.astype(jnp.int32)
    pl.semaphore_wait(barrier, count)


def send(source, target, send_sem, recv_sem, device):
    return pltpu.make_async_remote_copy(
        src_ref=source,
        dst_ref=target,
        send_sem=send_sem,
        recv_sem=recv_sem,
        device_id=device,
        device_id_type=MESH,
    )


class Line:
    def __init__(self, place, own, full, send_sem, recv_sem, keep_sem):
        self.place, self.own, self.full = place, own, full
        self.send_sem, self.recv_sem = send_sem, recv_sem
        self.rows = own.shape[0]
        self.pending = []
        self.keep = pltpu.make_async_copy(own, self.block(place.layer), keep_sem)

    def block(self, source):
        return self.full.at[pl.ds(pl.multiple_of(source * self.rows, 16), self.rows)]

    def copy(self, piece, target, way, hop, device):
        return send(piece, target, self.send_sem.at[way, hop], self.recv_sem.at[way, hop], device)

    def launch(self, copy, condition):
        pl.when(condition)(copy.start)
        self.pending.append((copy, condition))

    def start(self):
        for way, (there, device) in enumerate(self.place.neighbours()):
            target = self.block(self.place.layer)
            self.launch(self.copy(self.own, target, way, 0, device), there)
        self.keep.start()

    def step(self, k):
        last = self.place.depth - 1
        for way, (onward, device) in enumerate(self.place.neighbours()):
            source = self.place.layer - k if way == 0 else self.place.layer + k
            there = (source >= 0) & (source <= last)
            piece = self.block(jnp.clip(source, 0, last))
            pl.when(there)(self.copy(piece, piece, way, k - 1, device).wait_recv)
            if k < last:
                self.launch(self.copy(piece, piece, way, k, device), there & onward)

    def end(self):
        for copy, condition in self.pending:
            pl.when(condition)(copy.wait_send)


def plane(place):
    found = [place.device(chip=place.ahead(k)) for k in range(1, place.chips)]
    return found + [place.across(), place.pair()]


def reduce(sizes, paired, turned, rights, small, collective_id, name):
    chips, halves = sizes["fsdp"] // 2, sizes["ctx"]
    groups = chips * halves
    paired_count, made_count = len(paired), len(rights)
    weight_count = paired_count + made_count
    whole_count = weight_count - 1
    block_rows = paired[0][0].shape[0] // (2 * groups)
    widths = [v.shape[1] for v, _ in paired] + [v.shape[0] for _, v in rights]
    sides = [turned[2 * a].shape[1] for a in range(paired_count)] + [block_rows // 2] * made_count

    def kernel(*refs):
        refs = list(refs)

        def take(count):
            taken = refs[:count]
            del refs[:count]
            return taken

        paired_in = [take(2) for _ in range(paired_count)]
        turned_in = take(2 * paired_count)
        lefts = [take(len(left)) for left, _ in rights]
        factors = take(made_count)
        small_in = take(len(small))
        weight_out = take(whole_count)
        small_outs = take(len(small))
        held_out, made = take(weight_count - whole_count), take(made_count)
        own, turn_a, turn_b = (take(weight_count) for _ in range(3))
        near = take(whole_count)
        pair = take(weight_count)
        load_sem, core_send, core_recv = take(3)
        turn_send, turn_recv, near_send, near_recv = take(4)
        small_ref, small_pair, small_near, small_far, small_send, small_recv = take(6)
        place = Place(sizes)
        greet(plane(place))
        pending = []

        def launch(copy, condition=None):
            if condition is None:
                copy.start()
            else:
                pl.when(condition)(copy.start)
            pending.append((copy, condition))

        other = 1 - place.core
        needed = [place.ahead(k) * halves + place.half for k in range(1, chips)]
        needed += [place.chip * halves + 1 - place.half, place.chip * halves + place.half]
        for a in range(paired_count):
            for at, number in enumerate(needed):
                chip = place.ahead(at + 1) if at < chips - 1 else place.chip
                half = 1 - place.half if at == chips - 1 else place.half
                mine = place.block(chip, place.core, half)
                pltpu.make_async_copy(
                    paired_in[a][0].at[pl.ds(pl.multiple_of(mine * block_rows, 16), block_rows)],
                    own[a].at[number],
                    load_sem.at[a, number],
                ).start()
                pltpu.make_async_copy(
                    paired_in[a][1].at[pl.ds(pl.multiple_of(number * block_rows, 16), block_rows)],
                    pair[a].at[at],
                    core_recv.at[a, number],
                ).start()
            for way, target in enumerate((turn_a[a], turn_b[a])):
                for k in range(1, chips):
                    pltpu.make_async_copy(
                        turned_in[2 * a + way].at[k - 1],
                        target.at[k - 1],
                        turn_recv.at[a, way, k],
                    ).start()

        def make(a):
            at = a - paired_count
            first = 0
            for left in lefts[at]:
                span = pl.ds(first, left.shape[1])
                multiply("tt", [(left, factors[at])], [made[at].at[span]])
                first += left.shape[1]
            for number in range(groups):
                chip, half = number // halves, number % halves
                theirs = place.block(chip, other, half)
                mine = place.block(chip, place.core, half)
                launch(
                    send(
                        made[at].at[pl.ds(pl.multiple_of(theirs * block_rows, 16), block_rows)],
                        pair[a].at[number],
                        core_send.at[a, number],
                        core_recv.at[a, number],
                        place.pair(),
                    )
                )
                pltpu.make_async_copy(
                    made[at].at[pl.ds(pl.multiple_of(mine * block_rows, 16), block_rows)],
                    own[a].at[number],
                    load_sem.at[a, number],
                ).start()

        def pair_sum(a, number, at_needed=None):
            mine = own[a].at[number]
            pltpu.make_async_copy(mine, mine, load_sem.at[a, number]).wait()
            if a < paired_count:
                theirs = pair[a].at[at_needed]
                pltpu.make_async_copy(theirs, theirs, core_recv.at[a, number]).wait()
            else:
                theirs = pair[a].at[number]
                send(
                    theirs, theirs, core_send.at[a, number], core_recv.at[a, number], place.pair()
                ).wait_recv()

            @pl.loop(0, block_rows, step=16)
            def _(r):
                at = pl.ds(pl.multiple_of(r, 16), 16)
                mine[at, :] = (mine[at, :].astype(f32) + theirs[at, :].astype(f32)).astype(bf16)

        def diagonal(a):
            for k in range(1, chips):
                number = place.ahead(k) * halves + 1 - place.half
                pair_sum(a, number)
                launch(
                    send(
                        own[a].at[number, pl.ds(0, sides[a])],
                        turn_a[a].at[k - 1],
                        turn_send.at[a, 0, k],
                        turn_recv.at[a, 0, k],
                        place.across(),
                    )
                )
                launch(
                    send(
                        own[a].at[number, pl.ds(sides[a], block_rows - sides[a])],
                        turn_b[a].at[k - 1],
                        turn_send.at[a, 1, k],
                        turn_recv.at[a, 1, k],
                        place.device(chip=place.ahead(k)),
                    )
                )

        def direct_pairs(a):
            for k in range(1, chips):
                pair_sum(a, place.ahead(k) * halves + place.half, k - 1)
            pair_sum(a, place.chip * halves + 1 - place.half, chips - 1)

        def add_turn(a, number, first, count, refs_at):
            @pl.loop(0, count, step=16)
            def _(r):
                at = pl.ds(pl.multiple_of(first + r, 16), 16)
                total = own[a][number, at, :].astype(f32)
                for ref, k in refs_at:
                    total += ref[k, pl.ds(pl.multiple_of(r, 16), 16), :].astype(f32)
                own[a][number, at, :] = total.astype(bf16)

        def turn_wait(a, way, k):
            piece = (turn_a, turn_b)[way][a].at[k - 1]
            if a < paired_count:
                pltpu.make_async_copy(piece, piece, turn_recv.at[a, way, k]).wait()
            else:
                send(
                    piece, piece, turn_send.at[a, way, k], turn_recv.at[a, way, k], place.across()
                ).wait_recv()

        def hand(a, at, number):
            pltpu.make_async_copy(
                own[a].at[number], held_out[a - whole_count].at[at], near_send.at[a, at]
            ).start()

        def direct(a):
            for k in range(1, chips):
                number = place.ahead(k) * halves + place.half
                turn_wait(a, 0, k)
                add_turn(a, number, 0, sides[a], [(turn_a[a], k - 1)])
                if a >= whole_count:
                    hand(a, k, number)
                    continue
                launch(
                    send(
                        own[a].at[number],
                        near[a].at[k],
                        near_send.at[a, k],
                        near_recv.at[a, k],
                        place.device(chip=place.ahead(k)),
                    )
                )
            for k in range(1, chips):
                turn_wait(a, 1, k)
            number = place.chip * halves + 1 - place.half
            add_turn(
                a,
                number,
                sides[a],
                block_rows - sides[a],
                [(turn_b[a], k - 1) for k in range(1, chips)],
            )
            if a >= whole_count:
                hand(a, 0, number)
                return
            launch(
                send(
                    own[a].at[number],
                    near[a].at[0],
                    near_send.at[a, 0],
                    near_recv.at[a, 0],
                    place.across(),
                )
            )

        def finish(a):
            for k in range(chips):
                piece = near[a].at[k]
                send(
                    piece, piece, near_send.at[a, k], near_recv.at[a, k], place.across()
                ).wait_recv()
            number = place.chip * halves + place.half

            @pl.loop(0, block_rows, step=16)
            def _(r):
                at = pl.ds(pl.multiple_of(r, 16), 16)
                total = own[a][number, at, :].astype(f32)
                for k in range(chips):
                    total += near[a][k, at, :].astype(f32)
                weight_out[a][at, :] = total

        def swap_small(source, target, at, device):
            copy = send(source, target, small_send.at[at], small_recv.at[at], device)
            launch(copy)
            return copy

        small_ref[...] = jnp.zeros_like(small_ref)
        first = 0
        for ref in small_in:
            small_ref[first : first + ref.shape[0], : ref.shape[1]] = ref[...]
            first += ref.shape[0]
        swap_small(small_ref, small_pair, 0, place.pair())
        for a in range(paired_count):
            direct_pairs(a)
            direct(a)
        for a in range(paired_count, weight_count):
            make(a)
        send(small_pair, small_pair, small_send.at[0], small_recv.at[0], place.pair()).wait_recv()
        small_near[0] = small_ref[...] + small_pair[...]
        for k in range(1, chips):
            swap_small(small_near.at[0], small_near.at[k], k, place.device(chip=place.ahead(k)))
        for a in range(paired_count, weight_count):
            diagonal(a)
            direct_pairs(a)
        total = small_near[0]
        for k in range(1, chips):
            piece = small_near.at[k]
            send(piece, piece, small_send.at[k], small_recv.at[k], place.pair()).wait_recv()
            total += small_near[k]
        small_far[0] = total
        swap_small(small_far.at[0], small_far.at[1], chips, place.across())
        for a in range(weight_count):
            pair_sum(a, place.chip * halves + place.half, chips)
        for a in range(paired_count, weight_count):
            direct(a)
            if a >= whole_count:
                hand(a, chips, place.chip * halves + place.half)
        for a in range(whole_count):
            finish(a)
        for a in range(whole_count, weight_count):
            for at in range(chips + 1):
                piece = held_out[a - whole_count].at[at]
                pltpu.make_async_copy(piece, piece, near_send.at[a, at]).wait()
        piece = small_far.at[1]
        send(piece, piece, small_send.at[chips], small_recv.at[chips], place.pair()).wait_recv()
        total = small_far[0] + small_far[1]
        first = 0
        for ref in small_outs:
            ref[...] = total[first : first + ref.shape[0], : ref.shape[1]]
            first += ref.shape[0]
        for copy, condition in pending:
            if condition is None:
                copy.wait_send()
            else:
                pl.when(condition)(copy.wait_send)

    shapes = [jax.ShapeDtypeStruct((block_rows, w), f32) for w in widths[:whole_count]]
    small_shape = (8, max(v.shape[1] for v in small))
    shapes += [jax.ShapeDtypeStruct(v.shape, f32) for v in small]
    held_shapes = [
        jax.ShapeDtypeStruct((chips + 1, block_rows, w), bf16) for w in widths[whole_count:]
    ]
    made_shapes = [
        jax.ShapeDtypeStruct((2 * groups * block_rows, w), bf16) for w in widths[paired_count:]
    ]
    scratch = [pltpu.VMEM((groups, block_rows, w), bf16) for w in widths]
    scratch += [pltpu.VMEM((chips - 1, n, w), bf16) for w, n in zip(widths, sides)]
    scratch += [pltpu.VMEM((chips - 1, block_rows - n, w), bf16) for w, n in zip(widths, sides)]
    scratch += [pltpu.VMEM((chips, block_rows, w), bf16) for w in widths[:whole_count]]
    scratch += [pltpu.VMEM((chips + 1, block_rows, w), bf16) for w in widths[:paired_count]]
    scratch += [pltpu.VMEM((groups, block_rows, w), bf16) for w in widths[paired_count:]]
    scratch += [
        DMA((weight_count, groups)),
        DMA((weight_count, groups)),
        DMA((weight_count, groups)),
        DMA((weight_count, 2, chips)),
        DMA((weight_count, 2, chips)),
        DMA((weight_count, chips + 1)),
        DMA((weight_count, chips + 1)),
        pltpu.VMEM(small_shape, f32),
        pltpu.VMEM(small_shape, f32),
        pltpu.VMEM((chips,) + small_shape, f32),
        pltpu.VMEM((2,) + small_shape, f32),
        DMA((chips + 1,)),
        DMA((chips + 1,)),
    ]
    lefts = [v for left, _ in rights for v in left]
    factors = [v for _, v in rights]
    return pl.pallas_call(
        kernel,
        out_shape=tuple(shapes + held_shapes + made_shapes),
        in_specs=[ANY] * (4 * paired_count + len(lefts) + made_count) + [VMEM] * len(small),
        out_specs=(VMEM,) * (whole_count + len(small))
        + (ANY,) * (weight_count - whole_count + made_count),
        scratch_shapes=scratch,
        compiler_params=pltpu.CompilerParams(
            collective_id=collective_id, has_side_effects=True, vmem_limit_bytes=60 << 20
        ),
        cost_estimate=pl.CostEstimate(flops=0, bytes_accessed=400_000_000, transcendentals=0),
        name=name,
    )(*[v for two in paired for v in two], *turned, *lefts, *factors, *small)[
        : weight_count + len(small)
    ]


def multiply(kind, parts, outs, finish=None, extra=(), tile=512):
    dims = (((0 if kind[0] == "t" else 1,), (1 if kind[1] == "t" else 0,)), ((), ()))
    left, right = parts[0]
    rows = left.shape[1] if kind[0] == "t" else left.shape[0]
    width = right.shape[0] if kind[1] == "t" else right.shape[1]
    tile = min(tile, width)
    specs = []
    for left, right in parts:
        specs.append(pl.BlockSpec(left.shape, lambda n: (0, 0)))
        if kind[1] == "t":
            specs.append(pl.BlockSpec((tile, right.shape[1]), lambda n: (n, 0)))
        else:
            specs.append(pl.BlockSpec((right.shape[0], tile), lambda n: (0, n)))
    specs += [pl.BlockSpec((v.shape[0], tile), lambda n: (0, n)) for v in extra]

    def step(*refs):
        found = None
        for number in range(len(parts)):
            product = lax.dot_general(
                refs[2 * number][...],
                refs[2 * number + 1][...],
                dims,
                preferred_element_type=f32,
            )
            found = product if found is None else found + product
        rest = refs[2 * len(parts) :]
        results = (found,)
        if finish is not None:
            results = finish(found, *(v[...] for v in rest[: len(extra)]))
        for ref, value in zip(rest[len(extra) :], results):
            ref[...] = value.astype(ref.dtype)

    factors = [v for pair in parts for v in pair]
    pltpu.emit_pipeline(
        step,
        grid=(width // tile,),
        in_specs=specs,
        out_specs=[pl.BlockSpec((v.shape[0], tile), lambda n: (0, n)) for v in outs],
    )(*factors, *extra, *outs)


def half_rows(ref, half, count):
    return ref.at[pl.ds(pl.multiple_of(half * count, count), count)]


def front(sizes, tokens, cotangent, vectors, numbers, weights, projection_bias, up_bias):
    chips, halves, depth = sizes["fsdp"] // 2, sizes["ctx"], sizes["tp"]
    groups = sizes["fsdp"] * halves
    own_len, model = tokens.shape
    length = own_len * depth
    projection, up, dense, down = weights
    weight_count = len(weights)
    kinds, local = projection.shape[0], projection.shape[2]
    count = local // 2
    hidden = up.shape[1]
    shard = vectors[0].shape[0]
    half_rot = ROT // 2
    early_width = model // 4 * 3
    first_width = model // 8

    def kernel(*refs):
        refs = list(refs)

        def take(number):
            taken = refs[:number]
            del refs[:number]
            return taken

        tokens_ref, cotangent_ref = take(2)
        vector_in, number_in = take(len(vectors)), take(len(numbers))
        weight_in = take(weight_count)
        bias_in, up_bias_in = take(2)
        vectors_out, *numbers_out = take(1 + len(numbers))
        normed, cotangent_rows, cotangent_late = take(3)
        weight_out = take(weight_count)
        both, activation, slope, triple = take(4)
        landed, normed_own, stage, vector_ref, bias_ref, up_bias_ref, cosine_ref, sine_ref = take(8)
        vector_send, vector_recv, number_sems, single, line_send, line_recv = take(6)
        keep, near_send, near_recv, turn_send, turn_recv, core_send, core_recv = take(7)
        place = Place(sizes)
        peers = place.group()
        greet_line(place, [place.device(chip=a, core=b, half=c) for a, b, c in peers])
        pending = []

        def launch(copy):
            copy.start()
            pending.append(copy)

        def part(a, block, first=0, rows=None):
            rows = weight_in[a].shape[-2] if rows is None else rows
            start = pl.multiple_of(block * weight_in[a].shape[-2] + first, 16)
            span = pl.ds(start, rows)
            return weight_out[a].at[:, span] if a == 0 else weight_out[a].at[span]

        def arrive(piece, recv_sem):
            send(piece, piece, recv_sem, recv_sem, place.pair()).wait_recv()

        mine = place.block()
        vector_ref[...] = jnp.zeros_like(vector_ref)
        for row, ref in enumerate(vector_in):
            vector_ref[row : row + 1, :] = ref[...].astype(f32).reshape(1, shard)
        vector_keep = pltpu.make_async_copy(vector_ref, landed.at[mine], single.at[0])
        vector_keep.start()
        for at, (chip, core, half) in enumerate(peers):
            launch(
                send(
                    vector_ref,
                    landed.at[mine],
                    vector_send.at[at],
                    vector_recv.at[at],
                    place.device(chip=chip, core=core, half=half),
                )
            )
        for number in range(len(numbers)):
            launch(
                send(
                    number_in[number],
                    numbers_out[number],
                    number_sems.at[0, number],
                    number_sems.at[1, number],
                    place.across(),
                )
            )

        def near_start(a):
            own = part(a, place.block())
            for k in range(1, chips):
                launch(
                    send(
                        weight_in[a],
                        own,
                        near_send.at[a, k],
                        near_recv.at[a, k],
                        place.device(chip=place.ahead(k)),
                    )
                )
            launch(
                send(weight_in[a], own, near_send.at[a, 0], near_recv.at[a, 0], place.across())
            )
            launch(send(weight_in[a], own, core_send.at[a, 0], core_recv.at[a, 0], place.pair()))
            pltpu.make_async_copy(weight_in[a], own, keep.at[a]).start()

        def near_step(a):
            side = weight_in[a].shape[-2] // 4
            rest = weight_in[a].shape[-2] - side
            for k in range(1, chips):
                block = place.block(chip=place.behind(k))
                piece = part(a, block)
                arrive(piece, near_recv.at[a, k])
                top = part(a, block, 0, side)
                launch(
                    send(top, top, turn_send.at[a, 0, k], turn_recv.at[a, 0, k], place.across())
                )
                launch(send(piece, piece, core_send.at[a, k], core_recv.at[a, k], place.pair()))
            block = place.block(half=1 - place.half)
            piece = part(a, block)
            arrive(piece, near_recv.at[a, 0])
            low = part(a, block, side, rest)
            for k in range(1, chips):
                launch(
                    send(
                        low,
                        low,
                        turn_send.at[a, 1, k],
                        turn_recv.at[a, 1, k],
                        place.device(chip=place.ahead(k)),
                    )
                )
            launch(
                send(piece, piece, core_send.at[a, chips], core_recv.at[a, chips], place.pair())
            )

        def turn_step(a):
            side = weight_in[a].shape[-2] // 4
            rest = weight_in[a].shape[-2] - side
            for k in range(1, chips):
                block = place.block(chip=place.behind(k), half=1 - place.half)
                arrive(part(a, block, 0, side), turn_recv.at[a, 0, k])
                arrive(part(a, block, side, rest), turn_recv.at[a, 1, k])
                piece = part(a, block)
                launch(
                    send(
                        piece,
                        piece,
                        core_send.at[a, chips + k],
                        core_recv.at[a, chips + k],
                        place.pair(),
                    )
                )

        def core_step(a):
            other = 1 - place.core
            blocks = [place.block(core=other)]
            blocks += [place.block(place.behind(k), other) for k in range(1, chips)]
            blocks += [place.block(None, other, 1 - place.half)]
            blocks += [
                place.block(place.behind(k), other, 1 - place.half) for k in range(1, chips)
            ]
            for at, block in enumerate(blocks):
                arrive(part(a, block), core_recv.at[a, at])
            pltpu.make_async_copy(weight_in[a], part(a, place.block()), keep.at[a]).wait()

        near_start(0)
        rest_width = early_width - first_width
        early = cotangent_ref.at[:, pl.ds(first_width, rest_width)]
        early_rows = cotangent_rows.at[:, pl.ds(first_width, rest_width)]
        first = cotangent_ref.at[:, pl.ds(0, first_width)]
        first_rows = cotangent_rows.at[:, pl.ds(0, first_width)]
        lines = (
            Line(place, normed_own, normed, line_send.at[0], line_recv.at[0], single.at[3]),
            Line(place, early, early_rows, line_send.at[1], line_recv.at[1], single.at[8]),
            Line(place, first, first_rows, line_send.at[2], line_recv.at[2], single.at[2]),
        )
        lines[2].start()

        vector_keep.wait()
        for at in range(len(peers)):
            place_in = at + 1
            source = place.block(
                place.behind(place_in // 4),
                (place.core + place_in // 2 % 2) % 2,
                (place.half + place_in % 2) % 2,
            )
            arrive(landed.at[source], vector_recv.at[at])
        for number in range(groups):
            vectors_out[:, number * shard : (number + 1) * shard] = landed[number]

        @pl.loop(0, own_len, step=32)
        def _(r):
            at = pl.ds(pl.multiple_of(r, 32), 32)
            values = tokens_ref[at, :].astype(f32)
            normed_own[at, :] = layer_norm(
                values, vectors_out[0:1, :], vectors_out[1:2, :]
            ).astype(bf16)

        lines[2].step(1)
        lines[0].start()
        near_start(1)
        late_keep = pltpu.make_async_copy(
            cotangent_ref.at[:, pl.ds(early_width, model - early_width)],
            cotangent_late,
            single.at[1],
        )
        late_keep.start()
        bias_ref[...] = bias_in[...].astype(f32).T
        up_bias_ref[...] = up_bias_in[...].astype(f32).reshape(1, hidden)
        turns = lax.broadcasted_iota(jnp.int32, (half_rot, 1), 0)
        inverse = jnp.zeros((half_rot, 1), f32)
        for row in range(half_rot):
            inverse = jnp.where(turns == row, 10000.0 ** (-2.0 * row / ROT), inverse)
        phase = inverse * number_in[1][...].astype(f32)
        cosine_ref[...] = jnp.cos(phase)
        sine_ref[...] = jnp.sin(phase)
        if depth > 2:
            lines[2].step(2)
        near_step(0)
        lines[0].step(1)
        for k in range(3, depth):
            lines[2].step(k)
        near_start(3)
        near_start(2)
        turn_step(0)
        near_step(1)
        for k in range(2, depth):
            lines[0].step(k)
        lines[1].start()
        lines[0].keep.wait()
        core_step(0)
        near_step(3)

        def project(weight, rows, cosine_here, sine_here, out):
            for kind in range(kinds):
                found = lax.dot_general(
                    weight[kind], rows[...], row_by_col, preferred_element_type=f32
                )
                found = found + bias_ref[:, kind : kind + 1]
                if kind == 2:
                    out[kind] = found.astype(bf16)
                    continue
                for head in range(local // HD):
                    first = head * HD
                    leading = found[first : first + half_rot]
                    trailing = found[first + half_rot : first + ROT]
                    turned = (
                        leading * cosine_here[...] - trailing * sine_here[...],
                        trailing * cosine_here[...] + leading * sine_here[...],
                        found[first + ROT : first + HD],
                    )
                    out[kind, first : first + HD] = jnp.concatenate(turned, axis=0).astype(bf16)

        tile = min(512, length)
        pltpu.emit_pipeline(
            project,
            grid=(length // tile,),
            in_specs=[
                pl.BlockSpec(weight_out[0].shape, lambda n: (0, 0, 0)),
                pl.BlockSpec((tile, model), lambda n: (n, 0)),
                pl.BlockSpec((half_rot, tile), lambda n: (0, n)),
                pl.BlockSpec((half_rot, tile), lambda n: (0, n)),
            ],
            out_specs=[pl.BlockSpec((kinds, local, tile), lambda n: (0, 0, n))],
        )(weight_out[0], normed, cosine_ref, sine_ref, triple)

        def heads(half):
            return triple.at[:, pl.ds(pl.multiple_of(half * count, count), count)]

        here, there = place.half, 1 - place.half
        launch(send(heads(there), both.at[here], single.at[4], single.at[5], place.across()))
        load = pltpu.make_async_copy(heads(here), stage, single.at[6])
        load.start()
        load.wait()
        stage_keep = pltpu.make_async_copy(stage, both.at[here], single.at[7])
        stage_keep.start()
        near_step(2)
        lines[1].step(1)
        turn_step(1)
        core_step(1)
        wide = hidden // 2
        for number in range(2):
            span = pl.ds(number * wide, wide)
            multiply(
                "nn",
                [(normed, weight_out[1].at[:, span])],
                [activation.at[:, span], slope.at[:, span]],
                lambda found, bias: gelu_and_slope(found + bias),
                [up_bias_ref.at[:, span]],
            )
            if number == 0 and depth > 2:
                lines[1].step(2)
        turn_step(3)
        core_step(3)
        turn_step(2)
        core_step(2)
        for k in range(3, depth):
            lines[1].step(k)
        lines[1].keep.wait()
        lines[2].keep.wait()
        stage_keep.wait()
        arrive(both.at[there], single.at[5])
        for number in range(len(numbers)):
            arrive(numbers_out[number], number_sems.at[1, number])
        late_keep.wait()
        for copy in pending:
            copy.wait_send()
        for run in lines:
            run.end()

    out_shape = [
        jax.ShapeDtypeStruct((8, groups * shard), f32),
        *[jax.ShapeDtypeStruct(v.shape, v.dtype) for v in numbers],
        jax.ShapeDtypeStruct((length, model), bf16),
        jax.ShapeDtypeStruct((length, early_width), bf16),
        jax.ShapeDtypeStruct((own_len, model - early_width), bf16),
    ]
    out_shape += [
        jax.ShapeDtypeStruct(v.shape[:-2] + (groups * v.shape[-2], v.shape[-1]), v.dtype)
        for v in weights
    ]
    out_shape += [
        jax.ShapeDtypeStruct((2, kinds, count, length), bf16),
        jax.ShapeDtypeStruct((length, hidden), bf16),
        jax.ShapeDtypeStruct((length, hidden), bf16),
        jax.ShapeDtypeStruct((kinds, local, length), bf16),
    ]
    results = pl.pallas_call(
        kernel,
        out_shape=tuple(out_shape),
        in_specs=[VMEM] * (4 + len(vectors) + len(numbers) + weight_count),
        out_specs=(VMEM,) * (1 + len(numbers)) + (ANY,) * (len(out_shape) - 1 - len(numbers)),
        scratch_shapes=[
            pltpu.VMEM((groups, 8, shard), f32),
            pltpu.VMEM((own_len, model), bf16),
            pltpu.VMEM((kinds, count, length), bf16),
            pltpu.VMEM((8, shard), f32),
            pltpu.VMEM((local, kinds), f32),
            pltpu.VMEM((1, hidden), f32),
            pltpu.VMEM((half_rot, length), f32),
            pltpu.VMEM((half_rot, length), f32),
            DMA((groups - 1,)),
            DMA((groups - 1,)),
            DMA((2, len(numbers))),
            DMA((9,)),
            DMA((3, 2, depth - 1)),
            DMA((3, 2, depth - 1)),
            DMA((weight_count,)),
            DMA((weight_count, chips)),
            DMA((weight_count, chips)),
            DMA((weight_count, 2, chips)),
            DMA((weight_count, 2, chips)),
            DMA((weight_count, 2 * chips)),
            DMA((weight_count, 2 * chips)),
        ],
        compiler_params=pltpu.CompilerParams(
            collective_id=0, has_side_effects=True, vmem_limit_bytes=60 << 20
        ),
        cost_estimate=pl.CostEstimate(flops=0, bytes_accessed=480_000_000, transcendentals=0),
        name="front",
    )(tokens, cotangent, *vectors, *numbers, *weights, projection_bias, up_bias)
    return results[:-1]


class Held:
    def __init__(self, sources, buffers, sems):
        self.copies = {}
        self.buffers = buffers
        for number, (source, buffer) in enumerate(zip(sources, buffers)):
            copy = pltpu.make_async_copy(source, buffer, sems.at[number])
            copy.start()
            self.copies[number] = copy

    def __getitem__(self, number):
        if number in self.copies:
            self.copies.pop(number).wait()
        return self.buffers[number]


def buffers_for(*arrays):
    return [pltpu.VMEM(v.shape, v.dtype) for v in arrays]


def exchange_middle(
    sizes, attended, activation, down_full, dense_full, cotangent_early, late_blocks, slope
):
    width, total = attended.shape
    length = total // 2
    rows, model = activation.shape[0], down_full.shape[0]
    hidden = slope.shape[1]
    depth = sizes["tp"]
    late_rows, late_width = late_blocks[0].shape
    holds = [activation, down_full, dense_full, cotangent_early, slope]

    def kernel(attended_ref, *refs):
        late_refs, refs = refs[:depth], refs[depth:]
        held_refs, refs = refs[: len(holds)], refs[len(holds) :]
        full_out, block_out, late_out, both, grad_hidden, hidden_sum = refs[:6]
        full, feed, late, made, *buffers, sems, held_sems, late_sems = refs[6:]
        place = Place(sizes)
        here, there = place.half, 1 - place.half

        def tokens(half):
            return attended_ref.at[:, pl.ds(pl.multiple_of(half * length, length), length)]

        mine = half_rows(full, here, width)
        load = pltpu.make_async_copy(tokens(here), mine, sems.at[0])
        load.start()
        held = Held(held_refs, buffers, held_sems)
        late_loads = []
        for k in range(depth):
            source = (place.layer + depth - k) % depth
            span = pl.ds(pl.multiple_of(source * late_rows, 16), late_rows)
            late_loads.append(pltpu.make_async_copy(late_refs[k], late.at[span], late_sems.at[k]))
            late_loads[-1].start()
        greet([place.across()])
        away = send(tokens(there), mine, sems.at[2], sems.at[3], place.across())
        away.start()
        multiply("nt", [(held[0], held[1])], [feed])
        load.wait()
        away.wait_send()
        came = half_rows(full, there, width)
        send(came, came, sems.at[2], sems.at[3], place.across()).wait_recv()
        full_keep = pltpu.make_async_copy(full, full_out, sems.at[4])
        full_keep.start()
        multiply(
            "tt",
            [(full, held[2])],
            [block_out],
            lambda found, before: (found + before,),
            [feed],
        )
        for copy in late_loads:
            copy.wait()
        late_keep = pltpu.make_async_copy(late, late_out, sems.at[5])
        late_keep.start()

        def parts(weight):
            first = model - late_width
            return [
                (held[3], weight.at[pl.ds(0, first)]),
                (late, weight.at[pl.ds(first, late_width)]),
            ]

        multiply("tt", [(b, a) for a, b in parts(held[2])], [made])
        away = send(
            half_rows(made, there, width), both.at[here], sems.at[6], sems.at[7], place.across()
        )
        keep = pltpu.make_async_copy(half_rows(made, here, width), both.at[here], sems.at[8])
        away.start()
        keep.start()

        def scaled(found, slope):
            found = found * slope.astype(f32)
            return found, jnp.sum(found, axis=0, keepdims=True)

        multiply("nn", parts(held[1]), [grad_hidden, hidden_sum], scaled, [held[4]])
        for copy in (keep, full_keep, late_keep):
            copy.wait()
        away.wait_send()
        came = both.at[there]
        send(came, came, sems.at[6], sems.at[7], place.across()).wait_recv()

    return pl.pallas_call(
        kernel,
        out_shape=(
            jax.ShapeDtypeStruct((2 * width, length), bf16),
            jax.ShapeDtypeStruct((rows, model), bf16),
            jax.ShapeDtypeStruct((rows, late_width), bf16),
            jax.ShapeDtypeStruct((2, width, length), bf16),
            jax.ShapeDtypeStruct((rows, hidden), bf16),
            jax.ShapeDtypeStruct((1, hidden), f32),
        ),
        in_specs=[ANY] * (1 + depth + len(holds)),
        out_specs=(ANY,) * 5 + (VMEM,),
        scratch_shapes=[
            pltpu.VMEM((2 * width, length), bf16),
            pltpu.VMEM((rows, model), f32),
            pltpu.VMEM((rows, late_width), bf16),
            pltpu.VMEM((2 * width, length), bf16),
            *buffers_for(*holds),
            DMA((9,)),
            DMA((len(holds),)),
            DMA((depth,)),
        ],
        compiler_params=pltpu.CompilerParams(
            collective_id=4, has_side_effects=True, vmem_limit_bytes=60 << 20
        ),
        cost_estimate=pl.CostEstimate(flops=0, bytes_accessed=140_000_000, transcendentals=0),
        name="exchange_middle",
    )(attended, *late_blocks, *holds)


def exchange_back(sizes, back, normed, grad_hidden, cotangents, activation, up_full, projection):
    kinds, width, total = back.shape
    length = total // 2
    chips, halves = sizes["fsdp"] // 2, sizes["ctx"]
    rows, model = normed.shape
    hidden = grad_hidden.shape[1]
    span = model // (2 * chips)
    shard = span // halves
    sides = (shard // 4, shard // 2)
    count = len(cotangents)

    def kernel(back_ref, *rest):
        held_refs, rest = rest[: 4 + count], rest[4 + count :]
        weight_ref, full_out, made, came, turns, block_in, feed = (
            rest[0],
            rest[1],
            rest[2:4],
            rest[4:6],
            rest[6:10],
            rest[10],
            rest[11],
        )
        sums, full, diagonal, stage = rest[12:16]
        normed_held, hidden_held, cotangent_held, activation_held, up_held = rest[16:21]
        held_sems, sems, stage_sems, core_send, core_recv, turn_send, turn_recv = rest[21:]
        buffers, first = [normed_held, hidden_held], 0
        for ref in held_refs[2 : 2 + count]:
            buffers.append(cotangent_held.at[:, pl.ds(first, ref.shape[1])])
            first += ref.shape[1]
        held = Held(held_refs, buffers + [activation_held, up_held], held_sems)
        place = Place(sizes)
        here, there = place.half, 1 - place.half
        other = 1 - place.core

        def tokens(half):
            return back_ref.at[:, :, pl.ds(pl.multiple_of(half * length, length), length)]

        def heads(half):
            return full.at[:, pl.ds(pl.multiple_of(half * width, width), width)]

        load = pltpu.make_async_copy(tokens(here), heads(here), sems.at[2])
        load.start()
        greet(plane(place))
        away = send(tokens(there), heads(here), sems.at[0], sems.at[1], place.across())
        away.start()

        def to_pair(number):
            copies = []
            for chip in range(chips):
                copies.append(
                    send(
                        made[number].at[pl.ds(pl.multiple_of((2 * chip + other) * span, 16), span)],
                        came[number].at[pl.ds(chip * span, span)],
                        core_send.at[number, chip],
                        core_recv.at[number, chip],
                        place.pair(),
                    )
                )
                copies[-1].start()
            return copies

        def stage_loads(number, k):
            chip = place.ahead(k)
            mine = place.block(chip, place.core, there) * shard
            theirs = (chip * halves + there) * shard
            return [
                pltpu.make_async_copy(
                    ref.at[pl.ds(pl.multiple_of(block, 16), shard)],
                    stage.at[at, k - 1],
                    stage_sems.at[at, k],
                )
                for at, (ref, block) in enumerate(((made[number], mine), (came[number], theirs)))
            ]

        def turn_load(number, copies):
            for copy in copies:
                copy.wait()
            for k in range(1, chips):
                for copy in stage_loads(number, k):
                    copy.start()

        def turn(number):
            sent = []
            step = min(64, shard)
            for k in range(1, chips):
                for copy in stage_loads(number, k):
                    copy.wait()

                @pl.loop(0, shard, step=step)
                def _(r):
                    at = pl.ds(pl.multiple_of(r, step), step)
                    diagonal[number, k - 1, at, :] = (
                        stage[0, k - 1, at, :].astype(f32) + stage[1, k - 1, at, :].astype(f32)
                    ).astype(bf16)

                for way, device in enumerate(
                    (place.across(), place.device(chip=place.ahead(k)))
                ):
                    side = sides[number]
                    part = pl.ds(0, side) if way == 0 else pl.ds(side, shard - side)
                    sent.append(
                        send(
                            diagonal.at[number, k - 1, part],
                            turns[2 * number + way].at[k - 1],
                            turn_send.at[number, way, k],
                            turn_recv.at[number, way, k],
                            device,
                        )
                    )
                    sent[-1].start()
            return sent

        multiply("tn", [(held[0], held[1])], [made[0]])
        up_copies = to_pair(0)
        for number in range(count):
            held[2 + number]
        half = hidden // 2
        for number in range(2):
            part = pl.ds(number * half, half)
            multiply(
                "tn",
                [(cotangent_held, held[2 + count].at[:, part])],
                [made[1].at[:, part]],
            )
            if number == 0:
                turn_load(0, up_copies)
                turned = turn(0)
        down_copies = to_pair(1)
        half = model // 2
        for number in range(2):
            part = pl.ds(number * half, half)
            multiply("nt", [(held[1], held[3 + count].at[part])], [feed.at[:, part]])
            if number == 0:
                turn_load(1, down_copies)
                turned += turn(1)
        load.wait()
        away.wait_send()
        send(heads(there), heads(there), sems.at[0], sems.at[1], place.across()).wait_recv()
        keep = pltpu.make_async_copy(full, full_out, sems.at[3])
        keep.start()
        ones = jnp.ones((8, length), bf16)
        for kind in range(kinds):
            total_of = lax.dot_general(ones, full[kind], contract_cols, preferred_element_type=f32)
            sums[kind : kind + 1, :] = total_of[0:1, :]

        def step(right_ref, before_ref, out_ref):
            found = before_ref[...]
            for kind in range(kinds):
                found += lax.dot_general(
                    full[kind], right_ref[kind], row_by_col, preferred_element_type=f32
                )
            out_ref[...] = found.astype(bf16)

        tile = min(512, model)
        pltpu.emit_pipeline(
            step,
            grid=(model // tile,),
            in_specs=[
                pl.BlockSpec((kinds, tile, 2 * width), lambda n: (0, n, 0)),
                pl.BlockSpec((rows, tile), lambda n: (0, n)),
            ],
            out_specs=[pl.BlockSpec((rows, tile), lambda n: (0, n))],
        )(weight_ref, feed, block_in)
        keep.wait()
        for copy in turned:
            copy.wait()

    product = jax.ShapeDtypeStruct((model, hidden), bf16)
    part = jax.ShapeDtypeStruct((model // 2, hidden), bf16)
    holds = [normed, grad_hidden, *cotangents, activation, up_full]
    results = pl.pallas_call(
        kernel,
        out_shape=(
            jax.ShapeDtypeStruct((kinds, 2 * width, length), bf16),
            product,
            product,
            part,
            part,
            *[
                jax.ShapeDtypeStruct((chips - 1, n, hidden), bf16)
                for side in sides
                for n in (side, shard - side)
            ],
            jax.ShapeDtypeStruct((rows, model), bf16),
            jax.ShapeDtypeStruct((rows, model), f32),
            jax.ShapeDtypeStruct((kinds, 2 * width), f32),
        ),
        in_specs=[ANY] * (len(holds) + 2),
        out_specs=(ANY,) * 11 + (VMEM,),
        scratch_shapes=[
            pltpu.VMEM((kinds, 2 * width, length), bf16),
            pltpu.VMEM((2, chips - 1, shard, hidden), bf16),
            pltpu.VMEM((2, chips - 1, shard, hidden), bf16),
            *buffers_for(normed, grad_hidden, normed, activation, up_full),
            DMA((len(holds),)),
            DMA((4,)),
            DMA((2, chips)),
            DMA((2, chips)),
            DMA((2, chips)),
            DMA((2, 2, chips)),
            DMA((2, 2, chips)),
        ],
        compiler_params=pltpu.CompilerParams(
            collective_id=5, has_side_effects=True, vmem_limit_bytes=60 << 20
        ),
        cost_estimate=pl.CostEstimate(flops=0, bytes_accessed=180_000_000, transcendentals=0),
        name="exchange_back",
    )(back, *holds, projection)
    full, up_made, down_made, up_came, down_came, *turned = results[:9]
    paired = [(up_made, up_came), (down_made, down_came)]
    return full, paired, turned, results[9], results[11]


def finish_all(sizes, grad, tokens, cotangent, vectors, partials, splits):
    chips, halves, depth = sizes["fsdp"] // 2, sizes["ctx"], sizes["tp"]
    groups = sizes["fsdp"] * halves
    own_len, model = tokens.shape
    shard = model // groups
    count = len(partials)
    step_rows = 64

    def kernel(grad_ref, tokens_ref, cotangent_ref, vector_ref, *refs):
        partial_in, refs = refs[:count], refs[count:]
        input_ref, small_ref = refs[:2]
        weight_out, refs = refs[2 : 2 + count], refs[2 + count :]
        near, refs = refs[:count], refs[count:]
        sums, blocks, landed, line, near_send, near_recv, load_sem, *sems = refs
        block_send, block_recv, line_send, line_recv = sems
        place = Place(sizes)
        peers = place.group()
        layers = [(place.layer + k) % depth for k in range(1, depth)]
        devices = [place.device(chip=a, core=b, half=c) for a, b, c in peers]
        greet(devices + [place.device(layer=k) for k in layers])
        pending = [[], []]
        for a in range(count):
            targets = [place.across()] + [
                place.device(chip=place.ahead(k)) for k in range(1, chips)
            ]
            for piece in range(2):
                side = partials[a].shape[1] // 2
                span = pl.ds(piece * side, side)
                for at, device in enumerate(targets):
                    pending[piece].append(
                        send(
                            partial_in[a].at[at, span],
                            near[a].at[at, span],
                            near_send.at[a, piece, at],
                            near_recv.at[a, piece, at],
                            device,
                        )
                    )
                    pending[piece][-1].start()
            pltpu.make_async_copy(
                partial_in[a].at[chips], near[a].at[chips], load_sem.at[a]
            ).start()

        gain = vector_ref[0:1, :]
        sums[...] = jnp.zeros_like(sums)

        @pl.loop(0, own_len, step=step_rows)
        def _(r):
            at = pl.ds(pl.multiple_of(r, step_rows), step_rows)
            values = tokens_ref[at, :].astype(f32)
            centered = values - jnp.mean(values, axis=-1, keepdims=True)
            spread = jnp.mean(centered * centered, axis=-1, keepdims=True)
            scale = lax.rsqrt(spread + epsilon)
            normal = centered * scale
            found = grad_ref[at, :].astype(f32)
            away = cotangent_ref[at, :].astype(f32)
            inner = found * gain
            mean = jnp.mean(inner, axis=-1, keepdims=True)
            along = jnp.mean(inner * normal, axis=-1, keepdims=True)
            input_ref[at, :] = (scale * (inner - mean - normal * along)).astype(bf16)
            sums[0:1, :] += jnp.sum(found * normal, axis=0, keepdims=True)
            sums[1:2, :] += jnp.sum(found, axis=0, keepdims=True)
            sums[2:3, :] += jnp.sum(away, axis=0, keepdims=True)

        for number in range(groups):
            blocks[number] = sums[:, number * shard : (number + 1) * shard]
        copies = []
        for at, (chip, core, half) in enumerate(peers):
            copies.append(
                send(
                    blocks.at[place.block(chip, core, half)],
                    landed.at[at],
                    block_send.at[at],
                    block_recv.at[at],
                    devices[at],
                )
            )
            copies[-1].start()
        total = blocks[place.block()]
        for at, copy in enumerate(copies):
            copy.wait()
            total += landed[at]
        line[0] = total
        copies = []
        for k, layer in enumerate(layers):
            copies.append(
                send(
                    line.at[0],
                    line.at[k + 1],
                    line_send.at[k],
                    line_recv.at[k],
                    place.device(layer=layer),
                )
            )
            copies[-1].start()
        for k, copy in enumerate(copies):
            copy.wait()
            total += line[k + 1]
        small_ref[...] = total

        for a in range(count):
            own = near[a].at[chips]
            pltpu.make_async_copy(own, own, load_sem.at[a]).wait()
        for piece in range(2):
            for copy in pending[piece]:
                copy.wait()
            for a in range(count):
                rows, width = partials[a].shape[1:]
                side = rows // 2
                step = min(32, side)

                @pl.loop(piece * side, (piece + 1) * side, step=step)
                def _(r, a=a, width=width, step=step):
                    at = pl.ds(pl.multiple_of(r, step), step)
                    found = near[a][0, at, :].astype(f32)
                    for number in range(1, chips + 1):
                        found += near[a][number, at, :].astype(f32)
                    if splits[a] == 1:
                        weight_out[a][at, :] = found
                    else:
                        wide = width // splits[a]
                        for kind in range(splits[a]):
                            weight_out[a][kind, at, :] = found[:, kind * wide : (kind + 1) * wide]

    out_shape = [
        jax.ShapeDtypeStruct((own_len, model), bf16),
        jax.ShapeDtypeStruct((8, shard), f32),
    ]
    for v, n in zip(partials, splits):
        rows, width = v.shape[1:]
        out_shape.append(
            jax.ShapeDtypeStruct((rows, width) if n == 1 else (n, rows, width // n), f32)
        )
    return pl.pallas_call(
        kernel,
        out_shape=tuple(out_shape),
        in_specs=[VMEM] * 4 + [ANY] * count,
        out_specs=(VMEM,) * len(out_shape),
        scratch_shapes=[
            *buffers_for(*partials),
            pltpu.VMEM((8, model), f32),
            pltpu.VMEM((groups, 8, shard), f32),
            pltpu.VMEM((groups - 1, 8, shard), f32),
            pltpu.VMEM((depth, 8, shard), f32),
            DMA((count, 2, chips)),
            DMA((count, 2, chips)),
            DMA((count,)),
            DMA((groups - 1,)),
            DMA((groups - 1,)),
            DMA((depth - 1,)),
            DMA((depth - 1,)),
        ],
        compiler_params=pltpu.CompilerParams(
            collective_id=3, has_side_effects=True, vmem_limit_bytes=60 << 20
        ),
        cost_estimate=pl.CostEstimate(flops=0, bytes_accessed=90_000_000, transcendentals=0),
        name="finish_all",
    )(grad, tokens, cotangent, vectors, *partials)


def tile_at(number):
    return pl.ds(pl.multiple_of(number * TILE, TILE), TILE)


def allowed(kb, j, start):
    places = kb * TILE + lax.broadcasted_iota(jnp.int32, (TILE, TILE), 0)
    own = j * TILE + lax.broadcasted_iota(jnp.int32, (TILE, TILE), 1)
    return (places >= start) & (places <= own)


def attend_kernel(
    low_ref,
    mid_ref,
    triple_ref,
    start_ref,
    attended_ref,
    log_ref,
    query_t,
    key_t,
    value_t,
    key_rows,
    scores,
):
    length = triple_ref.shape[3]
    heads = triple_ref.shape[2] // HD
    score_scale = 1.0 / math.sqrt(HD)
    for number, ref in enumerate((query_t, key_t, value_t)):
        for part in range(2):
            piece = triple_ref[part, number]
            ref[:, part * length : (part + 1) * length] = (
                piece * score_scale if number == 0 else piece
            )
    rows = [slice(h * HD, (h + 1) * HD) for h in range(heads)]
    for h in range(heads):
        key_rows[h] = key_t[rows[h], :].T

    @pl.loop(0, 2 * length // TILE)
    def _(j):
        here = tile_at(j)
        start = start_ref[:, here]
        low, mid = low_ref[j], mid_ref[j]
        queries = [query_t[row, here] for row in rows]

        def score_with(masked):
            def score(kb, highest):
                ok = allowed(kb, j, start) if masked else None
                raised = []
                for h in range(heads):
                    found = jnp.dot(
                        key_rows[h, tile_at(kb), :], queries[h], preferred_element_type=f32
                    )
                    if masked:
                        found = jnp.where(ok, found, big_negative)
                    scores[h, tile_at(kb), :] = found
                    raised.append(
                        jnp.maximum(highest[h], jnp.max(found, axis=0, keepdims=True))
                    )
                return tuple(raised)

            return score

        highest = tuple(jnp.full((1, TILE), big_negative, f32) for _ in range(heads))
        highest = lax.fori_loop(low, mid, score_with(True), highest)
        highest = lax.fori_loop(mid, j, score_with(False), highest)
        highest = score_with(True)(j, highest)

        def weigh(kb, carry):
            after = []
            for h in range(heads):
                total, mixed = carry[h]
                prob = jnp.exp(scores[h, tile_at(kb), :] - highest[h])
                total = total + jnp.sum(prob, axis=0, keepdims=True)
                mixed = mixed + jnp.dot(
                    value_t[rows[h], tile_at(kb)], prob.astype(bf16), preferred_element_type=f32
                )
                after.append((total, mixed))
            return tuple(after)

        empty = tuple(
            (jnp.zeros((1, TILE), f32), jnp.zeros((HD, TILE), f32)) for _ in range(heads)
        )
        result = lax.fori_loop(low, j + 1, weigh, empty)
        for h in range(heads):
            total, mixed = result[h]
            attended_ref[rows[h], here] = (mixed / total).astype(bf16)
            log_ref[h, :, here] = highest[h] + jnp.log(total)


def turned_back(values, cosine, sine):
    half_rot = ROT // 2
    leading = values[:half_rot]
    trailing = values[half_rot:ROT]
    return jnp.concatenate(
        [
            leading * cosine + trailing * sine,
            trailing * cosine - leading * sine,
            values[ROT:],
        ],
        axis=0,
    )


def attend_back_kernel(
    low_ref,
    mid_ref,
    triple_ref,
    grad_ref,
    attended_ref,
    log_ref,
    start_ref,
    cosine_ref,
    sine_ref,
    back_ref,
    query_t,
    key_t,
    grad_t,
    key_rows,
    value_rows,
    key_sum,
    value_sum,
):
    length = triple_ref.shape[3]
    heads = triple_ref.shape[2] // HD
    score_scale = 1.0 / math.sqrt(HD)
    rows = [slice(h * HD, (h + 1) * HD) for h in range(heads)]
    for part in range(2):
        span = slice(part * length, (part + 1) * length)
        query_t[:, span] = triple_ref[part, 0] * score_scale
        key_t[:, span] = triple_ref[part, 1]
        grad_t[:, span] = grad_ref[part]
        for h in range(heads):
            value_rows[h, span, :] = triple_ref[part, 2, rows[h]].T
    for h in range(heads):
        key_rows[h] = key_t[rows[h], :].T
    key_sum[...] = jnp.zeros_like(key_sum)
    value_sum[...] = jnp.zeros_like(value_sum)

    @pl.loop(0, 2 * length // TILE)
    def _(j):
        here = tile_at(j)
        start = start_ref[:, here]
        low, mid = low_ref[j], mid_ref[j]
        queries = [query_t[row, here] for row in rows]
        grads = [grad_t[row, here] for row in rows]
        query_rows = [value.T for value in queries]
        grad_rows = [value.T for value in grads]
        logs = [log_ref[h, :, here] for h in range(heads)]
        deltas = [
            jnp.sum(
                grads[h].astype(f32) * attended_ref[rows[h], here].astype(f32),
                axis=0,
                keepdims=True,
            )
            for h in range(heads)
        ]

        def pull_with(masked):
            def pull(kb, query_back):
                ok = allowed(kb, j, start) if masked else None
                after = []
                for h in range(heads):
                    score = jnp.dot(
                        key_rows[h, tile_at(kb), :], queries[h], preferred_element_type=f32
                    )
                    if masked:
                        score = jnp.where(ok, score, big_negative)
                    prob = jnp.exp(score - logs[h])
                    down = jnp.dot(
                        value_rows[h, tile_at(kb), :], grads[h], preferred_element_type=f32
                    )
                    score_back = (prob * (down - deltas[h])).astype(bf16)
                    value_sum[h, tile_at(kb), :] += jnp.dot(
                        prob.astype(bf16), grad_rows[h], preferred_element_type=f32
                    )
                    key_sum[h, tile_at(kb), :] += jnp.dot(
                        score_back, query_rows[h], preferred_element_type=f32
                    )
                    after.append(
                        query_back[h]
                        + jnp.dot(
                            key_t[rows[h], tile_at(kb)], score_back, preferred_element_type=f32
                        )
                    )
                return tuple(after)

            return pull

        query_back = tuple(jnp.zeros((HD, TILE), f32) for _ in range(heads))
        query_back = lax.fori_loop(low, mid, pull_with(True), query_back)
        query_back = lax.fori_loop(mid, j, pull_with(False), query_back)
        query_back = pull_with(True)(j, query_back)
        for h in range(heads):
            back_ref[0, rows[h], here] = turned_back(
                query_back[h] * score_scale, cosine_ref[:, here], sine_ref[:, here]
            ).astype(bf16)

    for h in range(heads):
        back_ref[1, rows[h], :] = turned_back(
            key_sum[h].T, cosine_ref[...], sine_ref[...]
        ).astype(bf16)
        back_ref[2, rows[h], :] = value_sum[h].T.astype(bf16)


def attend(low, mid, triple, start):
    width, length = triple.shape[2], triple.shape[3]
    total, heads = 2 * length, width // HD
    area = total * total // 3 * heads
    return pl.pallas_call(
        attend_kernel,
        out_shape=(
            jax.ShapeDtypeStruct((width, total), bf16),
            jax.ShapeDtypeStruct((heads, 1, total), f32),
        ),
        in_specs=[SMEM, SMEM, VMEM, VMEM],
        out_specs=(VMEM, VMEM),
        scratch_shapes=[pltpu.VMEM((width, total), bf16)] * 3
        + [pltpu.VMEM((heads, total, HD), bf16), pltpu.VMEM((heads, total, TILE), f32)],
        compiler_params=pltpu.CompilerParams(vmem_limit_bytes=48 << 20),
        cost_estimate=pl.CostEstimate(
            flops=50 * area * HD, bytes_accessed=8 * width * total, transcendentals=area
        ),
        name="attend",
    )(low, mid, triple, start)


def attend_back(low, mid, triple, grad, attended, log_sum, start, cosine, sine):
    width, length = triple.shape[2], triple.shape[3]
    total, heads = 2 * length, width // HD
    area = total * total // 3 * heads
    return pl.pallas_call(
        attend_back_kernel,
        out_shape=jax.ShapeDtypeStruct((3, width, total), bf16),
        in_specs=[SMEM, SMEM] + [VMEM] * 7,
        out_specs=VMEM,
        scratch_shapes=[pltpu.VMEM((width, total), bf16)] * 3
        + [pltpu.VMEM((heads, total, HD), bf16)] * 2
        + [pltpu.VMEM((heads, total, HD), f32)] * 2,
        compiler_params=pltpu.CompilerParams(vmem_limit_bytes=48 << 20),
        cost_estimate=pl.CostEstimate(
            flops=100 * area * HD, bytes_accessed=12 * width * total, transcendentals=area
        ),
        name="attend_back",
    )(low, mid, triple, grad, attended, log_sum, start, cosine, sine)


def rotate_rows(values, cosine, sine):
    half_rot = ROT // 2
    leading = values[:, :half_rot]
    trailing = values[:, half_rot:ROT]
    return jnp.concatenate(
        [
            leading * cosine - trailing * sine,
            trailing * cosine + leading * sine,
            values[:, ROT:],
        ],
        axis=1,
    )


def ordered(*values):
    return lax.optimization_barrier(values)


def body(
    sizes,
    tokens,
    segments,
    positions,
    norm_gain,
    norm_bias,
    projection_weight,
    projection_bias,
    dense_weight,
    dense_bias,
    up_weight,
    up_bias,
    down_weight,
    down_bias,
    cotangent,
):
    own_len, model_width = tokens.shape[1], tokens.shape[2]
    half_len = segments.shape[1]
    local_width = projection_weight.shape[2]
    hidden_width = up_weight.shape[1]
    shard_rows = norm_gain.shape[0]
    half = lax.axis_index("ctx")
    total_len = 2 * half_len

    numbers = [segments, positions]
    (
        vectors_full,
        segments_other,
        positions_other,
        normed,
        cotangent_early,
        cotangent_late,
        projection,
        up_full,
        dense_full,
        down_full,
        both,
        activation,
        slope,
    ) = front(
        sizes,
        tokens[0],
        cotangent[0],
        [norm_gain, norm_bias, dense_bias, down_bias],
        numbers,
        [projection_weight.transpose(1, 0, 2), up_weight, dense_weight, down_weight],
        projection_bias,
        up_bias,
    )

    def in_order(own, other, axis):
        return jnp.where(
            half == 0,
            jnp.concatenate([own, other], axis=axis),
            jnp.concatenate([other, own], axis=axis),
        )

    segment_row = in_order(segments[0], segments_other[0], 0)
    position_row = in_order(positions[0], positions_other[0], 0)
    places = jnp.arange(total_len, dtype=jnp.int32)
    edges = jnp.concatenate([jnp.ones((1,), bool), segment_row[1:] != segment_row[:-1]])
    start = lax.cummax(jnp.where(edges, places, 0))
    tile_count = total_len // TILE
    low = start[::TILE] // TILE
    mid = jnp.minimum(
        jnp.maximum((start[TILE - 1 :: TILE] + TILE - 1) // TILE, low),
        jnp.arange(tile_count, dtype=jnp.int32),
    )
    exponent = jnp.arange(ROT // 2, dtype=f32) * 2.0 / ROT
    phase_angle = (10000.0 ** (-exponent))[:, None] * position_row.astype(f32)[None, :]
    cosine_full, sine_full = jnp.cos(phase_angle), jnp.sin(phase_angle)
    depth = sizes["tp"]
    late_blocks = [cotangent_late] + [
        lax.ppermute(cotangent_late, "tp", [(z, (z + k) % depth) for z in range(depth)])
        for k in range(1, depth)
    ]
    attended_heads, log_sum = attend(low, mid, both, start[None, :])
    attended, block_out, cotangent_late, grad_both, grad_hidden, hidden_sum = exchange_middle(
        sizes,
        attended_heads,
        activation,
        down_full,
        dense_full,
        cotangent_early,
        late_blocks,
        slope,
    )
    cotangents = [cotangent_early, cotangent_late]
    branch_own = lax.psum_scatter(block_out, "tp", scatter_dimension=0, tiled=True)
    back_heads = attend_back(
        low,
        mid,
        both,
        grad_both,
        attended_heads,
        log_sum,
        start[None, :],
        cosine_full,
        sine_full,
    )
    grad_projected, paired, turned, block_in, projected_sum = exchange_back(
        sizes, back_heads, normed, grad_hidden, cotangents, activation, up_full, projection
    )
    grad_projected = grad_projected.reshape(3 * local_width, half_len)
    block_in, branch_own = ordered(block_in, branch_own)
    grad_normed_own = lax.psum_scatter(block_in, "tp", scatter_dimension=0, tiled=True)
    up_part, down_part, dense_part, hidden_total, projected_total, partial = reduce(
        sizes,
        paired,
        turned,
        [(cotangents, attended), ([normed], grad_projected)],
        [hidden_sum, projected_sum],
        2,
        "reduce_weights",
    )
    input_part, totals, projection_part = finish_all(
        sizes,
        grad_normed_own,
        tokens[0],
        cotangent[0],
        vectors_full,
        [partial],
        [3],
    )
    bias_dense, bias_down = vectors_full[2], vectors_full[3]
    layer_output = (
        tokens[0].astype(f32) + branch_own.astype(f32) + (bias_dense + bias_down)
    ).astype(bf16)
    input_grad = cotangent[0].astype(f32) + input_part.astype(f32)
    return (
        layer_output[None],
        input_grad[None],
        totals[0],
        totals[1],
        projection_part.transpose(1, 0, 2),
        projected_total,
        dense_part,
        totals[2],
        up_part,
        hidden_total[0],
        down_part,
        totals[2],
    )


def solution(mesh):
    placed = (
        P("fsdp", ("ctx", "tp"), None),
        P("fsdp", "ctx"),
        P("fsdp", "ctx"),
        P(("fsdp", "ctx")),
        P(("fsdp", "ctx")),
        P(("fsdp", "ctx"), None, "tp"),
        P(None, "tp"),
        P(("fsdp", "ctx"), "tp"),
        P(("fsdp", "ctx")),
        P(("fsdp", "ctx"), "tp"),
        P("tp"),
        P(("fsdp", "ctx"), "tp"),
        P(("fsdp", "ctx")),
        P("fsdp", ("ctx", "tp"), None),
    )
    return jax.shard_map(
        functools.partial(body, dict(mesh.shape)),
        mesh=mesh,
        in_specs=placed,
        out_specs=(
            P("fsdp", ("ctx", "tp"), None),
            P("fsdp", ("ctx", "tp"), None),
            P(("fsdp", "ctx")),
            P(("fsdp", "ctx")),
            P(("fsdp", "ctx"), None, "tp"),
            P(None, "tp"),
            P(("fsdp", "ctx"), "tp"),
            P(("fsdp", "ctx")),
            P(("fsdp", "ctx"), "tp"),
            P("tp"),
            P(("fsdp", "ctx"), "tp"),
            P(("fsdp", "ctx")),
        ),
        check_vma=False,
    )
```

```python
import functools
import math

import jax
import jax.numpy as jnp
from jax import lax
from jax.experimental import pallas as pl
from jax.experimental.pallas import tpu as pltpu
from jax.sharding import PartitionSpec as P

HD = 64
ROT = 32
TILE = 256

epsilon = 1e-05
big_negative = -1000000000.0
root_two_over_pi = 0.7978845608028654
contract_rows = (((0,), (0,)), ((), ()))
contract_cols = (((1,), (1,)), ((), ()))
row_by_col = (((0,), (1,)), ((), ()))
MESH = pl.DeviceIdType.MESH
ANY = pl.BlockSpec(memory_space=pl.ANY)
VMEM = pl.BlockSpec(memory_space=pltpu.VMEM)
SMEM = pl.BlockSpec(memory_space=pltpu.SMEM)
DMA = pltpu.SemaphoreType.DMA
f32 = jnp.float32
bf16 = jnp.bfloat16


def layer_norm(values, gain_full, shift_full):
    center = jnp.mean(values, axis=-1, keepdims=True)
    centered = values - center
    spread = jnp.mean(centered * centered, axis=-1, keepdims=True)
    return centered * lax.rsqrt(spread + epsilon) * gain_full + shift_full


def gelu_and_slope(values):
    turned = jnp.tanh(root_two_over_pi * (values + 0.044715 * values * values * values))
    slope = 0.5 * (1.0 + turned) + 0.5 * values * (1.0 - turned * turned) * root_two_over_pi * (
        1.0 + 3.0 * 0.044715 * values * values
    )
    return 0.5 * values * (1.0 + turned), slope


class Place:
    def __init__(self, sizes):
        self.chips = sizes["fsdp"] // 2
        self.halves = sizes["ctx"]
        self.depth = sizes["tp"]
        lane = lax.axis_index("fsdp")
        self.chip = lane // 2
        self.core = lane % 2
        self.half = lax.axis_index("ctx")
        self.layer = lax.axis_index("tp")

    def device(self, chip=None, core=None, half=None, layer=None):
        chip = self.chip if chip is None else chip
        core = self.core if core is None else core
        half = self.half if half is None else half
        layer = self.layer if layer is None else layer
        return (chip * 2 + core, half, layer)

    def block(self, chip=None, core=None, half=None):
        chip = self.chip if chip is None else chip
        core = self.core if core is None else core
        half = self.half if half is None else half
        return (chip * 2 + core) * self.halves + half

    def ahead(self, k):
        return (self.chip + k) % self.chips

    def behind(self, k):
        return (self.chip + self.chips - k) % self.chips

    def neighbours(self):
        last = self.depth - 1
        return (
            (self.layer < last, self.device(layer=jnp.minimum(self.layer + 1, last))),
            (self.layer > 0, self.device(layer=jnp.maximum(self.layer - 1, 0))),
        )

    def pair(self):
        return self.device(core=1 - self.core)

    def across(self):
        return self.device(half=1 - self.half)

    def group(self):
        found = []
        for k in range(self.chips):
            for core in range(2):
                for half in range(2):
                    if k or core or half:
                        found.append(
                            (self.ahead(k), (self.core + core) % 2, (self.half + half) % 2)
                        )
        return found


def greet(devices):
    barrier = pltpu.get_barrier_semaphore()
    for device in devices:
        pl.semaphore_signal(barrier, inc=1, device_id=device, device_id_type=MESH)
    pl.semaphore_wait(barrier, len(devices))


def greet_line(place, devices):
    barrier = pltpu.get_barrier_semaphore()
    for device in devices:
        pl.semaphore_signal(barrier, inc=1, device_id=device, device_id_type=MESH)
    count = len(devices)
    for there, device in place.neighbours():

        @pl.when(there)
        def _(device=device):
            pl.semaphore_signal(barrier, inc=1, device_id=device, device_id_type=MESH)

        count = count + there.astype(jnp.int32)
    pl.semaphore_wait(barrier, count)


def send(source, target, send_sem, recv_sem, device):
    return pltpu.make_async_remote_copy(
        src_ref=source,
        dst_ref=target,
        send_sem=send_sem,
        recv_sem=recv_sem,
        device_id=device,
        device_id_type=MESH,
    )


class Line:
    def __init__(self, place, own, full, send_sem, recv_sem, keep_sem):
        self.place, self.own, self.full = place, own, full
        self.send_sem, self.recv_sem = send_sem, recv_sem
        self.rows = own.shape[0]
        self.pending = []
        self.keep = pltpu.make_async_copy(own, self.block(place.layer), keep_sem)

    def block(self, source):
        return self.full.at[pl.ds(pl.multiple_of(source * self.rows, 16), self.rows)]

    def copy(self, piece, target, way, hop, device):
        return send(piece, target, self.send_sem.at[way, hop], self.recv_sem.at[way, hop], device)

    def launch(self, copy, condition):
        pl.when(condition)(copy.start)
        self.pending.append((copy, condition))

    def start(self):
        for way, (there, device) in enumerate(self.place.neighbours()):
            target = self.block(self.place.layer)
            self.launch(self.copy(self.own, target, way, 0, device), there)
        self.keep.start()

    def step(self, k):
        last = self.place.depth - 1
        for way, (onward, device) in enumerate(self.place.neighbours()):
            source = self.place.layer - k if way == 0 else self.place.layer + k
            there = (source >= 0) & (source <= last)
            piece = self.block(jnp.clip(source, 0, last))
            pl.when(there)(self.copy(piece, piece, way, k - 1, device).wait_recv)
            if k < last:
                self.launch(self.copy(piece, piece, way, k, device), there & onward)

    def end(self):
        for copy, condition in self.pending:
            pl.when(condition)(copy.wait_send)


def plane(place):
    found = [place.device(chip=place.ahead(k)) for k in range(1, place.chips)]
    return found + [place.across(), place.pair()]


def reduce(sizes, paired, turned, rights, small, collective_id, name):
    chips, halves = sizes["fsdp"] // 2, sizes["ctx"]
    groups = chips * halves
    paired_count, made_count = len(paired), len(rights)
    weight_count = paired_count + made_count
    whole_count = weight_count - 1
    block_rows = paired[0][0].shape[0] // (2 * groups)
    widths = [v.shape[1] for v, _ in paired] + [v.shape[0] for _, v in rights]
    tall = min(64, block_rows)
    sides = [turned[2 * a].shape[1] for a in range(paired_count)] + [block_rows // 2] * made_count

    def kernel(*refs):
        refs = list(refs)

        def take(count):
            taken = refs[:count]
            del refs[:count]
            return taken

        paired_in = [take(2) for _ in range(paired_count)]
        turned_in = take(2 * paired_count)
        lefts = [take(len(left)) for left, _ in rights]
        factors = take(made_count)
        small_in = take(len(small))
        weight_out = take(whole_count)
        small_outs = take(len(small))
        held_out, made = take(weight_count - whole_count), take(made_count)
        own, turn_a, turn_b = (take(weight_count) for _ in range(3))
        near = take(whole_count)
        pair = take(weight_count)
        load_sem, core_send, core_recv = take(3)
        turn_send, turn_recv, near_send, near_recv = take(4)
        small_ref, small_pair, small_near, small_far, small_send, small_recv = take(6)
        place = Place(sizes)
        greet(plane(place))
        pending = []

        def launch(copy, condition=None):
            if condition is None:
                copy.start()
            else:
                pl.when(condition)(copy.start)
            pending.append((copy, condition))

        other = 1 - place.core
        needed = [place.ahead(k) * halves + place.half for k in range(1, chips)]
        needed += [place.chip * halves + 1 - place.half, place.chip * halves + place.half]
        for a in range(paired_count):
            for at, number in enumerate(needed):
                chip = place.ahead(at + 1) if at < chips - 1 else place.chip
                half = 1 - place.half if at == chips - 1 else place.half
                mine = place.block(chip, place.core, half)
                pltpu.make_async_copy(
                    paired_in[a][0].at[pl.ds(pl.multiple_of(mine * block_rows, 16), block_rows)],
                    own[a].at[number],
                    load_sem.at[a, number],
                ).start()
                pltpu.make_async_copy(
                    paired_in[a][1].at[pl.ds(pl.multiple_of(number * block_rows, 16), block_rows)],
                    pair[a].at[at],
                    core_recv.at[a, number],
                ).start()
            for way, target in enumerate((turn_a[a], turn_b[a])):
                for k in range(1, chips):
                    pltpu.make_async_copy(
                        turned_in[2 * a + way].at[k - 1],
                        target.at[k - 1],
                        turn_recv.at[a, way, k],
                    ).start()

        def make(a):
            at = a - paired_count
            first = 0
            for left in lefts[at]:
                span = pl.ds(first, left.shape[1])
                multiply("tt", [(left, factors[at])], [made[at].at[span]])
                first += left.shape[1]
            for number in range(groups):
                chip, half = number // halves, number % halves
                theirs = place.block(chip, other, half)
                mine = place.block(chip, place.core, half)
                launch(
                    send(
                        made[at].at[pl.ds(pl.multiple_of(theirs * block_rows, 16), block_rows)],
                        pair[a].at[number],
                        core_send.at[a, number],
                        core_recv.at[a, number],
                        place.pair(),
                    )
                )
                pltpu.make_async_copy(
                    made[at].at[pl.ds(pl.multiple_of(mine * block_rows, 16), block_rows)],
                    own[a].at[number],
                    load_sem.at[a, number],
                ).start()

        def pair_sum(a, number, at_needed=None):
            mine = own[a].at[number]
            pltpu.make_async_copy(mine, mine, load_sem.at[a, number]).wait()
            if a < paired_count:
                theirs = pair[a].at[at_needed]
                pltpu.make_async_copy(theirs, theirs, core_recv.at[a, number]).wait()
            else:
                theirs = pair[a].at[number]
                send(
                    theirs, theirs, core_send.at[a, number], core_recv.at[a, number], place.pair()
                ).wait_recv()

            @pl.loop(0, block_rows, step=tall)
            def _(r):
                at = pl.ds(pl.multiple_of(r, tall), tall)
                mine[at, :] = (mine[at, :].astype(f32) + theirs[at, :].astype(f32)).astype(bf16)

        def diagonal(a):
            for k in range(1, chips):
                number = place.ahead(k) * halves + 1 - place.half
                pair_sum(a, number)
                launch(
                    send(
                        own[a].at[number, pl.ds(0, sides[a])],
                        turn_a[a].at[k - 1],
                        turn_send.at[a, 0, k],
                        turn_recv.at[a, 0, k],
                        place.across(),
                    )
                )
                launch(
                    send(
                        own[a].at[number, pl.ds(sides[a], block_rows - sides[a])],
                        turn_b[a].at[k - 1],
                        turn_send.at[a, 1, k],
                        turn_recv.at[a, 1, k],
                        place.device(chip=place.ahead(k)),
                    )
                )

        def direct_pairs(a):
            for k in range(1, chips):
                pair_sum(a, place.ahead(k) * halves + place.half, k - 1)
            pair_sum(a, place.chip * halves + 1 - place.half, chips - 1)

        def add_turn(a, number, first, count, refs_at):
            @pl.loop(0, count, step=16)
            def _(r):
                at = pl.ds(pl.multiple_of(first + r, 16), 16)
                total = own[a][number, at, :].astype(f32)
                for ref, k in refs_at:
                    total += ref[k, pl.ds(pl.multiple_of(r, 16), 16), :].astype(f32)
                own[a][number, at, :] = total.astype(bf16)

        def turn_wait(a, way, k):
            piece = (turn_a, turn_b)[way][a].at[k - 1]
            if a < paired_count:
                pltpu.make_async_copy(piece, piece, turn_recv.at[a, way, k]).wait()
            else:
                send(
                    piece, piece, turn_send.at[a, way, k], turn_recv.at[a, way, k], place.across()
                ).wait_recv()

        def hand(a, at, number):
            pltpu.make_async_copy(
                own[a].at[number], held_out[a - whole_count].at[at], near_send.at[a, at]
            ).start()

        def direct(a):
            for k in range(1, chips):
                number = place.ahead(k) * halves + place.half
                turn_wait(a, 0, k)
                add_turn(a, number, 0, sides[a], [(turn_a[a], k - 1)])
                if a >= whole_count:
                    hand(a, k, number)
                    continue
                launch(
                    send(
                        own[a].at[number],
                        near[a].at[k],
                        near_send.at[a, k],
                        near_recv.at[a, k],
                        place.device(chip=place.ahead(k)),
                    )
                )
            for k in range(1, chips):
                turn_wait(a, 1, k)
            number = place.chip * halves + 1 - place.half
            add_turn(
                a,
                number,
                sides[a],
                block_rows - sides[a],
                [(turn_b[a], k - 1) for k in range(1, chips)],
            )
            if a >= whole_count:
                hand(a, 0, number)
                return
            launch(
                send(
                    own[a].at[number],
                    near[a].at[0],
                    near_send.at[a, 0],
                    near_recv.at[a, 0],
                    place.across(),
                )
            )

        def finish(a):
            for k in range(chips):
                piece = near[a].at[k]
                send(
                    piece, piece, near_send.at[a, k], near_recv.at[a, k], place.across()
                ).wait_recv()
            number = place.chip * halves + place.half

            @pl.loop(0, block_rows, step=tall)
            def _(r):
                at = pl.ds(pl.multiple_of(r, tall), tall)
                total = own[a][number, at, :].astype(f32)
                for k in range(chips):
                    total += near[a][k, at, :].astype(f32)
                weight_out[a][at, :] = total

        def swap_small(source, target, at, device):
            copy = send(source, target, small_send.at[at], small_recv.at[at], device)
            launch(copy)
            return copy

        small_ref[...] = jnp.zeros_like(small_ref)
        first = 0
        for ref in small_in:
            small_ref[first : first + ref.shape[0], : ref.shape[1]] = ref[...]
            first += ref.shape[0]
        swap_small(small_ref, small_pair, 0, place.pair())
        for a in range(paired_count):
            direct_pairs(a)
            direct(a)
        for a in range(paired_count, weight_count):
            make(a)
        send(small_pair, small_pair, small_send.at[0], small_recv.at[0], place.pair()).wait_recv()
        small_near[0] = small_ref[...] + small_pair[...]
        for k in range(1, chips):
            swap_small(small_near.at[0], small_near.at[k], k, place.device(chip=place.ahead(k)))
        for a in range(paired_count, weight_count):
            diagonal(a)
            direct_pairs(a)
        total = small_near[0]
        for k in range(1, chips):
            piece = small_near.at[k]
            send(piece, piece, small_send.at[k], small_recv.at[k], place.pair()).wait_recv()
            total += small_near[k]
        small_far[0] = total
        swap_small(small_far.at[0], small_far.at[1], chips, place.across())
        for a in range(weight_count):
            pair_sum(a, place.chip * halves + place.half, chips)
        for a in range(paired_count, weight_count):
            direct(a)
            if a >= whole_count:
                hand(a, chips, place.chip * halves + place.half)
        for a in range(whole_count):
            finish(a)
        for a in range(whole_count, weight_count):
            for at in range(chips + 1):
                piece = held_out[a - whole_count].at[at]
                pltpu.make_async_copy(piece, piece, near_send.at[a, at]).wait()
        piece = small_far.at[1]
        send(piece, piece, small_send.at[chips], small_recv.at[chips], place.pair()).wait_recv()
        total = small_far[0] + small_far[1]
        first = 0
        for ref in small_outs:
            ref[...] = total[first : first + ref.shape[0], : ref.shape[1]]
            first += ref.shape[0]
        for copy, condition in pending:
            if condition is None:
                copy.wait_send()
            else:
                pl.when(condition)(copy.wait_send)

    shapes = [jax.ShapeDtypeStruct((block_rows, w), f32) for w in widths[:whole_count]]
    small_shape = (8, max(v.shape[1] for v in small))
    shapes += [jax.ShapeDtypeStruct(v.shape, f32) for v in small]
    held_shapes = [
        jax.ShapeDtypeStruct((chips + 1, block_rows, w), bf16) for w in widths[whole_count:]
    ]
    made_shapes = [
        jax.ShapeDtypeStruct((2 * groups * block_rows, w), bf16) for w in widths[paired_count:]
    ]
    scratch = [pltpu.VMEM((groups, block_rows, w), bf16) for w in widths]
    scratch += [pltpu.VMEM((chips - 1, n, w), bf16) for w, n in zip(widths, sides)]
    scratch += [pltpu.VMEM((chips - 1, block_rows - n, w), bf16) for w, n in zip(widths, sides)]
    scratch += [pltpu.VMEM((chips, block_rows, w), bf16) for w in widths[:whole_count]]
    scratch += [pltpu.VMEM((chips + 1, block_rows, w), bf16) for w in widths[:paired_count]]
    scratch += [pltpu.VMEM((groups, block_rows, w), bf16) for w in widths[paired_count:]]
    scratch += [
        DMA((weight_count, groups)),
        DMA((weight_count, groups)),
        DMA((weight_count, groups)),
        DMA((weight_count, 2, chips)),
        DMA((weight_count, 2, chips)),
        DMA((weight_count, chips + 1)),
        DMA((weight_count, chips + 1)),
        pltpu.VMEM(small_shape, f32),
        pltpu.VMEM(small_shape, f32),
        pltpu.VMEM((chips,) + small_shape, f32),
        pltpu.VMEM((2,) + small_shape, f32),
        DMA((chips + 1,)),
        DMA((chips + 1,)),
    ]
    lefts = [v for left, _ in rights for v in left]
    factors = [v for _, v in rights]
    return pl.pallas_call(
        kernel,
        out_shape=tuple(shapes + held_shapes + made_shapes),
        in_specs=[ANY] * (4 * paired_count + len(lefts) + made_count) + [VMEM] * len(small),
        out_specs=(VMEM,) * (whole_count + len(small))
        + (ANY,) * (weight_count - whole_count + made_count),
        scratch_shapes=scratch,
        compiler_params=pltpu.CompilerParams(
            collective_id=collective_id, has_side_effects=True, vmem_limit_bytes=60 << 20
        ),
        cost_estimate=pl.CostEstimate(flops=0, bytes_accessed=400_000_000, transcendentals=0),
        name=name,
    )(*[v for two in paired for v in two], *turned, *lefts, *factors, *small)[
        : weight_count + len(small)
    ]


def multiply(kind, parts, outs, finish=None, extra=(), tile=512):
    dims = (((0 if kind[0] == "t" else 1,), (1 if kind[1] == "t" else 0,)), ((), ()))
    left, right = parts[0]
    rows = left.shape[1] if kind[0] == "t" else left.shape[0]
    width = right.shape[0] if kind[1] == "t" else right.shape[1]
    tile = min(tile, width)
    specs = []
    for left, right in parts:
        specs.append(pl.BlockSpec(left.shape, lambda n: (0, 0)))
        if kind[1] == "t":
            specs.append(pl.BlockSpec((tile, right.shape[1]), lambda n: (n, 0)))
        else:
            specs.append(pl.BlockSpec((right.shape[0], tile), lambda n: (0, n)))
    specs += [pl.BlockSpec((v.shape[0], tile), lambda n: (0, n)) for v in extra]

    def step(*refs):
        found = None
        for number in range(len(parts)):
            product = lax.dot_general(
                refs[2 * number][...],
                refs[2 * number + 1][...],
                dims,
                preferred_element_type=f32,
            )
            found = product if found is None else found + product
        rest = refs[2 * len(parts) :]
        results = (found,)
        if finish is not None:
            results = finish(found, *(v[...] for v in rest[: len(extra)]))
        for ref, value in zip(rest[len(extra) :], results):
            ref[...] = value.astype(ref.dtype)

    factors = [v for pair in parts for v in pair]
    pltpu.emit_pipeline(
        step,
        grid=(width // tile,),
        in_specs=specs,
        out_specs=[pl.BlockSpec((v.shape[0], tile), lambda n: (0, n)) for v in outs],
    )(*factors, *extra, *outs)


def half_rows(ref, half, count):
    return ref.at[pl.ds(pl.multiple_of(half * count, count), count)]


def front(sizes, tokens, cotangent, vectors, numbers, weights, projection_bias, up_bias):
    chips, halves, depth = sizes["fsdp"] // 2, sizes["ctx"], sizes["tp"]
    groups = sizes["fsdp"] * halves
    own_len, model = tokens.shape
    length = own_len * depth
    projection, up, dense, down = weights
    weight_count = len(weights)
    kinds, local = projection.shape[0], projection.shape[2]
    count = local // 2
    hidden = up.shape[1]
    shard = vectors[0].shape[0]
    half_rot = ROT // 2
    early_width = model // 4 * 3
    first_width = model // 8

    def kernel(*refs):
        refs = list(refs)

        def take(number):
            taken = refs[:number]
            del refs[:number]
            return taken

        tokens_ref, cotangent_ref = take(2)
        vector_in, number_in = take(len(vectors)), take(len(numbers))
        weight_in = take(weight_count)
        bias_in, up_bias_in = take(2)
        vectors_out, *numbers_out = take(1 + len(numbers))
        normed, cotangent_rows, cotangent_late = take(3)
        weight_out = take(weight_count)
        both, activation, slope, triple = take(4)
        landed, normed_own, stage, vector_ref, bias_ref, up_bias_ref, cosine_ref, sine_ref = take(8)
        vector_send, vector_recv, number_sems, single, line_send, line_recv = take(6)
        keep, near_send, near_recv, turn_send, turn_recv, core_send, core_recv = take(7)
        place = Place(sizes)
        peers = place.group()
        greet_line(place, [place.device(chip=a, core=b, half=c) for a, b, c in peers])
        pending = []

        def launch(copy):
            copy.start()
            pending.append(copy)

        def part(a, block, first=0, rows=None):
            rows = weight_in[a].shape[-2] if rows is None else rows
            start = pl.multiple_of(block * weight_in[a].shape[-2] + first, 16)
            span = pl.ds(start, rows)
            return weight_out[a].at[:, span] if a == 0 else weight_out[a].at[span]

        def arrive(piece, recv_sem):
            send(piece, piece, recv_sem, recv_sem, place.pair()).wait_recv()

        mine = place.block()
        vector_ref[...] = jnp.zeros_like(vector_ref)
        for row, ref in enumerate(vector_in):
            vector_ref[row : row + 1, :] = ref[...].astype(f32).reshape(1, shard)
        vector_keep = pltpu.make_async_copy(vector_ref, landed.at[mine], single.at[0])
        vector_keep.start()
        for at, (chip, core, half) in enumerate(peers):
            launch(
                send(
                    vector_ref,
                    landed.at[mine],
                    vector_send.at[at],
                    vector_recv.at[at],
                    place.device(chip=chip, core=core, half=half),
                )
            )
        for number in range(len(numbers)):
            launch(
                send(
                    number_in[number],
                    numbers_out[number],
                    number_sems.at[0, number],
                    number_sems.at[1, number],
                    place.across(),
                )
            )

        def near_start(a):
            own = part(a, place.block())
            for k in range(1, chips):
                launch(
                    send(
                        weight_in[a],
                        own,
                        near_send.at[a, k],
                        near_recv.at[a, k],
                        place.device(chip=place.ahead(k)),
                    )
                )
            launch(
                send(weight_in[a], own, near_send.at[a, 0], near_recv.at[a, 0], place.across())
            )
            launch(send(weight_in[a], own, core_send.at[a, 0], core_recv.at[a, 0], place.pair()))
            pltpu.make_async_copy(weight_in[a], own, keep.at[a]).start()

        def near_step(a):
            side = weight_in[a].shape[-2] // 4
            rest = weight_in[a].shape[-2] - side
            for k in range(1, chips):
                block = place.block(chip=place.behind(k))
                piece = part(a, block)
                arrive(piece, near_recv.at[a, k])
                top = part(a, block, 0, side)
                launch(
                    send(top, top, turn_send.at[a, 0, k], turn_recv.at[a, 0, k], place.across())
                )
                launch(send(piece, piece, core_send.at[a, k], core_recv.at[a, k], place.pair()))
            block = place.block(half=1 - place.half)
            piece = part(a, block)
            arrive(piece, near_recv.at[a, 0])
            low = part(a, block, side, rest)
            for k in range(1, chips):
                launch(
                    send(
                        low,
                        low,
                        turn_send.at[a, 1, k],
                        turn_recv.at[a, 1, k],
                        place.device(chip=place.ahead(k)),
                    )
                )
            launch(
                send(piece, piece, core_send.at[a, chips], core_recv.at[a, chips], place.pair())
            )

        def turn_step(a):
            side = weight_in[a].shape[-2] // 4
            rest = weight_in[a].shape[-2] - side
            for k in range(1, chips):
                block = place.block(chip=place.behind(k), half=1 - place.half)
                arrive(part(a, block, 0, side), turn_recv.at[a, 0, k])
                arrive(part(a, block, side, rest), turn_recv.at[a, 1, k])
                piece = part(a, block)
                launch(
                    send(
                        piece,
                        piece,
                        core_send.at[a, chips + k],
                        core_recv.at[a, chips + k],
                        place.pair(),
                    )
                )

        def core_step(a):
            other = 1 - place.core
            blocks = [place.block(core=other)]
            blocks += [place.block(place.behind(k), other) for k in range(1, chips)]
            blocks += [place.block(None, other, 1 - place.half)]
            blocks += [
                place.block(place.behind(k), other, 1 - place.half) for k in range(1, chips)
            ]
            for at, block in enumerate(blocks):
                arrive(part(a, block), core_recv.at[a, at])
            pltpu.make_async_copy(weight_in[a], part(a, place.block()), keep.at[a]).wait()

        near_start(0)
        rest_width = early_width - first_width
        early = cotangent_ref.at[:, pl.ds(first_width, rest_width)]
        early_rows = cotangent_rows.at[:, pl.ds(first_width, rest_width)]
        first = cotangent_ref.at[:, pl.ds(0, first_width)]
        first_rows = cotangent_rows.at[:, pl.ds(0, first_width)]
        lines = (
            Line(place, normed_own, normed, line_send.at[0], line_recv.at[0], single.at[3]),
            Line(place, early, early_rows, line_send.at[1], line_recv.at[1], single.at[8]),
            Line(place, first, first_rows, line_send.at[2], line_recv.at[2], single.at[2]),
        )
        lines[2].start()

        vector_keep.wait()
        for at in range(len(peers)):
            place_in = at + 1
            source = place.block(
                place.behind(place_in // 4),
                (place.core + place_in // 2 % 2) % 2,
                (place.half + place_in % 2) % 2,
            )
            arrive(landed.at[source], vector_recv.at[at])
        for number in range(groups):
            vectors_out[:, number * shard : (number + 1) * shard] = landed[number]

        @pl.loop(0, own_len, step=32)
        def _(r):
            at = pl.ds(pl.multiple_of(r, 32), 32)
            values = tokens_ref[at, :].astype(f32)
            normed_own[at, :] = layer_norm(
                values, vectors_out[0:1, :], vectors_out[1:2, :]
            ).astype(bf16)

        lines[2].step(1)
        lines[0].start()
        near_start(1)
        late_keep = pltpu.make_async_copy(
            cotangent_ref.at[:, pl.ds(early_width, model - early_width)],
            cotangent_late,
            single.at[1],
        )
        late_keep.start()
        bias_ref[...] = bias_in[...].astype(f32).T
        up_bias_ref[...] = up_bias_in[...].astype(f32).reshape(1, hidden)
        turns = lax.broadcasted_iota(jnp.int32, (half_rot, 1), 0)
        inverse = jnp.zeros((half_rot, 1), f32)
        for row in range(half_rot):
            inverse = jnp.where(turns == row, 10000.0 ** (-2.0 * row / ROT), inverse)
        phase = inverse * number_in[1][...].astype(f32)
        cosine_ref[...] = jnp.cos(phase)
        sine_ref[...] = jnp.sin(phase)
        if depth > 2:
            lines[2].step(2)
        near_step(0)
        lines[0].step(1)
        for k in range(3, depth):
            lines[2].step(k)
        near_start(3)
        near_start(2)
        turn_step(0)
        near_step(1)
        for k in range(2, depth):
            lines[0].step(k)
        lines[1].start()
        lines[0].keep.wait()
        core_step(0)
        near_step(3)

        def project(weight, rows, cosine_here, sine_here, out):
            for kind in range(kinds):
                found = lax.dot_general(
                    weight[kind], rows[...], row_by_col, preferred_element_type=f32
                )
                found = found + bias_ref[:, kind : kind + 1]
                if kind == 2:
                    out[kind] = found.astype(bf16)
                    continue
                for head in range(local // HD):
                    first = head * HD
                    leading = found[first : first + half_rot]
                    trailing = found[first + half_rot : first + ROT]
                    turned = (
                        leading * cosine_here[...] - trailing * sine_here[...],
                        trailing * cosine_here[...] + leading * sine_here[...],
                        found[first + ROT : first + HD],
                    )
                    out[kind, first : first + HD] = jnp.concatenate(turned, axis=0).astype(bf16)

        tile = min(512, length)
        pltpu.emit_pipeline(
            project,
            grid=(length // tile,),
            in_specs=[
                pl.BlockSpec(weight_out[0].shape, lambda n: (0, 0, 0)),
                pl.BlockSpec((tile, model), lambda n: (n, 0)),
                pl.BlockSpec((half_rot, tile), lambda n: (0, n)),
                pl.BlockSpec((half_rot, tile), lambda n: (0, n)),
            ],
            out_specs=[pl.BlockSpec((kinds, local, tile), lambda n: (0, 0, n))],
        )(weight_out[0], normed, cosine_ref, sine_ref, triple)

        def heads(half):
            return triple.at[:, pl.ds(pl.multiple_of(half * count, count), count)]

        here, there = place.half, 1 - place.half
        launch(send(heads(there), both.at[here], single.at[4], single.at[5], place.across()))
        load = pltpu.make_async_copy(heads(here), stage, single.at[6])
        load.start()
        load.wait()
        stage_keep = pltpu.make_async_copy(stage, both.at[here], single.at[7])
        stage_keep.start()
        near_step(2)
        lines[1].step(1)
        turn_step(1)
        core_step(1)
        wide = hidden // 2
        for number in range(2):
            span = pl.ds(number * wide, wide)
            multiply(
                "nn",
                [(normed, weight_out[1].at[:, span])],
                [activation.at[:, span], slope.at[:, span]],
                lambda found, bias: gelu_and_slope(found + bias),
                [up_bias_ref.at[:, span]],
            )
            if number == 0 and depth > 2:
                lines[1].step(2)
        turn_step(3)
        core_step(3)
        turn_step(2)
        core_step(2)
        for k in range(3, depth):
            lines[1].step(k)
        lines[1].keep.wait()
        lines[2].keep.wait()
        stage_keep.wait()
        arrive(both.at[there], single.at[5])
        for number in range(len(numbers)):
            arrive(numbers_out[number], number_sems.at[1, number])
        late_keep.wait()
        for copy in pending:
            copy.wait_send()
        for run in lines:
            run.end()

    out_shape = [
        jax.ShapeDtypeStruct((8, groups * shard), f32),
        *[jax.ShapeDtypeStruct(v.shape, v.dtype) for v in numbers],
        jax.ShapeDtypeStruct((length, model), bf16),
        jax.ShapeDtypeStruct((length, early_width), bf16),
        jax.ShapeDtypeStruct((own_len, model - early_width), bf16),
    ]
    out_shape += [
        jax.ShapeDtypeStruct(v.shape[:-2] + (groups * v.shape[-2], v.shape[-1]), v.dtype)
        for v in weights
    ]
    out_shape += [
        jax.ShapeDtypeStruct((2, kinds, count, length), bf16),
        jax.ShapeDtypeStruct((length, hidden), bf16),
        jax.ShapeDtypeStruct((length, hidden), bf16),
        jax.ShapeDtypeStruct((kinds, local, length), bf16),
    ]
    results = pl.pallas_call(
        kernel,
        out_shape=tuple(out_shape),
        in_specs=[VMEM] * (4 + len(vectors) + len(numbers) + weight_count),
        out_specs=(VMEM,) * (1 + len(numbers)) + (ANY,) * (len(out_shape) - 1 - len(numbers)),
        scratch_shapes=[
            pltpu.VMEM((groups, 8, shard), f32),
            pltpu.VMEM((own_len, model), bf16),
            pltpu.VMEM((kinds, count, length), bf16),
            pltpu.VMEM((8, shard), f32),
            pltpu.VMEM((local, kinds), f32),
            pltpu.VMEM((1, hidden), f32),
            pltpu.VMEM((half_rot, length), f32),
            pltpu.VMEM((half_rot, length), f32),
            DMA((groups - 1,)),
            DMA((groups - 1,)),
            DMA((2, len(numbers))),
            DMA((9,)),
            DMA((3, 2, depth - 1)),
            DMA((3, 2, depth - 1)),
            DMA((weight_count,)),
            DMA((weight_count, chips)),
            DMA((weight_count, chips)),
            DMA((weight_count, 2, chips)),
            DMA((weight_count, 2, chips)),
            DMA((weight_count, 2 * chips)),
            DMA((weight_count, 2 * chips)),
        ],
        compiler_params=pltpu.CompilerParams(
            collective_id=0, has_side_effects=True, vmem_limit_bytes=60 << 20
        ),
        cost_estimate=pl.CostEstimate(flops=0, bytes_accessed=480_000_000, transcendentals=0),
        name="front",
    )(tokens, cotangent, *vectors, *numbers, *weights, projection_bias, up_bias)
    return results[:-1]


class Held:
    def __init__(self, sources, buffers, sems):
        self.copies = {}
        self.buffers = buffers
        for number, (source, buffer) in enumerate(zip(sources, buffers)):
            copy = pltpu.make_async_copy(source, buffer, sems.at[number])
            copy.start()
            self.copies[number] = copy

    def __getitem__(self, number):
        if number in self.copies:
            self.copies.pop(number).wait()
        return self.buffers[number]


def buffers_for(*arrays):
    return [pltpu.VMEM(v.shape, v.dtype) for v in arrays]


def exchange_middle(
    sizes, attended, activation, down_full, dense_full, cotangent_early, late_blocks, slope
):
    width, total = attended.shape
    length = total // 2
    rows, model = activation.shape[0], down_full.shape[0]
    hidden = slope.shape[1]
    depth = sizes["tp"]
    late_rows, late_width = late_blocks[0].shape
    holds = [activation, down_full, dense_full, cotangent_early, slope]

    def kernel(attended_ref, *refs):
        late_refs, refs = refs[:depth], refs[depth:]
        held_refs, refs = refs[: len(holds)], refs[len(holds) :]
        full_out, block_out, late_out, both, grad_hidden, hidden_sum = refs[:6]
        full, feed, late, made, *buffers, sems, held_sems, late_sems = refs[6:]
        place = Place(sizes)
        here, there = place.half, 1 - place.half

        def tokens(half):
            return attended_ref.at[:, pl.ds(pl.multiple_of(half * length, length), length)]

        mine = half_rows(full, here, width)
        load = pltpu.make_async_copy(tokens(here), mine, sems.at[0])
        load.start()
        held = Held(held_refs, buffers, held_sems)
        late_loads = []
        for k in range(depth):
            source = (place.layer + depth - k) % depth
            span = pl.ds(pl.multiple_of(source * late_rows, 16), late_rows)
            late_loads.append(pltpu.make_async_copy(late_refs[k], late.at[span], late_sems.at[k]))
            late_loads[-1].start()
        greet([place.across()])
        away = send(tokens(there), mine, sems.at[2], sems.at[3], place.across())
        away.start()
        multiply("nt", [(held[0], held[1])], [feed])
        load.wait()
        away.wait_send()
        came = half_rows(full, there, width)
        send(came, came, sems.at[2], sems.at[3], place.across()).wait_recv()
        full_keep = pltpu.make_async_copy(full, full_out, sems.at[4])
        full_keep.start()
        multiply(
            "tt",
            [(full, held[2])],
            [block_out],
            lambda found, before: (found + before,),
            [feed],
        )
        for copy in late_loads:
            copy.wait()
        late_keep = pltpu.make_async_copy(late, late_out, sems.at[5])
        late_keep.start()

        def parts(weight):
            first = model - late_width
            return [
                (held[3], weight.at[pl.ds(0, first)]),
                (late, weight.at[pl.ds(first, late_width)]),
            ]

        multiply("tt", [(b, a) for a, b in parts(held[2])], [made])
        away = send(
            half_rows(made, there, width), both.at[here], sems.at[6], sems.at[7], place.across()
        )
        keep = pltpu.make_async_copy(half_rows(made, here, width), both.at[here], sems.at[8])
        away.start()
        keep.start()

        def scaled(found, slope):
            found = found * slope.astype(f32)
            return found, jnp.sum(found, axis=0, keepdims=True)

        multiply("nn", parts(held[1]), [grad_hidden, hidden_sum], scaled, [held[4]])
        for copy in (keep, full_keep, late_keep):
            copy.wait()
        away.wait_send()
        came = both.at[there]
        send(came, came, sems.at[6], sems.at[7], place.across()).wait_recv()

    return pl.pallas_call(
        kernel,
        out_shape=(
            jax.ShapeDtypeStruct((2 * width, length), bf16),
            jax.ShapeDtypeStruct((rows, model), bf16),
            jax.ShapeDtypeStruct((rows, late_width), bf16),
            jax.ShapeDtypeStruct((2, width, length), bf16),
            jax.ShapeDtypeStruct((rows, hidden), bf16),
            jax.ShapeDtypeStruct((1, hidden), f32),
        ),
        in_specs=[ANY] * (1 + depth + len(holds)),
        out_specs=(ANY,) * 5 + (VMEM,),
        scratch_shapes=[
            pltpu.VMEM((2 * width, length), bf16),
            pltpu.VMEM((rows, model), f32),
            pltpu.VMEM((rows, late_width), bf16),
            pltpu.VMEM((2 * width, length), bf16),
            *buffers_for(*holds),
            DMA((9,)),
            DMA((len(holds),)),
            DMA((depth,)),
        ],
        compiler_params=pltpu.CompilerParams(
            collective_id=4, has_side_effects=True, vmem_limit_bytes=60 << 20
        ),
        cost_estimate=pl.CostEstimate(flops=0, bytes_accessed=140_000_000, transcendentals=0),
        name="exchange_middle",
    )(attended, *late_blocks, *holds)


def exchange_back(sizes, back, normed, grad_hidden, cotangents, activation, up_full, projection):
    kinds, width, total = back.shape
    length = total // 2
    chips, halves = sizes["fsdp"] // 2, sizes["ctx"]
    rows, model = normed.shape
    hidden = grad_hidden.shape[1]
    span = model // (2 * chips)
    shard = span // halves
    sides = (shard // 4, shard // 2)
    count = len(cotangents)

    def kernel(back_ref, *rest):
        held_refs, rest = rest[: 4 + count], rest[4 + count :]
        weight_ref, full_out, made, came, turns, block_in, feed = (
            rest[0],
            rest[1],
            rest[2:4],
            rest[4:6],
            rest[6:10],
            rest[10],
            rest[11],
        )
        sums, full, diagonal, stage = rest[12:16]
        normed_held, hidden_held, cotangent_held, activation_held, up_held = rest[16:21]
        held_sems, sems, stage_sems, core_send, core_recv, turn_send, turn_recv = rest[21:]
        buffers, first = [normed_held, hidden_held], 0
        for ref in held_refs[2 : 2 + count]:
            buffers.append(cotangent_held.at[:, pl.ds(first, ref.shape[1])])
            first += ref.shape[1]
        held = Held(held_refs, buffers + [activation_held, up_held], held_sems)
        place = Place(sizes)
        here, there = place.half, 1 - place.half
        other = 1 - place.core

        def tokens(half):
            return back_ref.at[:, :, pl.ds(pl.multiple_of(half * length, length), length)]

        def heads(half):
            return full.at[:, pl.ds(pl.multiple_of(half * width, width), width)]

        load = pltpu.make_async_copy(tokens(here), heads(here), sems.at[2])
        load.start()
        greet(plane(place))
        away = send(tokens(there), heads(here), sems.at[0], sems.at[1], place.across())
        away.start()

        def to_pair(number):
            copies = []
            for chip in range(chips):
                copies.append(
                    send(
                        made[number].at[pl.ds(pl.multiple_of((2 * chip + other) * span, 16), span)],
                        came[number].at[pl.ds(chip * span, span)],
                        core_send.at[number, chip],
                        core_recv.at[number, chip],
                        place.pair(),
                    )
                )
                copies[-1].start()
            return copies

        def stage_loads(number, k):
            chip = place.ahead(k)
            mine = place.block(chip, place.core, there) * shard
            theirs = (chip * halves + there) * shard
            return [
                pltpu.make_async_copy(
                    ref.at[pl.ds(pl.multiple_of(block, 16), shard)],
                    stage.at[at, k - 1],
                    stage_sems.at[at, k],
                )
                for at, (ref, block) in enumerate(((made[number], mine), (came[number], theirs)))
            ]

        def turn_load(number, copies):
            for copy in copies:
                copy.wait()
            for k in range(1, chips):
                for copy in stage_loads(number, k):
                    copy.start()

        def turn(number):
            sent = []
            step = min(64, shard)
            for k in range(1, chips):
                for copy in stage_loads(number, k):
                    copy.wait()

                @pl.loop(0, shard, step=step)
                def _(r):
                    at = pl.ds(pl.multiple_of(r, step), step)
                    diagonal[number, k - 1, at, :] = (
                        stage[0, k - 1, at, :].astype(f32) + stage[1, k - 1, at, :].astype(f32)
                    ).astype(bf16)

                for way, device in enumerate(
                    (place.across(), place.device(chip=place.ahead(k)))
                ):
                    side = sides[number]
                    part = pl.ds(0, side) if way == 0 else pl.ds(side, shard - side)
                    sent.append(
                        send(
                            diagonal.at[number, k - 1, part],
                            turns[2 * number + way].at[k - 1],
                            turn_send.at[number, way, k],
                            turn_recv.at[number, way, k],
                            device,
                        )
                    )
                    sent[-1].start()
            return sent

        multiply("tn", [(held[0], held[1])], [made[0]])
        up_copies = to_pair(0)
        for number in range(count):
            held[2 + number]
        half = hidden // 2
        for number in range(2):
            part = pl.ds(number * half, half)
            multiply(
                "tn",
                [(cotangent_held, held[2 + count].at[:, part])],
                [made[1].at[:, part]],
            )
            if number == 0:
                turn_load(0, up_copies)
                turned = turn(0)
        down_copies = to_pair(1)
        half = model // 2
        for number in range(2):
            part = pl.ds(number * half, half)
            multiply("nt", [(held[1], held[3 + count].at[part])], [feed.at[:, part]])
            if number == 0:
                turn_load(1, down_copies)
                turned += turn(1)
        load.wait()
        away.wait_send()
        send(heads(there), heads(there), sems.at[0], sems.at[1], place.across()).wait_recv()
        keep = pltpu.make_async_copy(full, full_out, sems.at[3])
        keep.start()
        ones = jnp.ones((8, length), bf16)
        for kind in range(kinds):
            total_of = lax.dot_general(ones, full[kind], contract_cols, preferred_element_type=f32)
            sums[kind : kind + 1, :] = total_of[0:1, :]

        def step(right_ref, before_ref, out_ref):
            found = before_ref[...]
            for kind in range(kinds):
                found += lax.dot_general(
                    full[kind], right_ref[kind], row_by_col, preferred_element_type=f32
                )
            out_ref[...] = found.astype(bf16)

        tile = min(512, model)
        pltpu.emit_pipeline(
            step,
            grid=(model // tile,),
            in_specs=[
                pl.BlockSpec((kinds, tile, 2 * width), lambda n: (0, n, 0)),
                pl.BlockSpec((rows, tile), lambda n: (0, n)),
            ],
            out_specs=[pl.BlockSpec((rows, tile), lambda n: (0, n))],
        )(weight_ref, feed, block_in)
        keep.wait()
        for copy in turned:
            copy.wait()

    product = jax.ShapeDtypeStruct((model, hidden), bf16)
    part = jax.ShapeDtypeStruct((model // 2, hidden), bf16)
    holds = [normed, grad_hidden, *cotangents, activation, up_full]
    results = pl.pallas_call(
        kernel,
        out_shape=(
            jax.ShapeDtypeStruct((kinds, 2 * width, length), bf16),
            product,
            product,
            part,
            part,
            *[
                jax.ShapeDtypeStruct((chips - 1, n, hidden), bf16)
                for side in sides
                for n in (side, shard - side)
            ],
            jax.ShapeDtypeStruct((rows, model), bf16),
            jax.ShapeDtypeStruct((rows, model), f32),
            jax.ShapeDtypeStruct((kinds, 2 * width), f32),
        ),
        in_specs=[ANY] * (len(holds) + 2),
        out_specs=(ANY,) * 11 + (VMEM,),
        scratch_shapes=[
            pltpu.VMEM((kinds, 2 * width, length), bf16),
            pltpu.VMEM((2, chips - 1, shard, hidden), bf16),
            pltpu.VMEM((2, chips - 1, shard, hidden), bf16),
            *buffers_for(normed, grad_hidden, normed, activation, up_full),
            DMA((len(holds),)),
            DMA((4,)),
            DMA((2, chips)),
            DMA((2, chips)),
            DMA((2, chips)),
            DMA((2, 2, chips)),
            DMA((2, 2, chips)),
        ],
        compiler_params=pltpu.CompilerParams(
            collective_id=5, has_side_effects=True, vmem_limit_bytes=60 << 20
        ),
        cost_estimate=pl.CostEstimate(flops=0, bytes_accessed=180_000_000, transcendentals=0),
        name="exchange_back",
    )(back, *holds, projection)
    full, up_made, down_made, up_came, down_came, *turned = results[:9]
    paired = [(up_made, up_came), (down_made, down_came)]
    return full, paired, turned, results[9], results[11]


def finish_all(sizes, grad, tokens, cotangent, vectors, partials, splits):
    chips, halves, depth = sizes["fsdp"] // 2, sizes["ctx"], sizes["tp"]
    groups = sizes["fsdp"] * halves
    own_len, model = tokens.shape
    shard = model // groups
    count = len(partials)
    step_rows = 64

    def kernel(grad_in, tokens_in, cotangent_in, vector_ref, *refs):
        partial_in, refs = refs[:count], refs[count:]
        input_ref, small_ref = refs[:2]
        weight_out, refs = refs[2 : 2 + count], refs[2 + count :]
        near, refs = refs[:count], refs[count:]
        grad_ref, tokens_ref, cotangent_ref, rows_sems, *refs = refs
        sums, blocks, landed, line, near_send, near_recv, load_sem, *sems = refs
        held = Held(
            (tokens_in, cotangent_in, grad_in),
            (tokens_ref, cotangent_ref, grad_ref),
            rows_sems,
        )
        block_send, block_recv, line_send, line_recv = sems
        place = Place(sizes)
        peers = place.group()
        layers = [(place.layer + k) % depth for k in range(1, depth)]
        devices = [place.device(chip=a, core=b, half=c) for a, b, c in peers]
        greet(devices + [place.device(layer=k) for k in layers])
        pending = [[], []]
        for a in range(count):
            targets = [place.across()] + [
                place.device(chip=place.ahead(k)) for k in range(1, chips)
            ]
            for piece in range(2):
                side = partials[a].shape[1] // 2
                span = pl.ds(piece * side, side)
                for at, device in enumerate(targets):
                    pending[piece].append(
                        send(
                            partial_in[a].at[at, span],
                            near[a].at[at, span],
                            near_send.at[a, piece, at],
                            near_recv.at[a, piece, at],
                            device,
                        )
                    )
                    pending[piece][-1].start()
            pltpu.make_async_copy(
                partial_in[a].at[chips], near[a].at[chips], load_sem.at[a]
            ).start()

        for number in range(3):
            held[number]
        gain = vector_ref[0:1, :]
        sums[...] = jnp.zeros_like(sums)

        @pl.loop(0, own_len, step=step_rows)
        def _(r):
            at = pl.ds(pl.multiple_of(r, step_rows), step_rows)
            values = tokens_ref[at, :].astype(f32)
            centered = values - jnp.mean(values, axis=-1, keepdims=True)
            spread = jnp.mean(centered * centered, axis=-1, keepdims=True)
            scale = lax.rsqrt(spread + epsilon)
            normal = centered * scale
            found = grad_ref[at, :].astype(f32)
            away = cotangent_ref[at, :].astype(f32)
            inner = found * gain
            mean = jnp.mean(inner, axis=-1, keepdims=True)
            along = jnp.mean(inner * normal, axis=-1, keepdims=True)
            input_ref[at, :] = (scale * (inner - mean - normal * along)).astype(bf16)
            sums[0:1, :] += jnp.sum(found * normal, axis=0, keepdims=True)
            sums[1:2, :] += jnp.sum(found, axis=0, keepdims=True)
            sums[2:3, :] += jnp.sum(away, axis=0, keepdims=True)

        for number in range(groups):
            blocks[number] = sums[:, number * shard : (number + 1) * shard]
        copies = []
        for at, (chip, core, half) in enumerate(peers):
            copies.append(
                send(
                    blocks.at[place.block(chip, core, half)],
                    landed.at[at],
                    block_send.at[at],
                    block_recv.at[at],
                    devices[at],
                )
            )
            copies[-1].start()
        total = blocks[place.block()]
        for at, copy in enumerate(copies):
            copy.wait()
            total += landed[at]
        line[0] = total
        copies = []
        for k, layer in enumerate(layers):
            copies.append(
                send(
                    line.at[0],
                    line.at[k + 1],
                    line_send.at[k],
                    line_recv.at[k],
                    place.device(layer=layer),
                )
            )
            copies[-1].start()
        for k, copy in enumerate(copies):
            copy.wait()
            total += line[k + 1]
        small_ref[...] = total

        for a in range(count):
            own = near[a].at[chips]
            pltpu.make_async_copy(own, own, load_sem.at[a]).wait()
        for piece in range(2):
            for copy in pending[piece]:
                copy.wait()
            for a in range(count):
                rows, width = partials[a].shape[1:]
                side = rows // 2
                step = min(32, side)

                @pl.loop(piece * side, (piece + 1) * side, step=step)
                def _(r, a=a, width=width, step=step):
                    at = pl.ds(pl.multiple_of(r, step), step)
                    found = near[a][0, at, :].astype(f32)
                    for number in range(1, chips + 1):
                        found += near[a][number, at, :].astype(f32)
                    if splits[a] == 1:
                        weight_out[a][at, :] = found
                    else:
                        wide = width // splits[a]
                        for kind in range(splits[a]):
                            weight_out[a][kind, at, :] = found[:, kind * wide : (kind + 1) * wide]

    out_shape = [
        jax.ShapeDtypeStruct((own_len, model), bf16),
        jax.ShapeDtypeStruct((8, shard), f32),
    ]
    for v, n in zip(partials, splits):
        rows, width = v.shape[1:]
        out_shape.append(
            jax.ShapeDtypeStruct((rows, width) if n == 1 else (n, rows, width // n), f32)
        )
    return pl.pallas_call(
        kernel,
        out_shape=tuple(out_shape),
        in_specs=[ANY] * 3 + [VMEM] + [ANY] * count,
        out_specs=(VMEM,) * len(out_shape),
        scratch_shapes=[
            *buffers_for(*partials),
            *buffers_for(grad, tokens, cotangent),
            DMA((3,)),
            pltpu.VMEM((8, model), f32),
            pltpu.VMEM((groups, 8, shard), f32),
            pltpu.VMEM((groups - 1, 8, shard), f32),
            pltpu.VMEM((depth, 8, shard), f32),
            DMA((count, 2, chips)),
            DMA((count, 2, chips)),
            DMA((count,)),
            DMA((groups - 1,)),
            DMA((groups - 1,)),
            DMA((depth - 1,)),
            DMA((depth - 1,)),
        ],
        compiler_params=pltpu.CompilerParams(
            collective_id=3, has_side_effects=True, vmem_limit_bytes=60 << 20
        ),
        cost_estimate=pl.CostEstimate(flops=0, bytes_accessed=90_000_000, transcendentals=0),
        name="finish_all",
    )(grad, tokens, cotangent, vectors, *partials)


def tile_at(number):
    return pl.ds(pl.multiple_of(number * TILE, TILE), TILE)


def allowed(kb, j, start):
    places = kb * TILE + lax.broadcasted_iota(jnp.int32, (TILE, TILE), 0)
    own = j * TILE + lax.broadcasted_iota(jnp.int32, (TILE, TILE), 1)
    return (places >= start) & (places <= own)


def attend_kernel(
    low_ref,
    mid_ref,
    triple_ref,
    start_ref,
    attended_ref,
    log_ref,
    query_t,
    key_t,
    value_t,
    key_rows,
    scores,
):
    length = triple_ref.shape[3]
    heads = triple_ref.shape[2] // HD
    score_scale = 1.0 / math.sqrt(HD)
    for number, ref in enumerate((query_t, key_t, value_t)):
        for part in range(2):
            piece = triple_ref[part, number]
            ref[:, part * length : (part + 1) * length] = (
                piece * score_scale if number == 0 else piece
            )
    rows = [slice(h * HD, (h + 1) * HD) for h in range(heads)]
    for h in range(heads):
        key_rows[h] = key_t[rows[h], :].T

    @pl.loop(0, 2 * length // TILE)
    def _(j):
        here = tile_at(j)
        start = start_ref[:, here]
        low, mid = low_ref[j], mid_ref[j]
        queries = [query_t[row, here] for row in rows]

        def score_with(masked):
            def score(kb, highest):
                ok = allowed(kb, j, start) if masked else None
                raised = []
                for h in range(heads):
                    found = jnp.dot(
                        key_rows[h, tile_at(kb), :], queries[h], preferred_element_type=f32
                    )
                    if masked:
                        found = jnp.where(ok, found, big_negative)
                    scores[h, tile_at(kb), :] = found
                    raised.append(
                        jnp.maximum(highest[h], jnp.max(found, axis=0, keepdims=True))
                    )
                return tuple(raised)

            return score

        highest = tuple(jnp.full((1, TILE), big_negative, f32) for _ in range(heads))
        highest = lax.fori_loop(low, mid, score_with(True), highest)
        highest = lax.fori_loop(mid, j, score_with(False), highest)
        highest = score_with(True)(j, highest)

        def weigh(kb, carry):
            after = []
            for h in range(heads):
                total, mixed = carry[h]
                prob = jnp.exp(scores[h, tile_at(kb), :] - highest[h])
                total = total + jnp.sum(prob, axis=0, keepdims=True)
                mixed = mixed + jnp.dot(
                    value_t[rows[h], tile_at(kb)], prob.astype(bf16), preferred_element_type=f32
                )
                after.append((total, mixed))
            return tuple(after)

        empty = tuple(
            (jnp.zeros((1, TILE), f32), jnp.zeros((HD, TILE), f32)) for _ in range(heads)
        )
        result = lax.fori_loop(low, j + 1, weigh, empty)
        for h in range(heads):
            total, mixed = result[h]
            attended_ref[rows[h], here] = (mixed / total).astype(bf16)
            log_ref[h, :, here] = highest[h] + jnp.log(total)


def turned_back(values, cosine, sine):
    half_rot = ROT // 2
    leading = values[:half_rot]
    trailing = values[half_rot:ROT]
    return jnp.concatenate(
        [
            leading * cosine + trailing * sine,
            trailing * cosine - leading * sine,
            values[ROT:],
        ],
        axis=0,
    )


def attend_back_kernel(
    low_ref,
    mid_ref,
    triple_ref,
    grad_ref,
    attended_ref,
    log_ref,
    start_ref,
    cosine_ref,
    sine_ref,
    back_ref,
    query_t,
    key_t,
    grad_t,
    key_rows,
    value_rows,
    key_sum,
    value_sum,
):
    length = triple_ref.shape[3]
    heads = triple_ref.shape[2] // HD
    score_scale = 1.0 / math.sqrt(HD)
    rows = [slice(h * HD, (h + 1) * HD) for h in range(heads)]
    for part in range(2):
        span = slice(part * length, (part + 1) * length)
        query_t[:, span] = triple_ref[part, 0] * score_scale
        key_t[:, span] = triple_ref[part, 1]
        grad_t[:, span] = grad_ref[part]
        for h in range(heads):
            value_rows[h, span, :] = triple_ref[part, 2, rows[h]].T
    for h in range(heads):
        key_rows[h] = key_t[rows[h], :].T
    key_sum[...] = jnp.zeros_like(key_sum)
    value_sum[...] = jnp.zeros_like(value_sum)

    @pl.loop(0, 2 * length // TILE)
    def _(j):
        here = tile_at(j)
        start = start_ref[:, here]
        low, mid = low_ref[j], mid_ref[j]
        queries = [query_t[row, here] for row in rows]
        grads = [grad_t[row, here] for row in rows]
        query_rows = [value.T for value in queries]
        grad_rows = [value.T for value in grads]
        logs = [log_ref[h, :, here] for h in range(heads)]
        deltas = [
            jnp.sum(
                grads[h].astype(f32) * attended_ref[rows[h], here].astype(f32),
                axis=0,
                keepdims=True,
            )
            for h in range(heads)
        ]

        def pull_with(masked):
            def pull(kb, query_back):
                ok = allowed(kb, j, start) if masked else None
                after = []
                for h in range(heads):
                    score = jnp.dot(
                        key_rows[h, tile_at(kb), :], queries[h], preferred_element_type=f32
                    )
                    if masked:
                        score = jnp.where(ok, score, big_negative)
                    prob = jnp.exp(score - logs[h])
                    down = jnp.dot(
                        value_rows[h, tile_at(kb), :], grads[h], preferred_element_type=f32
                    )
                    score_back = (prob * (down - deltas[h])).astype(bf16)
                    value_sum[h, tile_at(kb), :] += jnp.dot(
                        prob.astype(bf16), grad_rows[h], preferred_element_type=f32
                    )
                    key_sum[h, tile_at(kb), :] += jnp.dot(
                        score_back, query_rows[h], preferred_element_type=f32
                    )
                    after.append(
                        query_back[h]
                        + jnp.dot(
                            key_t[rows[h], tile_at(kb)], score_back, preferred_element_type=f32
                        )
                    )
                return tuple(after)

            return pull

        query_back = tuple(jnp.zeros((HD, TILE), f32) for _ in range(heads))
        query_back = lax.fori_loop(low, mid, pull_with(True), query_back)
        query_back = lax.fori_loop(mid, j, pull_with(False), query_back)
        query_back = pull_with(True)(j, query_back)
        for h in range(heads):
            back_ref[0, rows[h], here] = turned_back(
                query_back[h] * score_scale, cosine_ref[:, here], sine_ref[:, here]
            ).astype(bf16)

    for h in range(heads):
        back_ref[1, rows[h], :] = turned_back(
            key_sum[h].T, cosine_ref[...], sine_ref[...]
        ).astype(bf16)
        back_ref[2, rows[h], :] = value_sum[h].T.astype(bf16)


def attend(low, mid, triple, start):
    width, length = triple.shape[2], triple.shape[3]
    total, heads = 2 * length, width // HD
    area = total * total // 3 * heads
    return pl.pallas_call(
        attend_kernel,
        out_shape=(
            jax.ShapeDtypeStruct((width, total), bf16),
            jax.ShapeDtypeStruct((heads, 1, total), f32),
        ),
        in_specs=[SMEM, SMEM, VMEM, VMEM],
        out_specs=(VMEM, VMEM),
        scratch_shapes=[pltpu.VMEM((width, total), bf16)] * 3
        + [pltpu.VMEM((heads, total, HD), bf16), pltpu.VMEM((heads, total, TILE), f32)],
        compiler_params=pltpu.CompilerParams(vmem_limit_bytes=48 << 20),
        cost_estimate=pl.CostEstimate(
            flops=50 * area * HD, bytes_accessed=8 * width * total, transcendentals=area
        ),
        name="attend",
    )(low, mid, triple, start)


def attend_back(low, mid, triple, grad, attended, log_sum, start, cosine, sine):
    width, length = triple.shape[2], triple.shape[3]
    total, heads = 2 * length, width // HD
    area = total * total // 3 * heads
    return pl.pallas_call(
        attend_back_kernel,
        out_shape=jax.ShapeDtypeStruct((3, width, total), bf16),
        in_specs=[SMEM, SMEM] + [VMEM] * 7,
        out_specs=VMEM,
        scratch_shapes=[pltpu.VMEM((width, total), bf16)] * 3
        + [pltpu.VMEM((heads, total, HD), bf16)] * 2
        + [pltpu.VMEM((heads, total, HD), f32)] * 2,
        compiler_params=pltpu.CompilerParams(vmem_limit_bytes=48 << 20),
        cost_estimate=pl.CostEstimate(
            flops=100 * area * HD, bytes_accessed=12 * width * total, transcendentals=area
        ),
        name="attend_back",
    )(low, mid, triple, grad, attended, log_sum, start, cosine, sine)


def rotate_rows(values, cosine, sine):
    half_rot = ROT // 2
    leading = values[:, :half_rot]
    trailing = values[:, half_rot:ROT]
    return jnp.concatenate(
        [
            leading * cosine - trailing * sine,
            trailing * cosine + leading * sine,
            values[:, ROT:],
        ],
        axis=1,
    )


def ordered(*values):
    return lax.optimization_barrier(values)


def body(
    sizes,
    tokens,
    segments,
    positions,
    norm_gain,
    norm_bias,
    projection_weight,
    projection_bias,
    dense_weight,
    dense_bias,
    up_weight,
    up_bias,
    down_weight,
    down_bias,
    cotangent,
):
    own_len, model_width = tokens.shape[1], tokens.shape[2]
    half_len = segments.shape[1]
    local_width = projection_weight.shape[2]
    hidden_width = up_weight.shape[1]
    shard_rows = norm_gain.shape[0]
    half = lax.axis_index("ctx")
    total_len = 2 * half_len

    numbers = [segments, positions]
    (
        vectors_full,
        segments_other,
        positions_other,
        normed,
        cotangent_early,
        cotangent_late,
        projection,
        up_full,
        dense_full,
        down_full,
        both,
        activation,
        slope,
    ) = front(
        sizes,
        tokens[0],
        cotangent[0],
        [norm_gain, norm_bias, dense_bias, down_bias],
        numbers,
        [projection_weight.transpose(1, 0, 2), up_weight, dense_weight, down_weight],
        projection_bias,
        up_bias,
    )

    def in_order(own, other, axis):
        return jnp.where(
            half == 0,
            jnp.concatenate([own, other], axis=axis),
            jnp.concatenate([other, own], axis=axis),
        )

    segment_row = in_order(segments[0], segments_other[0], 0)
    position_row = in_order(positions[0], positions_other[0], 0)
    places = jnp.arange(total_len, dtype=jnp.int32)
    edges = jnp.concatenate([jnp.ones((1,), bool), segment_row[1:] != segment_row[:-1]])
    start = lax.cummax(jnp.where(edges, places, 0))
    tile_count = total_len // TILE
    low = start[::TILE] // TILE
    mid = jnp.minimum(
        jnp.maximum((start[TILE - 1 :: TILE] + TILE - 1) // TILE, low),
        jnp.arange(tile_count, dtype=jnp.int32),
    )
    exponent = jnp.arange(ROT // 2, dtype=f32) * 2.0 / ROT
    phase_angle = (10000.0 ** (-exponent))[:, None] * position_row.astype(f32)[None, :]
    cosine_full, sine_full = jnp.cos(phase_angle), jnp.sin(phase_angle)
    depth = sizes["tp"]
    late_blocks = [cotangent_late] + [
        lax.ppermute(cotangent_late, "tp", [(z, (z + k) % depth) for z in range(depth)])
        for k in range(1, depth)
    ]
    attended_heads, log_sum = attend(low, mid, both, start[None, :])
    attended, block_out, cotangent_late, grad_both, grad_hidden, hidden_sum = exchange_middle(
        sizes,
        attended_heads,
        activation,
        down_full,
        dense_full,
        cotangent_early,
        late_blocks,
        slope,
    )
    cotangents = [cotangent_early, cotangent_late]
    branch_own = lax.psum_scatter(block_out, "tp", scatter_dimension=0, tiled=True)
    back_heads = attend_back(
        low,
        mid,
        both,
        grad_both,
        attended_heads,
        log_sum,
        start[None, :],
        cosine_full,
        sine_full,
    )
    grad_projected, paired, turned, block_in, projected_sum = exchange_back(
        sizes, back_heads, normed, grad_hidden, cotangents, activation, up_full, projection
    )
    grad_projected = grad_projected.reshape(3 * local_width, half_len)
    block_in, branch_own = ordered(block_in, branch_own)
    grad_normed_own = lax.psum_scatter(block_in, "tp", scatter_dimension=0, tiled=True)
    up_part, down_part, dense_part, hidden_total, projected_total, partial = reduce(
        sizes,
        paired,
        turned,
        [(cotangents, attended), ([normed], grad_projected)],
        [hidden_sum, projected_sum],
        2,
        "reduce_weights",
    )
    input_part, totals, projection_part = finish_all(
        sizes,
        grad_normed_own,
        tokens[0],
        cotangent[0],
        vectors_full,
        [partial],
        [3],
    )
    bias_dense, bias_down = vectors_full[2], vectors_full[3]
    layer_output = (
        tokens[0].astype(f32) + branch_own.astype(f32) + (bias_dense + bias_down)
    ).astype(bf16)
    input_grad = cotangent[0].astype(f32) + input_part.astype(f32)
    return (
        layer_output[None],
        input_grad[None],
        totals[0],
        totals[1],
        projection_part.transpose(1, 0, 2),
        projected_total,
        dense_part,
        totals[2],
        up_part,
        hidden_total[0],
        down_part,
        totals[2],
    )


def solution(mesh):
    placed = (
        P("fsdp", ("ctx", "tp"), None),
        P("fsdp", "ctx"),
        P("fsdp", "ctx"),
        P(("fsdp", "ctx")),
        P(("fsdp", "ctx")),
        P(("fsdp", "ctx"), None, "tp"),
        P(None, "tp"),
        P(("fsdp", "ctx"), "tp"),
        P(("fsdp", "ctx")),
        P(("fsdp", "ctx"), "tp"),
        P("tp"),
        P(("fsdp", "ctx"), "tp"),
        P(("fsdp", "ctx")),
        P("fsdp", ("ctx", "tp"), None),
    )
    return jax.shard_map(
        functools.partial(body, dict(mesh.shape)),
        mesh=mesh,
        in_specs=placed,
        out_specs=(
            P("fsdp", ("ctx", "tp"), None),
            P("fsdp", ("ctx", "tp"), None),
            P(("fsdp", "ctx")),
            P(("fsdp", "ctx")),
            P(("fsdp", "ctx"), None, "tp"),
            P(None, "tp"),
            P(("fsdp", "ctx"), "tp"),
            P(("fsdp", "ctx")),
            P(("fsdp", "ctx"), "tp"),
            P("tp"),
            P(("fsdp", "ctx"), "tp"),
            P(("fsdp", "ctx")),
        ),
        check_vma=False,
    )
```
